32 devices in a mesh: ctx: 8 (over z, core), fsdp: 4 (over y, x).
Axes of the slice: x: 2, y: 2, z: 4, core: 2. Of those that a mesh axis runs over, the one named last changes fastest.
Arguments:
- tokens: bfloat16 [4, 1536, 2048], P('fsdp', 'ctx'), may hold values from -6 to 6
- query_weight: bfloat16 [2048, 2048], P('fsdp'), may hold values from -0.125 to 0.125
- key_weight: bfloat16 [2048, 1024], P('fsdp'), may hold values from -0.125 to 0.125
- value_weight: bfloat16 [2048, 1024], P('fsdp'), may hold values from -0.125 to 0.125
- output_weight: bfloat16 [2048, 2048], P(None, 'fsdp'), may hold values from -2 to 2
- first_gain: bfloat16 [2048], P('fsdp'), may hold values from 0.099609375 to 1.8984375
- gate_weight: bfloat16 [2048, 8192], P('fsdp'), may hold values from -0.125 to 0.125
- up_weight: bfloat16 [2048, 8192], P('fsdp'), may hold values from -0.125 to 0.125
- down_weight: bfloat16 [8192, 2048], P(None, 'fsdp'), may hold values from -0.0625 to 0.0625
- second_gain: bfloat16 [2048], P('fsdp'), may hold values from 0.099609375 to 1.8984375
- cotangent: bfloat16 [4, 1536, 2048], P('fsdp', 'ctx'), may hold values from -6 to 6
- block_ids: int32 [4, 1536], replicated, may hold values from 0 to 5, never falling along the last dimension, each value on 1 to 512 neighbouring positions
- piece_order: int32 [8], replicated, may hold values from 0 to 7, each once
Outputs:
- output: bfloat16 [4, 1536, 2048], P('fsdp', 'ctx')
- tokens_grad: float32 [4, 1536, 2048], P('fsdp', 'ctx')
- query_weight_grad: float32 [2048, 2048], P('fsdp')
- key_weight_grad: float32 [2048, 1024], P('fsdp')
- value_weight_grad: float32 [2048, 1024], P('fsdp')
- output_weight_grad: float32 [2048, 2048], P(None, 'fsdp')
- first_gain_grad: float32 [2048], P('fsdp')
- gate_weight_grad: float32 [2048, 8192], P('fsdp')
- up_weight_grad: float32 [2048, 8192], P('fsdp')
- down_weight_grad: float32 [8192, 2048], P(None, 'fsdp')
- second_gain_grad: float32 [2048], P('fsdp')
The draws below stay inside these ranges and needn't reach their ends.
Inputs may be any that keep to these rules, and one draw needn't show every extreme that they name: `block_ids`: along each sequence by position the block never falls; each block holds 1 to 512 positions, some block exactly 512; every block number up to the largest is used. `piece_order`: names every ctx index once.
All inputs are finite; a program needn't handle non-finite values.
Results may differ from the reference program's by a relative error of at most 0.025.
Values may be sent and summed in bfloat16 or wider, within the bound.
A program may use at most 896 MiB of HBM per device.

```python
import math
import jax
import jax.numpy as jnp
import numpy as np
from jax import lax

D = 2048
H = 8
KVH = 4
HD = 256
FF = 8192
LOCAL = 192
BLOCK = 256
SEQ = 1536
SEQS = 4
N_CTX = 8


def strengthened(array, own_key, source, target, blocks, factor):
    def block_of(dim):
        return (jnp.arange(array.shape[dim]) // (array.shape[dim] // blocks)).reshape((-1,) + (1,) * (array.ndim - 1 - dim))

    near = jax.random.permutation(own_key, blocks)[block_of(target)]
    other_side = (block_of(target) + blocks // 2) % blocks
    return jnp.where((block_of(source) == near) | (block_of(source) == other_side), factor * array, array)


def steps_of(own_key, dims, pieces, smallest, high):
    def one(axis_at, shards_of):
        draws = jax.random.uniform(jax.random.fold_in(jax.random.fold_in(own_key, 6), axis_at), (shards_of,), jnp.float32, smallest / len(pieces), high / len(pieces))
        return jnp.repeat(jnp.exp(draws), dims[axis_at] // shards_of).reshape((-1,) + (1,) * (len(dims) - axis_at - 1))

    gain = one(*pieces[0])
    for cut in pieces[1:]:
        gain = gain * one(*cut)
    return gain


def profile(count, total, bound, slope):
    loads = [(1 << 20) // math.isqrt(rank ** slope) + 1 for rank in range(2, count + 1)]
    surplus, counts = total - bound - (count - 1), [1] * (count - 1)
    while surplus > 0:
        candidates = [i for i in range(count - 1) if counts[i] < bound]
        whole, budget = sum([loads[i] for i in candidates]), surplus
        for i in candidates:
            addition = min(bound - counts[i], max(1, budget * loads[i] // whole), surplus)
            counts[i] = counts[i] + addition
            surplus = surplus - addition
    return np.array([bound] + counts)


def ragged(key, amount, total, reach, slope):
    if amount == 2:
        one = jax.random.randint(key, (), max(1, total - reach), min(reach, total - 1) + 1)
        return jnp.stack([one, total - one])
    tallies = jnp.asarray(profile(amount, total, reach, slope), jnp.int32)
    couples = (amount - 1) // 2
    giver, taker = tallies[1:1 + 2 * couples:2], tallies[2:2 + 2 * couples:2]
    room = jnp.minimum(giver - 1, reach - taker)
    passed = jax.random.randint(jax.random.fold_in(key, 1), (couples,), 0, 1 << 20) % (room + 1)
    tallies = tallies.at[1:1 + 2 * couples:2].set(giver - passed).at[2:2 + 2 * couples:2].set(taker + passed)
    return tallies[jax.random.permutation(jax.random.fold_in(key, 2), amount)]


def scatter_about(key, shape, deviation, most, shards=(), kind=jnp.bfloat16):
    drawn = deviation * jax.random.normal(key, shape, jnp.float32)
    if shards:
        drawn = drawn * steps_of(key, shape, shards, -0.22, 0.18)
    return jnp.clip(drawn, -most, most).astype(kind)


def bell_draw_with(own_key, shape, width, limit, cuts, heavy, held_as=jnp.bfloat16):
    values = width * jax.random.normal(own_key, shape, jnp.float32)
    if cuts:
        values = values * steps_of(own_key, shape, cuts, -0.22, 0.18)
    return jnp.clip(strengthened(values, jax.random.fold_in(own_key, 3), *heavy), -limit, limit).astype(held_as)


def setup_inputs(seed: int = 0) -> dict:
    arg_keys = jax.random.split(jax.random.key(seed), 14)
    tokens = scatter_about(arg_keys[0], (SEQS, SEQ, D), 1.0, 6.0, ((0, 4), (1, 8)))
    query_weight = scatter_about(arg_keys[1], (D, H * HD), D ** -0.5, 0.125, ((0, 4),))
    key_weight = scatter_about(arg_keys[2], (D, KVH * HD), D ** -0.5, 0.125, ((0, 4),))
    value_weight = scatter_about(arg_keys[3], (D, KVH * HD), D ** -0.5, 0.125, ((0, 4),))
    output_weight = scatter_about(arg_keys[4], (H * HD, D), (max(1, H * HD * 8 // SEQ)) ** -0.5, 2.0, ((1, 4),))
    first_gain = jnp.clip(1.0 + 0.18 * jax.random.normal(arg_keys[5], (D,), jnp.float32), 0.099609375, 1.8984375).astype(jnp.bfloat16)
    gate_weight = scatter_about(arg_keys[6], (D, FF), D ** -0.5, 0.125, ((0, 4),))
    up_weight = scatter_about(arg_keys[7], (D, FF), D ** -0.5, 0.125, ((0, 4),))
    down_weight = scatter_about(arg_keys[8], (FF, D), FF ** -0.5, 0.0625, ((1, 4),))
    second_gain = jnp.clip(1.0 + 0.18 * jax.random.normal(arg_keys[9], (D,), jnp.float32), 0.099609375, 1.8984375).astype(jnp.bfloat16)
    cotangent = bell_draw_with(arg_keys[10], (SEQS, SEQ, D), 1.0, 6.0, ((0, 4), (1, 8)), (1, 2, 8, 2.0))
    block_ids = jax.vmap(lambda own: jnp.searchsorted(jnp.cumsum(ragged(own, SEQ // BLOCK, SEQ, 2 * BLOCK, 1)), jnp.arange(SEQ), side="right"))(jax.random.split(arg_keys[11], SEQS)).reshape((SEQS, SEQ)).astype(jnp.int32)
    piece_order = jax.random.permutation(arg_keys[12], N_CTX).astype(jnp.int32)
    return dict(tokens=tokens, query_weight=query_weight, key_weight=key_weight, value_weight=value_weight, output_weight=output_weight, first_gain=first_gain, gate_weight=gate_weight, up_weight=up_weight, down_weight=down_weight, second_gain=second_gain, cotangent=cotangent, block_ids=block_ids, piece_order=piece_order)


@jax.custom_vjp
def low(v):
    return lax.optimization_barrier(v.astype(jnp.bfloat16)).astype(jnp.float32)

@jax.custom_vjp
def low_back(v):
    return v

def low_keep(v):
    return (low(v), None)

def low_pass(kept, grad):
    return (grad,)

def back_keep(v):
    return (v, None)

def back_low(kept, grad):
    return (low(grad),)
low.defvjp(low_keep, low_pass)
low_back.defvjp(back_keep, back_low)
epsilon = 1e-06
theta = 1000042.0
masked_score = -1e+30
highest = lax.Precision.HIGHEST

def rope_tables(positions):
    half = HD // 2
    frequency = theta ** (-(jnp.arange(half, dtype=jnp.float32) * 2.0 / HD))
    angle = positions[:, None] * frequency[None, :]
    angle = jnp.concatenate([angle, angle], axis=-1)
    return (jnp.cos(angle), jnp.sin(angle))

def rotate(values, cosine, sine):
    half = values.shape[-1] // 2
    turned = jnp.concatenate([-values[..., half:], values[..., :half]], axis=-1)
    return values * cosine[:, None, :] + turned * sine[:, None, :]

def rms_factor(values):
    return lax.rsqrt(lax.optimization_barrier(jnp.mean(values * values, axis=-1, keepdims=True)) + epsilon)

def attend(query, keys, values, block_rows):
    group = H // KVH
    span = math.gcd(SEQ, 512)
    count = SEQ // span

    def one_block(index):
        sequence_index = index // count
        first = index % count * span
        picked = lax.dynamic_index_in_dim(query, sequence_index, 0, keepdims=False)
        picked = lax.dynamic_slice_in_dim(picked, first, span, 0).reshape(span, KVH, group, HD)
        key_rows = lax.dynamic_index_in_dim(keys, sequence_index, 0, keepdims=False)
        value_rows = lax.dynamic_index_in_dim(values, sequence_index, 0, keepdims=False)
        id_rows = lax.dynamic_index_in_dim(block_rows, sequence_index, 0, keepdims=False)
        query_ids = lax.dynamic_slice_in_dim(id_rows, first, span)
        allowed = id_rows[None, :] <= query_ids[:, None]
        scores = jnp.einsum('qhgd,khd->hgqk', picked, key_rows, precision=highest) * HD ** (-0.5)
        scores = low_back(scores)
        scores = jnp.where(allowed, scores, masked_score)
        top = lax.optimization_barrier(jnp.max(scores, axis=-1, keepdims=True))
        raised = jnp.exp(scores - top)
        shares = low(raised / lax.optimization_barrier(jnp.sum(raised, axis=-1, keepdims=True)))
        mixed = jnp.einsum('hgqk,khd->qhgd', shares, value_rows, precision=highest)
        return mixed.reshape(span, H * HD)
    blocks = lax.map(jax.checkpoint(one_block), jnp.arange(SEQS * count, dtype=jnp.int32))
    return blocks.reshape(SEQS * SEQ, H * HD)

def layer(inputs, query_weight, key_weight, value_weight, output_weight, first_gain, gate_weight, up_weight, down_weight, second_gain, positions, block_rows):
    flat = inputs.reshape(SEQS * SEQ, D)
    cosine, sine = rope_tables(positions)
    normed = low(flat * rms_factor(flat) * first_gain)
    query = low_back(jnp.dot(normed, query_weight, precision=highest)).reshape(SEQS, SEQ, H, HD)
    query = low(rotate(query, cosine, sine))
    keys = low_back(jnp.dot(normed, key_weight, precision=highest)).reshape(SEQS, SEQ, KVH, HD)
    keys = low(rotate(keys, cosine, sine))
    values = low(low_back(jnp.dot(normed, value_weight, precision=highest))).reshape(SEQS, SEQ, KVH, HD)
    attended = low(low_back(attend(query, keys, values, block_rows)))
    middle = flat + low_back(jnp.dot(attended, output_weight, precision=highest))
    normed_two = low(middle * rms_factor(middle) * second_gain)
    gate = low_back(jnp.dot(normed_two, gate_weight, precision=highest))
    up = low_back(jnp.dot(normed_two, up_weight, precision=highest))
    hidden = low(jax.nn.silu(gate) * up)
    result = middle + low_back(jnp.dot(hidden, down_weight, precision=highest))
    return result.reshape(SEQS, SEQ, D)

def reference(tokens, query_weight, key_weight, value_weight, output_weight, first_gain, gate_weight, up_weight, down_weight, second_gain, cotangent, block_ids, piece_order):
    slots = jnp.arange(SEQ, dtype=jnp.int32)
    places = (piece_order[slots // LOCAL] * LOCAL + slots % LOCAL).astype(jnp.int32)
    positions = places.astype(jnp.float32)
    block_rows = block_ids[:, places]
    params = [matrix.astype(jnp.float32) for matrix in (tokens, query_weight, key_weight, value_weight, output_weight, first_gain, gate_weight, up_weight, down_weight, second_gain)]

    def forward(*inputs):
        return layer(*inputs, positions, block_rows)
    result, pullback = jax.vjp(forward, *params)
    grads = pullback(cotangent.astype(jnp.float32))
    return (result.astype(jnp.bfloat16), grads[0], grads[1], grads[2], grads[3], grads[4], grads[5], grads[6], grads[7], grads[8], grads[9])
```

```python
import functools

import jax
import jax.numpy as jnp
from jax import lax
from jax.experimental import pallas as pl
from jax.experimental.pallas import tpu as pltpu
from jax.sharding import PartitionSpec as P

H = 8
KVH = 4
HD = 256


epsilon = 1e-06
theta = 1000042.0
masked_score = -1e30


def passed_along(value, axis, by):
    devices = lax.axis_size(axis)
    return lax.ppermute(value, axis, [(i, (i + by) % devices) for i in range(devices)])


def rope_tables(positions):
    half = HD // 2
    frequency = theta ** (-(jnp.arange(half, dtype=jnp.float32) * 2.0 / HD))
    angle = positions[:, None] * frequency[None, :]
    angle = jnp.concatenate([angle, angle], axis=-1)
    return (jnp.cos(angle), jnp.sin(angle))


def rotate(values, cosine, sine):
    half = values.shape[-1] // 2
    turned = jnp.concatenate([-values[..., half:], values[..., :half]], axis=-1)
    return values * cosine[:, None, :] + turned * sine[:, None, :]


def rotate_back(grads, cosine, sine):
    half = grads.shape[-1] // 2
    scaled = grads * sine[:, None, :]
    turned = jnp.concatenate([scaled[..., half:], -scaled[..., :half]], axis=-1)
    return grads * cosine[:, None, :] + turned


def split_heads(block):
    count = block.shape[0]
    key_cols = KVH * HD
    key_part = block[:, :key_cols].reshape(count, KVH, HD).transpose(1, 0, 2)
    value_part = block[:, key_cols:].reshape(count, KVH, HD).transpose(1, 0, 2)
    return (key_part, value_part)


def merge_heads(grouped):
    return grouped.transpose(1, 0, 2).reshape(grouped.shape[1], KVH * HD)


def weight_terms(lefts, rights):
    pieces = []
    for index in range(4):
        column = lefts[index]
        pieces.append(
            jnp.einsum("tc,tn->cn", column, rights[index], preferred_element_type=jnp.float32)
        )
    return jnp.concatenate(pieces, axis=1)


def ring_layer(
    tokens,
    query_weight,
    key_weight,
    value_weight,
    output_weight,
    first_gain,
    gate_weight,
    up_weight,
    down_weight,
    second_gain,
    cotangent,
    block_ids,
    piece_order,
):
    ctx_count = lax.axis_size("ctx")
    fsdp_count = lax.axis_size("fsdp")
    here = lax.axis_index("ctx")
    rows = tokens.shape[1]
    width = tokens.shape[2]
    group = H // KVH
    query_cols = H * HD
    key_cols = KVH * HD
    hidden_cols = gate_weight.shape[1]
    scale = HD ** (-0.5)
    whole_query, whole_key, whole_value, whole_output, gain_one = (
        lax.all_gather(query_weight, "fsdp", axis=0, tiled=True),
        lax.all_gather(key_weight, "fsdp", axis=0, tiled=True),
        lax.all_gather(value_weight, "fsdp", axis=0, tiled=True),
        lax.all_gather(output_weight, "fsdp", axis=1, tiled=True),
        lax.all_gather(first_gain, "fsdp", axis=0, tiled=True),
    )
    id_row = lax.dynamic_index_in_dim(block_ids, lax.axis_index("fsdp"), 0, keepdims=False)
    start_own = lax.dynamic_index_in_dim(piece_order, here, 0, keepdims=False) * rows
    offsets = jnp.arange(rows, dtype=jnp.int32)
    cosine, sine = rope_tables((start_own + offsets).astype(jnp.float32))
    own_ids = lax.dynamic_slice_in_dim(id_row, start_own, rows)
    query_ids = jnp.tile(own_ids, group)

    def visible(source):
        key_start = lax.dynamic_index_in_dim(piece_order, source, 0, keepdims=False) * rows
        key_ids = lax.dynamic_slice_in_dim(id_row, key_start, rows)
        return key_ids[None, :] <= query_ids[:, None]

    inputs = tokens[0].astype(jnp.float32)
    scale_one = lax.rsqrt(jnp.mean(inputs * inputs, axis=-1, keepdims=True) + epsilon)
    unit_one = inputs * scale_one
    normed = (unit_one * gain_one.astype(jnp.float32)).astype(jnp.bfloat16)
    query = jnp.dot(normed, whole_query, preferred_element_type=jnp.float32).reshape(rows, H, HD)
    query_rot = rotate(query, cosine, sine).astype(jnp.bfloat16)
    keys = jnp.dot(normed, whole_key, preferred_element_type=jnp.float32).reshape(rows, KVH, HD)
    keys_rot = rotate(keys, cosine, sine).astype(jnp.bfloat16).reshape(rows, key_cols)
    values = jnp.dot(normed, whole_value, preferred_element_type=jnp.float32).astype(jnp.bfloat16)
    key_value = jnp.concatenate([keys_rot, values], axis=-1)
    grouped = (
        query_rot.reshape(rows, KVH, group, HD).transpose(1, 2, 0, 3).reshape(KVH, group * rows, HD)
    )

    def forward_step(state, block, source):
        running, total, weighted = state
        key_part, value_part = split_heads(block)
        allowed = visible(source)
        scores = (
            jnp.einsum("hqd,hkd->hqk", grouped, key_part, preferred_element_type=jnp.float32)
            * scale
        )
        scores = jnp.where(allowed[None], scores, masked_score)
        newest = jnp.maximum(running, jnp.max(scores, axis=-1))
        factor = jnp.exp(running - newest)
        shares = jnp.where(allowed[None], jnp.exp(scores - newest[..., None]), 0.0)
        total = total * factor + jnp.sum(shares, axis=-1)
        weighted = weighted * factor[..., None] + jnp.einsum(
            "hqk,hkd->hqd",
            shares.astype(jnp.bfloat16),
            value_part,
            preferred_element_type=jnp.float32,
        )
        return (newest, total, weighted)

    start_state = (
        jnp.full((KVH, group * rows), masked_score, jnp.float32),
        jnp.zeros((KVH, group * rows), jnp.float32),
        jnp.zeros((KVH, group * rows, HD), jnp.float32),
    )
    state = forward_step(start_state, key_value, here)

    def forward_turn(turn, carry):
        block, inner = carry
        block = passed_along(block, "ctx", 1)
        source = (here - turn) % ctx_count
        return (block, forward_step(inner, block, source))

    passed_block, state = lax.fori_loop(1, ctx_count, forward_turn, (key_value, state))
    running, total, weighted = state
    attended = weighted / total[..., None]
    log_total = running + jnp.log(total)
    attended_low = (
        attended.reshape(KVH, group, rows, HD)
        .transpose(2, 0, 1, 3)
        .reshape(rows, query_cols)
        .astype(jnp.bfloat16)
    )
    middle = inputs + jnp.dot(attended_low, whole_output, preferred_element_type=jnp.float32)
    gain_two, whole_gate, whole_up, whole_down = (
        lax.all_gather(second_gain, "fsdp", axis=0, tiled=True),
        lax.all_gather(gate_weight, "fsdp", axis=0, tiled=True),
        lax.all_gather(up_weight, "fsdp", axis=0, tiled=True),
        lax.all_gather(down_weight, "fsdp", axis=1, tiled=True),
    )
    scale_two = lax.rsqrt(jnp.mean(middle * middle, axis=-1, keepdims=True) + epsilon)
    unit_two = middle * scale_two
    normed_two = (unit_two * gain_two.astype(jnp.float32)).astype(jnp.bfloat16)
    gate = jnp.dot(normed_two, whole_gate, preferred_element_type=jnp.float32)
    up = jnp.dot(normed_two, whole_up, preferred_element_type=jnp.float32)
    sigmoid_gate = jax.nn.sigmoid(gate)
    activated = gate * sigmoid_gate
    hidden = (activated * up).astype(jnp.bfloat16)
    result = middle + jnp.dot(hidden, whole_down, preferred_element_type=jnp.float32)
    output = result.astype(jnp.bfloat16)[None]
    upstream = cotangent[0]
    hidden_grad = jnp.einsum("tm,fm->tf", upstream, whole_down, preferred_element_type=jnp.float32)
    gate_grad = (hidden_grad * up * sigmoid_gate * (1.0 + gate * (1.0 - sigmoid_gate))).astype(
        jnp.bfloat16
    )
    up_grad = (hidden_grad * activated).astype(jnp.bfloat16)
    normed_two_grad = jnp.einsum(
        "tf,mf->tm", gate_grad, whole_gate, preferred_element_type=jnp.float32
    ) + jnp.einsum("tf,mf->tm", up_grad, whole_up, preferred_element_type=jnp.float32)
    gain_two_term = jnp.sum(normed_two_grad * unit_two, axis=0)
    unit_two_grad = normed_two_grad * gain_two.astype(jnp.float32)
    middle_grad = upstream.astype(jnp.float32) + scale_two * (
        unit_two_grad - unit_two * jnp.mean(unit_two_grad * unit_two, axis=-1, keepdims=True)
    )
    branch_grad = middle_grad.astype(jnp.bfloat16)
    attended_grad = jnp.einsum(
        "tm,cm->tc", branch_grad, whole_output, preferred_element_type=jnp.float32
    ).astype(jnp.bfloat16)
    grad_grouped = (
        attended_grad.reshape(rows, KVH, group, HD)
        .transpose(1, 2, 0, 3)
        .reshape(KVH, group * rows, HD)
    )
    delta = jnp.sum(grad_grouped.astype(jnp.float32) * attended, axis=-1)

    def backward_step(query_total, block, source):
        key_part, value_part = split_heads(block)
        allowed = visible(source)
        scores = (
            jnp.einsum("hqd,hkd->hqk", grouped, key_part, preferred_element_type=jnp.float32)
            * scale
        )
        scores = jnp.where(allowed[None], scores, masked_score)
        shares = jnp.where(allowed[None], jnp.exp(scores - log_total[..., None]), 0.0)
        value_grad = jnp.einsum(
            "hqk,hqd->hkd",
            shares.astype(jnp.bfloat16),
            grad_grouped,
            preferred_element_type=jnp.float32,
        )
        share_grad = jnp.einsum(
            "hqd,hkd->hqk", grad_grouped, value_part, preferred_element_type=jnp.float32
        )
        score_grad = (shares * (share_grad - delta[..., None])).astype(jnp.bfloat16)
        query_total = query_total + jnp.einsum(
            "hqk,hkd->hqd", score_grad, key_part, preferred_element_type=jnp.float32
        )
        key_grad = (
            jnp.einsum("hqk,hqd->hkd", score_grad, grouped, preferred_element_type=jnp.float32)
            * scale
        )
        return (
            query_total,
            jnp.concatenate([merge_heads(key_grad), merge_heads(value_grad)], axis=-1),
        )

    query_total, first_grad = backward_step(
        jnp.zeros((KVH, group * rows, HD), jnp.float32), key_value, here
    )
    held = first_grad

    def backward_turn(turn, carry):
        block, kept, total_query = carry
        block = passed_along(block, "ctx", 1)
        source = (here - turn) % ctx_count
        total_query, block_grad = backward_step(total_query, block, source)
        kept = passed_along(kept.astype(jnp.bfloat16), "ctx", 1).astype(kept.dtype) + block_grad
        return (block, kept, total_query)

    passed_again, held, query_total = lax.fori_loop(
        1, ctx_count, backward_turn, (key_value, held, query_total)
    )
    own_grad = passed_along(held.astype(jnp.bfloat16), "ctx", 1).astype(held.dtype)
    query_rot_grad = (
        (query_total * scale)
        .reshape(KVH, group, rows, HD)
        .transpose(2, 0, 1, 3)
        .reshape(rows, H, HD)
    )
    query_grad = (
        rotate_back(query_rot_grad, cosine, sine).reshape(rows, query_cols).astype(jnp.bfloat16)
    )
    key_grad = (
        rotate_back(own_grad[:, :key_cols].reshape(rows, KVH, HD), cosine, sine)
        .reshape(rows, key_cols)
        .astype(jnp.bfloat16)
    )
    value_grad = own_grad[:, key_cols:].astype(jnp.bfloat16)
    normed_grad = jnp.einsum(
        "tc,mc->tm", query_grad, whole_query, preferred_element_type=jnp.float32
    )
    normed_grad = normed_grad + jnp.einsum(
        "tc,mc->tm", key_grad, whole_key, preferred_element_type=jnp.float32
    )
    normed_grad = normed_grad + jnp.einsum(
        "tc,mc->tm", value_grad, whole_value, preferred_element_type=jnp.float32
    )
    gain_one_term = jnp.sum(normed_grad * unit_one, axis=0)
    unit_one_grad = normed_grad * gain_one.astype(jnp.float32)
    tokens_grad = middle_grad + scale_one * (
        unit_one_grad - unit_one * jnp.mean(unit_one_grad * unit_one, axis=-1, keepdims=True)
    )
    projected = jnp.concatenate([query_grad, key_grad, value_grad], axis=-1)
    gate_up = jnp.concatenate([gate_grad, up_grad], axis=-1)
    lefts = jnp.stack([normed, branch_grad, normed_two, upstream])
    rights = (projected, attended_low, gate_up, hidden)
    piece = lax.psum_scatter(
        weight_terms(lefts, rights).astype(jnp.bfloat16), "fsdp", scatter_dimension=0, tiled=True
    )
    shard = lax.psum(piece, "ctx").astype(jnp.float32)
    gain_one_sum, gain_two_sum = lax.psum((gain_one_term, gain_two_term), ("ctx", "fsdp"))
    own_rows = width // fsdp_count
    own_start = lax.axis_index("fsdp") * own_rows
    value_begin = query_cols + key_cols
    output_begin = value_begin + key_cols
    gate_begin = output_begin + query_cols
    up_begin = gate_begin + hidden_cols
    down_begin = up_begin + hidden_cols
    return (
        output,
        tokens_grad[None],
        shard[:, :query_cols],
        shard[:, query_cols:value_begin],
        shard[:, value_begin:output_begin],
        shard[:, output_begin:gate_begin].T,
        lax.dynamic_slice_in_dim(gain_one_sum, own_start, own_rows),
        shard[:, gate_begin:up_begin],
        shard[:, up_begin:down_begin],
        shard[:, down_begin : down_begin + hidden_cols].T,
        lax.dynamic_slice_in_dim(gain_two_sum, own_start, own_rows),
    )


VMEM_BYTES = 58 * 1024 * 1024
BF16 = jnp.bfloat16
F32 = jnp.float32
QUARTERS = 4


def matmul(a, b):
    return lax.dot_general(a, b, (((1,), (0,)), ((), ())), preferred_element_type=F32)


def matmul_nt(a, b):
    return lax.dot_general(a, b, (((1,), (1,)), ((), ())), preferred_element_type=F32)


def matmul_tn(a, b):
    return lax.dot_general(a, b, (((0,), (0,)), ((), ())), preferred_element_type=F32)


def cost(flops, arrays, outs, exps=0):
    moved = sum(a.size * a.dtype.itemsize for a in arrays) + sum(
        o.size * o.dtype.itemsize for o in outs
    )
    return pl.CostEstimate(flops=int(flops), bytes_accessed=int(moved), transcendentals=int(exps))


def run_whole(body, me, arrays, outs, scratch=(), flops=0, in_hbm=0, name=None):
    count = len(arrays) - in_hbm
    return pl.pallas_call(
        body,
        out_shape=outs,
        in_specs=[pl.BlockSpec(memory_space=pltpu.SMEM)]
        + [pl.BlockSpec(memory_space=pltpu.VMEM)] * count
        + [pl.BlockSpec(memory_space=pl.ANY)] * in_hbm,
        out_specs=jax.tree.map(lambda _: pl.BlockSpec(memory_space=pltpu.VMEM), outs),
        scratch_shapes=list(scratch),
        cost_estimate=cost(flops, arrays, jax.tree.leaves(outs)),
        compiler_params=pltpu.CompilerParams(vmem_limit_bytes=VMEM_BYTES),
        name=name,
    )(me, *arrays)


def run_grid(body, me, grid, arrays, in_specs, outs, out_specs, scratch=(), flops=0, aliases=None, name=None):
    return pl.pallas_call(
        body,
        out_shape=outs,
        grid_spec=pltpu.PrefetchScalarGridSpec(
            num_scalar_prefetch=1,
            grid=grid,
            in_specs=in_specs,
            out_specs=out_specs,
            scratch_shapes=list(scratch),
        ),
        cost_estimate=cost(flops, arrays, jax.tree.leaves(outs)),
        input_output_aliases=aliases or {},
        compiler_params=pltpu.CompilerParams(vmem_limit_bytes=VMEM_BYTES),
        name=name,
    )(me, *arrays)


def shape(dims, kind=BF16):
    return jax.ShapeDtypeStruct(tuple(dims), kind)


def fixed(block):
    return pl.BlockSpec(block, lambda i, me: (0,) * len(block), pipeline_mode=pl.Buffered(1))


def column(index, wide):
    return pl.ds(pl.multiple_of(index * wide, wide), wide)


def turn(values):
    half = values.shape[-1] // 2
    return jnp.concatenate([-values[:, half:], values[:, :half]], axis=-1)


def turn_back(values):
    half = values.shape[-1] // 2
    return jnp.concatenate([values[:, half:], -values[:, :half]], axis=-1)


def plane_layer(
    tokens,
    query_weight,
    key_weight,
    value_weight,
    output_weight,
    first_gain,
    gate_weight,
    up_weight,
    down_weight,
    second_gain,
    cotangent,
    block_ids,
    piece_order,
):
    ctx_count = lax.axis_size("ctx")
    n = lax.axis_size("fsdp")
    planes = ctx_count // 2
    ctx = lax.axis_index("ctx")
    z, core = ctx // 2, ctx % 2
    f = lax.axis_index("fsdp")
    me = jnp.stack([f, core]).astype(jnp.int32)
    rows, width = tokens.shape[1:]
    pair = 2 * rows
    plane_rows = n * pair
    wide = width // n
    hidden_cols = gate_weight.shape[1]
    part = hidden_cols // (2 * n)
    quarter = part // QUARTERS
    scale = HD ** (-0.5)

    def across(value, d):
        return lax.ppermute(value, "fsdp", [(i, i ^ d) for i in range(n)])

    def sibling(value):
        return lax.ppermute(value, "ctx", [(i, i ^ 1) for i in range(ctx_count)])

    def along(value, step):
        pairs = [(i, i + 2 * step) for i in range(ctx_count)]
        return lax.ppermute(value, "ctx", [(a, b) for a, b in pairs if 0 <= b < ctx_count])

    def between_planes(value, moves):
        return lax.ppermute(
            value, "ctx", [(2 * a + side, 2 * b + side) for a, b in moves for side in range(2)]
        )

    def gathered(value):
        own = [value] + [across(value, d) for d in range(1, n)]
        return own, [sibling(block) for block in own]

    def reduced(own, other):
        near = [sibling(block) for block in other]
        sent = [
            across((own[d].astype(F32) + near[d].astype(F32)).astype(BF16), d) for d in range(1, n)
        ]
        return [own[0], near[0]] + sent

    middle_left, middle_right = planes // 2 - 1, planes // 2
    folds = [
        [(s, s + 1), (planes - 1 - s, planes - 2 - s)] for s in range(middle_left)
    ]

    def summed_over_planes(value, last=True):
        for moves in folds:
            value = (
                value.astype(F32) + between_planes(value, moves).astype(F32)
            ).astype(value.dtype)
        crossed = between_planes(value, [(middle_left, middle_right), (middle_right, middle_left)])
        value = (value.astype(F32) + crossed.astype(F32)).astype(value.dtype)
        for s, moves in reversed(list(enumerate(folds))):
            back = between_planes(value, [(b, a) for a, b in moves])
            if s == 0 and not last:
                return value, back
            receives = (z == s) | (z == planes - 1 - s)
            value = jnp.where(receives, back, value)
        return value

    place = jnp.arange(rows, dtype=jnp.int32)
    own_pieces = lax.dynamic_slice_in_dim(piece_order, 2 * z, 2)
    positions = (own_pieces[:, None] * rows + place[None, :]).reshape(pair).astype(F32)
    cosine, sine = rope_tables(positions)
    is_value = core == 1
    kv_cosine = jnp.where(is_value, 1.0, cosine)
    kv_sine = jnp.where(is_value, 0.0, sine)
    chips = f ^ jnp.arange(n, dtype=jnp.int32)
    ring = (z - jnp.arange(planes, dtype=jnp.int32)) % planes
    ring_ctx = (2 * ring[:, None] + jnp.arange(2, dtype=jnp.int32)[None, :]).reshape(-1)
    id_pieces = block_ids.reshape(n, ctx_count, rows)
    ids = id_pieces[chips[:, None], piece_order[ring_ctx][None, :]]
    key_ids = ids.reshape(n, planes, 1, pair)
    query_ids = ids[:, :2].reshape(n, pair, 1)

    def cut_attention(me_ref, *refs):
        wq, wk, wv, wo = (refs[i * n : (i + 1) * n] for i in range(4))
        one, two = refs[4 * n : 4 * n + 2]
        outs = refs[4 * n + 2 :]
        keys_here = me_ref[1] == 0
        for d in range(n):
            first = outs[d]
            first[:wide, :HD] = wq[d][...]

            @pl.when(keys_here)
            def _():
                first[:wide, HD:] = wk[d][...]

            @pl.when(jnp.logical_not(keys_here))
            def _():
                first[:wide, HD:] = wv[d][...]

            pick = lax.broadcasted_iota(jnp.int32, (16, wide), 0) < 8
            first[wide:, :] = jnp.where(pick, one[...].astype(F32), two[...].astype(F32)).astype(
                BF16
            )
            outs[n + d][...] = wo[d][...]

    def head_of(d):
        return lambda i, me: (0, 2 * (me[0] ^ d) + me[1])

    def chip_of(d):
        return lambda i, me: (0, me[0] ^ d)

    def head_rows_of(d):
        return lambda i, me: (2 * (me[0] ^ d) + me[1], 0)

    gain_spec = pl.BlockSpec((1, wide), lambda i, me: (0, 0))
    cut = run_grid(
        cut_attention,
        me,
        (1,),
        [query_weight] * n
        + [key_weight] * n
        + [value_weight] * n
        + [output_weight] * n
        + [first_gain.reshape(1, wide), second_gain.reshape(1, wide)],
        [pl.BlockSpec((wide, HD), head_of(d)) for d in range(n)]
        + [pl.BlockSpec((wide, HD), chip_of(d)) for d in range(n)] * 2
        + [pl.BlockSpec((HD, wide), head_rows_of(d)) for d in range(n)]
        + [gain_spec, gain_spec],
        [shape((wide + 16, 2 * HD))] * n + [shape((HD, wide))] * n,
        [pl.BlockSpec((wide + 16, 2 * HD), lambda i, me: (0, 0))] * n
        + [pl.BlockSpec((HD, wide), lambda i, me: (0, 0))] * n,
        name="cut_attention",
    )
    own_tokens = tokens[0]
    token_own, token_near = gathered(own_tokens)
    weights_in = [cut[0]] + [across(cut[d], d) for d in range(1, n)]
    weights_out = [cut[n]] + [across(cut[n + d], d) for d in range(1, n)]

    def cut_hidden_body(me_ref, *refs):
        gates, ups, downs, outs = (refs[i * n : (i + 1) * n] for i in range(4))
        for d in range(n):
            outs[d][:wide, :quarter] = gates[d][...]
            outs[d][:wide, quarter:] = ups[d][...]
            outs[d][wide:, :] = downs[d][...]

    def cut_hidden(q):
        def columns(d):
            return lambda i, me: (0, (2 * (me[0] ^ d) + me[1]) * QUARTERS + q)

        def down_rows(d):
            return lambda i, me: ((2 * (me[0] ^ d) + me[1]) * QUARTERS + q, 0)

        return run_grid(
            cut_hidden_body,
            me,
            (1,),
            [gate_weight] * n + [up_weight] * n + [down_weight] * n,
            [pl.BlockSpec((wide, quarter), columns(d)) for d in range(n)] * 2
            + [pl.BlockSpec((quarter, wide), down_rows(d)) for d in range(n)],
            [shape((wide + quarter, 2 * quarter))] * n,
            [pl.BlockSpec((wide + quarter, 2 * quarter), lambda i, me: (0, 0))] * n,
            name="cut_hidden",
        )

    def hidden_weights(q):
        pieces = cut_hidden(q)
        return [pieces[0]] + [across(pieces[d], d) for d in range(1, n)]

    feed = [hidden_weights(q) for q in range(QUARTERS)]
    own_cotangent = cotangent[0]
    cot_own, cot_near = gathered(own_cotangent)

    def project(me_ref, *refs):
        near_tokens = refs[: 2 * n]
        pieces = refs[2 * n : 3 * n]
        cos_ref, sin_ref, kvcos_ref, kvsin_ref = refs[3 * n : 3 * n + 4]
        normed_ref, query_ref, kv_ref, gains_ref = refs[3 * n + 4 :]
        chip, side = me_ref[0], me_ref[1]
        for j in range(n):
            both = pieces[j][wide:, :].astype(F32)
            gains_ref[0:1, column(chip ^ j, wide)] = both[0:1]
            gains_ref[1:2, column(chip ^ j, wide)] = both[8:9]
        for d in range(n):
            for e in range(2):
                slot = side ^ e
                values = near_tokens[e * n + d][...].astype(F32)
                inverse = lax.rsqrt(jnp.mean(values * values, axis=-1, keepdims=True) + epsilon)
                normed_ref[d, slot] = (values * inverse * gains_ref[0:1, :]).astype(BF16)
                both = jnp.zeros((rows, 2 * HD), F32)
                for j in range(n):
                    both += matmul(
                        normed_ref[d, slot, :, column(chip ^ j, wide)], pieces[j][:wide, :]
                    )
                query, kv = both[:, :HD], both[:, HD:]
                query_ref[d, slot] = (
                    query * cos_ref[slot] + turn(query) * sin_ref[slot]
                ).astype(BF16)
                kv_ref[d, slot] = (kv * kvcos_ref[slot] + turn(kv) * kvsin_ref[slot]).astype(BF16)

    head_shape = (n, 2, rows, HD)
    tables = [t.reshape(2, rows, HD) for t in (cosine, sine, kv_cosine, kv_sine)]
    normed, query_rot, own_kv, gains = run_whole(
        project,
        me,
        token_own + token_near + weights_in + tables,
        [
            shape((n, 2, rows, width)),
            shape(head_shape),
            shape(head_shape),
            shape((2, width), F32),
        ],
        flops=2 * plane_rows * width * 2 * HD,
        name="project",
    )

    rightward, leftward = [own_kv], [own_kv]
    for _ in range(planes - 1):
        rightward.append(along(rightward[-1], 1))
        leftward.append(along(leftward[-1], -1))
    kv_mine = [own_kv] + [rightward[k] + leftward[planes - k] for k in range(1, planes)]
    kv_near = [sibling(block) for block in kv_mine]

    head_spec = pl.BlockSpec((1, 2, rows, HD), lambda i, me: (i, 0, 0, 0))
    id_specs = [
        pl.BlockSpec((1, pair, 1), lambda i, me: (i, 0, 0)),
        pl.BlockSpec((1, planes, 1, pair), lambda i, me: (i, 0, 0, 0)),
    ]

    def scored(side, query, query_id, key_id, mine, near):
        keys, values, scores = [], [], []
        for k in range(planes):
            a = mine[k][0].reshape(pair, HD)
            b = near[k][0].reshape(pair, HD)
            keys.append(jnp.where(side == 0, a, b))
            values.append(jnp.where(side == 0, b, a))
            score = matmul_nt(query, keys[k]) * scale
            scores.append(jnp.where(key_id[0, k] <= query_id[0], score, masked_score))
        top = functools.reduce(jnp.maximum, [jnp.max(s, axis=-1, keepdims=True) for s in scores])
        raised = [jnp.exp(s - top) for s in scores]
        inverse = 1.0 / sum(jnp.sum(r, axis=-1, keepdims=True) for r in raised)
        return keys, values, [r * inverse for r in raised]

    def spread(step, side, whole, own_refs, near_refs):
        for d in range(n):

            @pl.when(step == d)
            def _():
                own_refs[d][...] = whole[side]
                near_refs[d][...] = whole[1 - side]

    def attend(me_ref, query_ref, query_id, key_id, *refs):
        mine, near, out_w = refs[:planes], refs[planes : 2 * planes], refs[2 * planes : 2 * planes + n]
        attended_ref = refs[2 * planes + n]
        own_refs = refs[2 * planes + n + 1 : 2 * planes + 2 * n + 1]
        near_refs = refs[2 * planes + 2 * n + 1 : 2 * planes + 3 * n + 1]
        whole = refs[-1]
        chip, side = me_ref[0], me_ref[1]
        query = query_ref[0].reshape(pair, HD)
        _, values, probs = scored(side, query, query_id, key_id, mine, near)
        total = jnp.zeros((pair, HD), F32)
        for k in range(planes):
            total += matmul(probs[k].astype(BF16), values[k])
        attended = total.astype(BF16)
        attended_ref[0] = attended.reshape(2, rows, HD)
        for j in range(n):
            whole[:, :, column(chip ^ j, wide)] = (
                matmul(attended, out_w[j][...]).astype(BF16).reshape(2, rows, wide)
            )
        spread(pl.program_id(0), side, whole, own_refs, near_refs)

    block = (rows, width)
    attend_flops = 4 * plane_rows * planes * pair * HD + 2 * plane_rows * HD * width
    attended, *partial = run_grid(
        attend,
        me,
        (n,),
        [query_rot, query_ids, key_ids] + kv_mine + kv_near + weights_out,
        [head_spec] + id_specs + [head_spec] * (2 * planes) + [fixed((HD, wide))] * n,
        [shape(head_shape)] + [shape(block)] * (2 * n),
        [head_spec] + [pl.BlockSpec(block, lambda i, me: (0, 0))] * (2 * n),
        scratch=[pltpu.VMEM((2, rows, width), BF16)],
        flops=attend_flops,
        name="attend",
    )
    middle_terms = reduced(partial[:n], partial[n:])

    def second_norm(me_ref, token_ref, gains_ref, *refs):
        terms, (middle_ref, normed_ref) = refs[:-2], refs[-2:]
        middle = token_ref[...].astype(F32)
        middle += sum(t[...].astype(F32) for t in terms)
        inverse = lax.rsqrt(jnp.mean(middle * middle, axis=-1, keepdims=True) + epsilon)
        middle_ref[...] = middle
        normed_ref[...] = (middle * inverse * gains_ref[1:2, :]).astype(BF16)

    middle, own_normed_two = run_whole(
        second_norm,
        me,
        [own_tokens, gains] + middle_terms,
        [shape(block, F32), shape(block)],
        name="second_norm",
    )
    two_own, two_near = gathered(own_normed_two)

    tile = plane_rows // 3

    def feed_forward(me_ref, *refs):
        pieces = refs[:n]
        two_refs, cot_refs = refs[n : 3 * n], refs[3 * n : 5 * n]
        hidden_ref, gate_ref, up_ref, dgate, dup, ddown = refs[5 * n : 5 * n + 6]
        two, cot, turned, two_sem, cot_sem = refs[5 * n + 6 :]
        chip = me_ref[0]
        copies = []
        for source, target, sems in ((two_refs, two, two_sem), (cot_refs, cot, cot_sem)):
            for i in range(2 * n):
                copies.append(
                    pltpu.make_async_copy(
                        source[i], target.at[pl.ds(i * rows, rows)], sems.at[i]
                    )
                )
        for copy in copies:
            copy.start()
        for copy in copies:
            copy.wait()

        def forward(t, _):
            here = pl.ds(pl.multiple_of(t * tile, tile), tile)
            both = jnp.zeros((tile, 2 * quarter), F32)
            hidden_grad = jnp.zeros((tile, quarter), F32)
            for j in range(n):
                both += matmul(two[here, column(chip ^ j, wide)], pieces[j][:wide, :])
                hidden_grad += matmul_nt(cot[here, column(chip ^ j, wide)], pieces[j][wide:, :])
            gate, up = both[:, :quarter], both[:, quarter:]
            share = 1.0 / (1.0 + jnp.exp(-gate))
            activated = gate * share
            results = (
                activated * up,
                hidden_grad * up * share * (1.0 + gate * (1.0 - share)),
                hidden_grad * activated,
            )
            for i, (result, ref) in enumerate(zip(results, (hidden_ref, gate_ref, up_ref))):
                ref[here, :] = result.astype(BF16)
                turned[i, :, here] = result.T.astype(BF16)
            return 0

        lax.fori_loop(0, plane_rows // tile, forward, 0)
        for j in range(n):
            here = column(chip ^ j, wide)
            dgate[j] = matmul(turned[1], two[:, here]).astype(BF16)
            dup[j] = matmul(turned[2], two[:, here]).astype(BF16)
            ddown[j] = matmul(turned[0], cot[:, here]).astype(BF16)

    grad_tile = (n, quarter, wide)
    hiddens, gate_grads, up_grads, hidden_tiles = [], [], [], []
    for q in range(QUARTERS):
        hidden, gate_grad, up_grad, *tiles = run_whole(
            feed_forward,
            me,
            feed[q] + two_own + two_near + cot_own + cot_near,
            [shape((plane_rows, quarter))] * 3 + [shape(grad_tile)] * 3,
            scratch=[
                pltpu.VMEM((plane_rows, width), BF16),
                pltpu.VMEM((plane_rows, width), BF16),
                pltpu.VMEM((3, quarter, plane_rows), BF16),
                pltpu.SemaphoreType.DMA((2 * n,)),
                pltpu.SemaphoreType.DMA((2 * n,)),
            ],
            flops=12 * plane_rows * width * quarter,
            in_hbm=4 * n,
            name="feed_forward",
        )
        hiddens.append(hidden)
        gate_grads.append(gate_grad)
        up_grads.append(up_grad)
        hidden_tiles.append(tiles)

    pieces = [feed[q][j] for q in range(QUARTERS) for j in range(n)]
    piece_specs = [fixed((wide + quarter, 2 * quarter))] * (QUARTERS * n)
    pair_spec = pl.BlockSpec((2, 1, rows, quarter), lambda i, me: (0, i, 0, 0))
    out_specs = [pl.BlockSpec(block, lambda i, me: (0, 0))] * (2 * n)

    def put(step, results, own_refs, near_refs, chip):
        for d in range(n):

            @pl.when(step == d)
            def _():
                for j in range(n):
                    here = column(chip ^ j, wide)
                    own_refs[d][:, here] = results[j][:rows]
                    near_refs[d][:, here] = results[j][rows:]

    def feed_forward_back(me_ref, *refs):
        gates, ups = refs[:QUARTERS], refs[QUARTERS : 2 * QUARTERS]
        pieces = refs[2 * QUARTERS : 2 * QUARTERS + QUARTERS * n]
        outs = refs[2 * QUARTERS + QUARTERS * n :]
        lefts = [
            jnp.concatenate(
                [g[:, 0].reshape(pair, quarter), u[:, 0].reshape(pair, quarter)], axis=1
            )
            for g, u in zip(gates, ups)
        ]
        results = []
        for j in range(n):
            total = jnp.zeros((pair, wide), F32)
            for q in range(QUARTERS):
                total += matmul_nt(lefts[q], pieces[q * n + j][:wide, :])
            results.append(total.astype(BF16))
        put(pl.program_id(0), results, outs[:n], outs[n:], me_ref[0])

    def by_block(value):
        return value.reshape(2, n, rows, quarter)

    back = run_grid(
        feed_forward_back,
        me,
        (n,),
        [by_block(g) for g in gate_grads] + [by_block(u) for u in up_grads] + pieces,
        [pair_spec] * (2 * QUARTERS) + piece_specs,
        [shape(block)] * (2 * n),
        out_specs,
        flops=4 * plane_rows * width * part,
        name="feed_forward_back",
    )
    two_grad_terms = reduced(back[:n], back[n:])

    def norm_back(values, inverse, gain, grad):
        unit = values * inverse
        scaled = grad * gain
        return inverse * (scaled - unit * jnp.mean(scaled * unit, axis=-1, keepdims=True)), jnp.sum(
            grad * unit, axis=0, keepdims=True
        )

    def second_norm_back(me_ref, middle_ref, cot_ref, gains_ref, *refs):
        terms, (middle_grad_ref, branch_ref, gain_ref, flat) = refs[:-4], refs[-4:]
        middle = middle_ref[...]
        inverse = lax.rsqrt(jnp.mean(middle * middle, axis=-1, keepdims=True) + epsilon)
        grad = sum(t[...].astype(F32) for t in terms)
        back, gain_term = norm_back(middle, inverse, gains_ref[1:2, :], grad)
        middle_grad = cot_ref[...].astype(F32) + back
        middle_grad_ref[...] = middle_grad
        branch_ref[...] = middle_grad.astype(BF16)
        flat[...] = gain_term
        for j in range(n):
            gain_ref[j] = flat[:, column(me_ref[0] ^ j, wide)]

    gain_shape = shape((n, 1, wide), F32)
    middle_grad, branch_grad, gain_two_term = run_whole(
        second_norm_back,
        me,
        [middle, own_cotangent, gains] + two_grad_terms,
        [shape(block, F32), shape(block), gain_shape],
        scratch=[pltpu.VMEM((1, width), F32)],
        name="second_norm_back",
    )
    branch_own, branch_near = gathered(branch_grad)

    def attend_back(me_ref, query_ref, query_id, key_id, cos_ref, sin_ref, *refs):
        mine, near, out_w = refs[:planes], refs[planes : 2 * planes], refs[2 * planes : 2 * planes + n]
        branch_refs = refs[2 * planes + n : 2 * planes + 3 * n]
        query_grad_ref = refs[2 * planes + 3 * n]
        keep_refs = refs[2 * planes + 3 * n + 1 : 3 * planes + 3 * n + 1]
        send_refs = refs[3 * planes + 3 * n + 1 : 4 * planes + 3 * n + 1]
        branch = refs[-1]
        chip, side = me_ref[0], me_ref[1]
        for d in range(n):

            @pl.when(pl.program_id(0) == d)
            def _():
                branch[side] = branch_refs[d][...]
                branch[1 - side] = branch_refs[n + d][...]

        query = query_ref[0].reshape(pair, HD)
        attended_grad = jnp.zeros((pair, HD), F32)
        for j in range(n):
            attended_grad += matmul_nt(
                branch[:, :, column(chip ^ j, wide)].reshape(pair, wide), out_w[j][...]
            )
        attended_grad = attended_grad.astype(BF16)
        keys, values, probs = scored(side, query, query_id, key_id, mine, near)
        low = [p.astype(BF16) for p in probs]
        shares = [matmul_nt(attended_grad, values[k]) for k in range(planes)]
        delta = sum(
            jnp.sum(low[k].astype(F32) * shares[k], axis=-1, keepdims=True) for k in range(planes)
        )
        query_grad = jnp.zeros((pair, HD), F32)
        for k in range(planes):
            score_grad = (probs[k] * (shares[k] - delta)).astype(BF16)
            query_grad += matmul(score_grad, keys[k])
            key_grad = matmul_tn(score_grad, query) * scale
            value_grad = matmul_tn(low[k], attended_grad)
            keep_refs[k][0] = jnp.where(side == 0, key_grad, value_grad).astype(BF16).reshape(
                2, rows, HD
            )
            send_refs[k][0] = jnp.where(side == 0, value_grad, key_grad).astype(BF16).reshape(
                2, rows, HD
            )
        query_grad = query_grad * scale
        query_grad = query_grad * cos_ref[...] + turn_back(query_grad * sin_ref[...])
        query_grad_ref[0] = query_grad.astype(BF16).reshape(2, rows, HD)

    query_grad, *kv_grads = run_grid(
        attend_back,
        me,
        (n,),
        [query_rot, query_ids, key_ids, cosine, sine]
        + kv_mine
        + kv_near
        + weights_out
        + branch_own
        + branch_near,
        [head_spec]
        + id_specs
        + [fixed((pair, HD))] * 2
        + [head_spec] * (2 * planes)
        + [fixed((HD, wide))] * n
        + [fixed(block)] * (2 * n),
        [shape(head_shape)] * (1 + 2 * planes),
        [head_spec] * (1 + 2 * planes),
        scratch=[pltpu.VMEM((2, rows, width), BF16)],
        flops=10 * plane_rows * planes * pair * HD + 2 * plane_rows * HD * width,
        name="attend_back",
    )
    kept, handed = kv_grads[:planes], kv_grads[planes:]
    kv_sums = [
        (kept[k].astype(F32) + sibling(handed[k]).astype(F32)).astype(BF16) for k in range(planes)
    ]
    from_above = jnp.zeros_like(own_kv)
    from_below = jnp.zeros_like(own_kv)
    for k in range(planes - 1, 0, -1):
        below = jnp.where(z >= k, kv_sums[k], 0).astype(F32) + from_above.astype(F32)
        above = jnp.where(z + k < planes, kv_sums[planes - k], 0).astype(F32) + from_below.astype(F32)
        from_above = along(below.astype(BF16), -1)
        from_below = along(above.astype(BF16), 1)

    def project_back(me_ref, *refs):
        own_ref, above_ref, below_ref, query_grad_ref, kvcos_ref, kvsin_ref = refs[:6]
        pieces = refs[6 : 6 + n]
        kv_ref = refs[6 + n]
        own_refs, near_refs = refs[7 + n : 7 + 2 * n], refs[7 + 2 * n : 7 + 3 * n]
        chip, side = me_ref[0], me_ref[1]
        for d in range(n):
            for e in range(2):
                slot = side ^ e
                grad = own_ref[d, slot].astype(F32) + above_ref[d, slot].astype(F32)
                grad = grad + below_ref[d, slot].astype(F32)
                grad = grad * kvcos_ref[slot] + turn_back(grad * kvsin_ref[slot])
                grad = grad.astype(BF16)
                kv_ref[d, slot] = grad
                left = jnp.concatenate([query_grad_ref[d, slot], grad], axis=1)
                target = (own_refs, near_refs)[e][d]
                for j in range(n):
                    target[:, column(chip ^ j, wide)] = matmul_nt(left, pieces[j][:wide, :]).astype(
                        BF16
                    )

    kv_grad, *partial = run_whole(
        project_back,
        me,
        [kv_sums[0], from_above, from_below, query_grad] + tables[2:] + weights_in,
        [shape(head_shape)] + [shape(block)] * (2 * n),
        flops=4 * plane_rows * width * HD,
        name="project_back",
    )
    one_grad_terms = reduced(partial[:n], partial[n:])

    def first_norm_back(me_ref, token_ref, middle_grad_ref, gains_ref, *refs):
        terms, (grad_ref, gain_ref, flat) = refs[:-3], refs[-3:]
        values = token_ref[...].astype(F32)
        inverse = lax.rsqrt(jnp.mean(values * values, axis=-1, keepdims=True) + epsilon)
        grad = sum(t[...].astype(F32) for t in terms)
        back, gain_term = norm_back(values, inverse, gains_ref[0:1, :], grad)
        grad_ref[...] = middle_grad_ref[...] + back
        flat[...] = gain_term
        for j in range(n):
            gain_ref[j] = flat[:, column(me_ref[0] ^ j, wide)]

    tokens_grad, gain_one_term = run_whole(
        first_norm_back,
        me,
        [own_tokens, middle_grad, gains] + one_grad_terms,
        [shape(block, F32), gain_shape],
        scratch=[pltpu.VMEM((1, width), F32)],
        name="first_norm_back",
    )
    gain_terms = jnp.concatenate([gain_one_term, gain_two_term], axis=1)
    gain_sum = gain_terms[0] + sum(across(gain_terms[d], d) for d in range(1, n))
    gain_sum = gain_sum + sibling(gain_sum)
    gain_sum = summed_over_planes(gain_sum)

    def outer(me_ref, left_ref, right_ref, out_ref):
        turned = left_ref[...].reshape(plane_rows, HD).astype(F32).T.astype(BF16)
        for j in range(n):
            right = right_ref[:, :, :, column(me_ref[0] ^ j, wide)].reshape(plane_rows, wide)
            out_ref[j] = matmul(turned, right).astype(BF16)

    def outer_branch(me_ref, left_ref, *refs):
        branch_refs, (out_ref, right_ref, sems) = refs[: 2 * n], refs[2 * n :]
        copies = []
        for e in range(2):
            for d in range(n):
                copies.append(
                    pltpu.make_async_copy(
                        branch_refs[e * n + d],
                        right_ref.at[d, me_ref[1] ^ e],
                        sems.at[e * n + d],
                    )
                )
        for copy in copies:
            copy.start()
        for copy in copies:
            copy.wait()
        outer(me_ref, left_ref, right_ref, out_ref)

    outer_flops = 2 * plane_rows * width * HD
    outer_tile = shape((n, HD, wide))
    query_tile = run_whole(
        outer, me, [query_grad, normed], outer_tile, flops=outer_flops, name="query_outer"
    )
    output_tile = run_whole(
        outer_branch,
        me,
        [attended] + branch_own + branch_near,
        outer_tile,
        scratch=[pltpu.VMEM((n, 2, rows, width), BF16), pltpu.SemaphoreType.DMA((2 * n,))],
        flops=outer_flops,
        in_hbm=2 * n,
        name="output_outer",
    )
    kv_tile = run_whole(outer, me, [kv_grad, normed], outer_tile, flops=outer_flops, name="kv_outer")

    def deal(me_ref, *refs):
        count = (len(refs) - n) // 2
        sums, backs, outs = refs[:count], refs[count : 2 * count], refs[2 * count :]
        outer_plane = me_ref[2] == 1

        @pl.when(outer_plane)
        def _():
            for d in range(n):
                for w in range(count):
                    outs[d][w] = backs[w][d]

        @pl.when(jnp.logical_not(outer_plane))
        def _():
            for d in range(n):
                for w in range(count):
                    outs[d][w] = sums[w][d]

    is_outer = ((z == 0) | (z == planes - 1)).astype(jnp.int32)
    me_and_plane = jnp.concatenate([me, is_outer[None]])

    def owned(tiles):
        ends = [summed_over_planes(t, last=False) for t in tiles]
        dealt = run_whole(
            deal,
            me_and_plane,
            [a for a, _ in ends] + [b for _, b in ends],
            [shape((len(tiles),) + tiles[0].shape[1:])] * n,
            name="deal",
        )
        own = [dealt[0]] + [across(dealt[d], d) for d in range(1, n)]
        return own + [sibling(block) for block in own]

    full = lambda count: [fixed((count, HD, wide))] * (2 * n)

    def slot_of(q, count):
        def where(i, me):
            return (2 * (me[0] ^ (i % n)) + (me[1] ^ (i // n))) * count + q

        return where

    def place_hidden(me_ref, *refs):
        tiles = refs[: 2 * n]
        gate_out, up_out, down_out = refs[-3:]
        for i in range(2 * n):

            @pl.when(pl.program_id(0) == i)
            def _():
                gate_out[...] = tiles[i][0].astype(F32).T
                up_out[...] = tiles[i][1].astype(F32).T
                down_out[...] = tiles[i][2].astype(F32)

    hidden_outs = [
        shape(gate_weight.shape, F32),
        shape(up_weight.shape, F32),
        shape(down_weight.shape, F32),
    ]
    held = None
    for q in range(QUARTERS):
        tiles = owned(hidden_tiles[q])
        where = slot_of(q, QUARTERS)
        by_columns = pl.BlockSpec((wide, quarter), lambda i, me, w=where: (0, w(i, me)))
        by_rows = pl.BlockSpec((quarter, wide), lambda i, me, w=where: (w(i, me), 0))
        rest = [] if held is None else list(held)
        held = run_grid(
            place_hidden,
            me,
            (2 * n,),
            tiles + rest,
            [fixed((3, quarter, wide))] * (2 * n) + [pl.BlockSpec(memory_space=pl.ANY)] * len(rest),
            hidden_outs,
            [by_columns, by_columns, by_rows],
            aliases={1 + 2 * n + i: i for i in range(len(rest))},
            name="place_hidden",
        )

    def place_query(me_ref, *refs):
        tiles, (query_out, output_out) = refs[: 2 * n], refs[2 * n :]
        for i in range(2 * n):

            @pl.when(pl.program_id(0) == i)
            def _():
                query_out[...] = tiles[i][0].astype(F32).T
                output_out[...] = tiles[i][1].astype(F32)

    where = slot_of(0, 1)
    query_weight_grad, output_weight_grad = run_grid(
        place_query,
        me,
        (2 * n,),
        owned([query_tile, output_tile]),
        [fixed((2, HD, wide))] * (2 * n),
        [shape(query_weight.shape, F32), shape(output_weight.shape, F32)],
        [
            pl.BlockSpec((wide, HD), lambda i, me: (0, where(i, me))),
            pl.BlockSpec((HD, wide), lambda i, me: (where(i, me), 0)),
        ],
        name="place_query",
    )

    def place_kv(me_ref, *refs):
        tiles, (key_out, value_out) = refs[: 2 * n], refs[2 * n :]
        keys_here = me_ref[1] == 0
        for d in range(n):

            @pl.when(pl.program_id(0) == d)
            def _():
                own, near = tiles[d][0].astype(F32).T, tiles[n + d][0].astype(F32).T
                key_out[...] = jnp.where(keys_here, own, near)
                value_out[...] = jnp.where(keys_here, near, own)

    by_chip = pl.BlockSpec((wide, HD), lambda i, me: (0, me[0] ^ i))
    key_weight_grad, value_weight_grad = run_grid(
        place_kv,
        me,
        (n,),
        owned([kv_tile]),
        [fixed((1, HD, wide))] * (2 * n),
        [shape(key_weight.shape, F32), shape(value_weight.shape, F32)],
        [by_chip, by_chip],
        name="place_kv",
    )

    def feed_forward_out(me_ref, *refs):
        hiddens = refs[:QUARTERS]
        pieces = refs[QUARTERS : QUARTERS + QUARTERS * n]
        outs = refs[QUARTERS + QUARTERS * n :]
        results = []
        for j in range(n):
            total = jnp.zeros((pair, wide), F32)
            for q in range(QUARTERS):
                total += matmul(hiddens[q][:, 0].reshape(pair, quarter), pieces[q * n + j][wide:, :])
            results.append(total.astype(BF16))
        put(pl.program_id(0), results, outs[:n], outs[n:], me_ref[0])

    partial = run_grid(
        feed_forward_out,
        me,
        (n,),
        [by_block(h) for h in hiddens] + pieces,
        [pair_spec] * QUARTERS + piece_specs,
        [shape(block)] * (2 * n),
        out_specs,
        flops=2 * plane_rows * width * part,
        name="feed_forward_out",
    )
    output = middle + sum(t.astype(F32) for t in reduced(partial[:n], partial[n:]))

    return (
        output.astype(BF16)[None],
        tokens_grad[None],
        query_weight_grad,
        key_weight_grad,
        value_weight_grad,
        output_weight_grad,
        gain_sum[0],
        held[0],
        held[1],
        held[2],
        gain_sum[1],
    )


def solution(mesh):
    chips, pieces = mesh.shape["fsdp"], mesh.shape["ctx"]
    one_head_each = 2 * chips == H and chips == KVH and pieces % 4 == 0 and pieces > 4
    return jax.shard_map(
        plane_layer if one_head_each else ring_layer,
        mesh=mesh,
        in_specs=(
            P("fsdp", "ctx", None),
            P("fsdp", None),
            P("fsdp", None),
            P("fsdp", None),
            P(None, "fsdp"),
            P("fsdp"),
            P("fsdp", None),
            P("fsdp", None),
            P(None, "fsdp"),
            P("fsdp"),
            P("fsdp", "ctx", None),
            P(),
            P(),
        ),
        out_specs=(
            P("fsdp", "ctx", None),
            P("fsdp", "ctx", None),
            P("fsdp", None),
            P("fsdp", None),
            P("fsdp", None),
            P(None, "fsdp"),
            P("fsdp"),
            P("fsdp", None),
            P("fsdp", None),
            P(None, "fsdp"),
            P("fsdp"),
        ),
        check_vma=False,
    )
```

```python
import functools

import jax
import jax.numpy as jnp
from jax import lax
from jax.experimental import pallas as pl
from jax.experimental.pallas import tpu as pltpu
from jax.sharding import PartitionSpec as P

H = 8
KVH = 4
HD = 256


epsilon = 1e-06
theta = 1000042.0
masked_score = -1e30


def passed_along(value, axis, by):
    devices = lax.axis_size(axis)
    return lax.ppermute(value, axis, [(i, (i + by) % devices) for i in range(devices)])


def rope_tables(positions):
    half = HD // 2
    frequency = theta ** (-(jnp.arange(half, dtype=jnp.float32) * 2.0 / HD))
    angle = positions[:, None] * frequency[None, :]
    angle = jnp.concatenate([angle, angle], axis=-1)
    return (jnp.cos(angle), jnp.sin(angle))


def rotate(values, cosine, sine):
    half = values.shape[-1] // 2
    turned = jnp.concatenate([-values[..., half:], values[..., :half]], axis=-1)
    return values * cosine[:, None, :] + turned * sine[:, None, :]


def rotate_back(grads, cosine, sine):
    half = grads.shape[-1] // 2
    scaled = grads * sine[:, None, :]
    turned = jnp.concatenate([scaled[..., half:], -scaled[..., :half]], axis=-1)
    return grads * cosine[:, None, :] + turned


def split_heads(block):
    count = block.shape[0]
    key_cols = KVH * HD
    key_part = block[:, :key_cols].reshape(count, KVH, HD).transpose(1, 0, 2)
    value_part = block[:, key_cols:].reshape(count, KVH, HD).transpose(1, 0, 2)
    return (key_part, value_part)


def merge_heads(grouped):
    return grouped.transpose(1, 0, 2).reshape(grouped.shape[1], KVH * HD)


def weight_terms(lefts, rights):
    pieces = []
    for index in range(4):
        column = lefts[index]
        pieces.append(
            jnp.einsum("tc,tn->cn", column, rights[index], preferred_element_type=jnp.float32)
        )
    return jnp.concatenate(pieces, axis=1)


def ring_layer(
    tokens,
    query_weight,
    key_weight,
    value_weight,
    output_weight,
    first_gain,
    gate_weight,
    up_weight,
    down_weight,
    second_gain,
    cotangent,
    block_ids,
    piece_order,
):
    ctx_count = lax.axis_size("ctx")
    fsdp_count = lax.axis_size("fsdp")
    here = lax.axis_index("ctx")
    rows = tokens.shape[1]
    width = tokens.shape[2]
    group = H // KVH
    query_cols = H * HD
    key_cols = KVH * HD
    hidden_cols = gate_weight.shape[1]
    scale = HD ** (-0.5)
    whole_query, whole_key, whole_value, whole_output, gain_one = (
        lax.all_gather(query_weight, "fsdp", axis=0, tiled=True),
        lax.all_gather(key_weight, "fsdp", axis=0, tiled=True),
        lax.all_gather(value_weight, "fsdp", axis=0, tiled=True),
        lax.all_gather(output_weight, "fsdp", axis=1, tiled=True),
        lax.all_gather(first_gain, "fsdp", axis=0, tiled=True),
    )
    id_row = lax.dynamic_index_in_dim(block_ids, lax.axis_index("fsdp"), 0, keepdims=False)
    start_own = lax.dynamic_index_in_dim(piece_order, here, 0, keepdims=False) * rows
    offsets = jnp.arange(rows, dtype=jnp.int32)
    cosine, sine = rope_tables((start_own + offsets).astype(jnp.float32))
    own_ids = lax.dynamic_slice_in_dim(id_row, start_own, rows)
    query_ids = jnp.tile(own_ids, group)

    def visible(source):
        key_start = lax.dynamic_index_in_dim(piece_order, source, 0, keepdims=False) * rows
        key_ids = lax.dynamic_slice_in_dim(id_row, key_start, rows)
        return key_ids[None, :] <= query_ids[:, None]

    inputs = tokens[0].astype(jnp.float32)
    scale_one = lax.rsqrt(jnp.mean(inputs * inputs, axis=-1, keepdims=True) + epsilon)
    unit_one = inputs * scale_one
    normed = (unit_one * gain_one.astype(jnp.float32)).astype(jnp.bfloat16)
    query = jnp.dot(normed, whole_query, preferred_element_type=jnp.float32).reshape(rows, H, HD)
    query_rot = rotate(query, cosine, sine).astype(jnp.bfloat16)
    keys = jnp.dot(normed, whole_key, preferred_element_type=jnp.float32).reshape(rows, KVH, HD)
    keys_rot = rotate(keys, cosine, sine).astype(jnp.bfloat16).reshape(rows, key_cols)
    values = jnp.dot(normed, whole_value, preferred_element_type=jnp.float32).astype(jnp.bfloat16)
    key_value = jnp.concatenate([keys_rot, values], axis=-1)
    grouped = (
        query_rot.reshape(rows, KVH, group, HD).transpose(1, 2, 0, 3).reshape(KVH, group * rows, HD)
    )

    def forward_step(state, block, source):
        running, total, weighted = state
        key_part, value_part = split_heads(block)
        allowed = visible(source)
        scores = (
            jnp.einsum("hqd,hkd->hqk", grouped, key_part, preferred_element_type=jnp.float32)
            * scale
        )
        scores = jnp.where(allowed[None], scores, masked_score)
        newest = jnp.maximum(running, jnp.max(scores, axis=-1))
        factor = jnp.exp(running - newest)
        shares = jnp.where(allowed[None], jnp.exp(scores - newest[..., None]), 0.0)
        total = total * factor + jnp.sum(shares, axis=-1)
        weighted = weighted * factor[..., None] + jnp.einsum(
            "hqk,hkd->hqd",
            shares.astype(jnp.bfloat16),
            value_part,
            preferred_element_type=jnp.float32,
        )
        return (newest, total, weighted)

    start_state = (
        jnp.full((KVH, group * rows), masked_score, jnp.float32),
        jnp.zeros((KVH, group * rows), jnp.float32),
        jnp.zeros((KVH, group * rows, HD), jnp.float32),
    )
    state = forward_step(start_state, key_value, here)

    def forward_turn(turn, carry):
        block, inner = carry
        block = passed_along(block, "ctx", 1)
        source = (here - turn) % ctx_count
        return (block, forward_step(inner, block, source))

    passed_block, state = lax.fori_loop(1, ctx_count, forward_turn, (key_value, state))
    running, total, weighted = state
    attended = weighted / total[..., None]
    log_total = running + jnp.log(total)
    attended_low = (
        attended.reshape(KVH, group, rows, HD)
        .transpose(2, 0, 1, 3)
        .reshape(rows, query_cols)
        .astype(jnp.bfloat16)
    )
    middle = inputs + jnp.dot(attended_low, whole_output, preferred_element_type=jnp.float32)
    gain_two, whole_gate, whole_up, whole_down = (
        lax.all_gather(second_gain, "fsdp", axis=0, tiled=True),
        lax.all_gather(gate_weight, "fsdp", axis=0, tiled=True),
        lax.all_gather(up_weight, "fsdp", axis=0, tiled=True),
        lax.all_gather(down_weight, "fsdp", axis=1, tiled=True),
    )
    scale_two = lax.rsqrt(jnp.mean(middle * middle, axis=-1, keepdims=True) + epsilon)
    unit_two = middle * scale_two
    normed_two = (unit_two * gain_two.astype(jnp.float32)).astype(jnp.bfloat16)
    gate = jnp.dot(normed_two, whole_gate, preferred_element_type=jnp.float32)
    up = jnp.dot(normed_two, whole_up, preferred_element_type=jnp.float32)
    sigmoid_gate = jax.nn.sigmoid(gate)
    activated = gate * sigmoid_gate
    hidden = (activated * up).astype(jnp.bfloat16)
    result = middle + jnp.dot(hidden, whole_down, preferred_element_type=jnp.float32)
    output = result.astype(jnp.bfloat16)[None]
    upstream = cotangent[0]
    hidden_grad = jnp.einsum("tm,fm->tf", upstream, whole_down, preferred_element_type=jnp.float32)
    gate_grad = (hidden_grad * up * sigmoid_gate * (1.0 + gate * (1.0 - sigmoid_gate))).astype(
        jnp.bfloat16
    )
    up_grad = (hidden_grad * activated).astype(jnp.bfloat16)
    normed_two_grad = jnp.einsum(
        "tf,mf->tm", gate_grad, whole_gate, preferred_element_type=jnp.float32
    ) + jnp.einsum("tf,mf->tm", up_grad, whole_up, preferred_element_type=jnp.float32)
    gain_two_term = jnp.sum(normed_two_grad * unit_two, axis=0)
    unit_two_grad = normed_two_grad * gain_two.astype(jnp.float32)
    middle_grad = upstream.astype(jnp.float32) + scale_two * (
        unit_two_grad - unit_two * jnp.mean(unit_two_grad * unit_two, axis=-1, keepdims=True)
    )
    branch_grad = middle_grad.astype(jnp.bfloat16)
    attended_grad = jnp.einsum(
        "tm,cm->tc", branch_grad, whole_output, preferred_element_type=jnp.float32
    ).astype(jnp.bfloat16)
    grad_grouped = (
        attended_grad.reshape(rows, KVH, group, HD)
        .transpose(1, 2, 0, 3)
        .reshape(KVH, group * rows, HD)
    )
    delta = jnp.sum(grad_grouped.astype(jnp.float32) * attended, axis=-1)

    def backward_step(query_total, block, source):
        key_part, value_part = split_heads(block)
        allowed = visible(source)
        scores = (
            jnp.einsum("hqd,hkd->hqk", grouped, key_part, preferred_element_type=jnp.float32)
            * scale
        )
        scores = jnp.where(allowed[None], scores, masked_score)
        shares = jnp.where(allowed[None], jnp.exp(scores - log_total[..., None]), 0.0)
        value_grad = jnp.einsum(
            "hqk,hqd->hkd",
            shares.astype(jnp.bfloat16),
            grad_grouped,
            preferred_element_type=jnp.float32,
        )
        share_grad = jnp.einsum(
            "hqd,hkd->hqk", grad_grouped, value_part, preferred_element_type=jnp.float32
        )
        score_grad = (shares * (share_grad - delta[..., None])).astype(jnp.bfloat16)
        query_total = query_total + jnp.einsum(
            "hqk,hkd->hqd", score_grad, key_part, preferred_element_type=jnp.float32
        )
        key_grad = (
            jnp.einsum("hqk,hqd->hkd", score_grad, grouped, preferred_element_type=jnp.float32)
            * scale
        )
        return (
            query_total,
            jnp.concatenate([merge_heads(key_grad), merge_heads(value_grad)], axis=-1),
        )

    query_total, first_grad = backward_step(
        jnp.zeros((KVH, group * rows, HD), jnp.float32), key_value, here
    )
    held = first_grad

    def backward_turn(turn, carry):
        block, kept, total_query = carry
        block = passed_along(block, "ctx", 1)
        source = (here - turn) % ctx_count
        total_query, block_grad = backward_step(total_query, block, source)
        kept = passed_along(kept.astype(jnp.bfloat16), "ctx", 1).astype(kept.dtype) + block_grad
        return (block, kept, total_query)

    passed_again, held, query_total = lax.fori_loop(
        1, ctx_count, backward_turn, (key_value, held, query_total)
    )
    own_grad = passed_along(held.astype(jnp.bfloat16), "ctx", 1).astype(held.dtype)
    query_rot_grad = (
        (query_total * scale)
        .reshape(KVH, group, rows, HD)
        .transpose(2, 0, 1, 3)
        .reshape(rows, H, HD)
    )
    query_grad = (
        rotate_back(query_rot_grad, cosine, sine).reshape(rows, query_cols).astype(jnp.bfloat16)
    )
    key_grad = (
        rotate_back(own_grad[:, :key_cols].reshape(rows, KVH, HD), cosine, sine)
        .reshape(rows, key_cols)
        .astype(jnp.bfloat16)
    )
    value_grad = own_grad[:, key_cols:].astype(jnp.bfloat16)
    normed_grad = jnp.einsum(
        "tc,mc->tm", query_grad, whole_query, preferred_element_type=jnp.float32
    )
    normed_grad = normed_grad + jnp.einsum(
        "tc,mc->tm", key_grad, whole_key, preferred_element_type=jnp.float32
    )
    normed_grad = normed_grad + jnp.einsum(
        "tc,mc->tm", value_grad, whole_value, preferred_element_type=jnp.float32
    )
    gain_one_term = jnp.sum(normed_grad * unit_one, axis=0)
    unit_one_grad = normed_grad * gain_one.astype(jnp.float32)
    tokens_grad = middle_grad + scale_one * (
        unit_one_grad - unit_one * jnp.mean(unit_one_grad * unit_one, axis=-1, keepdims=True)
    )
    projected = jnp.concatenate([query_grad, key_grad, value_grad], axis=-1)
    gate_up = jnp.concatenate([gate_grad, up_grad], axis=-1)
    lefts = jnp.stack([normed, branch_grad, normed_two, upstream])
    rights = (projected, attended_low, gate_up, hidden)
    piece = lax.psum_scatter(
        weight_terms(lefts, rights).astype(jnp.bfloat16), "fsdp", scatter_dimension=0, tiled=True
    )
    shard = lax.psum(piece, "ctx").astype(jnp.float32)
    gain_one_sum, gain_two_sum = lax.psum((gain_one_term, gain_two_term), ("ctx", "fsdp"))
    own_rows = width // fsdp_count
    own_start = lax.axis_index("fsdp") * own_rows
    value_begin = query_cols + key_cols
    output_begin = value_begin + key_cols
    gate_begin = output_begin + query_cols
    up_begin = gate_begin + hidden_cols
    down_begin = up_begin + hidden_cols
    return (
        output,
        tokens_grad[None],
        shard[:, :query_cols],
        shard[:, query_cols:value_begin],
        shard[:, value_begin:output_begin],
        shard[:, output_begin:gate_begin].T,
        lax.dynamic_slice_in_dim(gain_one_sum, own_start, own_rows),
        shard[:, gate_begin:up_begin],
        shard[:, up_begin:down_begin],
        shard[:, down_begin : down_begin + hidden_cols].T,
        lax.dynamic_slice_in_dim(gain_two_sum, own_start, own_rows),
    )


VMEM_BYTES = 58 * 1024 * 1024
BF16 = jnp.bfloat16
F32 = jnp.float32
QUARTERS = 4
LINES = 2


def matmul(a, b):
    return lax.dot_general(a, b, (((1,), (0,)), ((), ())), preferred_element_type=F32)


def matmul_nt(a, b):
    return lax.dot_general(a, b, (((1,), (1,)), ((), ())), preferred_element_type=F32)


def matmul_tn(a, b):
    return lax.dot_general(a, b, (((0,), (0,)), ((), ())), preferred_element_type=F32)


def cost(flops, arrays, outs, exps=0):
    moved = sum(a.size * a.dtype.itemsize for a in arrays) + sum(
        o.size * o.dtype.itemsize for o in outs
    )
    return pl.CostEstimate(flops=int(flops), bytes_accessed=int(moved), transcendentals=int(exps))


def run_whole(body, me, arrays, outs, scratch=(), flops=0, in_hbm=0, name=None):
    count = len(arrays) - in_hbm
    return pl.pallas_call(
        body,
        out_shape=outs,
        in_specs=[pl.BlockSpec(memory_space=pltpu.SMEM)]
        + [pl.BlockSpec(memory_space=pltpu.VMEM)] * count
        + [pl.BlockSpec(memory_space=pl.ANY)] * in_hbm,
        out_specs=jax.tree.map(lambda _: pl.BlockSpec(memory_space=pltpu.VMEM), outs),
        scratch_shapes=list(scratch),
        cost_estimate=cost(flops, arrays, jax.tree.leaves(outs)),
        compiler_params=pltpu.CompilerParams(vmem_limit_bytes=VMEM_BYTES),
        name=name,
    )(me, *arrays)


def run_grid(body, me, grid, arrays, in_specs, outs, out_specs, scratch=(), flops=0, aliases=None, name=None):
    return pl.pallas_call(
        body,
        out_shape=outs,
        grid_spec=pltpu.PrefetchScalarGridSpec(
            num_scalar_prefetch=1,
            grid=grid,
            in_specs=in_specs,
            out_specs=out_specs,
            scratch_shapes=list(scratch),
        ),
        cost_estimate=cost(flops, arrays, jax.tree.leaves(outs)),
        input_output_aliases=aliases or {},
        compiler_params=pltpu.CompilerParams(vmem_limit_bytes=VMEM_BYTES),
        name=name,
    )(me, *arrays)


def shape(dims, kind=BF16):
    return jax.ShapeDtypeStruct(tuple(dims), kind)


def fixed(block):
    return pl.BlockSpec(block, lambda i, me: (0,) * len(block), pipeline_mode=pl.Buffered(1))


def column(index, wide):
    return pl.ds(pl.multiple_of(index * wide, wide), wide)


def turn(values):
    half = values.shape[-1] // 2
    return jnp.concatenate([-values[:, half:], values[:, :half]], axis=-1)


def turn_back(values):
    half = values.shape[-1] // 2
    return jnp.concatenate([values[:, half:], -values[:, :half]], axis=-1)


def plane_layer(
    tokens,
    query_weight,
    key_weight,
    value_weight,
    output_weight,
    first_gain,
    gate_weight,
    up_weight,
    down_weight,
    second_gain,
    cotangent,
    block_ids,
    piece_order,
):
    ctx_count = lax.axis_size("ctx")
    n = lax.axis_size("fsdp")
    planes = ctx_count // 2
    ctx = lax.axis_index("ctx")
    z, core = ctx // 2, ctx % 2
    f = lax.axis_index("fsdp")
    me = jnp.stack([f, core]).astype(jnp.int32)
    rows, width = tokens.shape[1:]
    pair = 2 * rows
    plane_rows = n * pair
    wide = width // n
    hidden_cols = gate_weight.shape[1]
    part = hidden_cols // (2 * n)
    quarter = part // QUARTERS
    scale = HD ** (-0.5)

    def across(value, d):
        return lax.ppermute(value, "fsdp", [(i, i ^ d) for i in range(n)])

    def sibling(value):
        return lax.ppermute(value, "ctx", [(i, i ^ 1) for i in range(ctx_count)])

    def along(value, step):
        pairs = [(i, i + 2 * step) for i in range(ctx_count)]
        return lax.ppermute(value, "ctx", [(a, b) for a, b in pairs if 0 <= b < ctx_count])

    def between_planes(value, moves):
        return lax.ppermute(
            value, "ctx", [(2 * a + side, 2 * b + side) for a, b in moves for side in range(2)]
        )

    def gathered(value):
        own = [value] + [across(value, d) for d in range(1, n)]
        return own, [sibling(block) for block in own]

    def reduced(own, other):
        near = [sibling(block) for block in other]
        sent = [
            across((own[d].astype(F32) + near[d].astype(F32)).astype(BF16), d) for d in range(1, n)
        ]
        return [own[0], near[0]] + sent

    middle_left, middle_right = planes // 2 - 1, planes // 2
    folds = [
        [(s, s + 1), (planes - 1 - s, planes - 2 - s)] for s in range(middle_left)
    ]

    def summed_over_planes(value):
        for moves in folds:
            value = (
                value.astype(F32) + between_planes(value, moves).astype(F32)
            ).astype(value.dtype)
        crossed = between_planes(value, [(middle_left, middle_right), (middle_right, middle_left)])
        value = (value.astype(F32) + crossed.astype(F32)).astype(value.dtype)
        for s, moves in reversed(list(enumerate(folds))):
            back = between_planes(value, [(b, a) for a, b in moves])
            receives = (z == s) | (z == planes - 1 - s)
            value = jnp.where(receives, back, value)
        return value

    place = jnp.arange(rows, dtype=jnp.int32)
    own_pieces = lax.dynamic_slice_in_dim(piece_order, 2 * z, 2)
    positions = (own_pieces[:, None] * rows + place[None, :]).reshape(pair).astype(F32)
    cosine, sine = rope_tables(positions)
    is_value = core == 1
    kv_cosine = jnp.where(is_value, 1.0, cosine)
    kv_sine = jnp.where(is_value, 0.0, sine)
    chips = f ^ jnp.arange(n, dtype=jnp.int32)
    ring = (z - jnp.arange(planes, dtype=jnp.int32)) % planes
    ring_ctx = (2 * ring[:, None] + jnp.arange(2, dtype=jnp.int32)[None, :]).reshape(-1)
    id_pieces = block_ids.reshape(n, ctx_count, rows)
    ids = id_pieces[chips[:, None], piece_order[ring_ctx][None, :]]
    key_ids = ids.reshape(n, planes, 1, pair)
    query_ids = ids[:, :2].reshape(n, pair, 1)

    def cut_attention(me_ref, *refs):
        wq, wk, wv, wo = (refs[i * n : (i + 1) * n] for i in range(4))
        one, two = refs[4 * n : 4 * n + 2]
        outs = refs[4 * n + 2 :]
        keys_here = me_ref[1] == 0
        for d in range(n):
            first = outs[d]
            first[:wide, :HD] = wq[d][...]

            @pl.when(keys_here)
            def _():
                first[:wide, HD:] = wk[d][...]

            @pl.when(jnp.logical_not(keys_here))
            def _():
                first[:wide, HD:] = wv[d][...]

            pick = lax.broadcasted_iota(jnp.int32, (16, wide), 0) < 8
            first[wide:, :] = jnp.where(pick, one[...].astype(F32), two[...].astype(F32)).astype(
                BF16
            )
            outs[n + d][...] = wo[d][...]

    def head_of(d):
        return lambda i, me: (0, 2 * (me[0] ^ d) + me[1])

    def chip_of(d):
        return lambda i, me: (0, me[0] ^ d)

    def head_rows_of(d):
        return lambda i, me: (2 * (me[0] ^ d) + me[1], 0)

    gain_spec = pl.BlockSpec((1, wide), lambda i, me: (0, 0))
    cut = run_grid(
        cut_attention,
        me,
        (1,),
        [query_weight] * n
        + [key_weight] * n
        + [value_weight] * n
        + [output_weight] * n
        + [first_gain.reshape(1, wide), second_gain.reshape(1, wide)],
        [pl.BlockSpec((wide, HD), head_of(d)) for d in range(n)]
        + [pl.BlockSpec((wide, HD), chip_of(d)) for d in range(n)] * 2
        + [pl.BlockSpec((HD, wide), head_rows_of(d)) for d in range(n)]
        + [gain_spec, gain_spec],
        [shape((wide + 16, 2 * HD))] * n + [shape((HD, wide))] * n,
        [pl.BlockSpec((wide + 16, 2 * HD), lambda i, me: (0, 0))] * n
        + [pl.BlockSpec((HD, wide), lambda i, me: (0, 0))] * n,
        name="cut_attention",
    )
    own_tokens = tokens[0]
    token_own, token_near = gathered(own_tokens)
    weights_in = [cut[0]] + [across(cut[d], d) for d in range(1, n)]
    weights_out = [cut[n]] + [across(cut[n + d], d) for d in range(1, n)]

    def cut_hidden_body(me_ref, *refs):
        gates, ups, downs, outs = (refs[i * n : (i + 1) * n] for i in range(4))
        for d in range(n):
            outs[d][:wide, :quarter] = gates[d][...]
            outs[d][:wide, quarter:] = ups[d][...]
            outs[d][wide:, :] = downs[d][...]

    def cut_hidden(q):
        def columns(d):
            return lambda i, me: (0, (2 * (me[0] ^ d) + me[1]) * QUARTERS + q)

        def down_rows(d):
            return lambda i, me: ((2 * (me[0] ^ d) + me[1]) * QUARTERS + q, 0)

        return run_grid(
            cut_hidden_body,
            me,
            (1,),
            [gate_weight] * n + [up_weight] * n + [down_weight] * n,
            [pl.BlockSpec((wide, quarter), columns(d)) for d in range(n)] * 2
            + [pl.BlockSpec((quarter, wide), down_rows(d)) for d in range(n)],
            [shape((wide + quarter, 2 * quarter))] * n,
            [pl.BlockSpec((wide + quarter, 2 * quarter), lambda i, me: (0, 0))] * n,
            name="cut_hidden",
        )

    def hidden_weights(q):
        pieces = cut_hidden(q)
        return [pieces[0]] + [across(pieces[d], d) for d in range(1, n)]

    feed = [hidden_weights(q) for q in range(QUARTERS)]
    own_cotangent = cotangent[0]
    cot_own = [own_cotangent] + [across(own_cotangent, d) for d in range(1, n)]

    def project(me_ref, *refs):
        near_tokens = refs[: 2 * n]
        pieces = refs[2 * n : 3 * n]
        cos_ref, sin_ref, kvcos_ref, kvsin_ref = refs[3 * n : 3 * n + 4]
        normed_ref, query_ref, kv_ref, gains_ref = refs[3 * n + 4 :]
        chip, side = me_ref[0], me_ref[1]
        for j in range(n):
            both = pieces[j][wide:, :].astype(F32)
            gains_ref[0:1, column(chip ^ j, wide)] = both[0:1]
            gains_ref[1:2, column(chip ^ j, wide)] = both[8:9]
        for d in range(n):
            for e in range(2):
                slot = side ^ e
                values = near_tokens[e * n + d][...].astype(F32)
                inverse = lax.rsqrt(jnp.mean(values * values, axis=-1, keepdims=True) + epsilon)
                normed_ref[d, slot] = (values * inverse * gains_ref[0:1, :]).astype(BF16)
                both = jnp.zeros((rows, 2 * HD), F32)
                for j in range(n):
                    both += matmul(
                        normed_ref[d, slot, :, column(chip ^ j, wide)], pieces[j][:wide, :]
                    )
                query, kv = both[:, :HD], both[:, HD:]
                query_ref[d, slot] = (
                    query * cos_ref[slot] + turn(query) * sin_ref[slot]
                ).astype(BF16)
                kv_ref[d, slot] = (kv * kvcos_ref[slot] + turn(kv) * kvsin_ref[slot]).astype(BF16)

    head_shape = (n, 2, rows, HD)
    tables = [t.reshape(2, rows, HD) for t in (cosine, sine, kv_cosine, kv_sine)]
    normed, query_rot, own_kv, gains = run_whole(
        project,
        me,
        token_own + token_near + weights_in + tables,
        [
            shape((n, 2, rows, width)),
            shape(head_shape),
            shape(head_shape),
            shape((2, width), F32),
        ],
        flops=2 * plane_rows * width * 2 * HD,
        name="project",
    )

    rightward, leftward = [own_kv], [own_kv]
    for _ in range(planes - 1):
        rightward.append(along(rightward[-1], 1))
        leftward.append(along(leftward[-1], -1))
    kv_mine = [own_kv] + [rightward[k] + leftward[planes - k] for k in range(1, planes)]
    kv_near = [sibling(block) for block in kv_mine]

    head_spec = pl.BlockSpec((1, 2, rows, HD), lambda i, me: (i, 0, 0, 0))
    id_specs = [
        pl.BlockSpec((1, pair, 1), lambda i, me: (i, 0, 0)),
        pl.BlockSpec((1, planes, 1, pair), lambda i, me: (i, 0, 0, 0)),
    ]

    def scored(side, query, query_id, key_id, mine, near):
        keys, values, scores = [], [], []
        for k in range(planes):
            a = mine[k][0].reshape(pair, HD)
            b = near[k][0].reshape(pair, HD)
            keys.append(jnp.where(side == 0, a, b))
            values.append(jnp.where(side == 0, b, a))
            score = matmul_nt(query, keys[k]) * scale
            scores.append(jnp.where(key_id[0, k] <= query_id[0], score, masked_score))
        top = functools.reduce(jnp.maximum, [jnp.max(s, axis=-1, keepdims=True) for s in scores])
        raised = [jnp.exp(s - top) for s in scores]
        inverse = 1.0 / sum(jnp.sum(r, axis=-1, keepdims=True) for r in raised)
        return keys, values, [r * inverse for r in raised]

    def spread(step, side, whole, own_refs, near_refs):
        for d in range(n):

            @pl.when(step == d)
            def _():
                own_refs[d][...] = whole[side]
                near_refs[d][...] = whole[1 - side]

    def attend(me_ref, query_ref, query_id, key_id, *refs):
        mine, near, out_w = refs[:planes], refs[planes : 2 * planes], refs[2 * planes : 2 * planes + n]
        attended_ref = refs[2 * planes + n]
        own_refs = refs[2 * planes + n + 1 : 2 * planes + 2 * n + 1]
        near_refs = refs[2 * planes + 2 * n + 1 : 2 * planes + 3 * n + 1]
        whole = refs[-1]
        chip, side = me_ref[0], me_ref[1]
        query = query_ref[0].reshape(pair, HD)
        _, values, probs = scored(side, query, query_id, key_id, mine, near)
        total = jnp.zeros((pair, HD), F32)
        for k in range(planes):
            total += matmul(probs[k].astype(BF16), values[k])
        attended = total.astype(BF16)
        attended_ref[0] = attended.reshape(2, rows, HD)
        for j in range(n):
            whole[:, :, column(chip ^ j, wide)] = (
                matmul(attended, out_w[j][...]).astype(BF16).reshape(2, rows, wide)
            )
        spread(pl.program_id(0), side, whole, own_refs, near_refs)

    early = lax.optimization_barrier([query_rot] + cot_own[1:] + feed[0][1:])
    query_rot, cot_own[1:], feed[0][1:] = early[0], early[1:n], early[n:]
    cot_near = [sibling(block) for block in cot_own]

    block = (rows, width)
    attend_flops = 4 * plane_rows * planes * pair * HD + 2 * plane_rows * HD * width
    attended, *partial = run_grid(
        attend,
        me,
        (n,),
        [query_rot, query_ids, key_ids] + kv_mine + kv_near + weights_out,
        [head_spec] + id_specs + [head_spec] * (2 * planes) + [fixed((HD, wide))] * n,
        [shape(head_shape)] + [shape(block)] * (2 * n),
        [head_spec] + [pl.BlockSpec(block, lambda i, me: (0, 0))] * (2 * n),
        scratch=[pltpu.VMEM((2, rows, width), BF16)],
        flops=attend_flops,
        name="attend",
    )
    middle_terms = reduced(partial[:n], partial[n:])

    def second_norm(me_ref, token_ref, gains_ref, *refs):
        terms, (middle_ref, normed_ref) = refs[:-2], refs[-2:]
        middle = token_ref[...].astype(F32)
        middle += sum(t[...].astype(F32) for t in terms)
        inverse = lax.rsqrt(jnp.mean(middle * middle, axis=-1, keepdims=True) + epsilon)
        middle_ref[...] = middle
        normed_ref[...] = (middle * inverse * gains_ref[1:2, :]).astype(BF16)

    middle, own_normed_two = run_whole(
        second_norm,
        me,
        [own_tokens, gains] + middle_terms,
        [shape(block, F32), shape(block)],
        name="second_norm",
    )
    two_own, two_near = gathered(own_normed_two)

    tile = plane_rows // 3

    def feed_forward(me_ref, *refs):
        pieces = refs[:n]
        two_refs, cot_refs = refs[n : 3 * n], refs[3 * n : 5 * n]
        hidden_ref, gate_ref, up_ref, dgate, dup, ddown = refs[5 * n : 5 * n + 6]
        two, cot, turned, two_sem, cot_sem = refs[5 * n + 6 :]
        chip = me_ref[0]
        copies = []
        for source, target, sems in ((two_refs, two, two_sem), (cot_refs, cot, cot_sem)):
            for i in range(2 * n):
                copies.append(
                    pltpu.make_async_copy(
                        source[i], target.at[pl.ds(i * rows, rows)], sems.at[i]
                    )
                )
        for copy in copies:
            copy.start()
        for copy in copies:
            copy.wait()

        def forward(t, _):
            here = pl.ds(pl.multiple_of(t * tile, tile), tile)
            both = jnp.zeros((tile, 2 * quarter), F32)
            hidden_grad = jnp.zeros((tile, quarter), F32)
            for j in range(n):
                both += matmul(two[here, column(chip ^ j, wide)], pieces[j][:wide, :])
                hidden_grad += matmul_nt(cot[here, column(chip ^ j, wide)], pieces[j][wide:, :])
            gate, up = both[:, :quarter], both[:, quarter:]
            share = 1.0 / (1.0 + jnp.exp(-gate))
            activated = gate * share
            results = (
                activated * up,
                hidden_grad * up * share * (1.0 + gate * (1.0 - share)),
                hidden_grad * activated,
            )
            for i, (result, ref) in enumerate(zip(results, (hidden_ref, gate_ref, up_ref))):
                ref[here, :] = result.astype(BF16)
                turned[i, :, here] = result.T.astype(BF16)
            return 0

        lax.fori_loop(0, plane_rows // tile, forward, 0)
        for j in range(n):
            here = column(chip ^ j, wide)
            dgate[j] = matmul(turned[1], two[:, here]).astype(BF16)
            dup[j] = matmul(turned[2], two[:, here]).astype(BF16)
            ddown[j] = matmul(turned[0], cot[:, here]).astype(BF16)

    grad_tile = (n, quarter, wide)
    hiddens, gate_grads, up_grads, hidden_tiles = [], [], [], []
    for q in range(QUARTERS):
        hidden, gate_grad, up_grad, *tiles = run_whole(
            feed_forward,
            me,
            feed[q] + two_own + two_near + cot_own + cot_near,
            [shape((plane_rows, quarter))] * 3 + [shape(grad_tile)] * 3,
            scratch=[
                pltpu.VMEM((plane_rows, width), BF16),
                pltpu.VMEM((plane_rows, width), BF16),
                pltpu.VMEM((3, quarter, plane_rows), BF16),
                pltpu.SemaphoreType.DMA((2 * n,)),
                pltpu.SemaphoreType.DMA((2 * n,)),
            ],
            flops=12 * plane_rows * width * quarter,
            in_hbm=4 * n,
            name="feed_forward",
        )
        hiddens.append(hidden)
        gate_grads.append(gate_grad)
        up_grads.append(up_grad)
        hidden_tiles.append(tiles)

    pieces = [feed[q][j] for q in range(QUARTERS) for j in range(n)]
    piece_specs = [fixed((wide + quarter, 2 * quarter))] * (QUARTERS * n)
    pair_spec = pl.BlockSpec((2, 1, rows, quarter), lambda i, me: (0, i, 0, 0))
    out_specs = [pl.BlockSpec(block, lambda i, me: (0, 0))] * (2 * n)

    def put(step, results, own_refs, near_refs, chip):
        for d in range(n):

            @pl.when(step == d)
            def _():
                for j in range(n):
                    here = column(chip ^ j, wide)
                    own_refs[d][:, here] = results[j][:rows]
                    near_refs[d][:, here] = results[j][rows:]

    def feed_forward_back(me_ref, *refs):
        gates, ups = refs[:QUARTERS], refs[QUARTERS : 2 * QUARTERS]
        pieces = refs[2 * QUARTERS : 2 * QUARTERS + QUARTERS * n]
        outs = refs[2 * QUARTERS + QUARTERS * n :]
        lefts = [
            jnp.concatenate(
                [g[:, 0].reshape(pair, quarter), u[:, 0].reshape(pair, quarter)], axis=1
            )
            for g, u in zip(gates, ups)
        ]
        results = []
        for j in range(n):
            total = jnp.zeros((pair, wide), F32)
            for q in range(QUARTERS):
                total += matmul_nt(lefts[q], pieces[q * n + j][:wide, :])
            results.append(total.astype(BF16))
        put(pl.program_id(0), results, outs[:n], outs[n:], me_ref[0])

    def by_block(value):
        return value.reshape(2, n, rows, quarter)

    back = run_grid(
        feed_forward_back,
        me,
        (n,),
        [by_block(g) for g in gate_grads] + [by_block(u) for u in up_grads] + pieces,
        [pair_spec] * (2 * QUARTERS) + piece_specs,
        [shape(block)] * (2 * n),
        out_specs,
        flops=4 * plane_rows * width * part,
        name="feed_forward_back",
    )
    two_grad_terms = reduced(back[:n], back[n:])

    def norm_back(values, inverse, gain, grad):
        unit = values * inverse
        scaled = grad * gain
        return inverse * (scaled - unit * jnp.mean(scaled * unit, axis=-1, keepdims=True)), jnp.sum(
            grad * unit, axis=0, keepdims=True
        )

    def second_norm_back(me_ref, middle_ref, cot_ref, gains_ref, *refs):
        terms, (middle_grad_ref, branch_ref, gain_ref, flat) = refs[:-4], refs[-4:]
        middle = middle_ref[...]
        inverse = lax.rsqrt(jnp.mean(middle * middle, axis=-1, keepdims=True) + epsilon)
        grad = sum(t[...].astype(F32) for t in terms)
        back, gain_term = norm_back(middle, inverse, gains_ref[1:2, :], grad)
        middle_grad = cot_ref[...].astype(F32) + back
        middle_grad_ref[...] = middle_grad
        branch_ref[...] = middle_grad.astype(BF16)
        flat[...] = gain_term
        for j in range(n):
            gain_ref[j] = flat[:, column(me_ref[0] ^ j, wide)]

    gain_shape = shape((n, 1, wide), F32)
    middle_grad, branch_grad, gain_two_term = run_whole(
        second_norm_back,
        me,
        [middle, own_cotangent, gains] + two_grad_terms,
        [shape(block, F32), shape(block), gain_shape],
        scratch=[pltpu.VMEM((1, width), F32)],
        name="second_norm_back",
    )
    branch_own, branch_near = gathered(branch_grad)

    def attend_back(me_ref, query_ref, query_id, key_id, cos_ref, sin_ref, *refs):
        mine, near, out_w = refs[:planes], refs[planes : 2 * planes], refs[2 * planes : 2 * planes + n]
        branch_refs = refs[2 * planes + n : 2 * planes + 3 * n]
        query_grad_ref = refs[2 * planes + 3 * n]
        keep_refs = refs[2 * planes + 3 * n + 1 : 3 * planes + 3 * n + 1]
        send_refs = refs[3 * planes + 3 * n + 1 : 4 * planes + 3 * n + 1]
        branch = refs[-1]
        chip, side = me_ref[0], me_ref[1]
        for d in range(n):

            @pl.when(pl.program_id(0) == d)
            def _():
                branch[side] = branch_refs[d][...]
                branch[1 - side] = branch_refs[n + d][...]

        query = query_ref[0].reshape(pair, HD)
        attended_grad = jnp.zeros((pair, HD), F32)
        for j in range(n):
            attended_grad += matmul_nt(
                branch[:, :, column(chip ^ j, wide)].reshape(pair, wide), out_w[j][...]
            )
        attended_grad = attended_grad.astype(BF16)
        keys, values, probs = scored(side, query, query_id, key_id, mine, near)
        low = [p.astype(BF16) for p in probs]
        shares = [matmul_nt(attended_grad, values[k]) for k in range(planes)]
        delta = sum(
            jnp.sum(low[k].astype(F32) * shares[k], axis=-1, keepdims=True) for k in range(planes)
        )
        query_grad = jnp.zeros((pair, HD), F32)
        for k in range(planes):
            score_grad = (probs[k] * (shares[k] - delta)).astype(BF16)
            query_grad += matmul(score_grad, keys[k])
            key_grad = matmul_tn(score_grad, query) * scale
            value_grad = matmul_tn(low[k], attended_grad)
            keep_refs[k][0] = jnp.where(side == 0, key_grad, value_grad).astype(BF16).reshape(
                2, rows, HD
            )
            send_refs[k][0] = jnp.where(side == 0, value_grad, key_grad).astype(BF16).reshape(
                2, rows, HD
            )
        query_grad = query_grad * scale
        query_grad = query_grad * cos_ref[...] + turn_back(query_grad * sin_ref[...])
        query_grad_ref[0] = query_grad.astype(BF16).reshape(2, rows, HD)

    query_grad, *kv_grads = run_grid(
        attend_back,
        me,
        (n,),
        [query_rot, query_ids, key_ids, cosine, sine]
        + kv_mine
        + kv_near
        + weights_out
        + branch_own
        + branch_near,
        [head_spec]
        + id_specs
        + [fixed((pair, HD))] * 2
        + [head_spec] * (2 * planes)
        + [fixed((HD, wide))] * n
        + [fixed(block)] * (2 * n),
        [shape(head_shape)] * (1 + 2 * planes),
        [head_spec] * (1 + 2 * planes),
        scratch=[pltpu.VMEM((2, rows, width), BF16)],
        flops=10 * plane_rows * planes * pair * HD + 2 * plane_rows * HD * width,
        name="attend_back",
    )
    kept, handed = kv_grads[:planes], kv_grads[planes:]
    kv_sums = [
        (kept[k].astype(F32) + sibling(handed[k]).astype(F32)).astype(BF16) for k in range(planes)
    ]
    from_above = jnp.zeros_like(own_kv)
    from_below = jnp.zeros_like(own_kv)
    for k in range(planes - 1, 0, -1):
        below = jnp.where(z >= k, kv_sums[k], 0).astype(F32) + from_above.astype(F32)
        above = jnp.where(z + k < planes, kv_sums[planes - k], 0).astype(F32) + from_below.astype(F32)
        from_above = along(below.astype(BF16), -1)
        from_below = along(above.astype(BF16), 1)

    def project_back(me_ref, *refs):
        own_ref, above_ref, below_ref, query_grad_ref, kvcos_ref, kvsin_ref = refs[:6]
        pieces = refs[6 : 6 + n]
        kv_ref = refs[6 + n]
        own_refs, near_refs = refs[7 + n : 7 + 2 * n], refs[7 + 2 * n : 7 + 3 * n]
        chip, side = me_ref[0], me_ref[1]
        for d in range(n):
            for e in range(2):
                slot = side ^ e
                grad = own_ref[d, slot].astype(F32) + above_ref[d, slot].astype(F32)
                grad = grad + below_ref[d, slot].astype(F32)
                grad = grad * kvcos_ref[slot] + turn_back(grad * kvsin_ref[slot])
                grad = grad.astype(BF16)
                kv_ref[d, slot] = grad
                left = jnp.concatenate([query_grad_ref[d, slot], grad], axis=1)
                target = (own_refs, near_refs)[e][d]
                for j in range(n):
                    target[:, column(chip ^ j, wide)] = matmul_nt(left, pieces[j][:wide, :]).astype(
                        BF16
                    )

    kv_grad, *partial = run_whole(
        project_back,
        me,
        [kv_sums[0], from_above, from_below, query_grad] + tables[2:] + weights_in,
        [shape(head_shape)] + [shape(block)] * (2 * n),
        flops=4 * plane_rows * width * HD,
        name="project_back",
    )
    one_grad_terms = reduced(partial[:n], partial[n:])

    def first_norm_back(me_ref, token_ref, middle_grad_ref, gains_ref, *refs):
        terms, (grad_ref, gain_ref, flat) = refs[:-3], refs[-3:]
        values = token_ref[...].astype(F32)
        inverse = lax.rsqrt(jnp.mean(values * values, axis=-1, keepdims=True) + epsilon)
        grad = sum(t[...].astype(F32) for t in terms)
        back, gain_term = norm_back(values, inverse, gains_ref[0:1, :], grad)
        grad_ref[...] = middle_grad_ref[...] + back
        flat[...] = gain_term
        for j in range(n):
            gain_ref[j] = flat[:, column(me_ref[0] ^ j, wide)]

    tokens_grad, gain_one_term = run_whole(
        first_norm_back,
        me,
        [own_tokens, middle_grad, gains] + one_grad_terms,
        [shape(block, F32), gain_shape],
        scratch=[pltpu.VMEM((1, width), F32)],
        name="first_norm_back",
    )
    gain_terms = jnp.concatenate([gain_one_term, gain_two_term], axis=1)
    gain_sum = gain_terms[0] + sum(across(gain_terms[d], d) for d in range(1, n))
    gain_sum = gain_sum + sibling(gain_sum)
    gain_sum = summed_over_planes(gain_sum)

    def outer(me_ref, left_ref, right_ref, out_ref):
        turned = left_ref[...].reshape(plane_rows, HD).astype(F32).T.astype(BF16)
        for j in range(n):
            right = right_ref[:, :, :, column(me_ref[0] ^ j, wide)].reshape(plane_rows, wide)
            out_ref[j] = matmul(turned, right).astype(BF16)

    def outer_branch(me_ref, left_ref, *refs):
        branch_refs, (out_ref, right_ref, sems) = refs[: 2 * n], refs[2 * n :]
        copies = []
        for e in range(2):
            for d in range(n):
                copies.append(
                    pltpu.make_async_copy(
                        branch_refs[e * n + d],
                        right_ref.at[d, me_ref[1] ^ e],
                        sems.at[e * n + d],
                    )
                )
        for copy in copies:
            copy.start()
        for copy in copies:
            copy.wait()
        outer(me_ref, left_ref, right_ref, out_ref)

    outer_flops = 2 * plane_rows * width * HD
    outer_tile = shape((n, HD, wide))
    query_tile = run_whole(
        outer, me, [query_grad, normed], outer_tile, flops=outer_flops, name="query_outer"
    )
    output_tile = run_whole(
        outer_branch,
        me,
        [attended] + branch_own + branch_near,
        outer_tile,
        scratch=[pltpu.VMEM((n, 2, rows, width), BF16), pltpu.SemaphoreType.DMA((2 * n,))],
        flops=outer_flops,
        in_hbm=2 * n,
        name="output_outer",
    )
    kv_tile = run_whole(outer, me, [kv_grad, normed], outer_tile, flops=outer_flops, name="kv_outer")

    def deal(me_ref, *refs):
        count = (len(refs) - n) // 2
        sums, backs, outs = refs[:count], refs[count : 2 * count], refs[2 * count :]
        outer_plane = me_ref[2] == 1

        @pl.when(outer_plane)
        def _():
            for d in range(n):
                for w in range(count):
                    outs[d][w] = backs[w][d]

        @pl.when(jnp.logical_not(outer_plane))
        def _():
            for d in range(n):
                for w in range(count):
                    outs[d][w] = sums[w][d]

    is_outer = ((z == 0) | (z == planes - 1)).astype(jnp.int32)
    me_and_plane = jnp.concatenate([me, is_outer[None]])
    stages = len(folds) * 2 + 1

    def stage_moves(stage):
        if stage < len(folds):
            return folds[stage]
        if stage == len(folds):
            return [(middle_left, middle_right), (middle_right, middle_left)]
        return [(b, a) for a, b in folds[stages - 1 - stage]]

    def pipelined(tiles):
        ends = {}
        for line in range(LINES):
            waiting = []
            feed_line = list(range(line, len(tiles), LINES))
            while feed_line or waiting:
                if feed_line:
                    first = feed_line.pop(0)
                    waiting.append((first, 0, tiles[first]))
                operands = lax.optimization_barrier([value for _, _, value in waiting])
                moved = []
                for (index, stage, _), value in zip(waiting, operands):
                    other = between_planes(value, stage_moves(stage))
                    if stage == stages - 1:
                        ends[index] = (value, other)
                        continue
                    if stage <= len(folds):
                        value = (value.astype(F32) + other.astype(F32)).astype(BF16)
                    else:
                        s = stages - 1 - stage
                        value = jnp.where((z == s) | (z == planes - 1 - s), other, value)
                    moved.append((index, stage + 1, value))
                waiting = moved
        return [ends[i] for i in range(len(tiles))]

    order = [t for q in range(QUARTERS) for t in hidden_tiles[q]] + [query_tile, output_tile, kv_tile]
    plane_sums = pipelined(order)

    def owned(ends):
        dealt = run_whole(
            deal,
            me_and_plane,
            [a for a, _ in ends] + [b for _, b in ends],
            [shape((len(ends),) + ends[0][0].shape[1:])] * n,
            name="deal",
        )
        own = [dealt[0]] + [across(dealt[d], d) for d in range(1, n)]
        return own + [sibling(block) for block in own]

    def slot_of(q, count):
        def where(i, me):
            return (2 * (me[0] ^ (i % n)) + (me[1] ^ (i // n))) * count + q

        return where

    def place_hidden(me_ref, *refs):
        tiles = refs[: 2 * n]
        gate_out, up_out, down_out = refs[-3:]
        for i in range(2 * n):

            @pl.when(pl.program_id(0) == i)
            def _():
                gate_out[...] = tiles[i][0].astype(F32).T
                up_out[...] = tiles[i][1].astype(F32).T
                down_out[...] = tiles[i][2].astype(F32)

    hidden_outs = [
        shape(gate_weight.shape, F32),
        shape(up_weight.shape, F32),
        shape(down_weight.shape, F32),
    ]
    held = None
    for q in range(QUARTERS):
        tiles = owned(plane_sums[3 * q : 3 * q + 3])
        where = slot_of(q, QUARTERS)
        by_columns = pl.BlockSpec((wide, quarter), lambda i, me, w=where: (0, w(i, me)))
        by_rows = pl.BlockSpec((quarter, wide), lambda i, me, w=where: (w(i, me), 0))
        rest = [] if held is None else list(held)
        held = run_grid(
            place_hidden,
            me,
            (2 * n,),
            tiles + rest,
            [fixed((3, quarter, wide))] * (2 * n) + [pl.BlockSpec(memory_space=pl.ANY)] * len(rest),
            hidden_outs,
            [by_columns, by_columns, by_rows],
            aliases={1 + 2 * n + i: i for i in range(len(rest))},
            name="place_hidden",
        )

    def place_query(me_ref, *refs):
        tiles, (query_out, output_out) = refs[: 2 * n], refs[2 * n :]
        for i in range(2 * n):

            @pl.when(pl.program_id(0) == i)
            def _():
                query_out[...] = tiles[i][0].astype(F32).T
                output_out[...] = tiles[i][1].astype(F32)

    where = slot_of(0, 1)
    query_weight_grad, output_weight_grad = run_grid(
        place_query,
        me,
        (2 * n,),
        owned(plane_sums[3 * QUARTERS : 3 * QUARTERS + 2]),
        [fixed((2, HD, wide))] * (2 * n),
        [shape(query_weight.shape, F32), shape(output_weight.shape, F32)],
        [
            pl.BlockSpec((wide, HD), lambda i, me: (0, where(i, me))),
            pl.BlockSpec((HD, wide), lambda i, me: (where(i, me), 0)),
        ],
        name="place_query",
    )

    def place_kv(me_ref, *refs):
        tiles, (key_out, value_out) = refs[: 2 * n], refs[2 * n :]
        keys_here = me_ref[1] == 0
        for d in range(n):

            @pl.when(pl.program_id(0) == d)
            def _():
                own, near = tiles[d][0].astype(F32).T, tiles[n + d][0].astype(F32).T
                key_out[...] = jnp.where(keys_here, own, near)
                value_out[...] = jnp.where(keys_here, near, own)

    by_chip = pl.BlockSpec((wide, HD), lambda i, me: (0, me[0] ^ i))
    key_weight_grad, value_weight_grad = run_grid(
        place_kv,
        me,
        (n,),
        owned(plane_sums[3 * QUARTERS + 2 :]),
        [fixed((1, HD, wide))] * (2 * n),
        [shape(key_weight.shape, F32), shape(value_weight.shape, F32)],
        [by_chip, by_chip],
        name="place_kv",
    )

    def feed_forward_out(me_ref, *refs):
        hiddens = refs[:QUARTERS]
        pieces = refs[QUARTERS : QUARTERS + QUARTERS * n]
        outs = refs[QUARTERS + QUARTERS * n :]
        results = []
        for j in range(n):
            total = jnp.zeros((pair, wide), F32)
            for q in range(QUARTERS):
                total += matmul(hiddens[q][:, 0].reshape(pair, quarter), pieces[q * n + j][wide:, :])
            results.append(total.astype(BF16))
        put(pl.program_id(0), results, outs[:n], outs[n:], me_ref[0])

    partial = run_grid(
        feed_forward_out,
        me,
        (n,),
        [by_block(h) for h in hiddens] + pieces,
        [pair_spec] * QUARTERS + piece_specs,
        [shape(block)] * (2 * n),
        out_specs,
        flops=2 * plane_rows * width * part,
        name="feed_forward_out",
    )
    output = middle + sum(t.astype(F32) for t in reduced(partial[:n], partial[n:]))

    return (
        output.astype(BF16)[None],
        tokens_grad[None],
        query_weight_grad,
        key_weight_grad,
        value_weight_grad,
        output_weight_grad,
        gain_sum[0],
        held[0],
        held[1],
        held[2],
        gain_sum[1],
    )


def solution(mesh):
    chips, pieces = mesh.shape["fsdp"], mesh.shape["ctx"]
    one_head_each = 2 * chips == H and chips == KVH and pieces % 4 == 0 and pieces > 4
    return jax.shard_map(
        plane_layer if one_head_each else ring_layer,
        mesh=mesh,
        in_specs=(
            P("fsdp", "ctx", None),
            P("fsdp", None),
            P("fsdp", None),
            P("fsdp", None),
            P(None, "fsdp"),
            P("fsdp"),
            P("fsdp", None),
            P("fsdp", None),
            P(None, "fsdp"),
            P("fsdp"),
            P("fsdp", "ctx", None),
            P(),
            P(),
        ),
        out_specs=(
            P("fsdp", "ctx", None),
            P("fsdp", "ctx", None),
            P("fsdp", None),
            P("fsdp", None),
            P("fsdp", None),
            P(None, "fsdp"),
            P("fsdp"),
            P("fsdp", None),
            P("fsdp", None),
            P(None, "fsdp"),
            P("fsdp"),
        ),
        check_vma=False,
    )
```

```python
import functools

import jax
import jax.numpy as jnp
from jax import lax
from jax.experimental import pallas as pl
from jax.experimental.pallas import tpu as pltpu
from jax.sharding import PartitionSpec as P

H = 8
KVH = 4
HD = 256


epsilon = 1e-06
theta = 1000042.0
masked_score = -1e30


def passed_along(value, axis, by):
    devices = lax.axis_size(axis)
    return lax.ppermute(value, axis, [(i, (i + by) % devices) for i in range(devices)])


def rope_tables(positions):
    half = HD // 2
    frequency = theta ** (-(jnp.arange(half, dtype=jnp.float32) * 2.0 / HD))
    angle = positions[:, None] * frequency[None, :]
    angle = jnp.concatenate([angle, angle], axis=-1)
    return (jnp.cos(angle), jnp.sin(angle))


def rotate(values, cosine, sine):
    half = values.shape[-1] // 2
    turned = jnp.concatenate([-values[..., half:], values[..., :half]], axis=-1)
    return values * cosine[:, None, :] + turned * sine[:, None, :]


def rotate_back(grads, cosine, sine):
    half = grads.shape[-1] // 2
    scaled = grads * sine[:, None, :]
    turned = jnp.concatenate([scaled[..., half:], -scaled[..., :half]], axis=-1)
    return grads * cosine[:, None, :] + turned


def split_heads(block):
    count = block.shape[0]
    key_cols = KVH * HD
    key_part = block[:, :key_cols].reshape(count, KVH, HD).transpose(1, 0, 2)
    value_part = block[:, key_cols:].reshape(count, KVH, HD).transpose(1, 0, 2)
    return (key_part, value_part)


def merge_heads(grouped):
    return grouped.transpose(1, 0, 2).reshape(grouped.shape[1], KVH * HD)


def weight_terms(lefts, rights):
    pieces = []
    for index in range(4):
        column = lefts[index]
        pieces.append(
            jnp.einsum("tc,tn->cn", column, rights[index], preferred_element_type=jnp.float32)
        )
    return jnp.concatenate(pieces, axis=1)


def ring_layer(
    tokens,
    query_weight,
    key_weight,
    value_weight,
    output_weight,
    first_gain,
    gate_weight,
    up_weight,
    down_weight,
    second_gain,
    cotangent,
    block_ids,
    piece_order,
):
    ctx_count = lax.axis_size("ctx")
    fsdp_count = lax.axis_size("fsdp")
    here = lax.axis_index("ctx")
    rows = tokens.shape[1]
    width = tokens.shape[2]
    group = H // KVH
    query_cols = H * HD
    key_cols = KVH * HD
    hidden_cols = gate_weight.shape[1]
    scale = HD ** (-0.5)
    whole_query, whole_key, whole_value, whole_output, gain_one = (
        lax.all_gather(query_weight, "fsdp", axis=0, tiled=True),
        lax.all_gather(key_weight, "fsdp", axis=0, tiled=True),
        lax.all_gather(value_weight, "fsdp", axis=0, tiled=True),
        lax.all_gather(output_weight, "fsdp", axis=1, tiled=True),
        lax.all_gather(first_gain, "fsdp", axis=0, tiled=True),
    )
    id_row = lax.dynamic_index_in_dim(block_ids, lax.axis_index("fsdp"), 0, keepdims=False)
    start_own = lax.dynamic_index_in_dim(piece_order, here, 0, keepdims=False) * rows
    offsets = jnp.arange(rows, dtype=jnp.int32)
    cosine, sine = rope_tables((start_own + offsets).astype(jnp.float32))
    own_ids = lax.dynamic_slice_in_dim(id_row, start_own, rows)
    query_ids = jnp.tile(own_ids, group)

    def visible(source):
        key_start = lax.dynamic_index_in_dim(piece_order, source, 0, keepdims=False) * rows
        key_ids = lax.dynamic_slice_in_dim(id_row, key_start, rows)
        return key_ids[None, :] <= query_ids[:, None]

    inputs = tokens[0].astype(jnp.float32)
    scale_one = lax.rsqrt(jnp.mean(inputs * inputs, axis=-1, keepdims=True) + epsilon)
    unit_one = inputs * scale_one
    normed = (unit_one * gain_one.astype(jnp.float32)).astype(jnp.bfloat16)
    query = jnp.dot(normed, whole_query, preferred_element_type=jnp.float32).reshape(rows, H, HD)
    query_rot = rotate(query, cosine, sine).astype(jnp.bfloat16)
    keys = jnp.dot(normed, whole_key, preferred_element_type=jnp.float32).reshape(rows, KVH, HD)
    keys_rot = rotate(keys, cosine, sine).astype(jnp.bfloat16).reshape(rows, key_cols)
    values = jnp.dot(normed, whole_value, preferred_element_type=jnp.float32).astype(jnp.bfloat16)
    key_value = jnp.concatenate([keys_rot, values], axis=-1)
    grouped = (
        query_rot.reshape(rows, KVH, group, HD).transpose(1, 2, 0, 3).reshape(KVH, group * rows, HD)
    )

    def forward_step(state, block, source):
        running, total, weighted = state
        key_part, value_part = split_heads(block)
        allowed = visible(source)
        scores = (
            jnp.einsum("hqd,hkd->hqk", grouped, key_part, preferred_element_type=jnp.float32)
            * scale
        )
        scores = jnp.where(allowed[None], scores, masked_score)
        newest = jnp.maximum(running, jnp.max(scores, axis=-1))
        factor = jnp.exp(running - newest)
        shares = jnp.where(allowed[None], jnp.exp(scores - newest[..., None]), 0.0)
        total = total * factor + jnp.sum(shares, axis=-1)
        weighted = weighted * factor[..., None] + jnp.einsum(
            "hqk,hkd->hqd",
            shares.astype(jnp.bfloat16),
            value_part,
            preferred_element_type=jnp.float32,
        )
        return (newest, total, weighted)

    start_state = (
        jnp.full((KVH, group * rows), masked_score, jnp.float32),
        jnp.zeros((KVH, group * rows), jnp.float32),
        jnp.zeros((KVH, group * rows, HD), jnp.float32),
    )
    state = forward_step(start_state, key_value, here)

    def forward_turn(turn, carry):
        block, inner = carry
        block = passed_along(block, "ctx", 1)
        source = (here - turn) % ctx_count
        return (block, forward_step(inner, block, source))

    passed_block, state = lax.fori_loop(1, ctx_count, forward_turn, (key_value, state))
    running, total, weighted = state
    attended = weighted / total[..., None]
    log_total = running + jnp.log(total)
    attended_low = (
        attended.reshape(KVH, group, rows, HD)
        .transpose(2, 0, 1, 3)
        .reshape(rows, query_cols)
        .astype(jnp.bfloat16)
    )
    middle = inputs + jnp.dot(attended_low, whole_output, preferred_element_type=jnp.float32)
    gain_two, whole_gate, whole_up, whole_down = (
        lax.all_gather(second_gain, "fsdp", axis=0, tiled=True),
        lax.all_gather(gate_weight, "fsdp", axis=0, tiled=True),
        lax.all_gather(up_weight, "fsdp", axis=0, tiled=True),
        lax.all_gather(down_weight, "fsdp", axis=1, tiled=True),
    )
    scale_two = lax.rsqrt(jnp.mean(middle * middle, axis=-1, keepdims=True) + epsilon)
    unit_two = middle * scale_two
    normed_two = (unit_two * gain_two.astype(jnp.float32)).astype(jnp.bfloat16)
    gate = jnp.dot(normed_two, whole_gate, preferred_element_type=jnp.float32)
    up = jnp.dot(normed_two, whole_up, preferred_element_type=jnp.float32)
    sigmoid_gate = jax.nn.sigmoid(gate)
    activated = gate * sigmoid_gate
    hidden = (activated * up).astype(jnp.bfloat16)
    result = middle + jnp.dot(hidden, whole_down, preferred_element_type=jnp.float32)
    output = result.astype(jnp.bfloat16)[None]
    upstream = cotangent[0]
    hidden_grad = jnp.einsum("tm,fm->tf", upstream, whole_down, preferred_element_type=jnp.float32)
    gate_grad = (hidden_grad * up * sigmoid_gate * (1.0 + gate * (1.0 - sigmoid_gate))).astype(
        jnp.bfloat16
    )
    up_grad = (hidden_grad * activated).astype(jnp.bfloat16)
    normed_two_grad = jnp.einsum(
        "tf,mf->tm", gate_grad, whole_gate, preferred_element_type=jnp.float32
    ) + jnp.einsum("tf,mf->tm", up_grad, whole_up, preferred_element_type=jnp.float32)
    gain_two_term = jnp.sum(normed_two_grad * unit_two, axis=0)
    unit_two_grad = normed_two_grad * gain_two.astype(jnp.float32)
    middle_grad = upstream.astype(jnp.float32) + scale_two * (
        unit_two_grad - unit_two * jnp.mean(unit_two_grad * unit_two, axis=-1, keepdims=True)
    )
    branch_grad = middle_grad.astype(jnp.bfloat16)
    attended_grad = jnp.einsum(
        "tm,cm->tc", branch_grad, whole_output, preferred_element_type=jnp.float32
    ).astype(jnp.bfloat16)
    grad_grouped = (
        attended_grad.reshape(rows, KVH, group, HD)
        .transpose(1, 2, 0, 3)
        .reshape(KVH, group * rows, HD)
    )
    delta = jnp.sum(grad_grouped.astype(jnp.float32) * attended, axis=-1)

    def backward_step(query_total, block, source):
        key_part, value_part = split_heads(block)
        allowed = visible(source)
        scores = (
            jnp.einsum("hqd,hkd->hqk", grouped, key_part, preferred_element_type=jnp.float32)
            * scale
        )
        scores = jnp.where(allowed[None], scores, masked_score)
        shares = jnp.where(allowed[None], jnp.exp(scores - log_total[..., None]), 0.0)
        value_grad = jnp.einsum(
            "hqk,hqd->hkd",
            shares.astype(jnp.bfloat16),
            grad_grouped,
            preferred_element_type=jnp.float32,
        )
        share_grad = jnp.einsum(
            "hqd,hkd->hqk", grad_grouped, value_part, preferred_element_type=jnp.float32
        )
        score_grad = (shares * (share_grad - delta[..., None])).astype(jnp.bfloat16)
        query_total = query_total + jnp.einsum(
            "hqk,hkd->hqd", score_grad, key_part, preferred_element_type=jnp.float32
        )
        key_grad = (
            jnp.einsum("hqk,hqd->hkd", score_grad, grouped, preferred_element_type=jnp.float32)
            * scale
        )
        return (
            query_total,
            jnp.concatenate([merge_heads(key_grad), merge_heads(value_grad)], axis=-1),
        )

    query_total, first_grad = backward_step(
        jnp.zeros((KVH, group * rows, HD), jnp.float32), key_value, here
    )
    held = first_grad

    def backward_turn(turn, carry):
        block, kept, total_query = carry
        block = passed_along(block, "ctx", 1)
        source = (here - turn) % ctx_count
        total_query, block_grad = backward_step(total_query, block, source)
        kept = passed_along(kept.astype(jnp.bfloat16), "ctx", 1).astype(kept.dtype) + block_grad
        return (block, kept, total_query)

    passed_again, held, query_total = lax.fori_loop(
        1, ctx_count, backward_turn, (key_value, held, query_total)
    )
    own_grad = passed_along(held.astype(jnp.bfloat16), "ctx", 1).astype(held.dtype)
    query_rot_grad = (
        (query_total * scale)
        .reshape(KVH, group, rows, HD)
        .transpose(2, 0, 1, 3)
        .reshape(rows, H, HD)
    )
    query_grad = (
        rotate_back(query_rot_grad, cosine, sine).reshape(rows, query_cols).astype(jnp.bfloat16)
    )
    key_grad = (
        rotate_back(own_grad[:, :key_cols].reshape(rows, KVH, HD), cosine, sine)
        .reshape(rows, key_cols)
        .astype(jnp.bfloat16)
    )
    value_grad = own_grad[:, key_cols:].astype(jnp.bfloat16)
    normed_grad = jnp.einsum(
        "tc,mc->tm", query_grad, whole_query, preferred_element_type=jnp.float32
    )
    normed_grad = normed_grad + jnp.einsum(
        "tc,mc->tm", key_grad, whole_key, preferred_element_type=jnp.float32
    )
    normed_grad = normed_grad + jnp.einsum(
        "tc,mc->tm", value_grad, whole_value, preferred_element_type=jnp.float32
    )
    gain_one_term = jnp.sum(normed_grad * unit_one, axis=0)
    unit_one_grad = normed_grad * gain_one.astype(jnp.float32)
    tokens_grad = middle_grad + scale_one * (
        unit_one_grad - unit_one * jnp.mean(unit_one_grad * unit_one, axis=-1, keepdims=True)
    )
    projected = jnp.concatenate([query_grad, key_grad, value_grad], axis=-1)
    gate_up = jnp.concatenate([gate_grad, up_grad], axis=-1)
    lefts = jnp.stack([normed, branch_grad, normed_two, upstream])
    rights = (projected, attended_low, gate_up, hidden)
    piece = lax.psum_scatter(
        weight_terms(lefts, rights).astype(jnp.bfloat16), "fsdp", scatter_dimension=0, tiled=True
    )
    shard = lax.psum(piece, "ctx").astype(jnp.float32)
    gain_one_sum, gain_two_sum = lax.psum((gain_one_term, gain_two_term), ("ctx", "fsdp"))
    own_rows = width // fsdp_count
    own_start = lax.axis_index("fsdp") * own_rows
    value_begin = query_cols + key_cols
    output_begin = value_begin + key_cols
    gate_begin = output_begin + query_cols
    up_begin = gate_begin + hidden_cols
    down_begin = up_begin + hidden_cols
    return (
        output,
        tokens_grad[None],
        shard[:, :query_cols],
        shard[:, query_cols:value_begin],
        shard[:, value_begin:output_begin],
        shard[:, output_begin:gate_begin].T,
        lax.dynamic_slice_in_dim(gain_one_sum, own_start, own_rows),
        shard[:, gate_begin:up_begin],
        shard[:, up_begin:down_begin],
        shard[:, down_begin : down_begin + hidden_cols].T,
        lax.dynamic_slice_in_dim(gain_two_sum, own_start, own_rows),
    )


VMEM_BYTES = 58 * 1024 * 1024
BF16 = jnp.bfloat16
F32 = jnp.float32
QUARTERS = 4
MESH = pl.DeviceIdType.MESH
LINES = 2


def matmul(a, b):
    return lax.dot_general(a, b, (((1,), (0,)), ((), ())), preferred_element_type=F32)


def matmul_nt(a, b):
    return lax.dot_general(a, b, (((1,), (1,)), ((), ())), preferred_element_type=F32)


def matmul_tn(a, b):
    return lax.dot_general(a, b, (((0,), (0,)), ((), ())), preferred_element_type=F32)


def cost(flops, arrays, outs, exps=0):
    moved = sum(a.size * a.dtype.itemsize for a in arrays) + sum(
        o.size * o.dtype.itemsize for o in outs
    )
    return pl.CostEstimate(flops=int(flops), bytes_accessed=int(moved), transcendentals=int(exps))


def run_whole(body, me, arrays, outs, scratch=(), flops=0, in_hbm=0, name=None):
    count = len(arrays) - in_hbm
    return pl.pallas_call(
        body,
        out_shape=outs,
        in_specs=[pl.BlockSpec(memory_space=pltpu.SMEM)]
        + [pl.BlockSpec(memory_space=pltpu.VMEM)] * count
        + [pl.BlockSpec(memory_space=pl.ANY)] * in_hbm,
        out_specs=jax.tree.map(lambda _: pl.BlockSpec(memory_space=pltpu.VMEM), outs),
        scratch_shapes=list(scratch),
        cost_estimate=cost(flops, arrays, jax.tree.leaves(outs)),
        compiler_params=pltpu.CompilerParams(vmem_limit_bytes=VMEM_BYTES),
        name=name,
    )(me, *arrays)


def run_grid(body, me, grid, arrays, in_specs, outs, out_specs, scratch=(), flops=0, aliases=None, name=None):
    return pl.pallas_call(
        body,
        out_shape=outs,
        grid_spec=pltpu.PrefetchScalarGridSpec(
            num_scalar_prefetch=1,
            grid=grid,
            in_specs=in_specs,
            out_specs=out_specs,
            scratch_shapes=list(scratch),
        ),
        cost_estimate=cost(flops, arrays, jax.tree.leaves(outs)),
        input_output_aliases=aliases or {},
        compiler_params=pltpu.CompilerParams(vmem_limit_bytes=VMEM_BYTES),
        name=name,
    )(me, *arrays)


def shape(dims, kind=BF16):
    return jax.ShapeDtypeStruct(tuple(dims), kind)


def fixed(block):
    return pl.BlockSpec(block, lambda i, me: (0,) * len(block), pipeline_mode=pl.Buffered(1))


def column(index, wide):
    return pl.ds(pl.multiple_of(index * wide, wide), wide)


def turn(values):
    half = values.shape[-1] // 2
    return jnp.concatenate([-values[:, half:], values[:, :half]], axis=-1)


def turn_back(values):
    half = values.shape[-1] // 2
    return jnp.concatenate([values[:, half:], -values[:, :half]], axis=-1)


def plane_layer(
    tokens,
    query_weight,
    key_weight,
    value_weight,
    output_weight,
    first_gain,
    gate_weight,
    up_weight,
    down_weight,
    second_gain,
    cotangent,
    block_ids,
    piece_order,
):
    ctx_count = lax.axis_size("ctx")
    n = lax.axis_size("fsdp")
    planes = ctx_count // 2
    ctx = lax.axis_index("ctx")
    z, core = ctx // 2, ctx % 2
    f = lax.axis_index("fsdp")
    me = jnp.stack([f, core]).astype(jnp.int32)
    rows, width = tokens.shape[1:]
    pair = 2 * rows
    plane_rows = n * pair
    wide = width // n
    hidden_cols = gate_weight.shape[1]
    part = hidden_cols // (2 * n)
    quarter = part // QUARTERS
    scale = HD ** (-0.5)

    def across(value, d):
        return lax.ppermute(value, "fsdp", [(i, i ^ d) for i in range(n)])

    def sibling(value):
        return lax.ppermute(value, "ctx", [(i, i ^ 1) for i in range(ctx_count)])

    def along(value, step):
        pairs = [(i, i + 2 * step) for i in range(ctx_count)]
        return lax.ppermute(value, "ctx", [(a, b) for a, b in pairs if 0 <= b < ctx_count])

    def between_planes(value, moves):
        return lax.ppermute(
            value, "ctx", [(2 * a + side, 2 * b + side) for a, b in moves for side in range(2)]
        )

    def gathered(value):
        own = [value] + [across(value, d) for d in range(1, n)]
        return own, [sibling(block) for block in own]

    def reduced(own, other):
        near = [sibling(block) for block in other]
        sent = [
            across((own[d].astype(F32) + near[d].astype(F32)).astype(BF16), d) for d in range(1, n)
        ]
        return [own[0], near[0]] + sent

    middle_left, middle_right = planes // 2 - 1, planes // 2
    folds = [
        [(s, s + 1), (planes - 1 - s, planes - 2 - s)] for s in range(middle_left)
    ]

    def summed_over_planes(value):
        for moves in folds:
            value = (
                value.astype(F32) + between_planes(value, moves).astype(F32)
            ).astype(value.dtype)
        crossed = between_planes(value, [(middle_left, middle_right), (middle_right, middle_left)])
        value = (value.astype(F32) + crossed.astype(F32)).astype(value.dtype)
        for s, moves in reversed(list(enumerate(folds))):
            back = between_planes(value, [(b, a) for a, b in moves])
            receives = (z == s) | (z == planes - 1 - s)
            value = jnp.where(receives, back, value)
        return value

    place = jnp.arange(rows, dtype=jnp.int32)
    own_pieces = lax.dynamic_slice_in_dim(piece_order, 2 * z, 2)
    positions = (own_pieces[:, None] * rows + place[None, :]).reshape(pair).astype(F32)
    cosine, sine = rope_tables(positions)
    is_value = core == 1
    kv_cosine = jnp.where(is_value, 1.0, cosine)
    kv_sine = jnp.where(is_value, 0.0, sine)
    chips = f ^ jnp.arange(n, dtype=jnp.int32)
    ring = (z - jnp.arange(planes, dtype=jnp.int32)) % planes
    ring_ctx = (2 * ring[:, None] + jnp.arange(2, dtype=jnp.int32)[None, :]).reshape(-1)
    id_pieces = block_ids.reshape(n, ctx_count, rows)
    ids = id_pieces[chips[:, None], piece_order[ring_ctx][None, :]]
    key_ids = ids.reshape(n, planes, 1, pair)
    query_ids = ids[:, :2].reshape(n, pair, 1)

    def cut_attention(me_ref, *refs):
        wq, wk, wv, wo = (refs[i * n : (i + 1) * n] for i in range(4))
        one, two = refs[4 * n : 4 * n + 2]
        outs = refs[4 * n + 2 :]
        keys_here = me_ref[1] == 0
        for d in range(n):
            first = outs[d]
            first[:wide, :HD] = wq[d][...]

            @pl.when(keys_here)
            def _():
                first[:wide, HD:] = wk[d][...]

            @pl.when(jnp.logical_not(keys_here))
            def _():
                first[:wide, HD:] = wv[d][...]

            pick = lax.broadcasted_iota(jnp.int32, (16, wide), 0) < 8
            first[wide:, :] = jnp.where(pick, one[...].astype(F32), two[...].astype(F32)).astype(
                BF16
            )
            outs[n + d][...] = wo[d][...]

    def head_of(d):
        return lambda i, me: (0, 2 * (me[0] ^ d) + me[1])

    def chip_of(d):
        return lambda i, me: (0, me[0] ^ d)

    def head_rows_of(d):
        return lambda i, me: (2 * (me[0] ^ d) + me[1], 0)

    gain_spec = pl.BlockSpec((1, wide), lambda i, me: (0, 0))
    cut = run_grid(
        cut_attention,
        me,
        (1,),
        [query_weight] * n
        + [key_weight] * n
        + [value_weight] * n
        + [output_weight] * n
        + [first_gain.reshape(1, wide), second_gain.reshape(1, wide)],
        [pl.BlockSpec((wide, HD), head_of(d)) for d in range(n)]
        + [pl.BlockSpec((wide, HD), chip_of(d)) for d in range(n)] * 2
        + [pl.BlockSpec((HD, wide), head_rows_of(d)) for d in range(n)]
        + [gain_spec, gain_spec],
        [shape((wide + 16, 2 * HD))] * n + [shape((HD, wide))] * n,
        [pl.BlockSpec((wide + 16, 2 * HD), lambda i, me: (0, 0))] * n
        + [pl.BlockSpec((HD, wide), lambda i, me: (0, 0))] * n,
        name="cut_attention",
    )
    own_tokens = tokens[0]
    token_own, token_near = gathered(own_tokens)
    weights_in = [cut[0]] + [across(cut[d], d) for d in range(1, n)]
    weights_out = [cut[n]] + [across(cut[n + d], d) for d in range(1, n)]

    def cut_hidden(me_ref, *refs):
        gates, ups, downs = (refs[i * n : (i + 1) * n] for i in range(3))
        for d in range(n):
            refs[-1][0, d, :wide, :quarter] = gates[d][...]
            refs[-1][0, d, :wide, quarter:] = ups[d][...]
            refs[-1][0, d, wide:, :] = downs[d][...]

    def columns_of(d):
        return lambda q, me: (0, (2 * (me[0] ^ d) + me[1]) * QUARTERS + q)

    def down_rows_of(d):
        return lambda q, me: ((2 * (me[0] ^ d) + me[1]) * QUARTERS + q, 0)

    piece = (wide + quarter, 2 * quarter)
    hidden_cut = run_grid(
        cut_hidden,
        me,
        (QUARTERS,),
        [gate_weight] * n + [up_weight] * n + [down_weight] * n,
        [pl.BlockSpec((wide, quarter), columns_of(d)) for d in range(n)] * 2
        + [pl.BlockSpec((quarter, wide), down_rows_of(d)) for d in range(n)],
        shape((QUARTERS, n) + piece),
        pl.BlockSpec((1, n) + piece, lambda q, me: (q, 0, 0, 0)),
        name="cut_hidden",
    )
    first_pieces = [across(hidden_cut[0, d], d) for d in range(1, n)]
    own_cotangent = cotangent[0]
    cot_own = [own_cotangent] + [across(own_cotangent, d) for d in range(1, n)]

    def project(me_ref, *refs):
        near_tokens = refs[: 2 * n]
        pieces = refs[2 * n : 3 * n]
        cos_ref, sin_ref, kvcos_ref, kvsin_ref = refs[3 * n : 3 * n + 4]
        normed_ref, query_ref, kv_ref, gains_ref = refs[3 * n + 4 :]
        chip, side = me_ref[0], me_ref[1]
        for j in range(n):
            both = pieces[j][wide:, :].astype(F32)
            gains_ref[0:1, column(chip ^ j, wide)] = both[0:1]
            gains_ref[1:2, column(chip ^ j, wide)] = both[8:9]
        for d in range(n):
            for e in range(2):
                slot = side ^ e
                values = near_tokens[e * n + d][...].astype(F32)
                inverse = lax.rsqrt(jnp.mean(values * values, axis=-1, keepdims=True) + epsilon)
                normed_ref[d, slot] = (values * inverse * gains_ref[0:1, :]).astype(BF16)
                both = jnp.zeros((rows, 2 * HD), F32)
                for j in range(n):
                    both += matmul(
                        normed_ref[d, slot, :, column(chip ^ j, wide)], pieces[j][:wide, :]
                    )
                query, kv = both[:, :HD], both[:, HD:]
                query_ref[d, slot] = (
                    query * cos_ref[slot] + turn(query) * sin_ref[slot]
                ).astype(BF16)
                kv_ref[d, slot] = (kv * kvcos_ref[slot] + turn(kv) * kvsin_ref[slot]).astype(BF16)

    head_shape = (n, 2, rows, HD)
    tables = [t.reshape(2, rows, HD) for t in (cosine, sine, kv_cosine, kv_sine)]
    normed, query_rot, own_kv, gains = run_whole(
        project,
        me,
        token_own + token_near + weights_in + tables,
        [
            shape((n, 2, rows, width)),
            shape(head_shape),
            shape(head_shape),
            shape((2, width), F32),
        ],
        flops=2 * plane_rows * width * 2 * HD,
        name="project",
    )

    rightward, leftward = [own_kv], [own_kv]
    for _ in range(planes - 1):
        rightward.append(along(rightward[-1], 1))
        leftward.append(along(leftward[-1], -1))
    kv_mine = [own_kv] + [rightward[k] + leftward[planes - k] for k in range(1, planes)]
    kv_near = [sibling(block) for block in kv_mine]

    head_spec = pl.BlockSpec((1, 2, rows, HD), lambda i, me: (i, 0, 0, 0))
    id_specs = [
        pl.BlockSpec((1, pair, 1), lambda i, me: (i, 0, 0)),
        pl.BlockSpec((1, planes, 1, pair), lambda i, me: (i, 0, 0, 0)),
    ]

    def scored(side, query, query_id, key_id, mine, near):
        keys, values, scores = [], [], []
        for k in range(planes):
            a = mine[k][0].reshape(pair, HD)
            b = near[k][0].reshape(pair, HD)
            keys.append(jnp.where(side == 0, a, b))
            values.append(jnp.where(side == 0, b, a))
            score = matmul_nt(query, keys[k]) * scale
            scores.append(jnp.where(key_id[0, k] <= query_id[0], score, masked_score))
        top = functools.reduce(jnp.maximum, [jnp.max(s, axis=-1, keepdims=True) for s in scores])
        raised = [jnp.exp(s - top) for s in scores]
        inverse = 1.0 / sum(jnp.sum(r, axis=-1, keepdims=True) for r in raised)
        return keys, values, [r * inverse for r in raised]

    def spread(step, side, whole, own_refs, near_refs):
        for d in range(n):

            @pl.when(step == d)
            def _():
                own_refs[d][...] = whole[side]
                near_refs[d][...] = whole[1 - side]

    def attend(me_ref, query_ref, query_id, key_id, *refs):
        mine, near, out_w = refs[:planes], refs[planes : 2 * planes], refs[2 * planes : 2 * planes + n]
        attended_ref = refs[2 * planes + n]
        own_refs = refs[2 * planes + n + 1 : 2 * planes + 2 * n + 1]
        near_refs = refs[2 * planes + 2 * n + 1 : 2 * planes + 3 * n + 1]
        whole = refs[-1]
        chip, side = me_ref[0], me_ref[1]
        query = query_ref[0].reshape(pair, HD)
        _, values, probs = scored(side, query, query_id, key_id, mine, near)
        total = jnp.zeros((pair, HD), F32)
        for k in range(planes):
            total += matmul(probs[k].astype(BF16), values[k])
        attended = total.astype(BF16)
        attended_ref[0] = attended.reshape(2, rows, HD)
        for j in range(n):
            whole[:, :, column(chip ^ j, wide)] = (
                matmul(attended, out_w[j][...]).astype(BF16).reshape(2, rows, wide)
            )
        spread(pl.program_id(0), side, whole, own_refs, near_refs)

    early = lax.optimization_barrier([query_rot] + cot_own[1:] + first_pieces)
    query_rot, cot_own[1:], first_pieces = early[0], early[1:n], early[n:]
    cot_near = [sibling(block) for block in cot_own]

    block = (rows, width)
    attend_flops = 4 * plane_rows * planes * pair * HD + 2 * plane_rows * HD * width
    attended, *partial = run_grid(
        attend,
        me,
        (n,),
        [query_rot, query_ids, key_ids] + kv_mine + kv_near + weights_out,
        [head_spec] + id_specs + [head_spec] * (2 * planes) + [fixed((HD, wide))] * n,
        [shape(head_shape)] + [shape(block)] * (2 * n),
        [head_spec] + [pl.BlockSpec(block, lambda i, me: (0, 0))] * (2 * n),
        scratch=[pltpu.VMEM((2, rows, width), BF16)],
        flops=attend_flops,
        name="attend",
    )
    middle_terms = reduced(partial[:n], partial[n:])

    def second_norm(me_ref, token_ref, gains_ref, *refs):
        terms, (middle_ref, normed_ref) = refs[:-2], refs[-2:]
        middle = token_ref[...].astype(F32)
        middle += sum(t[...].astype(F32) for t in terms)
        inverse = lax.rsqrt(jnp.mean(middle * middle, axis=-1, keepdims=True) + epsilon)
        middle_ref[...] = middle
        normed_ref[...] = (middle * inverse * gains_ref[1:2, :]).astype(BF16)

    middle, own_normed_two = run_whole(
        second_norm,
        me,
        [own_tokens, gains] + middle_terms,
        [shape(block, F32), shape(block)],
        name="second_norm",
    )
    two_own, two_near = gathered(own_normed_two)

    tile = plane_rows // 3
    tiles_count = 3 * QUARTERS
    units = 2 * tiles_count
    unit = (2, quarter, wide)
    held_sums, held_ends = 4, 3

    def feed_forward(*refs):
        two_refs, cot_refs, first_refs = refs[: 2 * n], refs[2 * n : 4 * n], refs[4 * n : 5 * n - 1]
        cut_ref = refs[5 * n - 1]
        back_refs, out_refs = refs[5 * n : 7 * n], refs[7 * n : 9 * n]
        tiles, from_end, from_middle, finals, owned_ref, near_ref = refs[9 * n : 9 * n + 6]
        (
            work,
            feed,
            hidden,
            turned,
            stage,
            mine,
            theirs,
            crossed,
            sums,
            ends,
            load_sem,
            feed_local,
            feed_send,
            feed_recv,
            stage_sem,
            one_send,
            one_recv,
            two_send,
            two_recv,
            three_send,
            three_recv,
            mine_sem,
            theirs_sem,
            crossed_sem,
            final_sem,
            deal_local,
            deal_send,
            deal_recv,
            near_send,
            near_recv,
        ) = refs[9 * n + 6 :]
        here = lax.axis_index("ctx")
        chip = lax.axis_index("fsdp")
        z, side = here // 2, here % 2
        is_middle = (z == 1) | (z == 2)
        is_end = jnp.logical_not(is_middle)
        chips = [chip, chip + 1 - 2 * (chip % 2), (chip + 2) % 4, 3 - chip]
        partner = (2 * (z + 1 - 2 * (z % 2)) + side, chip)
        other_middle = (2 * (3 - z) + side, chip)
        sibling_core = (here + 1 - 2 * side, chip)
        blocks = [pl.ds(pl.multiple_of(c * wide, wide), wide) for c in chips]

        barrier = pltpu.get_barrier_semaphore()
        for peer in [(here, c) for c in chips[1:]] + [partner, sibling_core]:
            pl.semaphore_signal(barrier, inc=1, device_id=peer, device_id_type=MESH)

        @pl.when(is_middle)
        def _():
            pl.semaphore_signal(barrier, inc=1, device_id=other_middle, device_id_type=MESH)
            pl.semaphore_wait(barrier, n + 2)

        @pl.when(is_end)
        def _():
            pl.semaphore_wait(barrier, n + 1)

        def remote(source, target, send, recv, peer):
            return pltpu.make_async_remote_copy(
                src_ref=source,
                dst_ref=target,
                send_sem=send,
                recv_sem=recv,
                device_id=peer,
                device_id_type=MESH,
            )

        def feed_copy(q, d):
            at = q * n + d
            return remote(
                cut_ref.at[q, d], feed.at[q, d], feed_send.at[at], feed_recv.at[at], (here, chips[d])
            )

        def feed_own(q):
            return pltpu.make_async_copy(cut_ref.at[q, 0], feed.at[q, 0], feed_local.at[q])

        def hop_one(i):
            return remote(tiles.at[i], from_end.at[i], one_send.at[i], one_recv.at[i], partner)

        def hop_two(i):
            return remote(
                sums.at[i % held_sums],
                from_middle.at[i],
                two_send.at[i],
                two_recv.at[i],
                other_middle,
            )

        def hop_three(i):
            return remote(
                ends.at[i % held_ends], finals.at[i], three_send.at[i], three_recv.at[i], partner
            )

        def load_mine(i):
            return pltpu.make_async_copy(tiles.at[i], mine.at[i % 2], mine_sem.at[i % 2])

        def load_theirs(i):
            return pltpu.make_async_copy(from_end.at[i], theirs.at[i % 2], theirs_sem.at[i % 2])

        def load_crossed(i):
            return pltpu.make_async_copy(from_middle.at[i], crossed.at[i % 2], crossed_sem.at[i % 2])

        def keep_final(i):
            return pltpu.make_async_copy(
                ends.at[i % held_ends], finals.at[i], final_sem.at[i % held_ends]
            )

        def keep_own(i):
            return pltpu.make_async_copy(finals.at[i, 0], owned_ref.at[i, 0], deal_local.at[i])

        def deal_to(i, b, d):
            at = 2 * i + b
            return remote(
                finals.at[i, b],
                owned_ref.at[i, b],
                deal_send.at[at],
                deal_recv.at[at],
                (here, chips[d]),
            )

        def to_sibling(i):
            return remote(
                owned_ref.at[i], near_ref.at[i], near_send.at[i], near_recv.at[i], sibling_core
            )

        def add(target, a, b):
            def some(r, _):
                at = (r // 4, pl.ds(pl.multiple_of((r % 4) * (quarter // 4), quarter // 4), quarter // 4))
                target[at] = (a[at].astype(F32) + b[at].astype(F32)).astype(BF16)
                return 0

            lax.fori_loop(0, 8, some, 0)

        def when_in(i, *conditions):
            return pl.when(functools.reduce(jnp.logical_and, conditions, (i >= 0) & (i < units)))

        def advance(i):
            @when_in(i - 1, is_middle)
            def _():
                at = i - 1
                load_mine(at).wait()
                load_theirs(at).wait()

                @pl.when(at >= held_sums)
                def _():
                    hop_two(at - held_sums).wait_send()

                add(sums.at[at % held_sums], mine.at[at % 2], theirs.at[at % 2])
                hop_two(at).start()

            @when_in(i - 4, is_middle)
            def _():
                at = i - 4
                load_crossed(at).wait()

                @pl.when(at >= held_ends)
                def _():
                    hop_three(at - held_ends).wait_send()

                add(ends.at[at % held_ends], sums.at[at % held_sums], crossed.at[at % 2])
                hop_three(at).start()
                keep_final(at).start()

            @when_in(i, is_middle)
            def _():
                hop_one(i).wait_recv()
                load_mine(i).start()
                load_theirs(i).start()

            @when_in(i - 3, is_middle)
            def _():
                hop_two(i - 3).wait_recv()
                load_crossed(i - 3).start()

            @when_in(i - 6)
            def _():
                at = i - 6

                @pl.when(is_middle)
                def _():
                    keep_final(at).wait()

                @pl.when(is_end)
                def _():
                    hop_three(at).wait_recv()

                @pl.when(at % 2 == 0)
                def _():
                    keep_own(at).start()
                    deal_to(at, 1, 1).start()

                @pl.when(at % 2 == 1)
                def _():
                    deal_to(at, 0, 2).start()
                    deal_to(at, 1, 3).start()

            @when_in(i - 9)
            def _():
                at = i - 9

                @pl.when(at % 2 == 0)
                def _():
                    keep_own(at).wait()

                @pl.when(at % 2 == 1)
                def _():
                    deal_to(at, 0, 2).wait_recv()

                deal_to(at, 1, 3).wait_recv()
                to_sibling(at).start()

        def finish():
            def one(i, _):
                @pl.when(is_end)
                def _():
                    hop_one(i).wait_send()

                @pl.when(is_middle & (i >= units - held_sums))
                def _():
                    hop_two(i).wait_send()

                @pl.when(is_middle & (i >= units - held_ends))
                def _():
                    hop_three(i).wait_send()

                @pl.when(i % 2 == 1)
                def _():
                    deal_to(i, 0, 2).wait_send()

                deal_to(i, 1, 3).wait_send()
                to_sibling(i).wait()
                return 0

            lax.fori_loop(0, units, one, 0)

        loads = []
        for base, sources in ((0, two_refs), (plane_rows, cot_refs)):
            for i in range(2 * n):
                loads.append(
                    pltpu.make_async_copy(
                        sources[i],
                        work.at[pl.ds(base + i * rows, rows)],
                        load_sem.at[len(loads)],
                    )
                )
        for d in range(1, n):
            loads.append(
                pltpu.make_async_copy(first_refs[d - 1], feed.at[0, d], load_sem.at[len(loads)])
            )
        for copy in loads:
            copy.start()
        for q in range(QUARTERS):
            feed_own(q).start()
        for d in range(1, n):
            feed_copy(1, d).start()
        for copy in loads:
            copy.wait()

        def stage_copy(t, h):
            return pltpu.make_async_copy(
                stage.at[t % 2, pl.ds(2 * h, 2)], tiles.at[2 * t + h], stage_sem.at[t % 2, h]
            )

        def quarter_step(q, _):
            feed_own(q).wait()

            @pl.when(q > 0)
            def _():
                for d in range(1, n):
                    feed_copy(q, d).wait_recv()

            @pl.when((q > 0) & (q < QUARTERS - 1))
            def _():
                for d in range(1, n):
                    feed_copy(q + 1, d).start()

            def forward(t, _):
                now = pl.ds(pl.multiple_of(t * tile, tile), tile)
                cot_now = pl.ds(pl.multiple_of(plane_rows + t * tile, tile), tile)
                both = jnp.zeros((tile, 2 * quarter), F32)
                hidden_grad = jnp.zeros((tile, quarter), F32)
                for j in range(n):
                    both += matmul(work[now, blocks[j]], feed[q, j, :wide, :])
                    hidden_grad += matmul_nt(work[cot_now, blocks[j]], feed[q, j, wide:, :])
                gate, up = both[:, :quarter], both[:, quarter:]
                share = 1.0 / (1.0 + jnp.exp(-gate))
                activated = gate * share
                results = (
                    activated * up,
                    hidden_grad * up * share * (1.0 + gate * (1.0 - share)),
                    hidden_grad * activated,
                )
                for w, result in enumerate(results):
                    hidden[q * 3 + w, now, :] = result.astype(BF16)
                    turned[w, :, now] = result.T.astype(BF16)
                return 0

            lax.fori_loop(0, plane_rows // tile, forward, 0)
            advance(2 * q - 2)

            def outer(w, _):
                t = 3 * q + w
                base = jnp.where(w == 0, plane_rows, 0)
                right = pl.ds(pl.multiple_of(base, plane_rows), plane_rows)

                @pl.when(t >= 2)
                def _():
                    for h in range(2):
                        stage_copy(t - 2, h).wait()

                    @pl.when(is_end)
                    def _():
                        for h in range(2):
                            hop_one(2 * (t - 2) + h).start()

                for j in range(n):
                    stage[t % 2, j] = matmul(turned[w], work[right, blocks[j]]).astype(BF16)
                for h in range(2):
                    stage_copy(t, h).start()
                return 0

            lax.fori_loop(0, 3, outer, 0)
            advance(2 * q - 1)
            return 0

        lax.fori_loop(0, QUARTERS, quarter_step, 0)
        for t in (tiles_count - 2, tiles_count - 1):
            for h in range(2):
                stage_copy(t, h).wait()

            @pl.when(is_end)
            def _():
                for h in range(2):
                    hop_one(2 * t + h).start()

        def back_step(r, _):
            now = pl.ds(pl.multiple_of(r * pair, pair), pair)
            lefts = [
                jnp.concatenate([hidden[q * 3 + 1, now, :], hidden[q * 3 + 2, now, :]], axis=1)
                for q in range(QUARTERS)
            ]
            for j in range(n):
                total = jnp.zeros((pair, wide), F32)
                for q in range(QUARTERS):
                    total += matmul_nt(lefts[q], feed[q, j, :wide, :])
                work[now, blocks[j]] = total.astype(BF16)
            advance(2 * QUARTERS - 2 + r)
            return 0

        lax.fori_loop(0, n, back_step, 0)

        def out_step(r, _):
            now = pl.ds(pl.multiple_of(r * pair, pair), pair)
            then = pl.ds(pl.multiple_of(plane_rows + r * pair, pair), pair)
            for j in range(n):
                total = jnp.zeros((pair, wide), F32)
                for q in range(QUARTERS):
                    total += matmul(hidden[q * 3, now, :], feed[q, j, wide:, :])
                work[then, blocks[j]] = total.astype(BF16)
            return 0

        lax.fori_loop(0, n, out_step, 0)
        stores = []
        for base, targets in ((0, back_refs), (plane_rows, out_refs)):
            for i in range(2 * n):
                stores.append(
                    pltpu.make_async_copy(
                        work.at[pl.ds(base + i * rows, rows)], targets[i], load_sem.at[len(stores)]
                    )
                )
        for copy in stores:
            copy.start()

        def rest(i, _):
            advance(i)
            return 0

        lax.fori_loop(2 * QUARTERS - 2 + n, units + 10, rest, 0)
        for copy in stores:
            copy.wait()
        for q in range(1, QUARTERS):
            for d in range(1, n):
                feed_copy(q, d).wait_send()
        finish()

    unit_array = shape((units,) + unit)
    dma = pltpu.SemaphoreType.DMA
    arrays = two_own + two_near + cot_own + cot_near + first_pieces + [hidden_cut]
    results = pl.pallas_call(
        feed_forward,
        out_shape=[shape(block)] * (4 * n) + [unit_array] * 6,
        in_specs=[pl.BlockSpec(memory_space=pl.ANY)] * len(arrays),
        out_specs=[pl.BlockSpec(memory_space=pl.ANY)] * (4 * n + 6),
        scratch_shapes=[
            pltpu.VMEM((2 * plane_rows, width), BF16),
            pltpu.VMEM((QUARTERS, n) + piece, BF16),
            pltpu.VMEM((3 * QUARTERS, plane_rows, quarter), BF16),
            pltpu.VMEM((3, quarter, plane_rows), BF16),
            pltpu.VMEM((2, n, quarter, wide), BF16),
            pltpu.VMEM((2,) + unit, BF16),
            pltpu.VMEM((2,) + unit, BF16),
            pltpu.VMEM((2,) + unit, BF16),
            pltpu.VMEM((held_sums,) + unit, BF16),
            pltpu.VMEM((held_ends,) + unit, BF16),
            dma((4 * n + n - 1,)),
            dma((QUARTERS,)),
            dma((QUARTERS * n,)),
            dma((QUARTERS * n,)),
            dma((2, 2)),
            dma((units,)),
            dma((units,)),
            dma((units,)),
            dma((units,)),
            dma((units,)),
            dma((units,)),
            dma((2,)),
            dma((2,)),
            dma((2,)),
            dma((held_ends,)),
            dma((units,)),
            dma((2 * units,)),
            dma((2 * units,)),
            dma((units,)),
            dma((units,)),
        ],
        cost_estimate=cost(18 * plane_rows * width * part, arrays, [unit_array] * 6),
        compiler_params=pltpu.CompilerParams(
            collective_id=0, has_side_effects=True, vmem_limit_bytes=62 * 1024 * 1024
        ),
        name="feed_forward",
    )(*arrays)
    back, out_partial = results[: 2 * n], results[2 * n : 4 * n]
    hidden_own, hidden_near = results[-2:]
    two_grad_terms = reduced(back[:n], back[n:])

    def norm_back(values, inverse, gain, grad):
        unit = values * inverse
        scaled = grad * gain
        return inverse * (scaled - unit * jnp.mean(scaled * unit, axis=-1, keepdims=True)), jnp.sum(
            grad * unit, axis=0, keepdims=True
        )

    def second_norm_back(me_ref, middle_ref, cot_ref, gains_ref, *refs):
        terms, (middle_grad_ref, branch_ref, gain_ref, flat) = refs[:-4], refs[-4:]
        middle = middle_ref[...]
        inverse = lax.rsqrt(jnp.mean(middle * middle, axis=-1, keepdims=True) + epsilon)
        grad = sum(t[...].astype(F32) for t in terms)
        back, gain_term = norm_back(middle, inverse, gains_ref[1:2, :], grad)
        middle_grad = cot_ref[...].astype(F32) + back
        middle_grad_ref[...] = middle_grad
        branch_ref[...] = middle_grad.astype(BF16)
        flat[...] = gain_term
        for j in range(n):
            gain_ref[j] = flat[:, column(me_ref[0] ^ j, wide)]

    gain_shape = shape((n, 1, wide), F32)
    middle_grad, branch_grad, gain_two_term = run_whole(
        second_norm_back,
        me,
        [middle, own_cotangent, gains] + two_grad_terms,
        [shape(block, F32), shape(block), gain_shape],
        scratch=[pltpu.VMEM((1, width), F32)],
        name="second_norm_back",
    )
    branch_own, branch_near = gathered(branch_grad)

    def attend_back(me_ref, query_ref, query_id, key_id, cos_ref, sin_ref, *refs):
        mine, near, out_w = refs[:planes], refs[planes : 2 * planes], refs[2 * planes : 2 * planes + n]
        branch_refs = refs[2 * planes + n : 2 * planes + 3 * n]
        query_grad_ref = refs[2 * planes + 3 * n]
        keep_refs = refs[2 * planes + 3 * n + 1 : 3 * planes + 3 * n + 1]
        send_refs = refs[3 * planes + 3 * n + 1 : 4 * planes + 3 * n + 1]
        branch = refs[-1]
        chip, side = me_ref[0], me_ref[1]
        for d in range(n):

            @pl.when(pl.program_id(0) == d)
            def _():
                branch[side] = branch_refs[d][...]
                branch[1 - side] = branch_refs[n + d][...]

        query = query_ref[0].reshape(pair, HD)
        attended_grad = jnp.zeros((pair, HD), F32)
        for j in range(n):
            attended_grad += matmul_nt(
                branch[:, :, column(chip ^ j, wide)].reshape(pair, wide), out_w[j][...]
            )
        attended_grad = attended_grad.astype(BF16)
        keys, values, probs = scored(side, query, query_id, key_id, mine, near)
        low = [p.astype(BF16) for p in probs]
        shares = [matmul_nt(attended_grad, values[k]) for k in range(planes)]
        delta = sum(
            jnp.sum(low[k].astype(F32) * shares[k], axis=-1, keepdims=True) for k in range(planes)
        )
        query_grad = jnp.zeros((pair, HD), F32)
        for k in range(planes):
            score_grad = (probs[k] * (shares[k] - delta)).astype(BF16)
            query_grad += matmul(score_grad, keys[k])
            key_grad = matmul_tn(score_grad, query) * scale
            value_grad = matmul_tn(low[k], attended_grad)
            keep_refs[k][0] = jnp.where(side == 0, key_grad, value_grad).astype(BF16).reshape(
                2, rows, HD
            )
            send_refs[k][0] = jnp.where(side == 0, value_grad, key_grad).astype(BF16).reshape(
                2, rows, HD
            )
        query_grad = query_grad * scale
        query_grad = query_grad * cos_ref[...] + turn_back(query_grad * sin_ref[...])
        query_grad_ref[0] = query_grad.astype(BF16).reshape(2, rows, HD)

    query_grad, *kv_grads = run_grid(
        attend_back,
        me,
        (n,),
        [query_rot, query_ids, key_ids, cosine, sine]
        + kv_mine
        + kv_near
        + weights_out
        + branch_own
        + branch_near,
        [head_spec]
        + id_specs
        + [fixed((pair, HD))] * 2
        + [head_spec] * (2 * planes)
        + [fixed((HD, wide))] * n
        + [fixed(block)] * (2 * n),
        [shape(head_shape)] * (1 + 2 * planes),
        [head_spec] * (1 + 2 * planes),
        scratch=[pltpu.VMEM((2, rows, width), BF16)],
        flops=10 * plane_rows * planes * pair * HD + 2 * plane_rows * HD * width,
        name="attend_back",
    )
    kept, handed = kv_grads[:planes], kv_grads[planes:]
    kv_sums = [
        (kept[k].astype(F32) + sibling(handed[k]).astype(F32)).astype(BF16) for k in range(planes)
    ]
    from_above = jnp.zeros_like(own_kv)
    from_below = jnp.zeros_like(own_kv)
    for k in range(planes - 1, 0, -1):
        below = jnp.where(z >= k, kv_sums[k], 0).astype(F32) + from_above.astype(F32)
        above = jnp.where(z + k < planes, kv_sums[planes - k], 0).astype(F32) + from_below.astype(F32)
        from_above = along(below.astype(BF16), -1)
        from_below = along(above.astype(BF16), 1)

    def project_back(me_ref, *refs):
        own_ref, above_ref, below_ref, query_grad_ref, kvcos_ref, kvsin_ref = refs[:6]
        pieces = refs[6 : 6 + n]
        kv_ref = refs[6 + n]
        own_refs, near_refs = refs[7 + n : 7 + 2 * n], refs[7 + 2 * n : 7 + 3 * n]
        chip, side = me_ref[0], me_ref[1]
        for d in range(n):
            for e in range(2):
                slot = side ^ e
                grad = own_ref[d, slot].astype(F32) + above_ref[d, slot].astype(F32)
                grad = grad + below_ref[d, slot].astype(F32)
                grad = grad * kvcos_ref[slot] + turn_back(grad * kvsin_ref[slot])
                grad = grad.astype(BF16)
                kv_ref[d, slot] = grad
                left = jnp.concatenate([query_grad_ref[d, slot], grad], axis=1)
                target = (own_refs, near_refs)[e][d]
                for j in range(n):
                    target[:, column(chip ^ j, wide)] = matmul_nt(left, pieces[j][:wide, :]).astype(
                        BF16
                    )

    kv_grad, *partial = run_whole(
        project_back,
        me,
        [kv_sums[0], from_above, from_below, query_grad] + tables[2:] + weights_in,
        [shape(head_shape)] + [shape(block)] * (2 * n),
        flops=4 * plane_rows * width * HD,
        name="project_back",
    )
    one_grad_terms = reduced(partial[:n], partial[n:])

    def first_norm_back(me_ref, token_ref, middle_grad_ref, gains_ref, *refs):
        terms, (grad_ref, gain_ref, flat) = refs[:-3], refs[-3:]
        values = token_ref[...].astype(F32)
        inverse = lax.rsqrt(jnp.mean(values * values, axis=-1, keepdims=True) + epsilon)
        grad = sum(t[...].astype(F32) for t in terms)
        back, gain_term = norm_back(values, inverse, gains_ref[0:1, :], grad)
        grad_ref[...] = middle_grad_ref[...] + back
        flat[...] = gain_term
        for j in range(n):
            gain_ref[j] = flat[:, column(me_ref[0] ^ j, wide)]

    tokens_grad, gain_one_term = run_whole(
        first_norm_back,
        me,
        [own_tokens, middle_grad, gains] + one_grad_terms,
        [shape(block, F32), gain_shape],
        scratch=[pltpu.VMEM((1, width), F32)],
        name="first_norm_back",
    )
    gain_terms = jnp.concatenate([gain_one_term, gain_two_term], axis=1)
    gain_sum = gain_terms[0] + sum(across(gain_terms[d], d) for d in range(1, n))
    gain_sum = gain_sum + sibling(gain_sum)
    gain_sum = summed_over_planes(gain_sum)

    def outer(me_ref, left_ref, right_ref, out_ref):
        turned = left_ref[...].reshape(plane_rows, HD).astype(F32).T.astype(BF16)
        for j in range(n):
            right = right_ref[:, :, :, column(me_ref[0] ^ j, wide)].reshape(plane_rows, wide)
            out_ref[j] = matmul(turned, right).astype(BF16)

    def outer_branch(me_ref, left_ref, *refs):
        branch_refs, (out_ref, right_ref, sems) = refs[: 2 * n], refs[2 * n :]
        copies = []
        for e in range(2):
            for d in range(n):
                copies.append(
                    pltpu.make_async_copy(
                        branch_refs[e * n + d],
                        right_ref.at[d, me_ref[1] ^ e],
                        sems.at[e * n + d],
                    )
                )
        for copy in copies:
            copy.start()
        for copy in copies:
            copy.wait()
        outer(me_ref, left_ref, right_ref, out_ref)

    outer_flops = 2 * plane_rows * width * HD
    outer_tile = shape((n, HD, wide))
    query_tile = run_whole(
        outer, me, [query_grad, normed], outer_tile, flops=outer_flops, name="query_outer"
    )
    output_tile = run_whole(
        outer_branch,
        me,
        [attended] + branch_own + branch_near,
        outer_tile,
        scratch=[pltpu.VMEM((n, 2, rows, width), BF16), pltpu.SemaphoreType.DMA((2 * n,))],
        flops=outer_flops,
        in_hbm=2 * n,
        name="output_outer",
    )
    kv_tile = run_whole(outer, me, [kv_grad, normed], outer_tile, flops=outer_flops, name="kv_outer")

    def deal(me_ref, *refs):
        count = (len(refs) - n) // 2
        sums, backs, outs = refs[:count], refs[count : 2 * count], refs[2 * count :]
        outer_plane = me_ref[2] == 1

        @pl.when(outer_plane)
        def _():
            for d in range(n):
                for w in range(count):
                    outs[d][w] = backs[w][d]

        @pl.when(jnp.logical_not(outer_plane))
        def _():
            for d in range(n):
                for w in range(count):
                    outs[d][w] = sums[w][d]

    is_outer = ((z == 0) | (z == planes - 1)).astype(jnp.int32)
    me_and_plane = jnp.concatenate([me, is_outer[None]])
    stages = len(folds) * 2 + 1

    def stage_moves(stage):
        if stage < len(folds):
            return folds[stage]
        if stage == len(folds):
            return [(middle_left, middle_right), (middle_right, middle_left)]
        return [(b, a) for a, b in folds[stages - 1 - stage]]

    def pipelined(tiles):
        ends = {}
        for line in range(LINES):
            waiting = []
            feed_line = list(range(line, len(tiles), LINES))
            while feed_line or waiting:
                if feed_line:
                    first = feed_line.pop(0)
                    waiting.append((first, 0, tiles[first]))
                operands = lax.optimization_barrier([value for _, _, value in waiting])
                moved = []
                for (index, stage, _), value in zip(waiting, operands):
                    other = between_planes(value, stage_moves(stage))
                    if stage == stages - 1:
                        ends[index] = (value, other)
                        continue
                    if stage <= len(folds):
                        value = (value.astype(F32) + other.astype(F32)).astype(BF16)
                    else:
                        s = stages - 1 - stage
                        value = jnp.where((z == s) | (z == planes - 1 - s), other, value)
                    moved.append((index, stage + 1, value))
                waiting = moved
        return [ends[i] for i in range(len(tiles))]

    plane_sums = pipelined([query_tile, output_tile, kv_tile])

    def owned(ends):
        dealt = run_whole(
            deal,
            me_and_plane,
            [a for a, _ in ends] + [b for _, b in ends],
            [shape((len(ends),) + ends[0][0].shape[1:])] * n,
            name="deal",
        )
        own = [dealt[0]] + [across(dealt[d], d) for d in range(1, n)]
        return own + [sibling(block) for block in own]

    def slot_of(q, count):
        def where(i, me):
            return (2 * (me[0] ^ (i % n)) + (me[1] ^ (i // n))) * count + q

        return where

    def place_hidden(me_ref, own_ref, near_ref, gate_out, up_out, down_out):
        for source, e in ((own_ref, 0), (near_ref, 1)):

            @pl.when(pl.program_id(0) // n == e)
            def _():
                down_out[...] = source[0, 0].astype(F32)
                gate_out[...] = source[1, 0].astype(F32).T
                up_out[...] = source[2, 0].astype(F32).T

    def hidden_slot(i, q, me):
        return (2 * (me[0] ^ (i % n)) + (me[1] ^ (i // n))) * QUARTERS + q

    by_columns = pl.BlockSpec((wide, quarter), lambda i, q, me: (0, hidden_slot(i, q, me)))
    by_rows = pl.BlockSpec((quarter, wide), lambda i, q, me: (hidden_slot(i, q, me), 0))
    held = run_grid(
        place_hidden,
        me,
        (2 * n, QUARTERS),
        [t.reshape(3 * QUARTERS, n, quarter, wide) for t in (hidden_own, hidden_near)],
        [
            pl.BlockSpec((3, 1, quarter, wide), lambda i, q, me: (q, jnp.where(i < n, i, n - 1), 0, 0)),
            pl.BlockSpec((3, 1, quarter, wide), lambda i, q, me: (q, jnp.where(i < n, 0, i - n), 0, 0)),
        ],
        [
            shape(gate_weight.shape, F32),
            shape(up_weight.shape, F32),
            shape(down_weight.shape, F32),
        ],
        [by_columns, by_columns, by_rows],
        name="place_hidden",
    )

    def place_query(me_ref, *refs):
        tiles, (query_out, output_out) = refs[: 2 * n], refs[2 * n :]
        for i in range(2 * n):

            @pl.when(pl.program_id(0) == i)
            def _():
                query_out[...] = tiles[i][0].astype(F32).T
                output_out[...] = tiles[i][1].astype(F32)

    where = slot_of(0, 1)
    query_weight_grad, output_weight_grad = run_grid(
        place_query,
        me,
        (2 * n,),
        owned(plane_sums[:2]),
        [fixed((2, HD, wide))] * (2 * n),
        [shape(query_weight.shape, F32), shape(output_weight.shape, F32)],
        [
            pl.BlockSpec((wide, HD), lambda i, me: (0, where(i, me))),
            pl.BlockSpec((HD, wide), lambda i, me: (where(i, me), 0)),
        ],
        name="place_query",
    )

    def place_kv(me_ref, *refs):
        tiles, (key_out, value_out) = refs[: 2 * n], refs[2 * n :]
        keys_here = me_ref[1] == 0
        for d in range(n):

            @pl.when(pl.program_id(0) == d)
            def _():
                own, near = tiles[d][0].astype(F32).T, tiles[n + d][0].astype(F32).T
                key_out[...] = jnp.where(keys_here, own, near)
                value_out[...] = jnp.where(keys_here, near, own)

    by_chip = pl.BlockSpec((wide, HD), lambda i, me: (0, me[0] ^ i))
    key_weight_grad, value_weight_grad = run_grid(
        place_kv,
        me,
        (n,),
        owned(plane_sums[2:]),
        [fixed((1, HD, wide))] * (2 * n),
        [shape(key_weight.shape, F32), shape(value_weight.shape, F32)],
        [by_chip, by_chip],
        name="place_kv",
    )

    output = middle + sum(t.astype(F32) for t in reduced(out_partial[:n], out_partial[n:]))

    return (
        output.astype(BF16)[None],
        tokens_grad[None],
        query_weight_grad,
        key_weight_grad,
        value_weight_grad,
        output_weight_grad,
        gain_sum[0],
        held[0],
        held[1],
        held[2],
        gain_sum[1],
    )


def solution(mesh):
    chips, pieces = mesh.shape["fsdp"], mesh.shape["ctx"]
    one_head_each = 2 * chips == H and chips == KVH and pieces == 8
    return jax.shard_map(
        plane_layer if one_head_each else ring_layer,
        mesh=mesh,
        in_specs=(
            P("fsdp", "ctx", None),
            P("fsdp", None),
            P("fsdp", None),
            P("fsdp", None),
            P(None, "fsdp"),
            P("fsdp"),
            P("fsdp", None),
            P("fsdp", None),
            P(None, "fsdp"),
            P("fsdp"),
            P("fsdp", "ctx", None),
            P(),
            P(),
        ),
        out_specs=(
            P("fsdp", "ctx", None),
            P("fsdp", "ctx", None),
            P("fsdp", None),
            P("fsdp", None),
            P("fsdp", None),
            P(None, "fsdp"),
            P("fsdp"),
            P("fsdp", None),
            P("fsdp", None),
            P(None, "fsdp"),
            P("fsdp"),
        ),
        check_vma=False,
    )
```

```python
import functools
import types

import jax
import jax.numpy as jnp
from jax import lax
from jax.experimental import pallas as pl
from jax.experimental.pallas import tpu as pltpu
from jax.sharding import PartitionSpec as P

H = 8
KVH = 4
HD = 256


epsilon = 1e-06
theta = 1000042.0
masked_score = -1e30


def passed_along(value, axis, by):
    devices = lax.axis_size(axis)
    return lax.ppermute(value, axis, [(i, (i + by) % devices) for i in range(devices)])


def rope_tables(positions):
    half = HD // 2
    frequency = theta ** (-(jnp.arange(half, dtype=jnp.float32) * 2.0 / HD))
    angle = positions[:, None] * frequency[None, :]
    angle = jnp.concatenate([angle, angle], axis=-1)
    return (jnp.cos(angle), jnp.sin(angle))


def rotate(values, cosine, sine):
    half = values.shape[-1] // 2
    turned = jnp.concatenate([-values[..., half:], values[..., :half]], axis=-1)
    return values * cosine[:, None, :] + turned * sine[:, None, :]


def rotate_back(grads, cosine, sine):
    half = grads.shape[-1] // 2
    scaled = grads * sine[:, None, :]
    turned = jnp.concatenate([scaled[..., half:], -scaled[..., :half]], axis=-1)
    return grads * cosine[:, None, :] + turned


def split_heads(block):
    count = block.shape[0]
    key_cols = KVH * HD
    key_part = block[:, :key_cols].reshape(count, KVH, HD).transpose(1, 0, 2)
    value_part = block[:, key_cols:].reshape(count, KVH, HD).transpose(1, 0, 2)
    return (key_part, value_part)


def merge_heads(grouped):
    return grouped.transpose(1, 0, 2).reshape(grouped.shape[1], KVH * HD)


def weight_terms(lefts, rights):
    pieces = []
    for index in range(4):
        column = lefts[index]
        pieces.append(
            jnp.einsum("tc,tn->cn", column, rights[index], preferred_element_type=jnp.float32)
        )
    return jnp.concatenate(pieces, axis=1)


def ring_layer(
    tokens,
    query_weight,
    key_weight,
    value_weight,
    output_weight,
    first_gain,
    gate_weight,
    up_weight,
    down_weight,
    second_gain,
    cotangent,
    block_ids,
    piece_order,
):
    ctx_count = lax.axis_size("ctx")
    fsdp_count = lax.axis_size("fsdp")
    here = lax.axis_index("ctx")
    rows = tokens.shape[1]
    width = tokens.shape[2]
    group = H // KVH
    query_cols = H * HD
    key_cols = KVH * HD
    hidden_cols = gate_weight.shape[1]
    scale = HD ** (-0.5)
    whole_query, whole_key, whole_value, whole_output, gain_one = (
        lax.all_gather(query_weight, "fsdp", axis=0, tiled=True),
        lax.all_gather(key_weight, "fsdp", axis=0, tiled=True),
        lax.all_gather(value_weight, "fsdp", axis=0, tiled=True),
        lax.all_gather(output_weight, "fsdp", axis=1, tiled=True),
        lax.all_gather(first_gain, "fsdp", axis=0, tiled=True),
    )
    id_row = lax.dynamic_index_in_dim(block_ids, lax.axis_index("fsdp"), 0, keepdims=False)
    start_own = lax.dynamic_index_in_dim(piece_order, here, 0, keepdims=False) * rows
    offsets = jnp.arange(rows, dtype=jnp.int32)
    cosine, sine = rope_tables((start_own + offsets).astype(jnp.float32))
    own_ids = lax.dynamic_slice_in_dim(id_row, start_own, rows)
    query_ids = jnp.tile(own_ids, group)

    def visible(source):
        key_start = lax.dynamic_index_in_dim(piece_order, source, 0, keepdims=False) * rows
        key_ids = lax.dynamic_slice_in_dim(id_row, key_start, rows)
        return key_ids[None, :] <= query_ids[:, None]

    inputs = tokens[0].astype(jnp.float32)
    scale_one = lax.rsqrt(jnp.mean(inputs * inputs, axis=-1, keepdims=True) + epsilon)
    unit_one = inputs * scale_one
    normed = (unit_one * gain_one.astype(jnp.float32)).astype(jnp.bfloat16)
    query = jnp.dot(normed, whole_query, preferred_element_type=jnp.float32).reshape(rows, H, HD)
    query_rot = rotate(query, cosine, sine).astype(jnp.bfloat16)
    keys = jnp.dot(normed, whole_key, preferred_element_type=jnp.float32).reshape(rows, KVH, HD)
    keys_rot = rotate(keys, cosine, sine).astype(jnp.bfloat16).reshape(rows, key_cols)
    values = jnp.dot(normed, whole_value, preferred_element_type=jnp.float32).astype(jnp.bfloat16)
    key_value = jnp.concatenate([keys_rot, values], axis=-1)
    grouped = (
        query_rot.reshape(rows, KVH, group, HD).transpose(1, 2, 0, 3).reshape(KVH, group * rows, HD)
    )

    def forward_step(state, block, source):
        running, total, weighted = state
        key_part, value_part = split_heads(block)
        allowed = visible(source)
        scores = (
            jnp.einsum("hqd,hkd->hqk", grouped, key_part, preferred_element_type=jnp.float32)
            * scale
        )
        scores = jnp.where(allowed[None], scores, masked_score)
        newest = jnp.maximum(running, jnp.max(scores, axis=-1))
        factor = jnp.exp(running - newest)
        shares = jnp.where(allowed[None], jnp.exp(scores - newest[..., None]), 0.0)
        total = total * factor + jnp.sum(shares, axis=-1)
        weighted = weighted * factor[..., None] + jnp.einsum(
            "hqk,hkd->hqd",
            shares.astype(jnp.bfloat16),
            value_part,
            preferred_element_type=jnp.float32,
        )
        return (newest, total, weighted)

    start_state = (
        jnp.full((KVH, group * rows), masked_score, jnp.float32),
        jnp.zeros((KVH, group * rows), jnp.float32),
        jnp.zeros((KVH, group * rows, HD), jnp.float32),
    )
    state = forward_step(start_state, key_value, here)

    def forward_turn(turn, carry):
        block, inner = carry
        block = passed_along(block, "ctx", 1)
        source = (here - turn) % ctx_count
        return (block, forward_step(inner, block, source))

    passed_block, state = lax.fori_loop(1, ctx_count, forward_turn, (key_value, state))
    running, total, weighted = state
    attended = weighted / total[..., None]
    log_total = running + jnp.log(total)
    attended_low = (
        attended.reshape(KVH, group, rows, HD)
        .transpose(2, 0, 1, 3)
        .reshape(rows, query_cols)
        .astype(jnp.bfloat16)
    )
    middle = inputs + jnp.dot(attended_low, whole_output, preferred_element_type=jnp.float32)
    gain_two, whole_gate, whole_up, whole_down = (
        lax.all_gather(second_gain, "fsdp", axis=0, tiled=True),
        lax.all_gather(gate_weight, "fsdp", axis=0, tiled=True),
        lax.all_gather(up_weight, "fsdp", axis=0, tiled=True),
        lax.all_gather(down_weight, "fsdp", axis=1, tiled=True),
    )
    scale_two = lax.rsqrt(jnp.mean(middle * middle, axis=-1, keepdims=True) + epsilon)
    unit_two = middle * scale_two
    normed_two = (unit_two * gain_two.astype(jnp.float32)).astype(jnp.bfloat16)
    gate = jnp.dot(normed_two, whole_gate, preferred_element_type=jnp.float32)
    up = jnp.dot(normed_two, whole_up, preferred_element_type=jnp.float32)
    sigmoid_gate = jax.nn.sigmoid(gate)
    activated = gate * sigmoid_gate
    hidden = (activated * up).astype(jnp.bfloat16)
    result = middle + jnp.dot(hidden, whole_down, preferred_element_type=jnp.float32)
    output = result.astype(jnp.bfloat16)[None]
    upstream = cotangent[0]
    hidden_grad = jnp.einsum("tm,fm->tf", upstream, whole_down, preferred_element_type=jnp.float32)
    gate_grad = (hidden_grad * up * sigmoid_gate * (1.0 + gate * (1.0 - sigmoid_gate))).astype(
        jnp.bfloat16
    )
    up_grad = (hidden_grad * activated).astype(jnp.bfloat16)
    normed_two_grad = jnp.einsum(
        "tf,mf->tm", gate_grad, whole_gate, preferred_element_type=jnp.float32
    ) + jnp.einsum("tf,mf->tm", up_grad, whole_up, preferred_element_type=jnp.float32)
    gain_two_term = jnp.sum(normed_two_grad * unit_two, axis=0)
    unit_two_grad = normed_two_grad * gain_two.astype(jnp.float32)
    middle_grad = upstream.astype(jnp.float32) + scale_two * (
        unit_two_grad - unit_two * jnp.mean(unit_two_grad * unit_two, axis=-1, keepdims=True)
    )
    branch_grad = middle_grad.astype(jnp.bfloat16)
    attended_grad = jnp.einsum(
        "tm,cm->tc", branch_grad, whole_output, preferred_element_type=jnp.float32
    ).astype(jnp.bfloat16)
    grad_grouped = (
        attended_grad.reshape(rows, KVH, group, HD)
        .transpose(1, 2, 0, 3)
        .reshape(KVH, group * rows, HD)
    )
    delta = jnp.sum(grad_grouped.astype(jnp.float32) * attended, axis=-1)

    def backward_step(query_total, block, source):
        key_part, value_part = split_heads(block)
        allowed = visible(source)
        scores = (
            jnp.einsum("hqd,hkd->hqk", grouped, key_part, preferred_element_type=jnp.float32)
            * scale
        )
        scores = jnp.where(allowed[None], scores, masked_score)
        shares = jnp.where(allowed[None], jnp.exp(scores - log_total[..., None]), 0.0)
        value_grad = jnp.einsum(
            "hqk,hqd->hkd",
            shares.astype(jnp.bfloat16),
            grad_grouped,
            preferred_element_type=jnp.float32,
        )
        share_grad = jnp.einsum(
            "hqd,hkd->hqk", grad_grouped, value_part, preferred_element_type=jnp.float32
        )
        score_grad = (shares * (share_grad - delta[..., None])).astype(jnp.bfloat16)
        query_total = query_total + jnp.einsum(
            "hqk,hkd->hqd", score_grad, key_part, preferred_element_type=jnp.float32
        )
        key_grad = (
            jnp.einsum("hqk,hqd->hkd", score_grad, grouped, preferred_element_type=jnp.float32)
            * scale
        )
        return (
            query_total,
            jnp.concatenate([merge_heads(key_grad), merge_heads(value_grad)], axis=-1),
        )

    query_total, first_grad = backward_step(
        jnp.zeros((KVH, group * rows, HD), jnp.float32), key_value, here
    )
    held = first_grad

    def backward_turn(turn, carry):
        block, kept, total_query = carry
        block = passed_along(block, "ctx", 1)
        source = (here - turn) % ctx_count
        total_query, block_grad = backward_step(total_query, block, source)
        kept = passed_along(kept.astype(jnp.bfloat16), "ctx", 1).astype(kept.dtype) + block_grad
        return (block, kept, total_query)

    passed_again, held, query_total = lax.fori_loop(
        1, ctx_count, backward_turn, (key_value, held, query_total)
    )
    own_grad = passed_along(held.astype(jnp.bfloat16), "ctx", 1).astype(held.dtype)
    query_rot_grad = (
        (query_total * scale)
        .reshape(KVH, group, rows, HD)
        .transpose(2, 0, 1, 3)
        .reshape(rows, H, HD)
    )
    query_grad = (
        rotate_back(query_rot_grad, cosine, sine).reshape(rows, query_cols).astype(jnp.bfloat16)
    )
    key_grad = (
        rotate_back(own_grad[:, :key_cols].reshape(rows, KVH, HD), cosine, sine)
        .reshape(rows, key_cols)
        .astype(jnp.bfloat16)
    )
    value_grad = own_grad[:, key_cols:].astype(jnp.bfloat16)
    normed_grad = jnp.einsum(
        "tc,mc->tm", query_grad, whole_query, preferred_element_type=jnp.float32
    )
    normed_grad = normed_grad + jnp.einsum(
        "tc,mc->tm", key_grad, whole_key, preferred_element_type=jnp.float32
    )
    normed_grad = normed_grad + jnp.einsum(
        "tc,mc->tm", value_grad, whole_value, preferred_element_type=jnp.float32
    )
    gain_one_term = jnp.sum(normed_grad * unit_one, axis=0)
    unit_one_grad = normed_grad * gain_one.astype(jnp.float32)
    tokens_grad = middle_grad + scale_one * (
        unit_one_grad - unit_one * jnp.mean(unit_one_grad * unit_one, axis=-1, keepdims=True)
    )
    projected = jnp.concatenate([query_grad, key_grad, value_grad], axis=-1)
    gate_up = jnp.concatenate([gate_grad, up_grad], axis=-1)
    lefts = jnp.stack([normed, branch_grad, normed_two, upstream])
    rights = (projected, attended_low, gate_up, hidden)
    piece = lax.psum_scatter(
        weight_terms(lefts, rights).astype(jnp.bfloat16), "fsdp", scatter_dimension=0, tiled=True
    )
    shard = lax.psum(piece, "ctx").astype(jnp.float32)
    gain_one_sum, gain_two_sum = lax.psum((gain_one_term, gain_two_term), ("ctx", "fsdp"))
    own_rows = width // fsdp_count
    own_start = lax.axis_index("fsdp") * own_rows
    value_begin = query_cols + key_cols
    output_begin = value_begin + key_cols
    gate_begin = output_begin + query_cols
    up_begin = gate_begin + hidden_cols
    down_begin = up_begin + hidden_cols
    return (
        output,
        tokens_grad[None],
        shard[:, :query_cols],
        shard[:, query_cols:value_begin],
        shard[:, value_begin:output_begin],
        shard[:, output_begin:gate_begin].T,
        lax.dynamic_slice_in_dim(gain_one_sum, own_start, own_rows),
        shard[:, gate_begin:up_begin],
        shard[:, up_begin:down_begin],
        shard[:, down_begin : down_begin + hidden_cols].T,
        lax.dynamic_slice_in_dim(gain_two_sum, own_start, own_rows),
    )


VMEM_BYTES = 58 * 1024 * 1024
BF16 = jnp.bfloat16
F32 = jnp.float32
QUARTERS = 4
MESH = pl.DeviceIdType.MESH
TICKS = (1, 1, 1, 2, 4, 2, 1, 2, 1, 3, 2, 1, 1)
LINES = 2


def matmul(a, b):
    return lax.dot_general(a, b, (((1,), (0,)), ((), ())), preferred_element_type=F32)


def matmul_nt(a, b):
    return lax.dot_general(a, b, (((1,), (1,)), ((), ())), preferred_element_type=F32)


def matmul_tn(a, b):
    return lax.dot_general(a, b, (((0,), (0,)), ((), ())), preferred_element_type=F32)


def cost(flops, arrays, outs, exps=0):
    moved = sum(a.size * a.dtype.itemsize for a in arrays) + sum(
        o.size * o.dtype.itemsize for o in outs
    )
    return pl.CostEstimate(flops=int(flops), bytes_accessed=int(moved), transcendentals=int(exps))


def run_whole(body, me, arrays, outs, scratch=(), flops=0, in_hbm=0, name=None):
    count = len(arrays) - in_hbm
    return pl.pallas_call(
        body,
        out_shape=outs,
        in_specs=[pl.BlockSpec(memory_space=pltpu.SMEM)]
        + [pl.BlockSpec(memory_space=pltpu.VMEM)] * count
        + [pl.BlockSpec(memory_space=pl.ANY)] * in_hbm,
        out_specs=jax.tree.map(lambda _: pl.BlockSpec(memory_space=pltpu.VMEM), outs),
        scratch_shapes=list(scratch),
        cost_estimate=cost(flops, arrays, jax.tree.leaves(outs)),
        compiler_params=pltpu.CompilerParams(vmem_limit_bytes=VMEM_BYTES),
        name=name,
    )(me, *arrays)


def run_grid(body, me, grid, arrays, in_specs, outs, out_specs, scratch=(), flops=0, aliases=None, name=None):
    return pl.pallas_call(
        body,
        out_shape=outs,
        grid_spec=pltpu.PrefetchScalarGridSpec(
            num_scalar_prefetch=1,
            grid=grid,
            in_specs=in_specs,
            out_specs=out_specs,
            scratch_shapes=list(scratch),
        ),
        cost_estimate=cost(flops, arrays, jax.tree.leaves(outs)),
        input_output_aliases=aliases or {},
        compiler_params=pltpu.CompilerParams(vmem_limit_bytes=VMEM_BYTES),
        name=name,
    )(me, *arrays)


def shape(dims, kind=BF16):
    return jax.ShapeDtypeStruct(tuple(dims), kind)


def fixed(block):
    return pl.BlockSpec(block, lambda i, me: (0,) * len(block), pipeline_mode=pl.Buffered(1))


def column(index, wide):
    return pl.ds(pl.multiple_of(index * wide, wide), wide)


def turn(values):
    half = values.shape[-1] // 2
    return jnp.concatenate([-values[:, half:], values[:, :half]], axis=-1)


def turn_back(values):
    half = values.shape[-1] // 2
    return jnp.concatenate([values[:, half:], -values[:, :half]], axis=-1)


def plane_layer(
    tokens,
    query_weight,
    key_weight,
    value_weight,
    output_weight,
    first_gain,
    gate_weight,
    up_weight,
    down_weight,
    second_gain,
    cotangent,
    block_ids,
    piece_order,
):
    ctx_count = lax.axis_size("ctx")
    n = lax.axis_size("fsdp")
    planes = ctx_count // 2
    ctx = lax.axis_index("ctx")
    z, core = ctx // 2, ctx % 2
    f = lax.axis_index("fsdp")
    me = jnp.stack([f, core]).astype(jnp.int32)
    rows, width = tokens.shape[1:]
    pair = 2 * rows
    plane_rows = n * pair
    wide = width // n
    hidden_cols = gate_weight.shape[1]
    part = hidden_cols // (2 * n)
    quarter = part // QUARTERS
    scale = HD ** (-0.5)

    def across(value, d):
        return lax.ppermute(value, "fsdp", [(i, i ^ d) for i in range(n)])

    def sibling(value):
        return lax.ppermute(value, "ctx", [(i, i ^ 1) for i in range(ctx_count)])

    def along(value, step):
        pairs = [(i, i + 2 * step) for i in range(ctx_count)]
        return lax.ppermute(value, "ctx", [(a, b) for a, b in pairs if 0 <= b < ctx_count])

    def between_planes(value, moves):
        return lax.ppermute(
            value, "ctx", [(2 * a + side, 2 * b + side) for a, b in moves for side in range(2)]
        )

    def gathered(value):
        own = [value] + [across(value, d) for d in range(1, n)]
        return own, [sibling(block) for block in own]

    def reduced(own, other):
        near = [sibling(block) for block in other]
        sent = [
            across((own[d].astype(F32) + near[d].astype(F32)).astype(BF16), d) for d in range(1, n)
        ]
        return [own[0], near[0]] + sent

    middle_left, middle_right = planes // 2 - 1, planes // 2
    folds = [
        [(s, s + 1), (planes - 1 - s, planes - 2 - s)] for s in range(middle_left)
    ]

    def summed_over_planes(value):
        for moves in folds:
            value = (
                value.astype(F32) + between_planes(value, moves).astype(F32)
            ).astype(value.dtype)
        crossed = between_planes(value, [(middle_left, middle_right), (middle_right, middle_left)])
        value = (value.astype(F32) + crossed.astype(F32)).astype(value.dtype)
        for s, moves in reversed(list(enumerate(folds))):
            back = between_planes(value, [(b, a) for a, b in moves])
            receives = (z == s) | (z == planes - 1 - s)
            value = jnp.where(receives, back, value)
        return value

    place = jnp.arange(rows, dtype=jnp.int32)
    own_pieces = lax.dynamic_slice_in_dim(piece_order, 2 * z, 2)
    positions = (own_pieces[:, None] * rows + place[None, :]).reshape(pair).astype(F32)
    cosine, sine = rope_tables(positions)
    is_value = core == 1
    kv_cosine = jnp.where(is_value, 1.0, cosine)
    kv_sine = jnp.where(is_value, 0.0, sine)
    chips = f ^ jnp.arange(n, dtype=jnp.int32)
    ring = (z - jnp.arange(planes, dtype=jnp.int32)) % planes
    ring_ctx = (2 * ring[:, None] + jnp.arange(2, dtype=jnp.int32)[None, :]).reshape(-1)
    id_pieces = block_ids.reshape(n, ctx_count, rows)
    ids = id_pieces[chips[:, None], piece_order[ring_ctx][None, :]]
    key_ids = ids.reshape(n, planes, 1, pair)
    query_ids = ids[:, :2].reshape(n, pair, 1)

    def cut_attention(me_ref, *refs):
        wq, wk, wv, wo = (refs[i * n : (i + 1) * n] for i in range(4))
        one, two = refs[4 * n : 4 * n + 2]
        outs = refs[4 * n + 2 :]
        keys_here = me_ref[1] == 0
        for d in range(n):
            first = outs[d]
            first[:wide, :HD] = wq[d][...]

            @pl.when(keys_here)
            def _():
                first[:wide, HD:] = wk[d][...]

            @pl.when(jnp.logical_not(keys_here))
            def _():
                first[:wide, HD:] = wv[d][...]

            pick = lax.broadcasted_iota(jnp.int32, (16, wide), 0) < 8
            first[wide:, :] = jnp.where(pick, one[...].astype(F32), two[...].astype(F32)).astype(
                BF16
            )
            outs[n + d][...] = wo[d][...]

    def head_of(d):
        return lambda i, me: (0, 2 * (me[0] ^ d) + me[1])

    def chip_of(d):
        return lambda i, me: (0, me[0] ^ d)

    def head_rows_of(d):
        return lambda i, me: (2 * (me[0] ^ d) + me[1], 0)

    gain_spec = pl.BlockSpec((1, wide), lambda i, me: (0, 0))
    cut = run_grid(
        cut_attention,
        me,
        (1,),
        [query_weight] * n
        + [key_weight] * n
        + [value_weight] * n
        + [output_weight] * n
        + [first_gain.reshape(1, wide), second_gain.reshape(1, wide)],
        [pl.BlockSpec((wide, HD), head_of(d)) for d in range(n)]
        + [pl.BlockSpec((wide, HD), chip_of(d)) for d in range(n)] * 2
        + [pl.BlockSpec((HD, wide), head_rows_of(d)) for d in range(n)]
        + [gain_spec, gain_spec],
        [shape((wide + 16, 2 * HD))] * n + [shape((HD, wide))] * n,
        [pl.BlockSpec((wide + 16, 2 * HD), lambda i, me: (0, 0))] * n
        + [pl.BlockSpec((HD, wide), lambda i, me: (0, 0))] * n,
        name="cut_attention",
    )
    own_tokens = tokens[0]
    token_own, token_near = gathered(own_tokens)
    weights_in = [cut[0]] + [across(cut[d], d) for d in range(1, n)]
    weights_out = [cut[n]] + [across(cut[n + d], d) for d in range(1, n)]

    def cut_hidden(me_ref, *refs):
        gates, ups, downs = (refs[i * n : (i + 1) * n] for i in range(3))
        for d in range(n):
            refs[-1][0, d, :wide, :quarter] = gates[d][...]
            refs[-1][0, d, :wide, quarter:] = ups[d][...]
            refs[-1][0, d, wide:, :] = downs[d][...]

    def columns_of(d):
        return lambda q, me: (0, (2 * (me[0] ^ d) + me[1]) * QUARTERS + q)

    def down_rows_of(d):
        return lambda q, me: ((2 * (me[0] ^ d) + me[1]) * QUARTERS + q, 0)

    piece = (wide + quarter, 2 * quarter)
    hidden_cut = run_grid(
        cut_hidden,
        me,
        (QUARTERS,),
        [gate_weight] * n + [up_weight] * n + [down_weight] * n,
        [pl.BlockSpec((wide, quarter), columns_of(d)) for d in range(n)] * 2
        + [pl.BlockSpec((quarter, wide), down_rows_of(d)) for d in range(n)],
        shape((QUARTERS, n) + piece),
        pl.BlockSpec((1, n) + piece, lambda q, me: (q, 0, 0, 0)),
        name="cut_hidden",
    )
    first_pieces = [across(hidden_cut[0, d], d) for d in range(1, n)]
    own_cotangent = cotangent[0]
    cot_own = [own_cotangent] + [across(own_cotangent, d) for d in range(1, n)]

    def project(me_ref, *refs):
        near_tokens = refs[: 2 * n]
        pieces = refs[2 * n : 3 * n]
        cos_ref, sin_ref, kvcos_ref, kvsin_ref = refs[3 * n : 3 * n + 4]
        normed_ref, query_ref, kv_ref, gains_ref = refs[3 * n + 4 :]
        chip, side = me_ref[0], me_ref[1]
        for j in range(n):
            both = pieces[j][wide:, :].astype(F32)
            gains_ref[0:1, column(chip ^ j, wide)] = both[0:1]
            gains_ref[1:2, column(chip ^ j, wide)] = both[8:9]
        for d in range(n):
            for e in range(2):
                slot = side ^ e
                values = near_tokens[e * n + d][...].astype(F32)
                inverse = lax.rsqrt(jnp.mean(values * values, axis=-1, keepdims=True) + epsilon)
                normed_ref[d, slot] = (values * inverse * gains_ref[0:1, :]).astype(BF16)
                both = jnp.zeros((rows, 2 * HD), F32)
                for j in range(n):
                    both += matmul(
                        normed_ref[d, slot, :, column(chip ^ j, wide)], pieces[j][:wide, :]
                    )
                query, kv = both[:, :HD], both[:, HD:]
                query_ref[d, slot] = (
                    query * cos_ref[slot] + turn(query) * sin_ref[slot]
                ).astype(BF16)
                kv_ref[d, slot] = (kv * kvcos_ref[slot] + turn(kv) * kvsin_ref[slot]).astype(BF16)

    head_shape = (n, 2, rows, HD)
    tables = [t.reshape(2, rows, HD) for t in (cosine, sine, kv_cosine, kv_sine)]
    normed, query_rot, own_kv, gains = run_whole(
        project,
        me,
        token_own + token_near + weights_in + tables,
        [
            shape((n, 2, rows, width)),
            shape(head_shape),
            shape(head_shape),
            shape((2, width), F32),
        ],
        flops=2 * plane_rows * width * 2 * HD,
        name="project",
    )

    rightward, leftward = [own_kv], [own_kv]
    for _ in range(planes - 1):
        rightward.append(along(rightward[-1], 1))
        leftward.append(along(leftward[-1], -1))
    kv_mine = [own_kv] + [rightward[k] + leftward[planes - k] for k in range(1, planes)]
    kv_near = [sibling(block) for block in kv_mine]

    head_spec = pl.BlockSpec((1, 2, rows, HD), lambda i, me: (i, 0, 0, 0))
    id_specs = [
        pl.BlockSpec((1, pair, 1), lambda i, me: (i, 0, 0)),
        pl.BlockSpec((1, planes, 1, pair), lambda i, me: (i, 0, 0, 0)),
    ]

    def scored(side, query, query_id, key_id, mine, near):
        keys, values, scores = [], [], []
        for k in range(planes):
            a = mine[k][0].reshape(pair, HD)
            b = near[k][0].reshape(pair, HD)
            keys.append(jnp.where(side == 0, a, b))
            values.append(jnp.where(side == 0, b, a))
            score = matmul_nt(query, keys[k]) * scale
            scores.append(jnp.where(key_id[0, k] <= query_id[0], score, masked_score))
        top = functools.reduce(jnp.maximum, [jnp.max(s, axis=-1, keepdims=True) for s in scores])
        raised = [jnp.exp(s - top) for s in scores]
        inverse = 1.0 / sum(jnp.sum(r, axis=-1, keepdims=True) for r in raised)
        return keys, values, [r * inverse for r in raised]

    def spread(step, side, whole, own_refs, near_refs):
        for d in range(n):

            @pl.when(step == d)
            def _():
                own_refs[d][...] = whole[side]
                near_refs[d][...] = whole[1 - side]

    def attend(me_ref, query_ref, query_id, key_id, *refs):
        mine, near, out_w = refs[:planes], refs[planes : 2 * planes], refs[2 * planes : 2 * planes + n]
        attended_ref = refs[2 * planes + n]
        own_refs = refs[2 * planes + n + 1 : 2 * planes + 2 * n + 1]
        near_refs = refs[2 * planes + 2 * n + 1 : 2 * planes + 3 * n + 1]
        whole = refs[-1]
        chip, side = me_ref[0], me_ref[1]
        query = query_ref[0].reshape(pair, HD)
        _, values, probs = scored(side, query, query_id, key_id, mine, near)
        total = jnp.zeros((pair, HD), F32)
        for k in range(planes):
            total += matmul(probs[k].astype(BF16), values[k])
        attended = total.astype(BF16)
        attended_ref[0] = attended.reshape(2, rows, HD)
        for j in range(n):
            whole[:, :, column(chip ^ j, wide)] = (
                matmul(attended, out_w[j][...]).astype(BF16).reshape(2, rows, wide)
            )
        spread(pl.program_id(0), side, whole, own_refs, near_refs)

    early = lax.optimization_barrier([query_rot] + cot_own[1:] + first_pieces)
    query_rot, cot_own[1:], first_pieces = early[0], early[1:n], early[n:]
    cot_near = [sibling(block) for block in cot_own]

    block = (rows, width)
    attend_flops = 4 * plane_rows * planes * pair * HD + 2 * plane_rows * HD * width
    attended, *partial = run_grid(
        attend,
        me,
        (n,),
        [query_rot, query_ids, key_ids] + kv_mine + kv_near + weights_out,
        [head_spec] + id_specs + [head_spec] * (2 * planes) + [fixed((HD, wide))] * n,
        [shape(head_shape)] + [shape(block)] * (2 * n),
        [head_spec] + [pl.BlockSpec(block, lambda i, me: (0, 0))] * (2 * n),
        scratch=[pltpu.VMEM((2, rows, width), BF16)],
        flops=attend_flops,
        name="attend",
    )
    middle_terms = reduced(partial[:n], partial[n:])

    def second_norm(me_ref, token_ref, gains_ref, *refs):
        terms, (middle_ref, normed_ref) = refs[:-2], refs[-2:]
        middle = token_ref[...].astype(F32)
        middle += sum(t[...].astype(F32) for t in terms)
        inverse = lax.rsqrt(jnp.mean(middle * middle, axis=-1, keepdims=True) + epsilon)
        middle_ref[...] = middle
        normed_ref[...] = (middle * inverse * gains_ref[1:2, :]).astype(BF16)

    middle, own_normed_two = run_whole(
        second_norm,
        me,
        [own_tokens, gains] + middle_terms,
        [shape(block, F32), shape(block)],
        name="second_norm",
    )
    two_own, two_near = gathered(own_normed_two)

    tile = plane_rows // 3
    tiles_count = 3 * QUARTERS + 3
    query_at, output_at, kv_at = tiles_count - 3, tiles_count - 2, tiles_count - 1
    units = 2 * tiles_count
    unit = (2, quarter, wide)
    held_sums, held_ends = 4, 3
    BACK, OUT, ONE = range(3)
    columns = (plane_rows, HD)
    lanes = (8, wide)
    dma = pltpu.SemaphoreType.DMA

    in_hbm = dict(
        two=two_own + two_near,
        cot=cot_own + cot_near,
        first=first_pieces,
        in_weight=weights_in,
        out_weight=weights_out,
        kv_mine=[a.reshape(columns) for a in kv_mine],
        kv_near=[a.reshape(columns) for a in kv_near],
        cut=hidden_cut,
        query=query_rot.reshape(columns),
        attended=attended.reshape(columns),
        normed=normed.reshape(plane_rows, width),
        middle=middle,
        tokens=own_tokens,
    )
    in_vmem = dict(
        gains=gains,
        tables=jnp.stack([cosine, sine, kv_cosine, kv_sine]),
        query_ids=query_ids,
        key_ids=key_ids,
    )
    unit_array = shape((units,) + unit)
    out_hbm = dict(
        tiles=unit_array,
        from_end=unit_array,
        from_middle=unit_array,
        finals=unit_array,
        owned=unit_array,
        near=unit_array,
        row_near=shape((3, n) + block),
        row_far=shape((3, n) + block),
        branch_all=shape((n, 2) + block),
        kv_other=shape((planes,) + columns),
        kv_down=shape((planes,) + columns),
        kv_up=shape((planes,) + columns),
        out_own=shape(block),
        tokens_grad=shape(block, F32),
        gain_out=shape(lanes, F32),
    )
    scratch = dict(
        work=pltpu.VMEM((2 * plane_rows, width), BF16),
        feed=pltpu.VMEM((QUARTERS, n) + piece, BF16),
        heads=pltpu.VMEM((3 * QUARTERS, plane_rows, HD), BF16),
        turned=pltpu.VMEM((3, HD, plane_rows), BF16),
        stage=pltpu.VMEM((2, n, quarter, wide), BF16),
        mine=pltpu.VMEM((2,) + unit, BF16),
        theirs=pltpu.VMEM((2,) + unit, BF16),
        crossed=pltpu.VMEM((2,) + unit, BF16),
        sums=pltpu.VMEM((held_sums,) + unit, BF16),
        ends=pltpu.VMEM((held_ends,) + unit, BF16),
        some_rows=pltpu.VMEM((n,) + block, BF16),
        wide_rows=pltpu.VMEM(block, F32),
        own_rows=pltpu.VMEM(block, BF16),
        kv_some=pltpu.VMEM((2,) + columns, BF16),
        flat=pltpu.VMEM((8, width), F32),
        gain_mine=pltpu.VMEM((n,) + lanes, F32),
        gain_far=pltpu.VMEM((n,) + lanes, F32),
        gain_sum=pltpu.VMEM((4,) + lanes, F32),
        gain_in=pltpu.VMEM((4,) + lanes, F32),
        load_sem=dma((4 * n + n - 1,)),
        feed_local=dma((QUARTERS,)),
        feed_send=dma((QUARTERS * n,)),
        feed_recv=dma((QUARTERS * n,)),
        stage_sem=dma((2, 2)),
        one_send=dma((units,)),
        one_recv=dma((units,)),
        two_send=dma((units,)),
        two_recv=dma((units,)),
        three_send=dma((units,)),
        three_recv=dma((units,)),
        mine_sem=dma((2,)),
        theirs_sem=dma((2,)),
        crossed_sem=dma((2,)),
        final_sem=dma((held_ends,)),
        deal_local=dma((units,)),
        deal_send=dma((2 * units,)),
        deal_recv=dma((2 * units,)),
        sib_send=dma((units,)),
        sib_recv=dma((units,)),
        row_sem=dma((n,)),
        row_near_send=dma((3 * n,)),
        row_near_recv=dma((3 * n,)),
        row_far_send=dma((3 * n,)),
        row_far_recv=dma((3 * n,)),
        branch_local=dma((1,)),
        branch_send=dma((n,)),
        branch_recv=dma((n,)),
        branch_near_send=dma((n,)),
        branch_near_recv=dma((n,)),
        kv_sem=dma((2,)),
        kv_send=dma((planes,)),
        kv_recv=dma((planes,)),
        down_send=dma((planes,)),
        down_recv=dma((planes,)),
        up_send=dma((planes,)),
        up_recv=dma((planes,)),
        gain_send=dma((n + 4,)),
        gain_recv=dma((n + 4,)),
    )

    def backward(*refs):
        r, first = types.SimpleNamespace(), 0
        for group in (in_hbm, in_vmem, out_hbm):
            leaves, form = jax.tree.flatten(group)
            vars(r).update(jax.tree.unflatten(form, refs[first : first + len(leaves)]))
            first += len(leaves)
        vars(r).update(zip(scratch, refs[first:]))
        here = lax.axis_index("ctx")
        chip = lax.axis_index("fsdp")
        z, side = here // 2, here % 2
        is_middle = (z == 1) | (z == 2)
        is_end = jnp.logical_not(is_middle)
        chips = [chip, chip + 1 - 2 * (chip % 2), (chip + 2) % 4, 3 - chip]
        partner = (2 * (z + 1 - 2 * (z % 2)) + side, chip)
        other_middle = (2 * (3 - z) + side, chip)
        other_core = (here + 1 - 2 * side, chip)
        below, above = (here - 2, chip), (here + 2, chip)
        blocks = [pl.ds(pl.multiple_of(c * wide, wide), wide) for c in chips]
        work, feed, heads, turned, stage = r.work, r.feed, r.heads, r.turned, r.stage

        barrier = pltpu.get_barrier_semaphore()
        for peer in [(here, c) for c in chips[1:]] + [partner, other_core]:
            pl.semaphore_signal(barrier, inc=1, device_id=peer, device_id_type=MESH)

        @pl.when(is_middle)
        def _():
            pl.semaphore_signal(barrier, inc=1, device_id=other_middle, device_id_type=MESH)
            pl.semaphore_wait(barrier, n + 2)

        @pl.when(is_end)
        def _():
            pl.semaphore_wait(barrier, n + 1)

        def remote(source, target, send, recv, peer):
            return pltpu.make_async_remote_copy(
                src_ref=source,
                dst_ref=target,
                send_sem=send,
                recv_sem=recv,
                device_id=peer,
                device_id_type=MESH,
            )

        local = pltpu.make_async_copy

        def span(first, count):
            return pl.ds(pl.multiple_of(first, count), count)

        def feed_copy(q, d):
            at = q * n + d
            return remote(
                r.cut.at[q, d], feed.at[q, d], r.feed_send.at[at], r.feed_recv.at[at], (here, chips[d])
            )

        def feed_own(q):
            return local(r.cut.at[q, 0], feed.at[q, 0], r.feed_local.at[q])

        def hop_one(i):
            return remote(r.tiles.at[i], r.from_end.at[i], r.one_send.at[i], r.one_recv.at[i], partner)

        def hop_two(i):
            return remote(
                r.sums.at[i % held_sums],
                r.from_middle.at[i],
                r.two_send.at[i],
                r.two_recv.at[i],
                other_middle,
            )

        def hop_three(i):
            return remote(
                r.ends.at[i % held_ends], r.finals.at[i], r.three_send.at[i], r.three_recv.at[i], partner
            )

        def load_mine(i):
            return local(r.tiles.at[i], r.mine.at[i % 2], r.mine_sem.at[i % 2])

        def load_theirs(i):
            return local(r.from_end.at[i], r.theirs.at[i % 2], r.theirs_sem.at[i % 2])

        def load_crossed(i):
            return local(r.from_middle.at[i], r.crossed.at[i % 2], r.crossed_sem.at[i % 2])

        def keep_final(i):
            return local(r.ends.at[i % held_ends], r.finals.at[i], r.final_sem.at[i % held_ends])

        def keep_own(i):
            return local(r.finals.at[i, 0], r.owned.at[i, 0], r.deal_local.at[i])

        def deal_to(i, b, d):
            at = 2 * i + b
            return remote(
                r.finals.at[i, b],
                r.owned.at[i, b],
                r.deal_send.at[at],
                r.deal_recv.at[at],
                (here, chips[d]),
            )

        def to_sibling(i):
            return remote(r.owned.at[i], r.near.at[i], r.sib_send.at[i], r.sib_recv.at[i], other_core)

        def add(target, a, b):
            def some(s, _):
                at = (s // 4, span((s % 4) * (quarter // 4), quarter // 4))
                target[at] = (a[at].astype(F32) + b[at].astype(F32)).astype(BF16)
                return 0

            lax.fori_loop(0, 8, some, 0)

        def when_in(i, *conditions):
            return pl.when(functools.reduce(jnp.logical_and, conditions, (i >= 0) & (i < units)))

        def step(i, _=0):
            @when_in(i - 1, is_middle)
            def _():
                at = i - 1
                load_mine(at).wait()
                load_theirs(at).wait()

                @pl.when(at >= held_sums)
                def _():
                    hop_two(at - held_sums).wait_send()

                add(r.sums.at[at % held_sums], r.mine.at[at % 2], r.theirs.at[at % 2])
                hop_two(at).start()

            @when_in(i - 4, is_middle)
            def _():
                at = i - 4
                load_crossed(at).wait()

                @pl.when(at >= held_ends)
                def _():
                    hop_three(at - held_ends).wait_send()

                add(r.ends.at[at % held_ends], r.sums.at[at % held_sums], r.crossed.at[at % 2])
                hop_three(at).start()
                keep_final(at).start()

            @when_in(i, is_middle)
            def _():
                hop_one(i).wait_recv()
                load_mine(i).start()
                load_theirs(i).start()

            @when_in(i - 3, is_middle)
            def _():
                hop_two(i - 3).wait_recv()
                load_crossed(i - 3).start()

            @when_in(i - 6)
            def _():
                at = i - 6

                @pl.when(is_middle)
                def _():
                    keep_final(at).wait()

                @pl.when(is_end)
                def _():
                    hop_three(at).wait_recv()

                @pl.when(at % 2 == 0)
                def _():
                    keep_own(at).start()
                    deal_to(at, 1, 1).start()

                @pl.when(at % 2 == 1)
                def _():
                    deal_to(at, 0, 2).start()
                    deal_to(at, 1, 3).start()

            @when_in(i - 9)
            def _():
                at = i - 9

                @pl.when(at % 2 == 0)
                def _():
                    keep_own(at).wait()

                @pl.when(at % 2 == 1)
                def _():
                    deal_to(at, 0, 2).wait_recv()

                deal_to(at, 1, 3).wait_recv()
                to_sibling(at).start()

            return 0

        steps_done = [0]

        def advance(count):
            first = steps_done[0]
            steps_done[0] = first + count
            lax.fori_loop(first, first + count, step, 0)

        def finish():
            def one(i, _):
                @pl.when(is_end)
                def _():
                    hop_one(i).wait_send()

                @pl.when(is_middle & (i >= units - held_sums))
                def _():
                    hop_two(i).wait_send()

                @pl.when(is_middle & (i >= units - held_ends))
                def _():
                    hop_three(i).wait_send()

                @pl.when(i % 2 == 1)
                def _():
                    deal_to(i, 0, 2).wait_send()

                deal_to(i, 1, 3).wait_send()
                to_sibling(i).wait()
                return 0

            lax.fori_loop(0, units, one, 0)

        def stage_copy(t, h):
            return local(r.stage.at[t % 2, pl.ds(2 * h, 2)], r.tiles.at[2 * t + h], r.stage_sem.at[t % 2, h])

        def staged(t):
            for h in range(2):
                stage_copy(t, h).wait()

            @pl.when(is_end)
            def _():
                for h in range(2):
                    hop_one(2 * t + h).start()

        def outer(t, left, right_rows):
            for j in range(n):
                stage[t % 2, j] = matmul(left, work[right_rows, blocks[j]]).astype(BF16)
            for h in range(2):
                stage_copy(t, h).start()

        def row_near(s, base, d):
            at = s * n + d
            return remote(
                work.at[pl.ds(base + (n + d) * rows, rows)],
                r.row_near.at[s, d],
                r.row_near_send.at[at],
                r.row_near_recv.at[at],
                other_core,
            )

        def row_far(s, base, d):
            at = s * n + d
            return remote(
                work.at[pl.ds(base + d * rows, rows)],
                r.row_far.at[s, d],
                r.row_far_send.at[at],
                r.row_far_recv.at[at],
                (here, chips[d]),
            )

        def near_load(s, d):
            return local(r.row_near.at[s, d], r.some_rows.at[d], r.row_sem.at[d])

        def far_load(s, d):
            return local(r.row_far.at[s, d], r.some_rows.at[d], r.row_sem.at[d])

        few = 16

        def rows_hand_over(s, base):
            for d in (3, 1, 2, 0):
                row_near(s, base, d).start()

        def rows_send(s, base):
            for d in (3, 1, 2):
                row_near(s, base, d).wait_recv()
                near_load(s, d).start()
            for d in (3, 1, 2):
                near_load(s, d).wait()

                def some(c, _, d=d):
                    at = span(c * few, few)
                    own = pl.ds(pl.multiple_of(base + d * rows + c * few, few), few)
                    work[own, :] = (
                        work[own, :].astype(F32) + r.some_rows[d, at, :].astype(F32)
                    ).astype(BF16)
                    return 0

                lax.fori_loop(0, rows // few, some, 0)
                row_far(s, base, d).start()

        def rows_arrive(s, base):
            row_near(s, base, 0).wait_recv()
            near_load(s, 0).start()
            for d in range(1, n):
                row_far(s, base, d).wait_recv()
                far_load(s, d).start()
            near_load(s, 0).wait()
            for d in range(1, n):
                far_load(s, d).wait()

        def rows_sent(s, base):
            for d in range(n):
                row_near(s, base, d).wait_send()
            for d in range(1, n):
                row_far(s, base, d).wait_send()

        def norm_rows_back(base, value_ref, gain_row, use):
            r.flat[...] = jnp.zeros_like(r.flat)

            def some(c, _):
                at = span(c * few, few)
                grad = work[pl.ds(pl.multiple_of(base + c * few, few), few), :].astype(F32)
                for d in range(n):
                    grad += r.some_rows[d, at, :].astype(F32)
                values = value_ref[at, :].astype(F32)
                inverse = lax.rsqrt(jnp.mean(values * values, axis=-1, keepdims=True) + epsilon)
                unit_rows = values * inverse
                scaled = grad * gain_row
                back = inverse * (
                    scaled - unit_rows * jnp.mean(scaled * unit_rows, axis=-1, keepdims=True)
                )
                use(at, back)
                terms = grad * unit_rows
                r.flat[...] += terms[:8] + terms[8:]
                return 0

            lax.fori_loop(0, rows // few, some, 0)

        def gain_terms(at):
            total = jnp.sum(r.flat[...], axis=0, keepdims=True)
            r.flat[0:1, :] = total
            for j in range(n):
                r.gain_mine[j, at : at + 1, :] = r.flat[0:1, blocks[j]]

        r.gain_mine[...] = jnp.zeros_like(r.gain_mine)
        loads = []

        def load(source, target):
            copy = local(source, target, r.load_sem.at[len(loads)])
            copy.start()
            loads.append(copy)

        def loaded():
            while loads:
                loads.pop().wait()

        for base, sources in ((0, r.two), (plane_rows, r.cot)):
            for i in range(2 * n):
                load(sources[i], work.at[pl.ds(base + i * rows, rows)])
        for d in range(1, n):
            load(r.first[d - 1], feed.at[0, d])
        for q in range(QUARTERS):
            feed_own(q).start()
        for d in range(1, n):
            feed_copy(1, d).start()
        loaded()

        def quarter_step(q, _):
            step(3 * q - 3)
            feed_own(q).wait()

            @pl.when(q > 0)
            def _():
                for d in range(1, n):
                    feed_copy(q, d).wait_recv()

            @pl.when((q > 0) & (q < QUARTERS - 1))
            def _():
                for d in range(1, n):
                    feed_copy(q + 1, d).start()

            def forward(t, _):
                now = span(t * tile, tile)
                cot_now = pl.ds(pl.multiple_of(plane_rows + t * tile, tile), tile)
                both = jnp.zeros((tile, 2 * quarter), F32)
                hidden_grad = jnp.zeros((tile, quarter), F32)
                for j in range(n):
                    both += matmul(work[now, blocks[j]], feed[q, j, :wide, :])
                    hidden_grad += matmul_nt(work[cot_now, blocks[j]], feed[q, j, wide:, :])
                gate, up = both[:, :quarter], both[:, quarter:]
                share = 1.0 / (1.0 + jnp.exp(-gate))
                activated = gate * share
                results = (
                    activated * up,
                    hidden_grad * up * share * (1.0 + gate * (1.0 - share)),
                    hidden_grad * activated,
                )
                for w, result in enumerate(results):
                    heads[q * 3 + w, now, :] = result.astype(BF16)
                    turned[w, :, now] = result.T.astype(BF16)
                return 0

            lax.fori_loop(0, plane_rows // tile, forward, 0)
            step(3 * q - 2)

            def one(w, _):
                t = 3 * q + w

                @pl.when(t >= 2)
                def _():
                    staged(t - 2)

                outer(t, turned[w], span(jnp.where(w == 0, plane_rows, 0), plane_rows))
                return 0

            lax.fori_loop(0, 3, one, 0)
            step(3 * q - 1)
            return 0

        lax.fori_loop(0, QUARTERS, quarter_step, 0)
        steps_done[0] = 3 * QUARTERS - 3
        for t in (query_at - 2, query_at - 1):
            staged(t)

        def back_step(s, _):
            now = span(s * pair, pair)
            lefts = [
                jnp.concatenate([heads[q * 3 + 1, now, :], heads[q * 3 + 2, now, :]], axis=1)
                for q in range(QUARTERS)
            ]
            for j in range(n):
                total = jnp.zeros((pair, wide), F32)
                for q in range(QUARTERS):
                    total += matmul_nt(lefts[q], feed[q, j, :wide, :])
                work[now, blocks[j]] = total.astype(BF16)
            return 0

        half = n // 2
        lax.fori_loop(half, n, back_step, 0)
        rows_hand_over(BACK, 0)
        advance(TICKS[0])
        lax.fori_loop(0, half, back_step, 0)
        rows_send(BACK, 0)
        advance(TICKS[1])

        def out_step(s, _):
            now = span(s * pair, pair)
            then = pl.ds(pl.multiple_of(plane_rows + s * pair, pair), pair)
            for j in range(n):
                total = jnp.zeros((pair, wide), F32)
                for q in range(QUARTERS):
                    total += matmul(heads[q * 3, now, :], feed[q, j, wide:, :])
                work[then, blocks[j]] = total.astype(BF16)
            return 0

        load(r.middle, r.wide_rows)
        lax.fori_loop(half, n, out_step, 0)
        rows_hand_over(OUT, plane_rows)
        advance(TICKS[2])
        lax.fori_loop(0, half, out_step, 0)
        advance(TICKS[3])

        for k in range(planes):
            load(r.kv_mine[k], heads.at[k])
            load(r.kv_near[k], heads.at[planes + k])
        load(r.query, heads.at[2 * planes])
        load(r.attended, heads.at[2 * planes + 1])
        for j in range(n):
            load(r.in_weight[j].at[pl.ds(0, wide)], feed.at[0, j, pl.ds(0, wide)])
            load(r.out_weight[j], feed.at[0, j, pl.ds(wide, HD)])

        rows_arrive(BACK, 0)
        loaded()
        load(r.cot[0], r.own_rows)
        loaded()

        def second_use(at, back):
            grad = r.own_rows[at, :].astype(F32) + back
            r.wide_rows[at, :] = grad
            r.own_rows[at, :] = grad.astype(BF16)

        norm_rows_back(0, r.wide_rows, r.gains[1:2, :], second_use)

        def branch_far(d):
            return remote(
                r.own_rows,
                r.branch_all.at[d, side],
                r.branch_send.at[d],
                r.branch_recv.at[d],
                (here, chips[d]),
            )

        def branch_near(d):
            source = r.own_rows if d == 0 else r.branch_all.at[d, side]
            return remote(
                source,
                r.branch_all.at[d, side],
                r.branch_near_send.at[d],
                r.branch_near_recv.at[d],
                other_core,
            )

        for d in (3, 1, 2):
            branch_far(d).start()
        branch_near(0).start()
        branch_own = local(r.own_rows, r.branch_all.at[0, side], r.branch_local.at[0])
        branch_own.start()
        gain_terms(1)
        advance(TICKS[4])
        for d in (1, 2, 3):
            branch_far(d).wait_recv()
            branch_near(d).start()
        rows_sent(BACK, 0)
        branch_own.wait()
        for d in range(n):
            branch_near(d).wait_recv()
        for d in range(n):
            for c in range(2):
                load(r.branch_all.at[d, c], work.at[pl.ds((2 * d + c) * rows, rows)])
        rows_send(OUT, plane_rows)
        loaded()

        query_slot, attended_slot, query_grad_slot, kv_grad_slot = range(2 * planes, 2 * planes + 4)

        def attend_back(d, _):
            now = span(d * pair, pair)
            query = heads[query_slot, now, :]
            attended_grad = jnp.zeros((pair, HD), F32)
            for j in range(n):
                attended_grad += matmul_nt(work[now, blocks[j]], feed[0, j, wide:, :])
            attended_grad = attended_grad.astype(BF16)
            keys, values, scores = [], [], []
            for k in range(planes):
                a, b = heads[k, now, :], heads[planes + k, now, :]
                keys.append(jnp.where(side == 0, a, b))
                values.append(jnp.where(side == 0, b, a))
                score = matmul_nt(query, keys[k]) * scale
                scores.append(jnp.where(r.key_ids[d, k] <= r.query_ids[d], score, masked_score))
            top = functools.reduce(jnp.maximum, [jnp.max(s, axis=-1, keepdims=True) for s in scores])
            raised = [jnp.exp(s - top) for s in scores]
            inverse = 1.0 / sum(jnp.sum(e, axis=-1, keepdims=True) for e in raised)
            probs = [e * inverse for e in raised]
            low = [p.astype(BF16) for p in probs]
            shares = [matmul_nt(attended_grad, values[k]) for k in range(planes)]
            delta = sum(
                jnp.sum(low[k].astype(F32) * shares[k], axis=-1, keepdims=True) for k in range(planes)
            )
            query_grad = jnp.zeros((pair, HD), F32)
            for k in range(planes):
                score_grad = (probs[k] * (shares[k] - delta)).astype(BF16)
                query_grad += matmul(score_grad, keys[k])
                key_grad = matmul_tn(score_grad, query) * scale
                value_grad = matmul_tn(low[k], attended_grad)
                heads[k, now, :] = jnp.where(side == 0, key_grad, value_grad).astype(BF16)
                heads[planes + k, now, :] = jnp.where(side == 0, value_grad, key_grad).astype(BF16)
            query_grad = query_grad * scale
            query_grad = query_grad * r.tables[0] + turn_back(query_grad * r.tables[1])
            heads[query_grad_slot, now, :] = query_grad.astype(BF16)
            return 0

        lax.fori_loop(0, half, attend_back, 0)
        advance(TICKS[5])
        lax.fori_loop(half, n, attend_back, 0)

        def kv_hand_over(k):
            return remote(
                heads.at[planes + k], r.kv_other.at[k], r.kv_send.at[k], r.kv_recv.at[k], other_core
            )

        def kv_load(source, slot):
            return local(source, r.kv_some.at[slot], r.kv_sem.at[slot])

        def kv_add(k, slot):
            def some(c, _):
                at = span(c * 64, 64)
                heads[k, at, :] = (
                    heads[k, at, :].astype(F32) + r.kv_some[slot, at, :].astype(F32)
                ).astype(BF16)
                return 0

            lax.fori_loop(0, plane_rows // 64, some, 0)

        def kv_down(k):
            return remote(heads.at[k], r.kv_down.at[k], r.down_send.at[k], r.down_recv.at[k], below)

        def kv_up(k):
            return remote(
                heads.at[planes - k], r.kv_up.at[k], r.up_send.at[k], r.up_recv.at[k], above
            )

        order = list(range(planes - 1, -1, -1))
        for k in order:
            kv_hand_over(k).start()
        for at, k in enumerate(order):
            kv_hand_over(k).wait_recv()
            kv_load(r.kv_other.at[k], at % 2).start()
            kv_load(r.kv_other.at[k], at % 2).wait()
            kv_add(k, at % 2)

        def kv_send(k):
            @pl.when(z >= k)
            def _():
                kv_down(k).start()

            @pl.when(z + k < planes)
            def _():
                kv_up(k).start()

        def kv_receive(k, down_to, up_to):
            @pl.when((z + 1 >= k) & (z + 1 < planes))
            def _():
                kv_down(k).wait_recv()
                if down_to is not None:
                    copy = kv_load(r.kv_down.at[k], 0)
                    copy.start()
                    copy.wait()
                    kv_add(down_to, 0)

            @pl.when((z >= 1) & (z - 1 + k < planes))
            def _():
                kv_up(k).wait_recv()
                if up_to is not None:
                    copy = kv_load(r.kv_up.at[k], 1)
                    copy.start()
                    copy.wait()
                    kv_add(up_to, 1)

        kv_send(3)
        rows_sent(OUT, plane_rows)
        load(work.at[pl.ds(plane_rows, rows)], r.out_own)
        loaded()
        load(r.normed, work.at[pl.ds(plane_rows, plane_rows)])
        low_half, high_half = pl.ds(0, plane_rows), pl.ds(plane_rows, plane_rows)
        advance(TICKS[6])
        turned[0] = heads[attended_slot].astype(F32).T.astype(BF16)
        turned[1] = heads[query_grad_slot].astype(F32).T.astype(BF16)
        loaded()
        outer(query_at, turned[1], high_half)
        outer(output_at, turned[0], low_half)
        advance(TICKS[7])
        kv_receive(3, 2, 2)
        kv_send(2)
        staged(query_at)
        staged(output_at)
        advance(TICKS[8])
        kv_receive(2, 1, 3)
        kv_send(1)
        advance(TICKS[9])
        kv_receive(1, 0, 0)

        def project_back(d, _):
            now = span(d * pair, pair)
            grad = heads[0, now, :].astype(F32)
            grad = grad * r.tables[2] + turn_back(grad * r.tables[3])
            heads[kv_grad_slot, now, :] = grad.astype(BF16)
            left = jnp.concatenate([heads[query_grad_slot, now, :], grad.astype(BF16)], axis=1)
            first = span((side * n + d) * rows, rows)
            second = span(((1 - side) * n + d) * rows, rows)
            for j in range(n):
                total = matmul_nt(left, feed[0, j, :wide, :]).astype(BF16)
                work[first, blocks[j]] = total[:rows]
                work[second, blocks[j]] = total[rows:]
            return 0

        lax.fori_loop(0, n, project_back, 0)
        rows_hand_over(ONE, 0)
        turned[2] = heads[kv_grad_slot].astype(F32).T.astype(BF16)
        outer(kv_at, turned[2], high_half)
        rows_send(ONE, 0)
        staged(kv_at)
        advance(TICKS[10])

        for d in range(1, n):
            branch_far(d).wait_send()
        for d in range(n):
            branch_near(d).wait_send()
        load(r.tokens, r.own_rows)
        rows_arrive(ONE, 0)
        loaded()

        def first_use(at, back):
            r.wide_rows[at, :] = r.wide_rows[at, :] + back

        norm_rows_back(0, r.own_rows, r.gains[0:1, :], first_use)
        load(r.wide_rows, r.tokens_grad)
        gain_terms(0)

        def gain_copy(at, source, target, peer):
            return remote(source, target, r.gain_send.at[at], r.gain_recv.at[at], peer)

        def gain_far(d):
            return gain_copy(d, r.gain_mine.at[d], r.gain_far.at[d], (here, chips[d]))

        def gain_hop(s, peer):
            return gain_copy(n + s, r.gain_sum.at[s], r.gain_in.at[s], peer)

        for d in range(1, n):
            gain_far(d).start()
        advance(TICKS[11])
        for d in range(1, n):
            gain_far(d).wait()
        r.gain_sum[0] = r.gain_mine[0] + r.gain_far[1] + r.gain_far[2] + r.gain_far[3]
        gain_hop(0, other_core).start()
        gain_hop(0, other_core).wait()
        r.gain_sum[1] = r.gain_sum[0] + r.gain_in[0]

        @pl.when(is_end)
        def _():
            gain_hop(1, partner).start()
            gain_hop(1, partner).wait_send()

        advance(TICKS[12])

        @pl.when(is_middle)
        def _():
            gain_hop(1, partner).wait_recv()
            r.gain_sum[2] = r.gain_sum[1] + r.gain_in[1]
            gain_hop(2, other_middle).start()
            gain_hop(2, other_middle).wait()
            r.gain_sum[3] = r.gain_sum[2] + r.gain_in[2]
            gain_hop(3, partner).start()
            gain_hop(3, partner).wait_send()

        @pl.when(is_end)
        def _():
            gain_hop(3, partner).wait_recv()
            r.gain_sum[3] = r.gain_in[3]

        load(r.gain_sum.at[3], r.gain_out)
        advance(units + 9 - steps_done[0])

        loaded()
        rows_arrive(OUT, plane_rows)
        rows_sent(ONE, 0)
        for q in range(1, QUARTERS):
            for d in range(1, n):
                feed_copy(q, d).wait_send()
        for k in range(planes):
            kv_hand_over(k).wait_send()
        for k in range(1, planes):

            @pl.when(z >= k)
            def _():
                kv_down(k).wait_send()

            @pl.when(z + k < planes)
            def _():
                kv_up(k).wait_send()

        finish()

    arrays = jax.tree.leaves((in_hbm, in_vmem))
    results = pl.pallas_call(
        backward,
        out_shape=jax.tree.leaves(out_hbm),
        in_specs=[pl.BlockSpec(memory_space=pl.ANY)] * len(jax.tree.leaves(in_hbm))
        + [pl.BlockSpec(memory_space=pltpu.VMEM)] * len(in_vmem),
        out_specs=[pl.BlockSpec(memory_space=pl.ANY)] * len(out_hbm),
        scratch_shapes=list(scratch.values()),
        cost_estimate=cost(30 * plane_rows * width * part, arrays, [unit_array] * 6),
        compiler_params=pltpu.CompilerParams(
            collective_id=0, has_side_effects=True, vmem_limit_bytes=63 * 1024 * 1024
        ),
        name="backward",
    )(*arrays)
    results = types.SimpleNamespace(**jax.tree.unflatten(jax.tree.structure(out_hbm), results))
    owned_tiles, near_tiles = (
        a.reshape(tiles_count, n, quarter, wide) for a in (results.owned, results.near)
    )

    def place_hidden(me_ref, own_ref, near_ref, gate_out, up_out, down_out):
        for source, e in ((own_ref, 0), (near_ref, 1)):

            @pl.when(pl.program_id(0) // n == e)
            def _():
                down_out[...] = source[0, 0].astype(F32)
                gate_out[...] = source[1, 0].T.astype(F32)
                up_out[...] = source[2, 0].T.astype(F32)

    def hidden_slot(i, q, me):
        return (2 * (me[0] ^ (i % n)) + (me[1] ^ (i // n))) * QUARTERS + q

    def own_hidden(i, q, me):
        return (jnp.where(i < n, q, QUARTERS - 1), jnp.minimum(i, n - 1), 0, 0)

    def near_hidden(i, q, me):
        return (jnp.where(i < n, 0, q), jnp.maximum(i - n, 0), 0, 0)

    by_columns = pl.BlockSpec((wide, quarter), lambda i, q, me: (0, hidden_slot(i, q, me)))
    by_rows = pl.BlockSpec((quarter, wide), lambda i, q, me: (hidden_slot(i, q, me), 0))
    held = run_grid(
        place_hidden,
        me,
        (2 * n, QUARTERS),
        [owned_tiles, near_tiles],
        [
            pl.BlockSpec((3, 1, quarter, wide), own_hidden),
            pl.BlockSpec((3, 1, quarter, wide), near_hidden),
        ],
        [
            shape(gate_weight.shape, F32),
            shape(up_weight.shape, F32),
            shape(down_weight.shape, F32),
        ],
        [by_columns, by_columns, by_rows],
        name="place_hidden",
    )

    def place_query(me_ref, own_ref, near_ref, query_out, output_out):
        for source, e in ((own_ref, 0), (near_ref, 1)):

            @pl.when(pl.program_id(0) // n == e)
            def _():
                query_out[...] = source[0, 0].T.astype(F32)
                output_out[...] = source[1, 0].astype(F32)

    def head_slot(i, me):
        return 2 * (me[0] ^ (i % n)) + (me[1] ^ (i // n))

    own_spec = lambda i, me: (query_at // 2, jnp.where(i < n, i, n - 1), 0, 0)
    near_spec = lambda i, me: (query_at // 2, jnp.where(i < n, 0, i - n), 0, 0)
    query_weight_grad, output_weight_grad = run_grid(
        place_query,
        me,
        (2 * n,),
        [owned_tiles, near_tiles],
        [pl.BlockSpec((2, 1, HD, wide), own_spec), pl.BlockSpec((2, 1, HD, wide), near_spec)],
        [shape(query_weight.shape, F32), shape(output_weight.shape, F32)],
        [
            pl.BlockSpec((wide, HD), lambda i, me: (0, head_slot(i, me))),
            pl.BlockSpec((HD, wide), lambda i, me: (head_slot(i, me), 0)),
        ],
        name="place_query",
    )

    def place_kv(me_ref, own_ref, near_ref, key_out, value_out):
        keys_here = me_ref[1] == 0
        own, near = own_ref[0, 0].T.astype(F32), near_ref[0, 0].T.astype(F32)
        key_out[...] = jnp.where(keys_here, own, near)
        value_out[...] = jnp.where(keys_here, near, own)

    by_chip = pl.BlockSpec((wide, HD), lambda i, me: (0, me[0] ^ i))
    kv_spec = pl.BlockSpec((1, 1, HD, wide), lambda i, me: (kv_at, i, 0, 0))
    key_weight_grad, value_weight_grad = run_grid(
        place_kv,
        me,
        (n,),
        [owned_tiles, near_tiles],
        [kv_spec, kv_spec],
        [shape(key_weight.shape, F32), shape(value_weight.shape, F32)],
        [by_chip, by_chip],
        name="place_kv",
    )

    output = middle + results.out_own.astype(F32) + results.row_near[OUT, 0].astype(F32)
    output = output + sum(results.row_far[OUT, d].astype(F32) for d in range(1, n))

    return (
        output.astype(BF16)[None],
        results.tokens_grad[None],
        query_weight_grad,
        key_weight_grad,
        value_weight_grad,
        output_weight_grad,
        results.gain_out[0],
        held[0],
        held[1],
        held[2],
        results.gain_out[1],
    )


def solution(mesh):
    chips, pieces = mesh.shape["fsdp"], mesh.shape["ctx"]
    one_head_each = 2 * chips == H and chips == KVH and pieces == 8
    return jax.shard_map(
        plane_layer if one_head_each else ring_layer,
        mesh=mesh,
        in_specs=(
            P("fsdp", "ctx", None),
            P("fsdp", None),
            P("fsdp", None),
            P("fsdp", None),
            P(None, "fsdp"),
            P("fsdp"),
            P("fsdp", None),
            P("fsdp", None),
            P(None, "fsdp"),
            P("fsdp"),
            P("fsdp", "ctx", None),
            P(),
            P(),
        ),
        out_specs=(
            P("fsdp", "ctx", None),
            P("fsdp", "ctx", None),
            P("fsdp", None),
            P("fsdp", None),
            P("fsdp", None),
            P(None, "fsdp"),
            P("fsdp"),
            P("fsdp", None),
            P("fsdp", None),
            P(None, "fsdp"),
            P("fsdp"),
        ),
        check_vma=False,
    )
```

```python
import functools
import types

import jax
import jax.numpy as jnp
from jax import lax
from jax.experimental import pallas as pl
from jax.experimental.pallas import tpu as pltpu
from jax.sharding import PartitionSpec as P

H = 8
KVH = 4
HD = 256


epsilon = 1e-06
theta = 1000042.0
masked_score = -1e30


def passed_along(value, axis, by):
    devices = lax.axis_size(axis)
    return lax.ppermute(value, axis, [(i, (i + by) % devices) for i in range(devices)])


def rope_tables(positions):
    half = HD // 2
    frequency = theta ** (-(jnp.arange(half, dtype=jnp.float32) * 2.0 / HD))
    angle = positions[:, None] * frequency[None, :]
    angle = jnp.concatenate([angle, angle], axis=-1)
    return (jnp.cos(angle), jnp.sin(angle))


def rotate(values, cosine, sine):
    half = values.shape[-1] // 2
    turned = jnp.concatenate([-values[..., half:], values[..., :half]], axis=-1)
    return values * cosine[:, None, :] + turned * sine[:, None, :]


def rotate_back(grads, cosine, sine):
    half = grads.shape[-1] // 2
    scaled = grads * sine[:, None, :]
    turned = jnp.concatenate([scaled[..., half:], -scaled[..., :half]], axis=-1)
    return grads * cosine[:, None, :] + turned


def split_heads(block):
    count = block.shape[0]
    key_cols = KVH * HD
    key_part = block[:, :key_cols].reshape(count, KVH, HD).transpose(1, 0, 2)
    value_part = block[:, key_cols:].reshape(count, KVH, HD).transpose(1, 0, 2)
    return (key_part, value_part)


def merge_heads(grouped):
    return grouped.transpose(1, 0, 2).reshape(grouped.shape[1], KVH * HD)


def weight_terms(lefts, rights):
    pieces = []
    for index in range(4):
        column = lefts[index]
        pieces.append(
            jnp.einsum("tc,tn->cn", column, rights[index], preferred_element_type=jnp.float32)
        )
    return jnp.concatenate(pieces, axis=1)


def ring_layer(
    tokens,
    query_weight,
    key_weight,
    value_weight,
    output_weight,
    first_gain,
    gate_weight,
    up_weight,
    down_weight,
    second_gain,
    cotangent,
    block_ids,
    piece_order,
):
    ctx_count = lax.axis_size("ctx")
    fsdp_count = lax.axis_size("fsdp")
    here = lax.axis_index("ctx")
    rows = tokens.shape[1]
    width = tokens.shape[2]
    group = H // KVH
    query_cols = H * HD
    key_cols = KVH * HD
    hidden_cols = gate_weight.shape[1]
    scale = HD ** (-0.5)
    whole_query, whole_key, whole_value, whole_output, gain_one = (
        lax.all_gather(query_weight, "fsdp", axis=0, tiled=True),
        lax.all_gather(key_weight, "fsdp", axis=0, tiled=True),
        lax.all_gather(value_weight, "fsdp", axis=0, tiled=True),
        lax.all_gather(output_weight, "fsdp", axis=1, tiled=True),
        lax.all_gather(first_gain, "fsdp", axis=0, tiled=True),
    )
    id_row = lax.dynamic_index_in_dim(block_ids, lax.axis_index("fsdp"), 0, keepdims=False)
    start_own = lax.dynamic_index_in_dim(piece_order, here, 0, keepdims=False) * rows
    offsets = jnp.arange(rows, dtype=jnp.int32)
    cosine, sine = rope_tables((start_own + offsets).astype(jnp.float32))
    own_ids = lax.dynamic_slice_in_dim(id_row, start_own, rows)
    query_ids = jnp.tile(own_ids, group)

    def visible(source):
        key_start = lax.dynamic_index_in_dim(piece_order, source, 0, keepdims=False) * rows
        key_ids = lax.dynamic_slice_in_dim(id_row, key_start, rows)
        return key_ids[None, :] <= query_ids[:, None]

    inputs = tokens[0].astype(jnp.float32)
    scale_one = lax.rsqrt(jnp.mean(inputs * inputs, axis=-1, keepdims=True) + epsilon)
    unit_one = inputs * scale_one
    normed = (unit_one * gain_one.astype(jnp.float32)).astype(jnp.bfloat16)
    query = jnp.dot(normed, whole_query, preferred_element_type=jnp.float32).reshape(rows, H, HD)
    query_rot = rotate(query, cosine, sine).astype(jnp.bfloat16)
    keys = jnp.dot(normed, whole_key, preferred_element_type=jnp.float32).reshape(rows, KVH, HD)
    keys_rot = rotate(keys, cosine, sine).astype(jnp.bfloat16).reshape(rows, key_cols)
    values = jnp.dot(normed, whole_value, preferred_element_type=jnp.float32).astype(jnp.bfloat16)
    key_value = jnp.concatenate([keys_rot, values], axis=-1)
    grouped = (
        query_rot.reshape(rows, KVH, group, HD).transpose(1, 2, 0, 3).reshape(KVH, group * rows, HD)
    )

    def forward_step(state, block, source):
        running, total, weighted = state
        key_part, value_part = split_heads(block)
        allowed = visible(source)
        scores = (
            jnp.einsum("hqd,hkd->hqk", grouped, key_part, preferred_element_type=jnp.float32)
            * scale
        )
        scores = jnp.where(allowed[None], scores, masked_score)
        newest = jnp.maximum(running, jnp.max(scores, axis=-1))
        factor = jnp.exp(running - newest)
        shares = jnp.where(allowed[None], jnp.exp(scores - newest[..., None]), 0.0)
        total = total * factor + jnp.sum(shares, axis=-1)
        weighted = weighted * factor[..., None] + jnp.einsum(
            "hqk,hkd->hqd",
            shares.astype(jnp.bfloat16),
            value_part,
            preferred_element_type=jnp.float32,
        )
        return (newest, total, weighted)

    start_state = (
        jnp.full((KVH, group * rows), masked_score, jnp.float32),
        jnp.zeros((KVH, group * rows), jnp.float32),
        jnp.zeros((KVH, group * rows, HD), jnp.float32),
    )
    state = forward_step(start_state, key_value, here)

    def forward_turn(turn, carry):
        block, inner = carry
        block = passed_along(block, "ctx", 1)
        source = (here - turn) % ctx_count
        return (block, forward_step(inner, block, source))

    passed_block, state = lax.fori_loop(1, ctx_count, forward_turn, (key_value, state))
    running, total, weighted = state
    attended = weighted / total[..., None]
    log_total = running + jnp.log(total)
    attended_low = (
        attended.reshape(KVH, group, rows, HD)
        .transpose(2, 0, 1, 3)
        .reshape(rows, query_cols)
        .astype(jnp.bfloat16)
    )
    middle = inputs + jnp.dot(attended_low, whole_output, preferred_element_type=jnp.float32)
    gain_two, whole_gate, whole_up, whole_down = (
        lax.all_gather(second_gain, "fsdp", axis=0, tiled=True),
        lax.all_gather(gate_weight, "fsdp", axis=0, tiled=True),
        lax.all_gather(up_weight, "fsdp", axis=0, tiled=True),
        lax.all_gather(down_weight, "fsdp", axis=1, tiled=True),
    )
    scale_two = lax.rsqrt(jnp.mean(middle * middle, axis=-1, keepdims=True) + epsilon)
    unit_two = middle * scale_two
    normed_two = (unit_two * gain_two.astype(jnp.float32)).astype(jnp.bfloat16)
    gate = jnp.dot(normed_two, whole_gate, preferred_element_type=jnp.float32)
    up = jnp.dot(normed_two, whole_up, preferred_element_type=jnp.float32)
    sigmoid_gate = jax.nn.sigmoid(gate)
    activated = gate * sigmoid_gate
    hidden = (activated * up).astype(jnp.bfloat16)
    result = middle + jnp.dot(hidden, whole_down, preferred_element_type=jnp.float32)
    output = result.astype(jnp.bfloat16)[None]
    upstream = cotangent[0]
    hidden_grad = jnp.einsum("tm,fm->tf", upstream, whole_down, preferred_element_type=jnp.float32)
    gate_grad = (hidden_grad * up * sigmoid_gate * (1.0 + gate * (1.0 - sigmoid_gate))).astype(
        jnp.bfloat16
    )
    up_grad = (hidden_grad * activated).astype(jnp.bfloat16)
    normed_two_grad = jnp.einsum(
        "tf,mf->tm", gate_grad, whole_gate, preferred_element_type=jnp.float32
    ) + jnp.einsum("tf,mf->tm", up_grad, whole_up, preferred_element_type=jnp.float32)
    gain_two_term = jnp.sum(normed_two_grad * unit_two, axis=0)
    unit_two_grad = normed_two_grad * gain_two.astype(jnp.float32)
    middle_grad = upstream.astype(jnp.float32) + scale_two * (
        unit_two_grad - unit_two * jnp.mean(unit_two_grad * unit_two, axis=-1, keepdims=True)
    )
    branch_grad = middle_grad.astype(jnp.bfloat16)
    attended_grad = jnp.einsum(
        "tm,cm->tc", branch_grad, whole_output, preferred_element_type=jnp.float32
    ).astype(jnp.bfloat16)
    grad_grouped = (
        attended_grad.reshape(rows, KVH, group, HD)
        .transpose(1, 2, 0, 3)
        .reshape(KVH, group * rows, HD)
    )
    delta = jnp.sum(grad_grouped.astype(jnp.float32) * attended, axis=-1)

    def backward_step(query_total, block, source):
        key_part, value_part = split_heads(block)
        allowed = visible(source)
        scores = (
            jnp.einsum("hqd,hkd->hqk", grouped, key_part, preferred_element_type=jnp.float32)
            * scale
        )
        scores = jnp.where(allowed[None], scores, masked_score)
        shares = jnp.where(allowed[None], jnp.exp(scores - log_total[..., None]), 0.0)
        value_grad = jnp.einsum(
            "hqk,hqd->hkd",
            shares.astype(jnp.bfloat16),
            grad_grouped,
            preferred_element_type=jnp.float32,
        )
        share_grad = jnp.einsum(
            "hqd,hkd->hqk", grad_grouped, value_part, preferred_element_type=jnp.float32
        )
        score_grad = (shares * (share_grad - delta[..., None])).astype(jnp.bfloat16)
        query_total = query_total + jnp.einsum(
            "hqk,hkd->hqd", score_grad, key_part, preferred_element_type=jnp.float32
        )
        key_grad = (
            jnp.einsum("hqk,hqd->hkd", score_grad, grouped, preferred_element_type=jnp.float32)
            * scale
        )
        return (
            query_total,
            jnp.concatenate([merge_heads(key_grad), merge_heads(value_grad)], axis=-1),
        )

    query_total, first_grad = backward_step(
        jnp.zeros((KVH, group * rows, HD), jnp.float32), key_value, here
    )
    held = first_grad

    def backward_turn(turn, carry):
        block, kept, total_query = carry
        block = passed_along(block, "ctx", 1)
        source = (here - turn) % ctx_count
        total_query, block_grad = backward_step(total_query, block, source)
        kept = passed_along(kept.astype(jnp.bfloat16), "ctx", 1).astype(kept.dtype) + block_grad
        return (block, kept, total_query)

    passed_again, held, query_total = lax.fori_loop(
        1, ctx_count, backward_turn, (key_value, held, query_total)
    )
    own_grad = passed_along(held.astype(jnp.bfloat16), "ctx", 1).astype(held.dtype)
    query_rot_grad = (
        (query_total * scale)
        .reshape(KVH, group, rows, HD)
        .transpose(2, 0, 1, 3)
        .reshape(rows, H, HD)
    )
    query_grad = (
        rotate_back(query_rot_grad, cosine, sine).reshape(rows, query_cols).astype(jnp.bfloat16)
    )
    key_grad = (
        rotate_back(own_grad[:, :key_cols].reshape(rows, KVH, HD), cosine, sine)
        .reshape(rows, key_cols)
        .astype(jnp.bfloat16)
    )
    value_grad = own_grad[:, key_cols:].astype(jnp.bfloat16)
    normed_grad = jnp.einsum(
        "tc,mc->tm", query_grad, whole_query, preferred_element_type=jnp.float32
    )
    normed_grad = normed_grad + jnp.einsum(
        "tc,mc->tm", key_grad, whole_key, preferred_element_type=jnp.float32
    )
    normed_grad = normed_grad + jnp.einsum(
        "tc,mc->tm", value_grad, whole_value, preferred_element_type=jnp.float32
    )
    gain_one_term = jnp.sum(normed_grad * unit_one, axis=0)
    unit_one_grad = normed_grad * gain_one.astype(jnp.float32)
    tokens_grad = middle_grad + scale_one * (
        unit_one_grad - unit_one * jnp.mean(unit_one_grad * unit_one, axis=-1, keepdims=True)
    )
    projected = jnp.concatenate([query_grad, key_grad, value_grad], axis=-1)
    gate_up = jnp.concatenate([gate_grad, up_grad], axis=-1)
    lefts = jnp.stack([normed, branch_grad, normed_two, upstream])
    rights = (projected, attended_low, gate_up, hidden)
    piece = lax.psum_scatter(
        weight_terms(lefts, rights).astype(jnp.bfloat16), "fsdp", scatter_dimension=0, tiled=True
    )
    shard = lax.psum(piece, "ctx").astype(jnp.float32)
    gain_one_sum, gain_two_sum = lax.psum((gain_one_term, gain_two_term), ("ctx", "fsdp"))
    own_rows = width // fsdp_count
    own_start = lax.axis_index("fsdp") * own_rows
    value_begin = query_cols + key_cols
    output_begin = value_begin + key_cols
    gate_begin = output_begin + query_cols
    up_begin = gate_begin + hidden_cols
    down_begin = up_begin + hidden_cols
    return (
        output,
        tokens_grad[None],
        shard[:, :query_cols],
        shard[:, query_cols:value_begin],
        shard[:, value_begin:output_begin],
        shard[:, output_begin:gate_begin].T,
        lax.dynamic_slice_in_dim(gain_one_sum, own_start, own_rows),
        shard[:, gate_begin:up_begin],
        shard[:, up_begin:down_begin],
        shard[:, down_begin : down_begin + hidden_cols].T,
        lax.dynamic_slice_in_dim(gain_two_sum, own_start, own_rows),
    )


VMEM_BYTES = 58 * 1024 * 1024
BF16 = jnp.bfloat16
F32 = jnp.float32
QUARTERS = 4
MESH = pl.DeviceIdType.MESH
TICKS = (1, 1, 1, 2, 4, 2, 1, 2, 1, 3, 2, 1, 1)
LINES = 2


def matmul(a, b):
    return lax.dot_general(a, b, (((1,), (0,)), ((), ())), preferred_element_type=F32)


def matmul_nt(a, b):
    return lax.dot_general(a, b, (((1,), (1,)), ((), ())), preferred_element_type=F32)


def matmul_tn(a, b):
    return lax.dot_general(a, b, (((0,), (0,)), ((), ())), preferred_element_type=F32)


def cost(flops, arrays, outs, exps=0):
    moved = sum(a.size * a.dtype.itemsize for a in arrays) + sum(
        o.size * o.dtype.itemsize for o in outs
    )
    return pl.CostEstimate(flops=int(flops), bytes_accessed=int(moved), transcendentals=int(exps))


def run_whole(body, me, arrays, outs, scratch=(), flops=0, in_hbm=0, name=None):
    count = len(arrays) - in_hbm
    return pl.pallas_call(
        body,
        out_shape=outs,
        in_specs=[pl.BlockSpec(memory_space=pltpu.SMEM)]
        + [pl.BlockSpec(memory_space=pltpu.VMEM)] * count
        + [pl.BlockSpec(memory_space=pl.ANY)] * in_hbm,
        out_specs=jax.tree.map(lambda _: pl.BlockSpec(memory_space=pltpu.VMEM), outs),
        scratch_shapes=list(scratch),
        cost_estimate=cost(flops, arrays, jax.tree.leaves(outs)),
        compiler_params=pltpu.CompilerParams(vmem_limit_bytes=VMEM_BYTES),
        name=name,
    )(me, *arrays)


def run_grid(body, me, grid, arrays, in_specs, outs, out_specs, scratch=(), flops=0, aliases=None, name=None):
    return pl.pallas_call(
        body,
        out_shape=outs,
        grid_spec=pltpu.PrefetchScalarGridSpec(
            num_scalar_prefetch=1,
            grid=grid,
            in_specs=in_specs,
            out_specs=out_specs,
            scratch_shapes=list(scratch),
        ),
        cost_estimate=cost(flops, arrays, jax.tree.leaves(outs)),
        input_output_aliases=aliases or {},
        compiler_params=pltpu.CompilerParams(vmem_limit_bytes=VMEM_BYTES),
        name=name,
    )(me, *arrays)


def shape(dims, kind=BF16):
    return jax.ShapeDtypeStruct(tuple(dims), kind)


def fixed(block):
    return pl.BlockSpec(block, lambda i, me: (0,) * len(block), pipeline_mode=pl.Buffered(1))


def column(index, wide):
    return pl.ds(pl.multiple_of(index * wide, wide), wide)


def turn(values):
    half = values.shape[-1] // 2
    return jnp.concatenate([-values[:, half:], values[:, :half]], axis=-1)


def turn_back(values):
    half = values.shape[-1] // 2
    return jnp.concatenate([values[:, half:], -values[:, :half]], axis=-1)


def plane_layer(
    tokens,
    query_weight,
    key_weight,
    value_weight,
    output_weight,
    first_gain,
    gate_weight,
    up_weight,
    down_weight,
    second_gain,
    cotangent,
    block_ids,
    piece_order,
):
    ctx_count = lax.axis_size("ctx")
    n = lax.axis_size("fsdp")
    planes = ctx_count // 2
    ctx = lax.axis_index("ctx")
    z, core = ctx // 2, ctx % 2
    f = lax.axis_index("fsdp")
    me = jnp.stack([f, core]).astype(jnp.int32)
    rows, width = tokens.shape[1:]
    pair = 2 * rows
    plane_rows = n * pair
    wide = width // n
    hidden_cols = gate_weight.shape[1]
    part = hidden_cols // (2 * n)
    quarter = part // QUARTERS
    scale = HD ** (-0.5)

    def across(value, d):
        return lax.ppermute(value, "fsdp", [(i, i ^ d) for i in range(n)])

    def sibling(value):
        return lax.ppermute(value, "ctx", [(i, i ^ 1) for i in range(ctx_count)])

    def along(value, step):
        pairs = [(i, i + 2 * step) for i in range(ctx_count)]
        return lax.ppermute(value, "ctx", [(a, b) for a, b in pairs if 0 <= b < ctx_count])

    def between_planes(value, moves):
        return lax.ppermute(
            value, "ctx", [(2 * a + side, 2 * b + side) for a, b in moves for side in range(2)]
        )

    def gathered(value):
        own = [value] + [across(value, d) for d in range(1, n)]
        return own, [sibling(block) for block in own]

    def reduced(own, other):
        near = [sibling(block) for block in other]
        sent = [
            across((own[d].astype(F32) + near[d].astype(F32)).astype(BF16), d) for d in range(1, n)
        ]
        return [own[0], near[0]] + sent

    middle_left, middle_right = planes // 2 - 1, planes // 2
    folds = [
        [(s, s + 1), (planes - 1 - s, planes - 2 - s)] for s in range(middle_left)
    ]

    def summed_over_planes(value):
        for moves in folds:
            value = (
                value.astype(F32) + between_planes(value, moves).astype(F32)
            ).astype(value.dtype)
        crossed = between_planes(value, [(middle_left, middle_right), (middle_right, middle_left)])
        value = (value.astype(F32) + crossed.astype(F32)).astype(value.dtype)
        for s, moves in reversed(list(enumerate(folds))):
            back = between_planes(value, [(b, a) for a, b in moves])
            receives = (z == s) | (z == planes - 1 - s)
            value = jnp.where(receives, back, value)
        return value

    place = jnp.arange(rows, dtype=jnp.int32)
    own_pieces = lax.dynamic_slice_in_dim(piece_order, 2 * z, 2)
    positions = (own_pieces[:, None] * rows + place[None, :]).reshape(pair).astype(F32)
    cosine, sine = rope_tables(positions)
    is_value = core == 1
    kv_cosine = jnp.where(is_value, 1.0, cosine)
    kv_sine = jnp.where(is_value, 0.0, sine)
    chips = f ^ jnp.arange(n, dtype=jnp.int32)
    ring = (z - jnp.arange(planes, dtype=jnp.int32)) % planes
    ring_ctx = (2 * ring[:, None] + jnp.arange(2, dtype=jnp.int32)[None, :]).reshape(-1)
    id_pieces = block_ids.reshape(n, ctx_count, rows)
    ids = id_pieces[chips[:, None], piece_order[ring_ctx][None, :]]
    key_ids = ids.reshape(n, planes, 1, pair)
    query_ids = ids[:, :2].reshape(n, pair, 1)

    def cut_attention(me_ref, *refs):
        wq, wk, wv, wo = (refs[i * n : (i + 1) * n] for i in range(4))
        one, two = refs[4 * n : 4 * n + 2]
        outs = refs[4 * n + 2 :]
        keys_here = me_ref[1] == 0
        for d in range(n):
            first = outs[d]
            first[:wide, :HD] = wq[d][...]

            @pl.when(keys_here)
            def _():
                first[:wide, HD:] = wk[d][...]

            @pl.when(jnp.logical_not(keys_here))
            def _():
                first[:wide, HD:] = wv[d][...]

            pick = lax.broadcasted_iota(jnp.int32, (16, wide), 0) < 8
            first[wide:, :] = jnp.where(pick, one[...].astype(F32), two[...].astype(F32)).astype(
                BF16
            )
            outs[n + d][...] = wo[d][...]

    def head_of(d):
        return lambda i, me: (0, 2 * (me[0] ^ d) + me[1])

    def chip_of(d):
        return lambda i, me: (0, me[0] ^ d)

    def head_rows_of(d):
        return lambda i, me: (2 * (me[0] ^ d) + me[1], 0)

    gain_spec = pl.BlockSpec((1, wide), lambda i, me: (0, 0))
    cut = run_grid(
        cut_attention,
        me,
        (1,),
        [query_weight] * n
        + [key_weight] * n
        + [value_weight] * n
        + [output_weight] * n
        + [first_gain.reshape(1, wide), second_gain.reshape(1, wide)],
        [pl.BlockSpec((wide, HD), head_of(d)) for d in range(n)]
        + [pl.BlockSpec((wide, HD), chip_of(d)) for d in range(n)] * 2
        + [pl.BlockSpec((HD, wide), head_rows_of(d)) for d in range(n)]
        + [gain_spec, gain_spec],
        [shape((wide + 16, 2 * HD))] * n + [shape((HD, wide))] * n,
        [pl.BlockSpec((wide + 16, 2 * HD), lambda i, me: (0, 0))] * n
        + [pl.BlockSpec((HD, wide), lambda i, me: (0, 0))] * n,
        name="cut_attention",
    )
    own_tokens = tokens[0]
    token_own, token_near = gathered(own_tokens)

    def cut_hidden(me_ref, *refs):
        gates, ups, downs = (refs[i * n : (i + 1) * n] for i in range(3))
        for d in range(n):
            refs[-1][0, d, :wide, :quarter] = gates[d][...]
            refs[-1][0, d, :wide, quarter:] = ups[d][...]
            refs[-1][0, d, wide:, :] = downs[d][...]

    def columns_of(d):
        return lambda q, me: (0, (2 * (me[0] ^ d) + me[1]) * QUARTERS + q)

    def down_rows_of(d):
        return lambda q, me: ((2 * (me[0] ^ d) + me[1]) * QUARTERS + q, 0)

    piece = (wide + quarter, 2 * quarter)
    hidden_cut = run_grid(
        cut_hidden,
        me,
        (QUARTERS,),
        [gate_weight] * n + [up_weight] * n + [down_weight] * n,
        [pl.BlockSpec((wide, quarter), columns_of(d)) for d in range(n)] * 2
        + [pl.BlockSpec((quarter, wide), down_rows_of(d)) for d in range(n)],
        shape((QUARTERS, n) + piece),
        pl.BlockSpec((1, n) + piece, lambda q, me: (q, 0, 0, 0)),
        name="cut_hidden",
    )
    cut, hidden_cut = lax.optimization_barrier((cut, hidden_cut))
    weights_in = [cut[0]] + [across(cut[d], d) for d in range(1, n)]
    own_cotangent = cotangent[0]
    block = (rows, width)

    tile = plane_rows // 3
    tiles_count = 3 * QUARTERS + 3
    query_at, output_at, kv_at = tiles_count - 3, tiles_count - 2, tiles_count - 1
    units = 2 * tiles_count
    unit = (2, quarter, wide)
    held_sums, held_ends = 4, 3
    MID, BACK, OUT, ONE = range(4)
    query_slot, attended_slot, query_grad_slot, kv_grad_slot = range(2 * planes, 2 * planes + 4)
    kept_slots = 2 * planes + 2
    columns = (plane_rows, HD)
    lanes = (8, wide)
    dma = pltpu.SemaphoreType.DMA

    in_hbm = dict(
        near_tokens=token_own + token_near,
        in_weight=weights_in,
        out_cut=cut[n:],
        cut=hidden_cut,
        cotangent=own_cotangent,
        tokens=own_tokens,
    )
    in_vmem = dict(
        tables=jnp.stack([cosine, sine, kv_cosine, kv_sine]),
        query_ids=query_ids,
        key_ids=key_ids,
    )
    unit_array = shape((units,) + unit)
    out_hbm = dict(
        tiles=unit_array,
        from_end=unit_array,
        from_middle=unit_array,
        finals=unit_array,
        owned=unit_array,
        near=unit_array,
        row_near=shape((4, n) + block),
        row_far=shape((4, n) + block),
        cot_all=shape((2, n) + block),
        kept=shape((kept_slots,) + columns),
        out_weight=shape((2, 2, HD, wide)),
        normed=shape((plane_rows, width)),
        middle=shape(block, F32),
        branch_all=shape((n, 2) + block),
        kv_other=shape((planes,) + columns),
        kv_down=shape((planes,) + columns),
        kv_up=shape((planes,) + columns),
        out_own=shape(block),
        tokens_grad=shape(block, F32),
        gain_out=shape(lanes, F32),
    )
    scratch = dict(
        work=pltpu.VMEM((2 * plane_rows, width), BF16),
        feed=pltpu.VMEM((QUARTERS, n) + piece, BF16),
        heads=pltpu.VMEM((3 * QUARTERS, plane_rows, HD), BF16),
        turned=pltpu.VMEM((3, HD, plane_rows), BF16),
        stage=pltpu.VMEM((2, n, quarter, wide), BF16),
        mine=pltpu.VMEM((2,) + unit, BF16),
        theirs=pltpu.VMEM((2,) + unit, BF16),
        crossed=pltpu.VMEM((2,) + unit, BF16),
        sums=pltpu.VMEM((held_sums,) + unit, BF16),
        ends=pltpu.VMEM((held_ends,) + unit, BF16),
        some_rows=pltpu.VMEM((n,) + block, BF16),
        wide_rows=pltpu.VMEM(block, F32),
        own_rows=pltpu.VMEM(block, BF16),
        kv_some=pltpu.VMEM((2,) + columns, BF16),
        flat=pltpu.VMEM((8, width), F32),
        gain_mine=pltpu.VMEM((n,) + lanes, F32),
        gain_far=pltpu.VMEM((n,) + lanes, F32),
        gain_sum=pltpu.VMEM((4,) + lanes, F32),
        gain_in=pltpu.VMEM((4,) + lanes, F32),
        load_sem=dma((4 * n + n,)),
        gains=pltpu.VMEM((8, width), F32),
        gain_rows=pltpu.VMEM((n, 16, wide), BF16),
        feed_local=dma((QUARTERS,)),
        feed_send=dma((QUARTERS * n,)),
        feed_recv=dma((QUARTERS * n,)),
        stage_sem=dma((2, 2)),
        one_send=dma((units,)),
        one_recv=dma((units,)),
        two_send=dma((units,)),
        two_recv=dma((units,)),
        three_send=dma((units,)),
        three_recv=dma((units,)),
        mine_sem=dma((2,)),
        theirs_sem=dma((2,)),
        crossed_sem=dma((2,)),
        final_sem=dma((held_ends,)),
        deal_local=dma((units,)),
        deal_send=dma((2 * units,)),
        deal_recv=dma((2 * units,)),
        sib_send=dma((units,)),
        sib_recv=dma((units,)),
        row_sem=dma((n,)),
        row_near_send=dma((4 * n,)),
        row_near_recv=dma((4 * n,)),
        row_far_send=dma((4 * n,)),
        row_far_recv=dma((4 * n,)),
        out_send=dma((n,)),
        out_recv=dma((n,)),
        cot_send=dma((n,)),
        cot_recv=dma((n,)),
        cot_near_send=dma((n,)),
        cot_near_recv=dma((n,)),
        two_local=dma((1,)),
        two_far_send=dma((n,)),
        two_far_recv=dma((n,)),
        two_near_send=dma((n,)),
        two_near_recv=dma((n,)),
        climb_send=dma((planes,)),
        climb_recv=dma((planes,)),
        fall_send=dma((planes,)),
        fall_recv=dma((planes,)),
        pass_send=dma((planes,)),
        pass_recv=dma((planes,)),
        keep_sem=dma((3,)),
        branch_local=dma((1,)),
        branch_send=dma((n,)),
        branch_recv=dma((n,)),
        branch_near_send=dma((n,)),
        branch_near_recv=dma((n,)),
        kv_sem=dma((2,)),
        kv_send=dma((planes,)),
        kv_recv=dma((planes,)),
        down_send=dma((planes,)),
        down_recv=dma((planes,)),
        up_send=dma((planes,)),
        up_recv=dma((planes,)),
        gain_send=dma((n + 4,)),
        gain_recv=dma((n + 4,)),
    )

    def backward(*refs):
        r, first = types.SimpleNamespace(), 0
        for group in (in_hbm, in_vmem, out_hbm):
            leaves, form = jax.tree.flatten(group)
            vars(r).update(jax.tree.unflatten(form, refs[first : first + len(leaves)]))
            first += len(leaves)
        vars(r).update(zip(scratch, refs[first:]))
        here = lax.axis_index("ctx")
        chip = lax.axis_index("fsdp")
        z, side = here // 2, here % 2
        is_middle = (z == 1) | (z == 2)
        is_end = jnp.logical_not(is_middle)
        chips = [chip, chip + 1 - 2 * (chip % 2), (chip + 2) % 4, 3 - chip]
        partner = (2 * (z + 1 - 2 * (z % 2)) + side, chip)
        other_middle = (2 * (3 - z) + side, chip)
        other_core = (here + 1 - 2 * side, chip)
        below, above = (here - 2, chip), (here + 2, chip)
        blocks = [pl.ds(pl.multiple_of(c * wide, wide), wide) for c in chips]
        work, feed, heads, turned, stage = r.work, r.feed, r.heads, r.turned, r.stage

        barrier = pltpu.get_barrier_semaphore()
        for peer in [(here, c) for c in chips[1:]] + [partner, other_core]:
            pl.semaphore_signal(barrier, inc=1, device_id=peer, device_id_type=MESH)

        @pl.when(is_middle)
        def _():
            pl.semaphore_signal(barrier, inc=1, device_id=other_middle, device_id_type=MESH)
            pl.semaphore_wait(barrier, n + 2)

        @pl.when(is_end)
        def _():
            pl.semaphore_wait(barrier, n + 1)

        def remote(source, target, send, recv, peer):
            return pltpu.make_async_remote_copy(
                src_ref=source,
                dst_ref=target,
                send_sem=send,
                recv_sem=recv,
                device_id=peer,
                device_id_type=MESH,
            )

        local = pltpu.make_async_copy

        def span(first, count):
            return pl.ds(pl.multiple_of(first, count), count)

        def feed_copy(q, d):
            at = q * n + d
            return remote(
                r.cut.at[q, d], feed.at[q, d], r.feed_send.at[at], r.feed_recv.at[at], (here, chips[d])
            )

        def feed_own(q):
            return local(r.cut.at[q, 0], feed.at[q, 0], r.feed_local.at[q])

        def hop_one(i):
            return remote(r.tiles.at[i], r.from_end.at[i], r.one_send.at[i], r.one_recv.at[i], partner)

        def hop_two(i):
            return remote(
                r.sums.at[i % held_sums],
                r.from_middle.at[i],
                r.two_send.at[i],
                r.two_recv.at[i],
                other_middle,
            )

        def hop_three(i):
            return remote(
                r.ends.at[i % held_ends], r.finals.at[i], r.three_send.at[i], r.three_recv.at[i], partner
            )

        def load_mine(i):
            return local(r.tiles.at[i], r.mine.at[i % 2], r.mine_sem.at[i % 2])

        def load_theirs(i):
            return local(r.from_end.at[i], r.theirs.at[i % 2], r.theirs_sem.at[i % 2])

        def load_crossed(i):
            return local(r.from_middle.at[i], r.crossed.at[i % 2], r.crossed_sem.at[i % 2])

        def keep_final(i):
            return local(r.ends.at[i % held_ends], r.finals.at[i], r.final_sem.at[i % held_ends])

        def keep_own(i):
            return local(r.finals.at[i, 0], r.owned.at[i, 0], r.deal_local.at[i])

        def deal_to(i, b, d):
            at = 2 * i + b
            return remote(
                r.finals.at[i, b],
                r.owned.at[i, b],
                r.deal_send.at[at],
                r.deal_recv.at[at],
                (here, chips[d]),
            )

        def to_sibling(i):
            return remote(r.owned.at[i], r.near.at[i], r.sib_send.at[i], r.sib_recv.at[i], other_core)

        def add(target, a, b):
            def some(s, _):
                at = (s // 4, span((s % 4) * (quarter // 4), quarter // 4))
                target[at] = (a[at].astype(F32) + b[at].astype(F32)).astype(BF16)
                return 0

            lax.fori_loop(0, 8, some, 0)

        def when_in(i, *conditions):
            return pl.when(functools.reduce(jnp.logical_and, conditions, (i >= 0) & (i < units)))

        def step(i, _=0):
            @when_in(i - 1, is_middle)
            def _():
                at = i - 1
                load_mine(at).wait()
                load_theirs(at).wait()

                @pl.when(at >= held_sums)
                def _():
                    hop_two(at - held_sums).wait_send()

                add(r.sums.at[at % held_sums], r.mine.at[at % 2], r.theirs.at[at % 2])
                hop_two(at).start()

            @when_in(i - 4, is_middle)
            def _():
                at = i - 4
                load_crossed(at).wait()

                @pl.when(at >= held_ends)
                def _():
                    hop_three(at - held_ends).wait_send()

                add(r.ends.at[at % held_ends], r.sums.at[at % held_sums], r.crossed.at[at % 2])
                hop_three(at).start()
                keep_final(at).start()

            @when_in(i, is_middle)
            def _():
                hop_one(i).wait_recv()
                load_mine(i).start()
                load_theirs(i).start()

            @when_in(i - 3, is_middle)
            def _():
                hop_two(i - 3).wait_recv()
                load_crossed(i - 3).start()

            @when_in(i - 6)
            def _():
                at = i - 6

                @pl.when(is_middle)
                def _():
                    keep_final(at).wait()

                @pl.when(is_end)
                def _():
                    hop_three(at).wait_recv()

                @pl.when(at % 2 == 0)
                def _():
                    keep_own(at).start()
                    deal_to(at, 1, 1).start()

                @pl.when(at % 2 == 1)
                def _():
                    deal_to(at, 0, 2).start()
                    deal_to(at, 1, 3).start()

            @when_in(i - 9)
            def _():
                at = i - 9

                @pl.when(at % 2 == 0)
                def _():
                    keep_own(at).wait()

                @pl.when(at % 2 == 1)
                def _():
                    deal_to(at, 0, 2).wait_recv()

                deal_to(at, 1, 3).wait_recv()
                to_sibling(at).start()

            return 0

        steps_done = [0]

        def advance(count):
            first = steps_done[0]
            steps_done[0] = first + count
            lax.fori_loop(first, first + count, step, 0)

        def finish():
            def one(i, _):
                @pl.when(is_end)
                def _():
                    hop_one(i).wait_send()

                @pl.when(is_middle & (i >= units - held_sums))
                def _():
                    hop_two(i).wait_send()

                @pl.when(is_middle & (i >= units - held_ends))
                def _():
                    hop_three(i).wait_send()

                @pl.when(i % 2 == 1)
                def _():
                    deal_to(i, 0, 2).wait_send()

                deal_to(i, 1, 3).wait_send()
                to_sibling(i).wait()
                return 0

            lax.fori_loop(0, units, one, 0)

        def stage_copy(t, h):
            return local(r.stage.at[t % 2, pl.ds(2 * h, 2)], r.tiles.at[2 * t + h], r.stage_sem.at[t % 2, h])

        def staged(t):
            for h in range(2):
                stage_copy(t, h).wait()

            @pl.when(is_end)
            def _():
                for h in range(2):
                    hop_one(2 * t + h).start()

        def outer(t, left, right_rows):
            for j in range(n):
                stage[t % 2, j] = matmul(left, work[right_rows, blocks[j]]).astype(BF16)
            for h in range(2):
                stage_copy(t, h).start()

        def row_near(s, base, d):
            at = s * n + d
            return remote(
                work.at[pl.ds(base + (n + d) * rows, rows)],
                r.row_near.at[s, d],
                r.row_near_send.at[at],
                r.row_near_recv.at[at],
                other_core,
            )

        def row_far(s, base, d):
            at = s * n + d
            return remote(
                work.at[pl.ds(base + d * rows, rows)],
                r.row_far.at[s, d],
                r.row_far_send.at[at],
                r.row_far_recv.at[at],
                (here, chips[d]),
            )

        def near_load(s, d):
            return local(r.row_near.at[s, d], r.some_rows.at[d], r.row_sem.at[d])

        def far_load(s, d):
            return local(r.row_far.at[s, d], r.some_rows.at[d], r.row_sem.at[d])

        few = 16

        def rows_hand_over(s, base):
            for d in (3, 1, 2, 0):
                row_near(s, base, d).start()

        def rows_send(s, base):
            for d in (3, 1, 2):
                row_near(s, base, d).wait_recv()
                near_load(s, d).start()
            for d in (3, 1, 2):
                near_load(s, d).wait()

                def some(c, _, d=d):
                    at = span(c * few, few)
                    own = pl.ds(pl.multiple_of(base + d * rows + c * few, few), few)
                    work[own, :] = (
                        work[own, :].astype(F32) + r.some_rows[d, at, :].astype(F32)
                    ).astype(BF16)
                    return 0

                lax.fori_loop(0, rows // few, some, 0)
                row_far(s, base, d).start()

        def rows_arrive(s, base):
            row_near(s, base, 0).wait_recv()
            near_load(s, 0).start()
            for d in range(1, n):
                row_far(s, base, d).wait_recv()
                far_load(s, d).start()
            near_load(s, 0).wait()
            for d in range(1, n):
                far_load(s, d).wait()

        def rows_sent(s, base):
            for d in range(n):
                row_near(s, base, d).wait_send()
            for d in range(1, n):
                row_far(s, base, d).wait_send()

        def norm_rows_back(base, value_ref, gain_row, use):
            r.flat[...] = jnp.zeros_like(r.flat)

            def some(c, _):
                at = span(c * few, few)
                grad = work[pl.ds(pl.multiple_of(base + c * few, few), few), :].astype(F32)
                for d in range(n):
                    grad += r.some_rows[d, at, :].astype(F32)
                values = value_ref[at, :].astype(F32)
                inverse = lax.rsqrt(jnp.mean(values * values, axis=-1, keepdims=True) + epsilon)
                unit_rows = values * inverse
                scaled = grad * gain_row
                back = inverse * (
                    scaled - unit_rows * jnp.mean(scaled * unit_rows, axis=-1, keepdims=True)
                )
                use(at, back)
                terms = grad * unit_rows
                r.flat[...] += terms[:8] + terms[8:]
                return 0

            lax.fori_loop(0, rows // few, some, 0)

        def gain_terms(at):
            total = jnp.sum(r.flat[...], axis=0, keepdims=True)
            r.flat[0:1, :] = total
            for j in range(n):
                r.gain_mine[j, at : at + 1, :] = r.flat[0:1, blocks[j]]

        r.gain_mine[...] = jnp.zeros_like(r.gain_mine)
        loads = []

        def load(source, target):
            copy = local(source, target, r.load_sem.at[len(loads)])
            copy.start()
            loads.append(copy)

        def loaded():
            while loads:
                loads.pop().wait()

        def out_far(d):
            return remote(
                r.out_cut[d],
                r.theirs.at[d // 2, d % 2],
                r.out_send.at[d],
                r.out_recv.at[d],
                (here, chips[d]),
            )

        def cot_far(d):
            return remote(
                r.cotangent, r.cot_all.at[0, d], r.cot_send.at[d], r.cot_recv.at[d], (here, chips[d])
            )

        def cot_near(d):
            source = r.cotangent if d == 0 else r.cot_all.at[0, d]
            return remote(
                source, r.cot_all.at[1, d], r.cot_near_send.at[d], r.cot_near_recv.at[d], other_core
            )

        for d in range(1, n):
            out_far(d).start()
        for d in range(1, n):
            feed_copy(0, d).start()
        for d in range(1, n):
            cot_far(d).start()
        cot_near(0).start()
        for i in range(2 * n):
            load(r.near_tokens[i], work.at[pl.ds(plane_rows + i * rows, rows)])
        for j in range(n):
            for h in range(2):
                load(r.in_weight[j].at[pl.ds(h * HD, HD)], r.sums.at[j, h])
            load(r.in_weight[j].at[pl.ds(wide, 16)], r.gain_rows.at[j])
        loaded()
        load(r.out_cut[0], r.theirs.at[0, 0])
        for q in range(QUARTERS):
            feed_own(q).start()
        for j in range(n):
            both = r.gain_rows[j].astype(F32)
            r.gains[0:1, blocks[j]] = both[0:1]
            r.gains[1:2, blocks[j]] = both[8:9]

        def project(d, _):
            for c in range(2):
                first = ((side + c) % 2 * n + d) * rows

                def some(s, _, c=c, first=first):
                    now = pl.ds(pl.multiple_of(plane_rows + first + s * few, few), few)
                    then = pl.ds(pl.multiple_of((2 * d + c) * rows + s * few, few), few)
                    values = work[now, :].astype(F32)
                    inverse = lax.rsqrt(jnp.mean(values * values, axis=-1, keepdims=True) + epsilon)
                    work[then, :] = (values * inverse * r.gains[0:1, :]).astype(BF16)
                    return 0

                lax.fori_loop(0, rows // few, some, 0)
            now = span(d * pair, pair)
            both = jnp.zeros((pair, 2 * HD), F32)
            for j in range(n):
                for h in range(2):
                    here_half = pl.ds(pl.multiple_of(chips[j] * wide + h * HD, HD), HD)
                    both += matmul(work[now, here_half], r.sums[j, h])
            query, kv = both[:, :HD], both[:, HD:]
            query = query * r.tables[0] + turn(query) * r.tables[1]
            heads[query_slot, now, :] = query.astype(BF16)
            kv = kv * r.tables[2] + turn(kv) * r.tables[3]
            heads[0, now, :] = kv.astype(BF16)
            return 0

        lax.fori_loop(0, n, project, 0)
        keep_normed = local(work.at[pl.ds(0, plane_rows)], r.normed, r.keep_sem.at[0])
        keep_normed.start()

        def climb(s):
            return remote(heads.at[s - 1], heads.at[s], r.climb_send.at[s], r.climb_recv.at[s], above)

        def fall(s):
            return remote(
                heads.at[(planes - s + 1) % planes],
                heads.at[planes - s],
                r.fall_send.at[s],
                r.fall_recv.at[s],
                below,
            )

        def pass_on(k):
            return remote(
                heads.at[k], heads.at[planes + k], r.pass_send.at[k], r.pass_recv.at[k], other_core
            )

        def kv_leave(s):
            @pl.when((z - s + 1 >= 0) & (z + 1 < planes))
            def _():
                climb(s).start()

            @pl.when((z + s - 1 < planes) & (z >= 1))
            def _():
                fall(s).start()

        def kv_come(s):
            @pl.when(z - s >= 0)
            def _():
                climb(s).wait_recv()

            @pl.when(z + s < planes)
            def _():
                fall(s).wait_recv()

        kv_leave(1)
        pass_on(0).start()
        for d in range(1, n):
            out_far(d).wait_recv()
        loaded()
        keep_out = local(r.theirs, r.out_weight, r.keep_sem.at[1])
        keep_out.start()
        kv_come(1)
        kv_leave(2)

        @pl.when(z >= 1)
        def _():
            pass_on(1).start()

        @pl.when(z + 1 < planes)
        def _():
            pass_on(3).start()

        kv_come(2)
        kv_leave(3)
        pass_on(2).start()
        for d in range(1, n):
            cot_far(d).wait_recv()
            cot_near(d).start()
        keep_normed.wait()
        kv_come(3)

        @pl.when(z == 0)
        def _():
            pass_on(1).start()

        @pl.when(z == planes - 1)
        def _():
            pass_on(3).start()

        for k in range(planes):
            pass_on(k).wait_recv()

        def scored(d, now):
            keys, values, scores = [], [], []
            for k in range(planes):
                a, b = heads[k, now, :], heads[planes + k, now, :]
                keys.append(jnp.where(side == 0, a, b))
                values.append(jnp.where(side == 0, b, a))
                score = matmul_nt(heads[query_slot, now, :], keys[k]) * scale
                scores.append(jnp.where(r.key_ids[d, k] <= r.query_ids[d], score, masked_score))
            top = functools.reduce(jnp.maximum, [jnp.max(s, axis=-1, keepdims=True) for s in scores])
            raised = [jnp.exp(s - top) for s in scores]
            inverse = 1.0 / sum(jnp.sum(e, axis=-1, keepdims=True) for e in raised)
            return keys, values, [e * inverse for e in raised]

        def put_rows(base, d, now_values, block_at):
            first = pl.ds(pl.multiple_of(base + (side * n + d) * rows, rows), rows)
            second = pl.ds(pl.multiple_of(base + ((1 - side) * n + d) * rows, rows), rows)
            work[first, block_at] = now_values[:rows]
            work[second, block_at] = now_values[rows:]

        def attend(d, _):
            now = span(d * pair, pair)
            _, values, probs = scored(d, now)
            total = jnp.zeros((pair, HD), F32)
            for k in range(planes):
                total += matmul(probs[k].astype(BF16), values[k])
            low_total = total.astype(BF16)
            heads[attended_slot, now, :] = low_total
            for j in range(n):
                put_rows(
                    plane_rows,
                    d,
                    matmul(low_total, r.theirs[j // 2, j % 2]).astype(BF16),
                    blocks[j],
                )
            return 0

        lax.fori_loop(0, n, attend, 0)
        rows_hand_over(MID, plane_rows)
        keep_heads = local(heads.at[pl.ds(0, kept_slots)], r.kept, r.keep_sem.at[2])
        keep_heads.start()
        load(r.tokens, r.own_rows)
        rows_send(MID, plane_rows)
        loaded()
        keep_out.wait()
        for s in range(1, planes):

            @pl.when((z - s + 1 >= 0) & (z + 1 < planes))
            def _():
                climb(s).wait_send()

            @pl.when((z + s - 1 < planes) & (z >= 1))
            def _():
                fall(s).wait_send()

        for k in range(planes):
            pass_on(k).wait_send()

        rows_arrive(MID, plane_rows)

        def second_norm(c, _):
            at = span(c * few, few)
            total = r.own_rows[at, :].astype(F32)
            total += work[pl.ds(pl.multiple_of(plane_rows + c * few, few), few), :].astype(F32)
            for d in range(n):
                total += r.some_rows[d, at, :].astype(F32)
            inverse = lax.rsqrt(jnp.mean(total * total, axis=-1, keepdims=True) + epsilon)
            r.wide_rows[at, :] = total
            r.own_rows[at, :] = (total * inverse * r.gains[1:2, :]).astype(BF16)
            return 0

        lax.fori_loop(0, rows // few, second_norm, 0)

        def two_far(d):
            return remote(
                r.own_rows,
                work.at[pl.ds(d * rows, rows)],
                r.two_far_send.at[d],
                r.two_far_recv.at[d],
                (here, chips[d]),
            )

        def two_near(d):
            source = r.own_rows if d == 0 else work.at[pl.ds(d * rows, rows)]
            return remote(
                source,
                work.at[pl.ds((n + d) * rows, rows)],
                r.two_near_send.at[d],
                r.two_near_recv.at[d],
                other_core,
            )

        for d in (3, 1, 2):
            two_far(d).start()
        two_near(0).start()
        two_own = local(r.own_rows, work.at[pl.ds(0, rows)], r.two_local.at[0])
        two_own.start()
        load(r.wide_rows, r.middle)
        rows_sent(MID, plane_rows)
        for d in range(n):
            cot_near(d).wait_recv()
            if d > 0:
                load(r.cot_all.at[0, d], work.at[pl.ds(plane_rows + d * rows, rows)])
            else:
                load(r.cotangent, work.at[pl.ds(plane_rows, rows)])
            load(r.cot_all.at[1, d], work.at[pl.ds(plane_rows + (n + d) * rows, rows)])
        keep_heads.wait()
        for d in (1, 2, 3):
            two_far(d).wait_recv()
            two_near(d).start()
        for d in range(1, n):
            feed_copy(0, d).wait_recv()
            feed_copy(1, d).start()
        two_own.wait()
        loaded()
        for d in range(n):
            two_near(d).wait_recv()

        def quarter_step(q, _):
            step(3 * q - 3)
            feed_own(q).wait()

            @pl.when(q > 0)
            def _():
                for d in range(1, n):
                    feed_copy(q, d).wait_recv()

            @pl.when((q > 0) & (q < QUARTERS - 1))
            def _():
                for d in range(1, n):
                    feed_copy(q + 1, d).start()

            def forward(t, _):
                now = span(t * tile, tile)
                cot_now = pl.ds(pl.multiple_of(plane_rows + t * tile, tile), tile)
                both = jnp.zeros((tile, 2 * quarter), F32)
                hidden_grad = jnp.zeros((tile, quarter), F32)
                for j in range(n):
                    both += matmul(work[now, blocks[j]], feed[q, j, :wide, :])
                    hidden_grad += matmul_nt(work[cot_now, blocks[j]], feed[q, j, wide:, :])
                gate, up = both[:, :quarter], both[:, quarter:]
                share = 1.0 / (1.0 + jnp.exp(-gate))
                activated = gate * share
                results = (
                    activated * up,
                    hidden_grad * up * share * (1.0 + gate * (1.0 - share)),
                    hidden_grad * activated,
                )
                for w, result in enumerate(results):
                    heads[q * 3 + w, now, :] = result.astype(BF16)
                    turned[w, :, now] = result.T.astype(BF16)
                return 0

            lax.fori_loop(0, plane_rows // tile, forward, 0)
            step(3 * q - 2)

            def one(w, _):
                t = 3 * q + w

                @pl.when(t >= 2)
                def _():
                    staged(t - 2)

                outer(t, turned[w], span(jnp.where(w == 0, plane_rows, 0), plane_rows))
                return 0

            lax.fori_loop(0, 3, one, 0)
            step(3 * q - 1)
            return 0

        lax.fori_loop(0, QUARTERS, quarter_step, 0)
        steps_done[0] = 3 * QUARTERS - 3
        for t in (query_at - 2, query_at - 1):
            staged(t)

        for d in range(1, n):
            two_near(d).wait_send()

        def back_step(s, _):
            now = span(s * pair, pair)
            lefts = [
                jnp.concatenate([heads[q * 3 + 1, now, :], heads[q * 3 + 2, now, :]], axis=1)
                for q in range(QUARTERS)
            ]
            for j in range(n):
                total = jnp.zeros((pair, wide), F32)
                for q in range(QUARTERS):
                    total += matmul_nt(lefts[q], feed[q, j, :wide, :])
                work[now, blocks[j]] = total.astype(BF16)
            return 0

        half = n // 2
        lax.fori_loop(half, n, back_step, 0)
        rows_hand_over(BACK, 0)
        advance(TICKS[0])
        lax.fori_loop(0, half, back_step, 0)
        rows_send(BACK, 0)
        advance(TICKS[1])

        def out_step(s, _):
            now = span(s * pair, pair)
            then = pl.ds(pl.multiple_of(plane_rows + s * pair, pair), pair)
            for j in range(n):
                total = jnp.zeros((pair, wide), F32)
                for q in range(QUARTERS):
                    total += matmul(heads[q * 3, now, :], feed[q, j, wide:, :])
                work[then, blocks[j]] = total.astype(BF16)
            return 0

        lax.fori_loop(half, n, out_step, 0)
        rows_hand_over(OUT, plane_rows)
        advance(TICKS[2])
        lax.fori_loop(0, half, out_step, 0)
        advance(TICKS[3])

        load(r.kept, heads.at[pl.ds(0, kept_slots)])
        for j in range(n):
            load(r.in_weight[j].at[pl.ds(0, wide)], feed.at[0, j, pl.ds(0, wide)])
            load(r.out_weight.at[j // 2, j % 2], feed.at[0, j, pl.ds(wide, HD)])

        rows_arrive(BACK, 0)
        loaded()
        for d in range(1, n):
            two_far(d).wait_send()
        two_near(0).wait_send()
        load(r.cotangent, r.own_rows)
        loaded()

        def second_use(at, back):
            grad = r.own_rows[at, :].astype(F32) + back
            r.wide_rows[at, :] = grad
            r.own_rows[at, :] = grad.astype(BF16)

        norm_rows_back(0, r.wide_rows, r.gains[1:2, :], second_use)

        def branch_far(d):
            return remote(
                r.own_rows,
                r.branch_all.at[d, side],
                r.branch_send.at[d],
                r.branch_recv.at[d],
                (here, chips[d]),
            )

        def branch_near(d):
            source = r.own_rows if d == 0 else r.branch_all.at[d, side]
            return remote(
                source,
                r.branch_all.at[d, side],
                r.branch_near_send.at[d],
                r.branch_near_recv.at[d],
                other_core,
            )

        for d in (3, 1, 2):
            branch_far(d).start()
        branch_near(0).start()
        branch_own = local(r.own_rows, r.branch_all.at[0, side], r.branch_local.at[0])
        branch_own.start()
        gain_terms(1)
        advance(TICKS[4])
        for d in (1, 2, 3):
            branch_far(d).wait_recv()
            branch_near(d).start()
        rows_sent(BACK, 0)
        branch_own.wait()
        for d in range(n):
            branch_near(d).wait_recv()
        for d in range(n):
            for c in range(2):
                load(r.branch_all.at[d, c], work.at[pl.ds((2 * d + c) * rows, rows)])
        rows_send(OUT, plane_rows)
        loaded()

        def attend_back(d, _):
            now = span(d * pair, pair)
            query = heads[query_slot, now, :]
            attended_grad = jnp.zeros((pair, HD), F32)
            for j in range(n):
                attended_grad += matmul_nt(work[now, blocks[j]], feed[0, j, wide:, :])
            attended_grad = attended_grad.astype(BF16)
            keys, values, probs = scored(d, now)
            low = [p.astype(BF16) for p in probs]
            shares = [matmul_nt(attended_grad, values[k]) for k in range(planes)]
            delta = sum(
                jnp.sum(low[k].astype(F32) * shares[k], axis=-1, keepdims=True) for k in range(planes)
            )
            query_grad = jnp.zeros((pair, HD), F32)
            for k in range(planes):
                score_grad = (probs[k] * (shares[k] - delta)).astype(BF16)
                query_grad += matmul(score_grad, keys[k])
                key_grad = matmul_tn(score_grad, query) * scale
                value_grad = matmul_tn(low[k], attended_grad)
                heads[k, now, :] = jnp.where(side == 0, key_grad, value_grad).astype(BF16)
                heads[planes + k, now, :] = jnp.where(side == 0, value_grad, key_grad).astype(BF16)
            query_grad = query_grad * scale
            query_grad = query_grad * r.tables[0] + turn_back(query_grad * r.tables[1])
            heads[query_grad_slot, now, :] = query_grad.astype(BF16)
            return 0

        lax.fori_loop(0, half, attend_back, 0)
        advance(TICKS[5])
        lax.fori_loop(half, n, attend_back, 0)

        def kv_hand_over(k):
            return remote(
                heads.at[planes + k], r.kv_other.at[k], r.kv_send.at[k], r.kv_recv.at[k], other_core
            )

        def kv_load(source, slot):
            return local(source, r.kv_some.at[slot], r.kv_sem.at[slot])

        def kv_add(k, slot):
            def some(c, _):
                at = span(c * 64, 64)
                heads[k, at, :] = (
                    heads[k, at, :].astype(F32) + r.kv_some[slot, at, :].astype(F32)
                ).astype(BF16)
                return 0

            lax.fori_loop(0, plane_rows // 64, some, 0)

        def kv_down(k):
            return remote(heads.at[k], r.kv_down.at[k], r.down_send.at[k], r.down_recv.at[k], below)

        def kv_up(k):
            return remote(
                heads.at[planes - k], r.kv_up.at[k], r.up_send.at[k], r.up_recv.at[k], above
            )

        order = list(range(planes - 1, -1, -1))
        for k in order:
            kv_hand_over(k).start()
        for at, k in enumerate(order):
            kv_hand_over(k).wait_recv()
            kv_load(r.kv_other.at[k], at % 2).start()
            kv_load(r.kv_other.at[k], at % 2).wait()
            kv_add(k, at % 2)

        def kv_send(k):
            @pl.when(z >= k)
            def _():
                kv_down(k).start()

            @pl.when(z + k < planes)
            def _():
                kv_up(k).start()

        def kv_receive(k, down_to, up_to):
            @pl.when((z + 1 >= k) & (z + 1 < planes))
            def _():
                kv_down(k).wait_recv()
                if down_to is not None:
                    copy = kv_load(r.kv_down.at[k], 0)
                    copy.start()
                    copy.wait()
                    kv_add(down_to, 0)

            @pl.when((z >= 1) & (z - 1 + k < planes))
            def _():
                kv_up(k).wait_recv()
                if up_to is not None:
                    copy = kv_load(r.kv_up.at[k], 1)
                    copy.start()
                    copy.wait()
                    kv_add(up_to, 1)

        kv_send(3)
        rows_sent(OUT, plane_rows)
        load(work.at[pl.ds(plane_rows, rows)], r.out_own)
        loaded()
        load(r.normed, work.at[pl.ds(plane_rows, plane_rows)])
        low_half, high_half = pl.ds(0, plane_rows), pl.ds(plane_rows, plane_rows)
        advance(TICKS[6])
        turned[0] = heads[attended_slot].astype(F32).T.astype(BF16)
        turned[1] = heads[query_grad_slot].astype(F32).T.astype(BF16)
        loaded()
        outer(query_at, turned[1], high_half)
        outer(output_at, turned[0], low_half)
        advance(TICKS[7])
        kv_receive(3, 2, 2)
        kv_send(2)
        staged(query_at)
        staged(output_at)
        advance(TICKS[8])
        kv_receive(2, 1, 3)
        kv_send(1)
        advance(TICKS[9])
        kv_receive(1, 0, 0)

        def project_back(d, _):
            now = span(d * pair, pair)
            grad = heads[0, now, :].astype(F32)
            grad = grad * r.tables[2] + turn_back(grad * r.tables[3])
            heads[kv_grad_slot, now, :] = grad.astype(BF16)
            left = jnp.concatenate([heads[query_grad_slot, now, :], grad.astype(BF16)], axis=1)
            for j in range(n):
                put_rows(0, d, matmul_nt(left, feed[0, j, :wide, :]).astype(BF16), blocks[j])
            return 0

        lax.fori_loop(0, n, project_back, 0)
        rows_hand_over(ONE, 0)
        turned[2] = heads[kv_grad_slot].astype(F32).T.astype(BF16)
        outer(kv_at, turned[2], high_half)
        rows_send(ONE, 0)
        staged(kv_at)
        advance(TICKS[10])

        for d in range(1, n):
            branch_far(d).wait_send()
        for d in range(n):
            branch_near(d).wait_send()
        load(r.tokens, r.own_rows)
        rows_arrive(ONE, 0)
        loaded()

        def first_use(at, back):
            r.wide_rows[at, :] = r.wide_rows[at, :] + back

        norm_rows_back(0, r.own_rows, r.gains[0:1, :], first_use)
        load(r.wide_rows, r.tokens_grad)
        gain_terms(0)

        def gain_copy(at, source, target, peer):
            return remote(source, target, r.gain_send.at[at], r.gain_recv.at[at], peer)

        def gain_far(d):
            return gain_copy(d, r.gain_mine.at[d], r.gain_far.at[d], (here, chips[d]))

        def gain_hop(s, peer):
            return gain_copy(n + s, r.gain_sum.at[s], r.gain_in.at[s], peer)

        for d in range(1, n):
            gain_far(d).start()
        advance(TICKS[11])
        for d in range(1, n):
            gain_far(d).wait()
        r.gain_sum[0] = r.gain_mine[0] + r.gain_far[1] + r.gain_far[2] + r.gain_far[3]
        gain_hop(0, other_core).start()
        gain_hop(0, other_core).wait()
        r.gain_sum[1] = r.gain_sum[0] + r.gain_in[0]

        @pl.when(is_end)
        def _():
            gain_hop(1, partner).start()
            gain_hop(1, partner).wait_send()

        advance(TICKS[12])

        @pl.when(is_middle)
        def _():
            gain_hop(1, partner).wait_recv()
            r.gain_sum[2] = r.gain_sum[1] + r.gain_in[1]
            gain_hop(2, other_middle).start()
            gain_hop(2, other_middle).wait()
            r.gain_sum[3] = r.gain_sum[2] + r.gain_in[2]
            gain_hop(3, partner).start()
            gain_hop(3, partner).wait_send()

        @pl.when(is_end)
        def _():
            gain_hop(3, partner).wait_recv()
            r.gain_sum[3] = r.gain_in[3]

        load(r.gain_sum.at[3], r.gain_out)
        advance(units + 9 - steps_done[0])

        loaded()
        rows_arrive(OUT, plane_rows)
        rows_sent(ONE, 0)
        for q in range(QUARTERS):
            for d in range(1, n):
                feed_copy(q, d).wait_send()
        for d in range(1, n):
            out_far(d).wait_send()
            cot_far(d).wait_send()
        for d in range(n):
            cot_near(d).wait_send()
        for k in range(planes):
            kv_hand_over(k).wait_send()
        for k in range(1, planes):

            @pl.when(z >= k)
            def _():
                kv_down(k).wait_send()

            @pl.when(z + k < planes)
            def _():
                kv_up(k).wait_send()

        finish()

    arrays = jax.tree.leaves((in_hbm, in_vmem))
    results = pl.pallas_call(
        backward,
        out_shape=jax.tree.leaves(out_hbm),
        in_specs=[pl.BlockSpec(memory_space=pl.ANY)] * len(jax.tree.leaves(in_hbm))
        + [pl.BlockSpec(memory_space=pltpu.VMEM)] * len(in_vmem),
        out_specs=[pl.BlockSpec(memory_space=pl.ANY)] * len(out_hbm),
        scratch_shapes=list(scratch.values()),
        cost_estimate=cost(30 * plane_rows * width * part, arrays, [unit_array] * 6),
        compiler_params=pltpu.CompilerParams(
            collective_id=0, has_side_effects=True, vmem_limit_bytes=63 * 1024 * 1024
        ),
        name="backward",
    )(*arrays)
    results = types.SimpleNamespace(**jax.tree.unflatten(jax.tree.structure(out_hbm), results))
    owned_tiles, near_tiles = (
        a.reshape(tiles_count, n, quarter, wide) for a in (results.owned, results.near)
    )

    def place_hidden(me_ref, own_ref, near_ref, gate_out, up_out, down_out):
        for source, e in ((own_ref, 0), (near_ref, 1)):

            @pl.when(pl.program_id(0) // n == e)
            def _():
                down_out[...] = source[0, 0].astype(F32)
                gate_out[...] = source[1, 0].T.astype(F32)
                up_out[...] = source[2, 0].T.astype(F32)

    def hidden_slot(i, q, me):
        return (2 * (me[0] ^ (i % n)) + (me[1] ^ (i // n))) * QUARTERS + q

    def own_hidden(i, q, me):
        return (jnp.where(i < n, q, QUARTERS - 1), jnp.minimum(i, n - 1), 0, 0)

    def near_hidden(i, q, me):
        return (jnp.where(i < n, 0, q), jnp.maximum(i - n, 0), 0, 0)

    by_columns = pl.BlockSpec((wide, quarter), lambda i, q, me: (0, hidden_slot(i, q, me)))
    by_rows = pl.BlockSpec((quarter, wide), lambda i, q, me: (hidden_slot(i, q, me), 0))
    held = run_grid(
        place_hidden,
        me,
        (2 * n, QUARTERS),
        [owned_tiles, near_tiles],
        [
            pl.BlockSpec((3, 1, quarter, wide), own_hidden),
            pl.BlockSpec((3, 1, quarter, wide), near_hidden),
        ],
        [
            shape(gate_weight.shape, F32),
            shape(up_weight.shape, F32),
            shape(down_weight.shape, F32),
        ],
        [by_columns, by_columns, by_rows],
        name="place_hidden",
    )

    def place_query(me_ref, own_ref, near_ref, query_out, output_out):
        for source, e in ((own_ref, 0), (near_ref, 1)):

            @pl.when(pl.program_id(0) // n == e)
            def _():
                query_out[...] = source[0, 0].T.astype(F32)
                output_out[...] = source[1, 0].astype(F32)

    def head_slot(i, me):
        return 2 * (me[0] ^ (i % n)) + (me[1] ^ (i // n))

    own_spec = lambda i, me: (query_at // 2, jnp.where(i < n, i, n - 1), 0, 0)
    near_spec = lambda i, me: (query_at // 2, jnp.where(i < n, 0, i - n), 0, 0)
    query_weight_grad, output_weight_grad = run_grid(
        place_query,
        me,
        (2 * n,),
        [owned_tiles, near_tiles],
        [pl.BlockSpec((2, 1, HD, wide), own_spec), pl.BlockSpec((2, 1, HD, wide), near_spec)],
        [shape(query_weight.shape, F32), shape(output_weight.shape, F32)],
        [
            pl.BlockSpec((wide, HD), lambda i, me: (0, head_slot(i, me))),
            pl.BlockSpec((HD, wide), lambda i, me: (head_slot(i, me), 0)),
        ],
        name="place_query",
    )

    def place_kv(me_ref, own_ref, near_ref, key_out, value_out):
        keys_here = me_ref[1] == 0
        own, near = own_ref[0, 0].T.astype(F32), near_ref[0, 0].T.astype(F32)
        key_out[...] = jnp.where(keys_here, own, near)
        value_out[...] = jnp.where(keys_here, near, own)

    by_chip = pl.BlockSpec((wide, HD), lambda i, me: (0, me[0] ^ i))
    kv_spec = pl.BlockSpec((1, 1, HD, wide), lambda i, me: (kv_at, i, 0, 0))
    key_weight_grad, value_weight_grad = run_grid(
        place_kv,
        me,
        (n,),
        [owned_tiles, near_tiles],
        [kv_spec, kv_spec],
        [shape(key_weight.shape, F32), shape(value_weight.shape, F32)],
        [by_chip, by_chip],
        name="place_kv",
    )

    output = results.middle + results.out_own.astype(F32) + results.row_near[OUT, 0].astype(F32)
    output = output + sum(results.row_far[OUT, d].astype(F32) for d in range(1, n))

    return (
        output.astype(BF16)[None],
        results.tokens_grad[None],
        query_weight_grad,
        key_weight_grad,
        value_weight_grad,
        output_weight_grad,
        results.gain_out[0],
        held[0],
        held[1],
        held[2],
        results.gain_out[1],
    )


def solution(mesh):
    chips, pieces = mesh.shape["fsdp"], mesh.shape["ctx"]
    one_head_each = 2 * chips == H and chips == KVH and pieces == 8
    return jax.shard_map(
        plane_layer if one_head_each else ring_layer,
        mesh=mesh,
        in_specs=(
            P("fsdp", "ctx", None),
            P("fsdp", None),
            P("fsdp", None),
            P("fsdp", None),
            P(None, "fsdp"),
            P("fsdp"),
            P("fsdp", None),
            P("fsdp", None),
            P(None, "fsdp"),
            P("fsdp"),
            P("fsdp", "ctx", None),
            P(),
            P(),
        ),
        out_specs=(
            P("fsdp", "ctx", None),
            P("fsdp", "ctx", None),
            P("fsdp", None),
            P("fsdp", None),
            P("fsdp", None),
            P(None, "fsdp"),
            P("fsdp"),
            P("fsdp", None),
            P("fsdp", None),
            P(None, "fsdp"),
            P("fsdp"),
        ),
        check_vma=False,
    )
```

```python
import functools
import types

import jax
import jax.numpy as jnp
from jax import lax
from jax.experimental import pallas as pl
from jax.experimental.pallas import tpu as pltpu
from jax.sharding import PartitionSpec as P

H = 8
KVH = 4
HD = 256


epsilon = 1e-06
theta = 1000042.0
masked_score = -1e30


def passed_along(value, axis, by):
    devices = lax.axis_size(axis)
    return lax.ppermute(value, axis, [(i, (i + by) % devices) for i in range(devices)])


def rope_tables(positions):
    half = HD // 2
    frequency = theta ** (-(jnp.arange(half, dtype=jnp.float32) * 2.0 / HD))
    angle = positions[:, None] * frequency[None, :]
    angle = jnp.concatenate([angle, angle], axis=-1)
    return (jnp.cos(angle), jnp.sin(angle))


def rotate(values, cosine, sine):
    half = values.shape[-1] // 2
    turned = jnp.concatenate([-values[..., half:], values[..., :half]], axis=-1)
    return values * cosine[:, None, :] + turned * sine[:, None, :]


def rotate_back(grads, cosine, sine):
    half = grads.shape[-1] // 2
    scaled = grads * sine[:, None, :]
    turned = jnp.concatenate([scaled[..., half:], -scaled[..., :half]], axis=-1)
    return grads * cosine[:, None, :] + turned


def split_heads(block):
    count = block.shape[0]
    key_cols = KVH * HD
    key_part = block[:, :key_cols].reshape(count, KVH, HD).transpose(1, 0, 2)
    value_part = block[:, key_cols:].reshape(count, KVH, HD).transpose(1, 0, 2)
    return (key_part, value_part)


def merge_heads(grouped):
    return grouped.transpose(1, 0, 2).reshape(grouped.shape[1], KVH * HD)


def weight_terms(lefts, rights):
    pieces = []
    for index in range(4):
        column = lefts[index]
        pieces.append(
            jnp.einsum("tc,tn->cn", column, rights[index], preferred_element_type=jnp.float32)
        )
    return jnp.concatenate(pieces, axis=1)


def ring_layer(
    tokens,
    query_weight,
    key_weight,
    value_weight,
    output_weight,
    first_gain,
    gate_weight,
    up_weight,
    down_weight,
    second_gain,
    cotangent,
    block_ids,
    piece_order,
):
    ctx_count = lax.axis_size("ctx")
    fsdp_count = lax.axis_size("fsdp")
    here = lax.axis_index("ctx")
    rows = tokens.shape[1]
    width = tokens.shape[2]
    group = H // KVH
    query_cols = H * HD
    key_cols = KVH * HD
    hidden_cols = gate_weight.shape[1]
    scale = HD ** (-0.5)
    whole_query, whole_key, whole_value, whole_output, gain_one = (
        lax.all_gather(query_weight, "fsdp", axis=0, tiled=True),
        lax.all_gather(key_weight, "fsdp", axis=0, tiled=True),
        lax.all_gather(value_weight, "fsdp", axis=0, tiled=True),
        lax.all_gather(output_weight, "fsdp", axis=1, tiled=True),
        lax.all_gather(first_gain, "fsdp", axis=0, tiled=True),
    )
    id_row = lax.dynamic_index_in_dim(block_ids, lax.axis_index("fsdp"), 0, keepdims=False)
    start_own = lax.dynamic_index_in_dim(piece_order, here, 0, keepdims=False) * rows
    offsets = jnp.arange(rows, dtype=jnp.int32)
    cosine, sine = rope_tables((start_own + offsets).astype(jnp.float32))
    own_ids = lax.dynamic_slice_in_dim(id_row, start_own, rows)
    query_ids = jnp.tile(own_ids, group)

    def visible(source):
        key_start = lax.dynamic_index_in_dim(piece_order, source, 0, keepdims=False) * rows
        key_ids = lax.dynamic_slice_in_dim(id_row, key_start, rows)
        return key_ids[None, :] <= query_ids[:, None]

    inputs = tokens[0].astype(jnp.float32)
    scale_one = lax.rsqrt(jnp.mean(inputs * inputs, axis=-1, keepdims=True) + epsilon)
    unit_one = inputs * scale_one
    normed = (unit_one * gain_one.astype(jnp.float32)).astype(jnp.bfloat16)
    query = jnp.dot(normed, whole_query, preferred_element_type=jnp.float32).reshape(rows, H, HD)
    query_rot = rotate(query, cosine, sine).astype(jnp.bfloat16)
    keys = jnp.dot(normed, whole_key, preferred_element_type=jnp.float32).reshape(rows, KVH, HD)
    keys_rot = rotate(keys, cosine, sine).astype(jnp.bfloat16).reshape(rows, key_cols)
    values = jnp.dot(normed, whole_value, preferred_element_type=jnp.float32).astype(jnp.bfloat16)
    key_value = jnp.concatenate([keys_rot, values], axis=-1)
    grouped = (
        query_rot.reshape(rows, KVH, group, HD).transpose(1, 2, 0, 3).reshape(KVH, group * rows, HD)
    )

    def forward_step(state, block, source):
        running, total, weighted = state
        key_part, value_part = split_heads(block)
        allowed = visible(source)
        scores = (
            jnp.einsum("hqd,hkd->hqk", grouped, key_part, preferred_element_type=jnp.float32)
            * scale
        )
        scores = jnp.where(allowed[None], scores, masked_score)
        newest = jnp.maximum(running, jnp.max(scores, axis=-1))
        factor = jnp.exp(running - newest)
        shares = jnp.where(allowed[None], jnp.exp(scores - newest[..., None]), 0.0)
        total = total * factor + jnp.sum(shares, axis=-1)
        weighted = weighted * factor[..., None] + jnp.einsum(
            "hqk,hkd->hqd",
            shares.astype(jnp.bfloat16),
            value_part,
            preferred_element_type=jnp.float32,
        )
        return (newest, total, weighted)

    start_state = (
        jnp.full((KVH, group * rows), masked_score, jnp.float32),
        jnp.zeros((KVH, group * rows), jnp.float32),
        jnp.zeros((KVH, group * rows, HD), jnp.float32),
    )
    state = forward_step(start_state, key_value, here)

    def forward_turn(turn, carry):
        block, inner = carry
        block = passed_along(block, "ctx", 1)
        source = (here - turn) % ctx_count
        return (block, forward_step(inner, block, source))

    passed_block, state = lax.fori_loop(1, ctx_count, forward_turn, (key_value, state))
    running, total, weighted = state
    attended = weighted / total[..., None]
    log_total = running + jnp.log(total)
    attended_low = (
        attended.reshape(KVH, group, rows, HD)
        .transpose(2, 0, 1, 3)
        .reshape(rows, query_cols)
        .astype(jnp.bfloat16)
    )
    middle = inputs + jnp.dot(attended_low, whole_output, preferred_element_type=jnp.float32)
    gain_two, whole_gate, whole_up, whole_down = (
        lax.all_gather(second_gain, "fsdp", axis=0, tiled=True),
        lax.all_gather(gate_weight, "fsdp", axis=0, tiled=True),
        lax.all_gather(up_weight, "fsdp", axis=0, tiled=True),
        lax.all_gather(down_weight, "fsdp", axis=1, tiled=True),
    )
    scale_two = lax.rsqrt(jnp.mean(middle * middle, axis=-1, keepdims=True) + epsilon)
    unit_two = middle * scale_two
    normed_two = (unit_two * gain_two.astype(jnp.float32)).astype(jnp.bfloat16)
    gate = jnp.dot(normed_two, whole_gate, preferred_element_type=jnp.float32)
    up = jnp.dot(normed_two, whole_up, preferred_element_type=jnp.float32)
    sigmoid_gate = jax.nn.sigmoid(gate)
    activated = gate * sigmoid_gate
    hidden = (activated * up).astype(jnp.bfloat16)
    result = middle + jnp.dot(hidden, whole_down, preferred_element_type=jnp.float32)
    output = result.astype(jnp.bfloat16)[None]
    upstream = cotangent[0]
    hidden_grad = jnp.einsum("tm,fm->tf", upstream, whole_down, preferred_element_type=jnp.float32)
    gate_grad = (hidden_grad * up * sigmoid_gate * (1.0 + gate * (1.0 - sigmoid_gate))).astype(
        jnp.bfloat16
    )
    up_grad = (hidden_grad * activated).astype(jnp.bfloat16)
    normed_two_grad = jnp.einsum(
        "tf,mf->tm", gate_grad, whole_gate, preferred_element_type=jnp.float32
    ) + jnp.einsum("tf,mf->tm", up_grad, whole_up, preferred_element_type=jnp.float32)
    gain_two_term = jnp.sum(normed_two_grad * unit_two, axis=0)
    unit_two_grad = normed_two_grad * gain_two.astype(jnp.float32)
    middle_grad = upstream.astype(jnp.float32) + scale_two * (
        unit_two_grad - unit_two * jnp.mean(unit_two_grad * unit_two, axis=-1, keepdims=True)
    )
    branch_grad = middle_grad.astype(jnp.bfloat16)
    attended_grad = jnp.einsum(
        "tm,cm->tc", branch_grad, whole_output, preferred_element_type=jnp.float32
    ).astype(jnp.bfloat16)
    grad_grouped = (
        attended_grad.reshape(rows, KVH, group, HD)
        .transpose(1, 2, 0, 3)
        .reshape(KVH, group * rows, HD)
    )
    delta = jnp.sum(grad_grouped.astype(jnp.float32) * attended, axis=-1)

    def backward_step(query_total, block, source):
        key_part, value_part = split_heads(block)
        allowed = visible(source)
        scores = (
            jnp.einsum("hqd,hkd->hqk", grouped, key_part, preferred_element_type=jnp.float32)
            * scale
        )
        scores = jnp.where(allowed[None], scores, masked_score)
        shares = jnp.where(allowed[None], jnp.exp(scores - log_total[..., None]), 0.0)
        value_grad = jnp.einsum(
            "hqk,hqd->hkd",
            shares.astype(jnp.bfloat16),
            grad_grouped,
            preferred_element_type=jnp.float32,
        )
        share_grad = jnp.einsum(
            "hqd,hkd->hqk", grad_grouped, value_part, preferred_element_type=jnp.float32
        )
        score_grad = (shares * (share_grad - delta[..., None])).astype(jnp.bfloat16)
        query_total = query_total + jnp.einsum(
            "hqk,hkd->hqd", score_grad, key_part, preferred_element_type=jnp.float32
        )
        key_grad = (
            jnp.einsum("hqk,hqd->hkd", score_grad, grouped, preferred_element_type=jnp.float32)
            * scale
        )
        return (
            query_total,
            jnp.concatenate([merge_heads(key_grad), merge_heads(value_grad)], axis=-1),
        )

    query_total, first_grad = backward_step(
        jnp.zeros((KVH, group * rows, HD), jnp.float32), key_value, here
    )
    held = first_grad

    def backward_turn(turn, carry):
        block, kept, total_query = carry
        block = passed_along(block, "ctx", 1)
        source = (here - turn) % ctx_count
        total_query, block_grad = backward_step(total_query, block, source)
        kept = passed_along(kept.astype(jnp.bfloat16), "ctx", 1).astype(kept.dtype) + block_grad
        return (block, kept, total_query)

    passed_again, held, query_total = lax.fori_loop(
        1, ctx_count, backward_turn, (key_value, held, query_total)
    )
    own_grad = passed_along(held.astype(jnp.bfloat16), "ctx", 1).astype(held.dtype)
    query_rot_grad = (
        (query_total * scale)
        .reshape(KVH, group, rows, HD)
        .transpose(2, 0, 1, 3)
        .reshape(rows, H, HD)
    )
    query_grad = (
        rotate_back(query_rot_grad, cosine, sine).reshape(rows, query_cols).astype(jnp.bfloat16)
    )
    key_grad = (
        rotate_back(own_grad[:, :key_cols].reshape(rows, KVH, HD), cosine, sine)
        .reshape(rows, key_cols)
        .astype(jnp.bfloat16)
    )
    value_grad = own_grad[:, key_cols:].astype(jnp.bfloat16)
    normed_grad = jnp.einsum(
        "tc,mc->tm", query_grad, whole_query, preferred_element_type=jnp.float32
    )
    normed_grad = normed_grad + jnp.einsum(
        "tc,mc->tm", key_grad, whole_key, preferred_element_type=jnp.float32
    )
    normed_grad = normed_grad + jnp.einsum(
        "tc,mc->tm", value_grad, whole_value, preferred_element_type=jnp.float32
    )
    gain_one_term = jnp.sum(normed_grad * unit_one, axis=0)
    unit_one_grad = normed_grad * gain_one.astype(jnp.float32)
    tokens_grad = middle_grad + scale_one * (
        unit_one_grad - unit_one * jnp.mean(unit_one_grad * unit_one, axis=-1, keepdims=True)
    )
    projected = jnp.concatenate([query_grad, key_grad, value_grad], axis=-1)
    gate_up = jnp.concatenate([gate_grad, up_grad], axis=-1)
    lefts = jnp.stack([normed, branch_grad, normed_two, upstream])
    rights = (projected, attended_low, gate_up, hidden)
    piece = lax.psum_scatter(
        weight_terms(lefts, rights).astype(jnp.bfloat16), "fsdp", scatter_dimension=0, tiled=True
    )
    shard = lax.psum(piece, "ctx").astype(jnp.float32)
    gain_one_sum, gain_two_sum = lax.psum((gain_one_term, gain_two_term), ("ctx", "fsdp"))
    own_rows = width // fsdp_count
    own_start = lax.axis_index("fsdp") * own_rows
    value_begin = query_cols + key_cols
    output_begin = value_begin + key_cols
    gate_begin = output_begin + query_cols
    up_begin = gate_begin + hidden_cols
    down_begin = up_begin + hidden_cols
    return (
        output,
        tokens_grad[None],
        shard[:, :query_cols],
        shard[:, query_cols:value_begin],
        shard[:, value_begin:output_begin],
        shard[:, output_begin:gate_begin].T,
        lax.dynamic_slice_in_dim(gain_one_sum, own_start, own_rows),
        shard[:, gate_begin:up_begin],
        shard[:, up_begin:down_begin],
        shard[:, down_begin : down_begin + hidden_cols].T,
        lax.dynamic_slice_in_dim(gain_two_sum, own_start, own_rows),
    )


VMEM_BYTES = 58 * 1024 * 1024
BF16 = jnp.bfloat16
F32 = jnp.float32
QUARTERS = 4
MESH = pl.DeviceIdType.MESH
TICKS = (2, 1, 2, 2, 3, 2, 1, 1, 1, 4, 4, 2, 2)
LINES = 2


def matmul(a, b):
    return lax.dot_general(a, b, (((1,), (0,)), ((), ())), preferred_element_type=F32)


def matmul_nt(a, b):
    return lax.dot_general(a, b, (((1,), (1,)), ((), ())), preferred_element_type=F32)


def matmul_tn(a, b):
    return lax.dot_general(a, b, (((0,), (0,)), ((), ())), preferred_element_type=F32)


def cost(flops, arrays, outs, exps=0):
    moved = sum(a.size * a.dtype.itemsize for a in arrays) + sum(
        o.size * o.dtype.itemsize for o in outs
    )
    return pl.CostEstimate(flops=int(flops), bytes_accessed=int(moved), transcendentals=int(exps))


def run_whole(body, me, arrays, outs, scratch=(), flops=0, in_hbm=0, name=None):
    count = len(arrays) - in_hbm
    return pl.pallas_call(
        body,
        out_shape=outs,
        in_specs=[pl.BlockSpec(memory_space=pltpu.SMEM)]
        + [pl.BlockSpec(memory_space=pltpu.VMEM)] * count
        + [pl.BlockSpec(memory_space=pl.ANY)] * in_hbm,
        out_specs=jax.tree.map(lambda _: pl.BlockSpec(memory_space=pltpu.VMEM), outs),
        scratch_shapes=list(scratch),
        cost_estimate=cost(flops, arrays, jax.tree.leaves(outs)),
        compiler_params=pltpu.CompilerParams(vmem_limit_bytes=VMEM_BYTES),
        name=name,
    )(me, *arrays)


def run_grid(body, me, grid, arrays, in_specs, outs, out_specs, scratch=(), flops=0, aliases=None, name=None):
    return pl.pallas_call(
        body,
        out_shape=outs,
        grid_spec=pltpu.PrefetchScalarGridSpec(
            num_scalar_prefetch=1,
            grid=grid,
            in_specs=in_specs,
            out_specs=out_specs,
            scratch_shapes=list(scratch),
        ),
        cost_estimate=cost(flops, arrays, jax.tree.leaves(outs)),
        input_output_aliases=aliases or {},
        compiler_params=pltpu.CompilerParams(vmem_limit_bytes=VMEM_BYTES),
        name=name,
    )(me, *arrays)


def shape(dims, kind=BF16):
    return jax.ShapeDtypeStruct(tuple(dims), kind)


def fixed(block):
    return pl.BlockSpec(block, lambda i, me: (0,) * len(block), pipeline_mode=pl.Buffered(1))


def column(index, wide):
    return pl.ds(pl.multiple_of(index * wide, wide), wide)


def turn(values):
    half = values.shape[-1] // 2
    return jnp.concatenate([-values[:, half:], values[:, :half]], axis=-1)


def turn_back(values):
    half = values.shape[-1] // 2
    return jnp.concatenate([values[:, half:], -values[:, :half]], axis=-1)


def plane_layer(
    tokens,
    query_weight,
    key_weight,
    value_weight,
    output_weight,
    first_gain,
    gate_weight,
    up_weight,
    down_weight,
    second_gain,
    cotangent,
    block_ids,
    piece_order,
):
    ctx_count = lax.axis_size("ctx")
    n = lax.axis_size("fsdp")
    planes = ctx_count // 2
    ctx = lax.axis_index("ctx")
    z, core = ctx // 2, ctx % 2
    f = lax.axis_index("fsdp")
    me = jnp.stack([f, core]).astype(jnp.int32)
    rows, width = tokens.shape[1:]
    pair = 2 * rows
    plane_rows = n * pair
    wide = width // n
    hidden_cols = gate_weight.shape[1]
    part = hidden_cols // (2 * n)
    quarter = part // QUARTERS
    scale = HD ** (-0.5)

    def across(value, d):
        return lax.ppermute(value, "fsdp", [(i, i ^ d) for i in range(n)])

    def sibling(value):
        return lax.ppermute(value, "ctx", [(i, i ^ 1) for i in range(ctx_count)])

    def along(value, step):
        pairs = [(i, i + 2 * step) for i in range(ctx_count)]
        return lax.ppermute(value, "ctx", [(a, b) for a, b in pairs if 0 <= b < ctx_count])

    def between_planes(value, moves):
        return lax.ppermute(
            value, "ctx", [(2 * a + side, 2 * b + side) for a, b in moves for side in range(2)]
        )

    def gathered(value):
        own = [value] + [across(value, d) for d in range(1, n)]
        return own, [sibling(block) for block in own]

    def reduced(own, other):
        near = [sibling(block) for block in other]
        sent = [
            across((own[d].astype(F32) + near[d].astype(F32)).astype(BF16), d) for d in range(1, n)
        ]
        return [own[0], near[0]] + sent

    middle_left, middle_right = planes // 2 - 1, planes // 2
    folds = [
        [(s, s + 1), (planes - 1 - s, planes - 2 - s)] for s in range(middle_left)
    ]

    def summed_over_planes(value):
        for moves in folds:
            value = (
                value.astype(F32) + between_planes(value, moves).astype(F32)
            ).astype(value.dtype)
        crossed = between_planes(value, [(middle_left, middle_right), (middle_right, middle_left)])
        value = (value.astype(F32) + crossed.astype(F32)).astype(value.dtype)
        for s, moves in reversed(list(enumerate(folds))):
            back = between_planes(value, [(b, a) for a, b in moves])
            receives = (z == s) | (z == planes - 1 - s)
            value = jnp.where(receives, back, value)
        return value

    place = jnp.arange(rows, dtype=jnp.int32)
    own_pieces = lax.dynamic_slice_in_dim(piece_order, 2 * z, 2)
    positions = (own_pieces[:, None] * rows + place[None, :]).reshape(pair).astype(F32)
    cosine, sine = rope_tables(positions)
    is_value = core == 1
    kv_cosine = jnp.where(is_value, 1.0, cosine)
    kv_sine = jnp.where(is_value, 0.0, sine)
    chips = f ^ jnp.arange(n, dtype=jnp.int32)
    ring = (z - jnp.arange(planes, dtype=jnp.int32)) % planes
    ring_ctx = (2 * ring[:, None] + jnp.arange(2, dtype=jnp.int32)[None, :]).reshape(-1)
    id_pieces = block_ids.reshape(n, ctx_count, rows)
    ids = id_pieces[chips[:, None], piece_order[ring_ctx][None, :]]
    key_ids = ids.reshape(n, planes, 1, pair)
    query_ids = ids[:, :2].reshape(n, pair, 1)

    def cut_attention(me_ref, *refs):
        wq, wk, wv, wo = (refs[i * n : (i + 1) * n] for i in range(4))
        one, two = refs[4 * n : 4 * n + 2]
        outs = refs[4 * n + 2 :]
        keys_here = me_ref[1] == 0
        for d in range(n):
            first = outs[d]
            outs[n + d][...] = wq[d][...]

            @pl.when(keys_here)
            def _():
                first[:wide, :] = wk[d][...]

            @pl.when(jnp.logical_not(keys_here))
            def _():
                first[:wide, :] = wv[d][...]

            pick = lax.broadcasted_iota(jnp.int32, (16, HD), 0) < 8
            for g, gain in enumerate((one, two)):
                halves = [gain[:, h * HD : (h + 1) * HD].astype(F32) for h in range(2)]
                first[wide + 16 * g : wide + 16 * (g + 1), :] = jnp.where(pick, *halves).astype(BF16)
            outs[2 * n + d][...] = wo[d][...]

    def head_of(d):
        return lambda i, me: (0, 2 * (me[0] ^ d) + me[1])

    def chip_of(d):
        return lambda i, me: (0, me[0] ^ d)

    def head_rows_of(d):
        return lambda i, me: (2 * (me[0] ^ d) + me[1], 0)

    gain_spec = pl.BlockSpec((1, wide), lambda i, me: (0, 0))
    cut = run_grid(
        cut_attention,
        me,
        (1,),
        [query_weight] * n
        + [key_weight] * n
        + [value_weight] * n
        + [output_weight] * n
        + [first_gain.reshape(1, wide), second_gain.reshape(1, wide)],
        [pl.BlockSpec((wide, HD), head_of(d)) for d in range(n)]
        + [pl.BlockSpec((wide, HD), chip_of(d)) for d in range(n)] * 2
        + [pl.BlockSpec((HD, wide), head_rows_of(d)) for d in range(n)]
        + [gain_spec, gain_spec],
        [shape((wide + 32, HD))] * n + [shape((wide, HD))] * n + [shape((HD, wide))] * n,
        [pl.BlockSpec((wide + 32, HD), lambda i, me: (0, 0))] * n
        + [pl.BlockSpec((wide, HD), lambda i, me: (0, 0))] * n
        + [pl.BlockSpec((HD, wide), lambda i, me: (0, 0))] * n,
        name="cut_attention",
    )
    own_tokens = tokens[0]
    near_tokens = [own_tokens] + [across(own_tokens, d) for d in range(1, n)]

    def cut_hidden(me_ref, *refs):
        gates, ups, downs = (refs[i * n : (i + 1) * n] for i in range(3))
        for d in range(n):
            refs[-1][0, d, :wide, :quarter] = gates[d][...]
            refs[-1][0, d, :wide, quarter:] = ups[d][...]
            refs[-1][0, d, wide:, :] = downs[d][...]

    def columns_of(d):
        return lambda q, me: (0, (2 * (me[0] ^ d) + me[1]) * QUARTERS + q)

    def down_rows_of(d):
        return lambda q, me: ((2 * (me[0] ^ d) + me[1]) * QUARTERS + q, 0)

    piece = (wide + quarter, 2 * quarter)
    hidden_cut = run_grid(
        cut_hidden,
        me,
        (QUARTERS,),
        [gate_weight] * n + [up_weight] * n + [down_weight] * n,
        [pl.BlockSpec((wide, quarter), columns_of(d)) for d in range(n)] * 2
        + [pl.BlockSpec((quarter, wide), down_rows_of(d)) for d in range(n)],
        shape((QUARTERS, n) + piece),
        pl.BlockSpec((1, n) + piece, lambda q, me: (q, 0, 0, 0)),
        name="cut_hidden",
    )
    cut, hidden_cut = lax.optimization_barrier((cut, hidden_cut))
    weights_in = [cut[0]] + [across(cut[d], d) for d in range(1, n)]
    own_cotangent = cotangent[0]
    block = (rows, width)

    tiles_count = 3 * QUARTERS + 3
    query_at, output_at, kv_at = tiles_count - 3, tiles_count - 2, tiles_count - 1
    units = 2 * tiles_count
    unit = (2, quarter, wide)
    held_sums, held_ends = 4, 3
    MID, BACK, OUT, ONE = range(4)
    query_slot, attended_slot, query_grad_slot, kv_grad_slot = range(2 * planes, 2 * planes + 4)
    kept_slots = 2 * planes + 2
    columns = (plane_rows, HD)
    lanes = (8, wide)
    dma = pltpu.SemaphoreType.DMA

    in_hbm = dict(
        near_tokens=near_tokens,
        in_weight=weights_in,
        query_cut=cut[n : 2 * n],
        out_cut=cut[2 * n :],
        cut=hidden_cut,
        cotangent=own_cotangent,
        tokens=own_tokens,
    )
    in_vmem = dict(
        tables=jnp.stack([cosine, sine, kv_cosine, kv_sine]),
        query_ids=query_ids,
        key_ids=key_ids,
    )
    unit_array = shape((units,) + unit)
    out_hbm = dict(
        tiles=unit_array,
        from_end=unit_array,
        from_middle=unit_array,
        finals=unit_array,
        owned=unit_array,
        near=unit_array,
        row_near=shape((4, n) + block),
        row_far=shape((4, n) + block),
        cot_all=shape((2, n) + block),
        query_in=shape((n, wide, HD)),
        kept=shape((kept_slots,) + columns),
        out_weight=shape((2, 2, HD, wide)),
        normed=shape((plane_rows, width)),
        middle=shape(block, F32),
        branch_all=shape((n, 2) + block),
        kv_other=shape((planes,) + columns),
        kv_down=shape((planes,) + columns),
        kv_up=shape((planes,) + columns),
        out_own=shape(block),
        tokens_grad=shape(block, F32),
        output=shape(block),
        gain_out=shape(lanes, F32),
    )
    scratch = dict(
        work=pltpu.VMEM((2 * plane_rows, width), BF16),
        feed=pltpu.VMEM((QUARTERS, n) + piece, BF16),
        heads=pltpu.VMEM((3 * QUARTERS, plane_rows, HD), BF16),
        turned=pltpu.VMEM((3, HD, plane_rows), BF16),
        stage=pltpu.VMEM((2, n, quarter, wide), BF16),
        mine=pltpu.VMEM((2,) + unit, BF16),
        theirs=pltpu.VMEM((2,) + unit, BF16),
        crossed=pltpu.VMEM((2,) + unit, BF16),
        sums=pltpu.VMEM((held_sums,) + unit, BF16),
        ends=pltpu.VMEM((held_ends,) + unit, BF16),
        some_rows=pltpu.VMEM((n,) + block, BF16),
        wide_rows=pltpu.VMEM(block, F32),
        own_rows=pltpu.VMEM(block, BF16),
        kv_some=pltpu.VMEM((2,) + columns, BF16),
        flat=pltpu.VMEM((8, width), F32),
        gain_mine=pltpu.VMEM((n,) + lanes, F32),
        gain_far=pltpu.VMEM((n,) + lanes, F32),
        gain_sum=pltpu.VMEM((4,) + lanes, F32),
        gain_in=pltpu.VMEM((4,) + lanes, F32),
        load_sem=dma((4 * n + n,)),
        gains=pltpu.VMEM((8, width), F32),
        gain_rows=pltpu.VMEM((n, 32, HD), BF16),
        feed_local=dma((QUARTERS,)),
        feed_send=dma((QUARTERS * n,)),
        feed_recv=dma((QUARTERS * n,)),
        stage_sem=dma((2, 2)),
        one_send=dma((units,)),
        one_recv=dma((units,)),
        two_send=dma((units,)),
        two_recv=dma((units,)),
        three_send=dma((units,)),
        three_recv=dma((units,)),
        mine_sem=dma((2,)),
        theirs_sem=dma((2,)),
        crossed_sem=dma((2,)),
        final_sem=dma((held_ends,)),
        deal_local=dma((units,)),
        deal_send=dma((2 * units,)),
        deal_recv=dma((2 * units,)),
        sib_send=dma((units,)),
        sib_recv=dma((units,)),
        row_sem=dma((n,)),
        row_near_send=dma((4 * n,)),
        row_near_recv=dma((4 * n,)),
        row_far_send=dma((4 * n,)),
        row_far_recv=dma((4 * n,)),
        token_send=dma((n,)),
        token_recv=dma((n,)),
        query_send=dma((n,)),
        query_recv=dma((n,)),
        out_send=dma((n,)),
        out_recv=dma((n,)),
        cot_send=dma((n,)),
        cot_recv=dma((n,)),
        cot_near_send=dma((n,)),
        cot_near_recv=dma((n,)),
        two_local=dma((1,)),
        two_far_send=dma((n,)),
        two_far_recv=dma((n,)),
        two_near_send=dma((n,)),
        two_near_recv=dma((n,)),
        two_half_send=dma((n,)),
        two_half_recv=dma((n,)),
        branch_half_send=dma((n,)),
        branch_half_recv=dma((n,)),
        climb_send=dma((2 * planes,)),
        climb_recv=dma((2 * planes,)),
        fall_send=dma((2 * planes,)),
        fall_recv=dma((2 * planes,)),
        soft=pltpu.VMEM((2 * n, pair, 1), F32),
        pass_send=dma((planes,)),
        pass_recv=dma((planes,)),
        keep_sem=dma((3,)),
        branch_local=dma((1,)),
        branch_send=dma((n,)),
        branch_recv=dma((n,)),
        branch_near_send=dma((n,)),
        branch_near_recv=dma((n,)),
        kv_sem=dma((2,)),
        kv_send=dma((planes,)),
        kv_recv=dma((planes,)),
        down_send=dma((planes,)),
        down_recv=dma((planes,)),
        up_send=dma((planes,)),
        up_recv=dma((planes,)),
        gain_send=dma((n + 4,)),
        gain_recv=dma((n + 4,)),
    )

    def backward(*refs):
        r, first = types.SimpleNamespace(), 0
        for group in (in_hbm, in_vmem, out_hbm):
            leaves, form = jax.tree.flatten(group)
            vars(r).update(jax.tree.unflatten(form, refs[first : first + len(leaves)]))
            first += len(leaves)
        vars(r).update(zip(scratch, refs[first:]))
        here = lax.axis_index("ctx")
        chip = lax.axis_index("fsdp")
        z, side = here // 2, here % 2
        is_middle = (z == 1) | (z == 2)
        is_end = jnp.logical_not(is_middle)
        chips = [chip, chip + 1 - 2 * (chip % 2), (chip + 2) % 4, 3 - chip]
        partner = (2 * (z + 1 - 2 * (z % 2)) + side, chip)
        other_middle = (2 * (3 - z) + side, chip)
        other_core = (here + 1 - 2 * side, chip)
        below, above = (here - 2, chip), (here + 2, chip)
        blocks = [pl.ds(pl.multiple_of(c * wide, wide), wide) for c in chips]
        work, feed, heads, turned, stage = r.work, r.feed, r.heads, r.turned, r.stage

        barrier = pltpu.get_barrier_semaphore()
        for peer in [(here, c) for c in chips[1:]] + [partner, other_core]:
            pl.semaphore_signal(barrier, inc=1, device_id=peer, device_id_type=MESH)

        @pl.when(is_middle)
        def _():
            pl.semaphore_signal(barrier, inc=1, device_id=other_middle, device_id_type=MESH)
            pl.semaphore_wait(barrier, n + 2)

        @pl.when(is_end)
        def _():
            pl.semaphore_wait(barrier, n + 1)

        def remote(source, target, send, recv, peer):
            return pltpu.make_async_remote_copy(
                src_ref=source,
                dst_ref=target,
                send_sem=send,
                recv_sem=recv,
                device_id=peer,
                device_id_type=MESH,
            )

        local = pltpu.make_async_copy

        def span(first, count):
            return pl.ds(pl.multiple_of(first, count), count)

        def feed_copy(q, d):
            at = q * n + d
            return remote(
                r.cut.at[q, d], feed.at[q, d], r.feed_send.at[at], r.feed_recv.at[at], (here, chips[d])
            )

        def feed_own(q):
            return local(r.cut.at[q, 0], feed.at[q, 0], r.feed_local.at[q])

        def hop_one(i):
            return remote(r.tiles.at[i], r.from_end.at[i], r.one_send.at[i], r.one_recv.at[i], partner)

        def hop_two(i):
            return remote(
                r.sums.at[i % held_sums],
                r.from_middle.at[i],
                r.two_send.at[i],
                r.two_recv.at[i],
                other_middle,
            )

        def hop_three(i):
            return remote(
                r.ends.at[i % held_ends], r.finals.at[i], r.three_send.at[i], r.three_recv.at[i], partner
            )

        def load_mine(i):
            return local(r.tiles.at[i], r.mine.at[i % 2], r.mine_sem.at[i % 2])

        def load_theirs(i):
            return local(r.from_end.at[i], r.theirs.at[i % 2], r.theirs_sem.at[i % 2])

        def load_crossed(i):
            return local(r.from_middle.at[i], r.crossed.at[i % 2], r.crossed_sem.at[i % 2])

        def keep_final(i):
            return local(r.ends.at[i % held_ends], r.finals.at[i], r.final_sem.at[i % held_ends])

        def keep_own(i):
            return local(r.finals.at[i, 0], r.owned.at[i, 0], r.deal_local.at[i])

        def deal_to(i, b, d):
            at = 2 * i + b
            return remote(
                r.finals.at[i, b],
                r.owned.at[i, b],
                r.deal_send.at[at],
                r.deal_recv.at[at],
                (here, chips[d]),
            )

        def to_sibling(i):
            return remote(r.owned.at[i], r.near.at[i], r.sib_send.at[i], r.sib_recv.at[i], other_core)

        def add(target, a, b):
            def some(s, _):
                at = (s // 4, span((s % 4) * (quarter // 4), quarter // 4))
                target[at] = (a[at].astype(F32) + b[at].astype(F32)).astype(BF16)
                return 0

            lax.fori_loop(0, 8, some, 0)

        def when_in(i, *conditions):
            return pl.when(functools.reduce(jnp.logical_and, conditions, (i >= 0) & (i < units)))

        def step(i, _=0):
            @when_in(i - 1, is_middle)
            def _():
                at = i - 1
                load_mine(at).wait()
                load_theirs(at).wait()

                @pl.when(at >= held_sums)
                def _():
                    hop_two(at - held_sums).wait_send()

                add(r.sums.at[at % held_sums], r.mine.at[at % 2], r.theirs.at[at % 2])
                hop_two(at).start()

            @when_in(i - 4, is_middle)
            def _():
                at = i - 4
                load_crossed(at).wait()

                @pl.when(at >= held_ends)
                def _():
                    hop_three(at - held_ends).wait_send()

                add(r.ends.at[at % held_ends], r.sums.at[at % held_sums], r.crossed.at[at % 2])
                hop_three(at).start()
                keep_final(at).start()

            @when_in(i, is_middle)
            def _():
                hop_one(i).wait_recv()
                load_mine(i).start()
                load_theirs(i).start()

            @when_in(i - 3, is_middle)
            def _():
                hop_two(i - 3).wait_recv()
                load_crossed(i - 3).start()

            @when_in(i - 6)
            def _():
                at = i - 6

                @pl.when(is_middle)
                def _():
                    keep_final(at).wait()

                @pl.when(is_end)
                def _():
                    hop_three(at).wait_recv()

                @pl.when(at % 2 == 0)
                def _():
                    keep_own(at).start()
                    deal_to(at, 1, 1).start()

                @pl.when(at % 2 == 1)
                def _():
                    deal_to(at, 0, 2).start()
                    deal_to(at, 1, 3).start()

            @when_in(i - 9)
            def _():
                at = i - 9

                @pl.when(at % 2 == 0)
                def _():
                    keep_own(at).wait()

                @pl.when(at % 2 == 1)
                def _():
                    deal_to(at, 0, 2).wait_recv()

                deal_to(at, 1, 3).wait_recv()
                to_sibling(at).start()

            return 0

        steps_done = [0]

        def advance(count):
            first = steps_done[0]
            steps_done[0] = first + count
            lax.fori_loop(first, first + count, step, 0)

        def finish():
            def one(i, _):
                @pl.when(is_end)
                def _():
                    hop_one(i).wait_send()

                @pl.when(is_middle & (i >= units - held_sums))
                def _():
                    hop_two(i).wait_send()

                @pl.when(is_middle & (i >= units - held_ends))
                def _():
                    hop_three(i).wait_send()

                @pl.when(i % 2 == 1)
                def _():
                    deal_to(i, 0, 2).wait_send()

                deal_to(i, 1, 3).wait_send()
                to_sibling(i).wait()
                return 0

            lax.fori_loop(0, units, one, 0)

        def stage_copy(t, h):
            return local(r.stage.at[t % 2, pl.ds(2 * h, 2)], r.tiles.at[2 * t + h], r.stage_sem.at[t % 2, h])

        def staged(t):
            for h in range(2):
                stage_copy(t, h).wait()

            @pl.when(is_end)
            def _():
                for h in range(2):
                    hop_one(2 * t + h).start()

        def outer(t, left, right_rows):
            for j in range(n):
                stage[t % 2, j] = matmul(left, work[right_rows, blocks[j]]).astype(BF16)
            for h in range(2):
                stage_copy(t, h).start()

        def row_near(s, base, d):
            at = s * n + d
            return remote(
                work.at[pl.ds(base + (2 * d + 1) * rows, rows)],
                r.row_near.at[s, d],
                r.row_near_send.at[at],
                r.row_near_recv.at[at],
                other_core,
            )

        def row_far(s, base, d):
            at = s * n + d
            return remote(
                work.at[pl.ds(base + 2 * d * rows, rows)],
                r.row_far.at[s, d],
                r.row_far_send.at[at],
                r.row_far_recv.at[at],
                (here, chips[d]),
            )

        def near_load(s, d):
            return local(r.row_near.at[s, d], r.some_rows.at[d], r.row_sem.at[d])

        def far_load(s, d):
            return local(r.row_far.at[s, d], r.some_rows.at[d], r.row_sem.at[d])

        few = 16

        def row_send(s, base, d):
            row_near(s, base, d).wait_recv()
            near_load(s, d).start()
            near_load(s, d).wait()

            def some(c, _):
                at = span(c * few, few)
                own = pl.ds(pl.multiple_of(base + 2 * d * rows + c * few, few), few)
                work[own, :] = (
                    work[own, :].astype(F32) + r.some_rows[d, at, :].astype(F32)
                ).astype(BF16)
                return 0

            lax.fori_loop(0, rows // few, some, 0)
            row_far(s, base, d).start()

        far_first = (3, 1, 2, 0)

        def rows_reduced(s, base, compute, send=True, ticks=0):
            def one(i, _):
                d = jnp.where(i == 0, 3, jnp.where(i == n - 1, 0, i))
                compute(d)
                for at in range(n):

                    @pl.when(i == at)
                    def _():
                        row_near(s, base, far_first[at]).start()
                        if send and at > 0:
                            row_send(s, base, far_first[at - 1])

                if ticks:

                    @pl.when(i >= n - ticks)
                    def _():
                        step(first + i - (n - ticks))

                return 0

            first = steps_done[0]
            steps_done[0] = first + ticks
            lax.fori_loop(0, n, one, 0)

        def rows_arrive(s, base):
            row_near(s, base, 0).wait_recv()
            near_load(s, 0).start()
            for d in range(1, n):
                row_far(s, base, d).wait_recv()
                far_load(s, d).start()
            near_load(s, 0).wait()
            for d in range(1, n):
                far_load(s, d).wait()

        def rows_sent(s, base):
            for d in range(n):
                row_near(s, base, d).wait_send()
            for d in range(1, n):
                row_far(s, base, d).wait_send()

        def norm_rows_back(base, value_ref, gain_row, use):
            r.flat[...] = jnp.zeros_like(r.flat)

            def some(c, _):
                at = span(c * few, few)
                grad = work[pl.ds(pl.multiple_of(base + c * few, few), few), :].astype(F32)
                for d in range(n):
                    grad += r.some_rows[d, at, :].astype(F32)
                values = value_ref[at, :].astype(F32)
                inverse = lax.rsqrt(jnp.mean(values * values, axis=-1, keepdims=True) + epsilon)
                unit_rows = values * inverse
                scaled = grad * gain_row
                back = inverse * (
                    scaled - unit_rows * jnp.mean(scaled * unit_rows, axis=-1, keepdims=True)
                )
                use(at, back)
                terms = grad * unit_rows
                r.flat[...] += terms[:8] + terms[8:]
                return 0

            lax.fori_loop(0, rows // few, some, 0)

        def gain_terms(at):
            total = jnp.sum(r.flat[...], axis=0, keepdims=True)
            r.flat[0:1, :] = total
            for j in range(n):
                r.gain_mine[j, at : at + 1, :] = r.flat[0:1, blocks[j]]

        r.gain_mine[...] = jnp.zeros_like(r.gain_mine)
        loads = []

        def load(source, target):
            copy = local(source, target, r.load_sem.at[len(loads)])
            copy.start()
            loads.append(copy)

        def loaded():
            while loads:
                loads.pop().wait()

        def out_far(d):
            return remote(
                r.out_cut[d],
                r.theirs.at[d // 2, d % 2],
                r.out_send.at[d],
                r.out_recv.at[d],
                (here, chips[d]),
            )

        def cot_far(d):
            return remote(
                r.cotangent, r.cot_all.at[0, d], r.cot_send.at[d], r.cot_recv.at[d], (here, chips[d])
            )

        def cot_near(d):
            source = r.cotangent if d == 0 else r.cot_all.at[0, d]
            return remote(
                source, r.cot_all.at[1, d], r.cot_near_send.at[d], r.cot_near_recv.at[d], other_core
            )

        def query_far(d):
            return remote(
                r.query_cut[d],
                r.query_in.at[d],
                r.query_send.at[d],
                r.query_recv.at[d],
                (here, chips[d]),
            )

        def kv_piece(j):
            return r.kv_some.at[j // 3, pl.ds(j % 3 * wide, wide)]

        def query_piece(j):
            return heads.at[query_grad_slot + j // 3, pl.ds(j % 3 * wide, wide)]

        for d in range(1, n):
            query_far(d).start()
        for d in range(1, n):
            out_far(d).start()
        for d in range(1, n):
            feed_copy(0, d).start()
        for d in range(1, n):
            cot_far(d).start()
        cot_near(0).start()
        def token_near(d):
            return remote(
                r.near_tokens[d],
                work.at[pl.ds(plane_rows + (2 * d + 1) * rows, rows)],
                r.token_send.at[d],
                r.token_recv.at[d],
                other_core,
            )

        for d in range(n):
            token_near(d).start()
            load(r.near_tokens[d], work.at[pl.ds(plane_rows + 2 * d * rows, rows)])
        for j in range(n):
            load(r.in_weight[j].at[pl.ds(0, wide)], kv_piece(j))
            load(r.in_weight[j].at[pl.ds(wide, 32)], r.gain_rows.at[j])
        loaded()
        load(r.out_cut[0], r.theirs.at[0, 0])
        load(r.query_cut[0], query_piece(0))
        for q in range(QUARTERS):
            feed_own(q).start()
        for j in range(n):
            both = r.gain_rows[j].astype(F32)
            for g in range(2):
                for h in range(2):
                    here_half = pl.ds(pl.multiple_of(chips[j] * wide + h * HD, HD), HD)
                    r.gains[g : g + 1, here_half] = both[16 * g + 8 * h : 16 * g + 8 * h + 1]

        for d in range(n):
            token_near(d).wait_recv()

        def project(d, _):
            for c in range(2):
                first = (2 * d + (side + c) % 2) * rows

                def some(s, _, c=c, first=first):
                    now = pl.ds(pl.multiple_of(plane_rows + first + s * few, few), few)
                    then = pl.ds(pl.multiple_of((2 * d + c) * rows + s * few, few), few)
                    values = work[now, :].astype(F32)
                    inverse = lax.rsqrt(jnp.mean(values * values, axis=-1, keepdims=True) + epsilon)
                    work[then, :] = (values * inverse * r.gains[0:1, :]).astype(BF16)
                    return 0

                lax.fori_loop(0, rows // few, some, 0)
            now = span(d * pair, pair)
            kv = jnp.zeros((pair, HD), F32)
            for j in range(n):
                kv += matmul(work[now, blocks[j]], kv_piece(j)[...])
            kv = kv * r.tables[2] + turn(kv) * r.tables[3]
            heads[0, now, :] = kv.astype(BF16)
            return 0

        lax.fori_loop(0, n, project, 0)
        keep_normed = local(work.at[pl.ds(0, plane_rows)], r.normed, r.keep_sem.at[0])
        keep_normed.start()

        kv_halves = [pl.ds(h * (plane_rows // 2), plane_rows // 2) for h in range(2)]

        def climb(s, h):
            at = 2 * s + h
            return remote(
                heads.at[s - 1, kv_halves[h]],
                heads.at[s, kv_halves[h]],
                r.climb_send.at[at],
                r.climb_recv.at[at],
                above,
            )

        def fall(s, h):
            at = 2 * s + h
            return remote(
                heads.at[(planes - s + 1) % planes, kv_halves[h]],
                heads.at[planes - s, kv_halves[h]],
                r.fall_send.at[at],
                r.fall_recv.at[at],
                below,
            )

        def pass_on(k):
            return remote(
                heads.at[k], heads.at[planes + k], r.pass_send.at[k], r.pass_recv.at[k], other_core
            )

        def kv_leave(s, h):
            @pl.when((z - s + 1 >= 0) & (z + 1 < planes))
            def _():
                climb(s, h).start()

            @pl.when((z + s - 1 < planes) & (z >= 1))
            def _():
                fall(s, h).start()

        def kv_come(s, h):
            @pl.when(z - s >= 0)
            def _():
                climb(s, h).wait_recv()

            @pl.when(z + s < planes)
            def _():
                fall(s, h).wait_recv()

        def kv_forward(s):
            for h in range(2):
                kv_come(s, h)
                if s + 1 < planes:
                    kv_leave(s + 1, h)

        for h in range(2):
            kv_leave(1, h)
        pass_on(0).start()
        for d in range(1, n):
            query_far(d).wait_recv()
            load(r.query_in.at[d], query_piece(d))
        loaded()

        def project_query(d, _):
            now = span(d * pair, pair)
            query = jnp.zeros((pair, HD), F32)
            for j in range(n):
                query += matmul(work[now, blocks[j]], query_piece(j)[...])
            query = query * r.tables[0] + turn(query) * r.tables[1]
            heads[query_slot, now, :] = query.astype(BF16)
            return 0

        lax.fori_loop(0, n, project_query, 0)
        for d in range(1, n):
            out_far(d).wait_recv()
        keep_out = local(r.theirs, r.out_weight, r.keep_sem.at[1])
        keep_out.start()

        def put_rows(base, d, now_values, block_at):
            first = pl.ds(pl.multiple_of(base + (2 * d + side) * rows, rows), rows)
            second = pl.ds(pl.multiple_of(base + (2 * d + 1 - side) * rows, rows), rows)
            work[first, block_at] = now_values[:rows]
            work[second, block_at] = now_values[rows:]

        def totals(d):
            return [r.wide_rows.at[:, span((2 * d + c) * HD, HD)] for c in range(2)]

        def attend_block(k, d, first, last):
            now = span(d * pair, pair)
            a, b = heads[k, now, :], heads[planes + k, now, :]
            keys, values = jnp.where(side == 0, a, b), jnp.where(side == 0, b, a)
            score = matmul_nt(heads[query_slot, now, :], keys) * scale
            score = jnp.where(r.key_ids[d, k] <= r.query_ids[d], score, masked_score)
            top = jnp.max(score, axis=-1, keepdims=True)
            if not first:
                before = r.soft[d]
                top = jnp.maximum(top, before)
                factor = jnp.exp(before - top)
            raised = jnp.exp(score - top)
            weight = jnp.sum(raised, axis=-1, keepdims=True)
            total = matmul(raised.astype(BF16), values)
            if not first:
                weight += r.soft[n + d] * factor
                total += jnp.concatenate([t[...] for t in totals(d)], axis=0) * factor
            if last:
                return total, weight
            r.soft[d] = top
            r.soft[n + d] = weight
            for c, target in enumerate(totals(d)):
                target[...] = total[c * rows : (c + 1) * rows]
            return None

        def attend_to(k, first=False):
            def one(d, _):
                attend_block(k, d, first, False)
                return 0

            lax.fori_loop(0, n, one, 0)

        def when_middle(there, otherwise):
            return jnp.where(is_middle, there, otherwise)

        def passed(condition, k):
            @pl.when(condition)
            def _():
                pass_on(k).wait_recv()

        def passing(condition, k):
            @pl.when(condition)
            def _():
                pass_on(k).start()

        pass_on(0).wait_recv()
        attend_to(0, first=True)
        kv_forward(1)
        passing(z >= 1, 1)
        passing(z + 1 < planes, 3)
        passed(z >= 1, 1)
        passed(z + 1 < planes, 3)
        attend_to(jnp.where(z >= 1, 1, 3))
        kv_forward(2)
        pass_on(2).start()
        for d in range(1, n):
            cot_far(d).wait_recv()
            cot_near(d).start()
        pass_on(2).wait_recv()
        attend_to(when_middle(3, 2))
        keep_normed.wait()
        kv_forward(3)
        passing(z == 0, 1)
        passing(z == planes - 1, 3)
        passed(z == 0, 1)
        passed(z == planes - 1, 3)

        def attend(d):
            now = span(d * pair, pair)
            last_block = jnp.where(z == 0, 1, when_middle(2, 3))
            total, weight = attend_block(last_block, d, False, True)
            low_total = (total * (1.0 / weight)).astype(BF16)
            heads[attended_slot, now, :] = low_total
            for j in range(n):
                put_rows(
                    plane_rows,
                    d,
                    matmul(low_total, r.theirs[j // 2, j % 2]).astype(BF16),
                    blocks[j],
                )

        rows_reduced(MID, plane_rows, attend)
        keep_heads = local(heads.at[pl.ds(0, kept_slots)], r.kept, r.keep_sem.at[2])
        keep_heads.start()
        load(r.tokens, r.own_rows)
        loaded()
        keep_out.wait()
        for s in range(1, planes):
            for h in range(2):

                @pl.when((z - s + 1 >= 0) & (z + 1 < planes))
                def _():
                    climb(s, h).wait_send()

                @pl.when((z + s - 1 < planes) & (z >= 1))
                def _():
                    fall(s, h).wait_send()

        for k in range(planes):
            pass_on(k).wait_send()

        rows_arrive(MID, plane_rows)

        def second_norm(c, _):
            at = span(c * few, few)
            total = r.own_rows[at, :].astype(F32)
            total += work[pl.ds(pl.multiple_of(plane_rows + c * few, few), few), :].astype(F32)
            for d in range(n):
                total += r.some_rows[d, at, :].astype(F32)
            inverse = lax.rsqrt(jnp.mean(total * total, axis=-1, keepdims=True) + epsilon)
            r.wide_rows[at, :] = total
            r.own_rows[at, :] = (total * inverse * r.gains[1:2, :]).astype(BF16)
            return 0

        lax.fori_loop(0, rows // few, second_norm, 0)

        def two_far(d):
            return remote(
                r.own_rows,
                work.at[pl.ds(2 * d * rows, rows)],
                r.two_far_send.at[d],
                r.two_far_recv.at[d],
                (here, chips[d]),
            )

        def two_near(d):
            source = r.own_rows if d == 0 else work.at[pl.ds(2 * d * rows, rows)]
            return remote(
                source,
                work.at[pl.ds((2 * d + 1) * rows, rows)],
                r.two_near_send.at[d],
                r.two_near_recv.at[d],
                other_core,
            )

        half_rows = rows // 2

        def two_half(d):
            return remote(
                work.at[pl.ds(2 * d * rows + (d - 1) * half_rows, half_rows)],
                work.at[pl.ds(2 * 3 * rows + (d - 1) * half_rows, half_rows)],
                r.two_half_send.at[d],
                r.two_half_recv.at[d],
                (here, chips[3 - d]),
            )

        for d in (1, 2):
            two_far(d).start()
        two_near(0).start()
        two_own = local(r.own_rows, work.at[pl.ds(0, rows)], r.two_local.at[0])
        two_own.start()
        load(r.wide_rows, r.middle)
        rows_sent(MID, plane_rows)
        for d in range(n):
            cot_near(d).wait_recv()
            source = r.cotangent if d == 0 else r.cot_all.at[0, d]
            load(source, work.at[pl.ds(plane_rows + 2 * d * rows, rows)])
            load(r.cot_all.at[1, d], work.at[pl.ds(plane_rows + (2 * d + 1) * rows, rows)])
        keep_heads.wait()
        for d in range(1, n):
            feed_copy(0, d).wait_recv()
        loaded()

        def rows_of_chip(t, arrive, half_way, pass_along):
            for at in range(n):

                @pl.when(t == at)
                def _():
                    for d in ((), (1, 2), (), ())[at]:
                        arrive(d).wait_recv()
                        half_way(d).start()
                        pass_along(d).start()
                    if at == 2:
                        half_way(1).wait_recv()
                        half_way(2).wait_recv()
                        pass_along(3).start()
                    pass_along(at).wait_recv()

        two_own.wait()

        def quarter_step(q, _):
            step(3 * q - 3)
            feed_own(q).wait()

            @pl.when(q > 0)
            def _():
                for d in range(1, n):
                    feed_copy(q, d).wait_recv()

            @pl.when((q > 0) & (q < QUARTERS - 1))
            def _():
                for d in range(1, n):
                    feed_copy(q + 1, d).start()

            def forward(t, _):
                @pl.when(q == 0)
                def _():
                    rows_of_chip(t, two_far, two_half, two_near)

                now = span(t * pair, pair)
                cot_now = pl.ds(pl.multiple_of(plane_rows + t * pair, pair), pair)
                both = jnp.zeros((pair, 2 * quarter), F32)
                hidden_grad = jnp.zeros((pair, quarter), F32)
                for j in range(n):
                    both += matmul(work[now, blocks[j]], feed[q, j, :wide, :])
                    hidden_grad += matmul_nt(work[cot_now, blocks[j]], feed[q, j, wide:, :])
                gate, up = both[:, :quarter], both[:, quarter:]
                share = 1.0 / (1.0 + jnp.exp(-gate))
                activated = gate * share
                results = (
                    activated * up,
                    hidden_grad * up * share * (1.0 + gate * (1.0 - share)),
                    hidden_grad * activated,
                )
                for w, result in enumerate(results):
                    heads[q * 3 + w, now, :] = result.astype(BF16)
                    turned[w, :, now] = result.T.astype(BF16)
                return 0

            lax.fori_loop(0, n, forward, 0)

            @pl.when(q == 0)
            def _():
                for d in range(1, n):
                    feed_copy(1, d).start()

            step(3 * q - 2)

            def one(w, _):
                t = 3 * q + w

                @pl.when(t >= 2)
                def _():
                    staged(t - 2)

                outer(t, turned[w], span(jnp.where(w == 0, plane_rows, 0), plane_rows))
                return 0

            lax.fori_loop(0, 3, one, 0)
            step(3 * q - 1)
            return 0

        lax.fori_loop(0, QUARTERS, quarter_step, 0)
        steps_done[0] = 3 * QUARTERS - 3
        for t in (query_at - 2, query_at - 1):
            staged(t)

        for d in range(1, n):
            two_near(d).wait_send()
        for d in (1, 2):
            two_half(d).wait_send()

        def back_step(d):
            now = span(d * pair, pair)
            lefts = [
                jnp.concatenate([heads[q * 3 + 1, now, :], heads[q * 3 + 2, now, :]], axis=1)
                for q in range(QUARTERS)
            ]
            for j in range(n):
                total = jnp.zeros((pair, wide), F32)
                for q in range(QUARTERS):
                    total += matmul_nt(lefts[q], feed[q, j, :wide, :])
                work[now, blocks[j]] = total.astype(BF16)

        half = n // 2
        rows_reduced(BACK, 0, back_step, ticks=TICKS[0] + TICKS[1])

        def out_step(d):
            now = span(d * pair, pair)
            then = pl.ds(pl.multiple_of(plane_rows + d * pair, pair), pair)
            for j in range(n):
                total = jnp.zeros((pair, wide), F32)
                for q in range(QUARTERS):
                    total += matmul(heads[q * 3, now, :], feed[q, j, wide:, :])
                work[then, blocks[j]] = total.astype(BF16)

        rows_reduced(OUT, plane_rows, out_step, send=False, ticks=TICKS[2] + TICKS[3])

        load(r.kept, heads.at[pl.ds(0, kept_slots)])
        for j in range(n):
            query_source = r.query_cut[0] if j == 0 else r.query_in.at[j]
            load(query_source, feed.at[0, j, pl.ds(0, wide), pl.ds(0, HD)])
            load(r.in_weight[j].at[pl.ds(0, wide)], feed.at[0, j, pl.ds(0, wide), pl.ds(HD, HD)])
            load(r.out_weight.at[j // 2, j % 2], feed.at[0, j, pl.ds(wide, HD)])

        rows_arrive(BACK, 0)
        loaded()
        for d in (1, 2):
            two_far(d).wait_send()
        two_near(0).wait_send()
        load(r.cotangent, r.own_rows)
        loaded()

        def second_use(at, back):
            grad = r.own_rows[at, :].astype(F32) + back
            r.wide_rows[at, :] = grad
            r.own_rows[at, :] = grad.astype(BF16)

        norm_rows_back(0, r.wide_rows, r.gains[1:2, :], second_use)

        def branch_far(d):
            return remote(
                r.own_rows,
                r.branch_all.at[d, side],
                r.branch_send.at[d],
                r.branch_recv.at[d],
                (here, chips[d]),
            )

        def branch_near(d):
            source = r.own_rows if d == 0 else r.branch_all.at[d, side]
            return remote(
                source,
                r.branch_all.at[d, side],
                r.branch_near_send.at[d],
                r.branch_near_recv.at[d],
                other_core,
            )

        def branch_half(d):
            some = pl.ds((d - 1) * half_rows, half_rows)
            return remote(
                r.branch_all.at[d, side, some],
                r.branch_all.at[3, side, some],
                r.branch_half_send.at[d],
                r.branch_half_recv.at[d],
                (here, chips[3 - d]),
            )

        for d in (1, 2):
            branch_far(d).start()
        branch_near(0).start()
        branch_own = local(r.own_rows, r.branch_all.at[0, side], r.branch_local.at[0])
        branch_own.start()
        gain_terms(1)
        advance(TICKS[4])
        rows_sent(BACK, 0)
        branch_own.wait()
        loaded()

        def scored(d, now):
            keys, values, scores = [], [], []
            for k in range(planes):
                a, b = heads[k, now, :], heads[planes + k, now, :]
                keys.append(jnp.where(side == 0, a, b))
                values.append(jnp.where(side == 0, b, a))
                score = matmul_nt(heads[query_slot, now, :], keys[k]) * scale
                scores.append(jnp.where(r.key_ids[d, k] <= r.query_ids[d], score, masked_score))
            top = functools.reduce(jnp.maximum, [jnp.max(s, axis=-1, keepdims=True) for s in scores])
            raised = [jnp.exp(s - top) for s in scores]
            inverse = 1.0 / sum(jnp.sum(e, axis=-1, keepdims=True) for e in raised)
            return keys, values, [e * inverse for e in raised]

        def attend_back(d, _):
            rows_of_chip(d, branch_far, branch_half, branch_near)

            @pl.when(d == half)
            def _():
                for at in (3, 1, 2):
                    row_send(OUT, plane_rows, at)

            now = span(d * pair, pair)
            for c in range(2):
                load(r.branch_all.at[d, c], work.at[pl.ds(pl.multiple_of((2 * d + c) * rows, rows), rows)])
            loaded()
            query = heads[query_slot, now, :]
            attended_grad = jnp.zeros((pair, HD), F32)
            for j in range(n):
                attended_grad += matmul_nt(work[now, blocks[j]], feed[0, j, wide:, :])
            attended_grad = attended_grad.astype(BF16)
            keys, values, probs = scored(d, now)
            low = [p.astype(BF16) for p in probs]
            shares = [matmul_nt(attended_grad, values[k]) for k in range(planes)]
            delta = sum(
                jnp.sum(low[k].astype(F32) * shares[k], axis=-1, keepdims=True) for k in range(planes)
            )
            query_grad = jnp.zeros((pair, HD), F32)
            for k in range(planes):
                score_grad = (probs[k] * (shares[k] - delta)).astype(BF16)
                query_grad += matmul(score_grad, keys[k])
                key_grad = matmul_tn(score_grad, query) * scale
                value_grad = matmul_tn(low[k], attended_grad)
                heads[k, now, :] = jnp.where(side == 0, key_grad, value_grad).astype(BF16)
                heads[planes + k, now, :] = jnp.where(side == 0, value_grad, key_grad).astype(BF16)
            query_grad = query_grad * scale
            query_grad = query_grad * r.tables[0] + turn_back(query_grad * r.tables[1])
            heads[query_grad_slot, now, :] = query_grad.astype(BF16)
            return 0

        lax.fori_loop(0, half, attend_back, 0)
        advance(TICKS[5])
        lax.fori_loop(half, n, attend_back, 0)

        def kv_hand_over(k):
            return remote(
                heads.at[planes + k], r.kv_other.at[k], r.kv_send.at[k], r.kv_recv.at[k], other_core
            )

        def kv_load(source, slot):
            return local(source, r.kv_some.at[slot], r.kv_sem.at[slot])

        def kv_add(k, slot):
            def some(c, _):
                at = span(c * 64, 64)
                heads[k, at, :] = (
                    heads[k, at, :].astype(F32) + r.kv_some[slot, at, :].astype(F32)
                ).astype(BF16)
                return 0

            lax.fori_loop(0, plane_rows // 64, some, 0)

        def kv_down(k):
            return remote(heads.at[k], r.kv_down.at[k], r.down_send.at[k], r.down_recv.at[k], below)

        def kv_up(k):
            return remote(
                heads.at[planes - k], r.kv_up.at[k], r.up_send.at[k], r.up_recv.at[k], above
            )

        order = list(range(planes - 1, -1, -1))
        for k in order:
            kv_hand_over(k).start()
        for at, k in enumerate(order):
            kv_hand_over(k).wait_recv()
            kv_load(r.kv_other.at[k], at % 2).start()
            kv_load(r.kv_other.at[k], at % 2).wait()
            kv_add(k, at % 2)

        def kv_send(k):
            @pl.when(z >= k)
            def _():
                kv_down(k).start()

            @pl.when(z + k < planes)
            def _():
                kv_up(k).start()

        def kv_receive(k, down_to, up_to):
            @pl.when((z + 1 >= k) & (z + 1 < planes))
            def _():
                kv_down(k).wait_recv()
                if down_to is not None:
                    copy = kv_load(r.kv_down.at[k], 0)
                    copy.start()
                    copy.wait()
                    kv_add(down_to, 0)

            @pl.when((z >= 1) & (z - 1 + k < planes))
            def _():
                kv_up(k).wait_recv()
                if up_to is not None:
                    copy = kv_load(r.kv_up.at[k], 1)
                    copy.start()
                    copy.wait()
                    kv_add(up_to, 1)

        kv_send(3)
        rows_sent(OUT, plane_rows)
        load(work.at[pl.ds(plane_rows, rows)], r.out_own)
        loaded()
        load(r.normed, work.at[pl.ds(plane_rows, plane_rows)])
        low_half, high_half = pl.ds(0, plane_rows), pl.ds(plane_rows, plane_rows)
        advance(TICKS[6])
        turned[0] = heads[attended_slot].astype(F32).T.astype(BF16)
        turned[1] = heads[query_grad_slot].astype(F32).T.astype(BF16)
        loaded()
        outer(query_at, turned[1], high_half)
        outer(output_at, turned[0], low_half)
        advance(TICKS[7])
        kv_receive(3, 2, 2)
        kv_send(2)
        staged(query_at)
        staged(output_at)
        advance(TICKS[8])
        kv_receive(2, 1, 3)
        kv_send(1)
        advance(TICKS[9])
        kv_receive(1, 0, 0)

        def project_back(d):
            now = span(d * pair, pair)
            grad = heads[0, now, :].astype(F32)
            grad = grad * r.tables[2] + turn_back(grad * r.tables[3])
            heads[kv_grad_slot, now, :] = grad.astype(BF16)
            left = jnp.concatenate([heads[query_grad_slot, now, :], grad.astype(BF16)], axis=1)
            for j in range(n):
                put_rows(0, d, matmul_nt(left, feed[0, j, :wide, :]).astype(BF16), blocks[j])

        rows_reduced(ONE, 0, project_back)
        turned[2] = heads[kv_grad_slot].astype(F32).T.astype(BF16)
        outer(kv_at, turned[2], high_half)
        staged(kv_at)
        advance(TICKS[10])

        for d in (1, 2):
            branch_far(d).wait_send()
            branch_half(d).wait_send()
        for d in range(n):
            branch_near(d).wait_send()
        load(r.tokens, r.own_rows)
        rows_arrive(ONE, 0)
        loaded()

        def first_use(at, back):
            r.wide_rows[at, :] = r.wide_rows[at, :] + back

        norm_rows_back(0, r.own_rows, r.gains[0:1, :], first_use)
        load(r.wide_rows, r.tokens_grad)
        gain_terms(0)

        def gain_copy(at, source, target, peer):
            return remote(source, target, r.gain_send.at[at], r.gain_recv.at[at], peer)

        def gain_far(d):
            return gain_copy(d, r.gain_mine.at[d], r.gain_far.at[d], (here, chips[d]))

        def gain_hop(s, peer):
            return gain_copy(n + s, r.gain_sum.at[s], r.gain_in.at[s], peer)

        for d in range(1, n):
            gain_far(d).start()
        advance(TICKS[11])
        for d in range(1, n):
            gain_far(d).wait()
        r.gain_sum[0] = r.gain_mine[0] + r.gain_far[1] + r.gain_far[2] + r.gain_far[3]
        gain_hop(0, other_core).start()
        gain_hop(0, other_core).wait()
        r.gain_sum[1] = r.gain_sum[0] + r.gain_in[0]

        @pl.when(is_end)
        def _():
            gain_hop(1, partner).start()
            gain_hop(1, partner).wait_send()

        advance(TICKS[12])

        @pl.when(is_middle)
        def _():
            gain_hop(1, partner).wait_recv()
            r.gain_sum[2] = r.gain_sum[1] + r.gain_in[1]
            gain_hop(2, other_middle).start()
            gain_hop(2, other_middle).wait()
            r.gain_sum[3] = r.gain_sum[2] + r.gain_in[2]
            gain_hop(3, partner).start()
            gain_hop(3, partner).wait_send()

        @pl.when(is_end)
        def _():
            gain_hop(3, partner).wait_recv()
            r.gain_sum[3] = r.gain_in[3]

        load(r.gain_sum.at[3], r.gain_out)

        loaded()
        load(r.middle, r.wide_rows)
        load(r.out_own, r.own_rows)
        rows_arrive(OUT, plane_rows)
        loaded()

        def last_rows(c, _):
            at = span(c * few, few)
            total = r.wide_rows[at, :] + r.own_rows[at, :].astype(F32)
            for d in range(n):
                total += r.some_rows[d, at, :].astype(F32)
            r.own_rows[at, :] = total.astype(BF16)
            return 0

        lax.fori_loop(0, rows // few, last_rows, 0)
        load(r.own_rows, r.output)
        advance(units + 9 - steps_done[0])

        loaded()
        rows_sent(ONE, 0)
        for q in range(QUARTERS):
            for d in range(1, n):
                feed_copy(q, d).wait_send()
        for d in range(1, n):
            query_far(d).wait_send()
            out_far(d).wait_send()
            token_near(d).wait_send()
            cot_far(d).wait_send()
        token_near(0).wait_send()
        for d in range(n):
            cot_near(d).wait_send()
        for k in range(planes):
            kv_hand_over(k).wait_send()
        for k in range(1, planes):

            @pl.when(z >= k)
            def _():
                kv_down(k).wait_send()

            @pl.when(z + k < planes)
            def _():
                kv_up(k).wait_send()

        finish()

    arrays = jax.tree.leaves((in_hbm, in_vmem))
    results = pl.pallas_call(
        backward,
        out_shape=jax.tree.leaves(out_hbm),
        in_specs=[pl.BlockSpec(memory_space=pl.ANY)] * len(jax.tree.leaves(in_hbm))
        + [pl.BlockSpec(memory_space=pltpu.VMEM)] * len(in_vmem),
        out_specs=[pl.BlockSpec(memory_space=pl.ANY)] * len(out_hbm),
        scratch_shapes=list(scratch.values()),
        cost_estimate=cost(30 * plane_rows * width * part, arrays, [unit_array] * 6),
        compiler_params=pltpu.CompilerParams(
            collective_id=0, has_side_effects=True, vmem_limit_bytes=63 * 1024 * 1024
        ),
        name="backward",
    )(*arrays)
    results = types.SimpleNamespace(**jax.tree.unflatten(jax.tree.structure(out_hbm), results))
    owned_tiles, near_tiles = (
        a.reshape(tiles_count, n, quarter, wide) for a in (results.owned, results.near)
    )

    def place(me_ref, own_ref, near_ref, gate, up, down, query, out, key, value):
        for source, e in ((own_ref, 0), (near_ref, 1)):

            @pl.when(pl.program_id(1) == e)
            def _():
                for q in range(QUARTERS):
                    here = slice(q * quarter, (q + 1) * quarter)
                    down[here, :] = source[3 * q, 0].astype(F32)
                    gate[:, here] = source[3 * q + 1, 0].T.astype(F32)
                    up[:, here] = source[3 * q + 2, 0].T.astype(F32)
                query[...] = source[query_at, 0].T.astype(F32)
                out[...] = source[output_at, 0].astype(F32)

                @pl.when(me_ref[1] == e)
                def _():
                    key[...] = source[kv_at, 0].T.astype(F32)

                @pl.when(me_ref[1] != e)
                def _():
                    value[...] = source[kv_at, 0].T.astype(F32)

    def owner(d, e, me):
        return 2 * (me[0] ^ d) + (me[1] ^ e)

    by_chip = pl.BlockSpec((tiles_count, 1, quarter, wide), lambda d, e, me: (0, d, 0, 0))
    placed = run_grid(
        place,
        me,
        (n, 2),
        [owned_tiles, near_tiles],
        [by_chip, by_chip],
        [
            shape(a.shape, F32)
            for a in (
                gate_weight,
                up_weight,
                down_weight,
                query_weight,
                output_weight,
                key_weight,
                value_weight,
            )
        ],
        [pl.BlockSpec((wide, part), lambda d, e, me: (0, owner(d, e, me)))] * 2
        + [
            pl.BlockSpec((part, wide), lambda d, e, me: (owner(d, e, me), 0)),
            pl.BlockSpec((wide, HD), lambda d, e, me: (0, owner(d, e, me))),
            pl.BlockSpec((HD, wide), lambda d, e, me: (owner(d, e, me), 0)),
        ]
        + [pl.BlockSpec((wide, HD), lambda d, e, me: (0, me[0] ^ d))] * 2,
        name="place",
    )
    gate_grad, up_grad, down_grad, query_grad, output_grad, key_grad, value_grad = placed

    return (
        results.output[None],
        results.tokens_grad[None],
        query_grad,
        key_grad,
        value_grad,
        output_grad,
        results.gain_out[0],
        gate_grad,
        up_grad,
        down_grad,
        results.gain_out[1],
    )


def solution(mesh):
    chips, pieces = mesh.shape["fsdp"], mesh.shape["ctx"]
    one_head_each = 2 * chips == H and chips == KVH and pieces == 8
    return jax.shard_map(
        plane_layer if one_head_each else ring_layer,
        mesh=mesh,
        in_specs=(
            P("fsdp", "ctx", None),
            P("fsdp", None),
            P("fsdp", None),
            P("fsdp", None),
            P(None, "fsdp"),
            P("fsdp"),
            P("fsdp", None),
            P("fsdp", None),
            P(None, "fsdp"),
            P("fsdp"),
            P("fsdp", "ctx", None),
            P(),
            P(),
        ),
        out_specs=(
            P("fsdp", "ctx", None),
            P("fsdp", "ctx", None),
            P("fsdp", None),
            P("fsdp", None),
            P("fsdp", None),
            P(None, "fsdp"),
            P("fsdp"),
            P("fsdp", None),
            P("fsdp", None),
            P(None, "fsdp"),
            P("fsdp"),
        ),
        check_vma=False,
    )
```

```python
import functools
import types

import jax
import jax.numpy as jnp
from jax import lax
from jax.experimental import pallas as pl
from jax.experimental.pallas import tpu as pltpu
from jax.sharding import PartitionSpec as P

H = 8
KVH = 4
HD = 256


epsilon = 1e-06
theta = 1000042.0
masked_score = -1e30


def passed_along(value, axis, by):
    devices = lax.axis_size(axis)
    return lax.ppermute(value, axis, [(i, (i + by) % devices) for i in range(devices)])


def rope_tables(positions):
    half = HD // 2
    frequency = theta ** (-(jnp.arange(half, dtype=jnp.float32) * 2.0 / HD))
    angle = positions[:, None] * frequency[None, :]
    angle = jnp.concatenate([angle, angle], axis=-1)
    return (jnp.cos(angle), jnp.sin(angle))


def rotate(values, cosine, sine):
    half = values.shape[-1] // 2
    turned = jnp.concatenate([-values[..., half:], values[..., :half]], axis=-1)
    return values * cosine[:, None, :] + turned * sine[:, None, :]


def rotate_back(grads, cosine, sine):
    half = grads.shape[-1] // 2
    scaled = grads * sine[:, None, :]
    turned = jnp.concatenate([scaled[..., half:], -scaled[..., :half]], axis=-1)
    return grads * cosine[:, None, :] + turned


def split_heads(block):
    count = block.shape[0]
    key_cols = KVH * HD
    key_part = block[:, :key_cols].reshape(count, KVH, HD).transpose(1, 0, 2)
    value_part = block[:, key_cols:].reshape(count, KVH, HD).transpose(1, 0, 2)
    return (key_part, value_part)


def merge_heads(grouped):
    return grouped.transpose(1, 0, 2).reshape(grouped.shape[1], KVH * HD)


def weight_terms(lefts, rights):
    pieces = []
    for index in range(4):
        column = lefts[index]
        pieces.append(
            jnp.einsum("tc,tn->cn", column, rights[index], preferred_element_type=jnp.float32)
        )
    return jnp.concatenate(pieces, axis=1)


def ring_layer(
    tokens,
    query_weight,
    key_weight,
    value_weight,
    output_weight,
    first_gain,
    gate_weight,
    up_weight,
    down_weight,
    second_gain,
    cotangent,
    block_ids,
    piece_order,
):
    ctx_count = lax.axis_size("ctx")
    fsdp_count = lax.axis_size("fsdp")
    here = lax.axis_index("ctx")
    rows = tokens.shape[1]
    width = tokens.shape[2]
    group = H // KVH
    query_cols = H * HD
    key_cols = KVH * HD
    hidden_cols = gate_weight.shape[1]
    scale = HD ** (-0.5)
    whole_query, whole_key, whole_value, whole_output, gain_one = (
        lax.all_gather(query_weight, "fsdp", axis=0, tiled=True),
        lax.all_gather(key_weight, "fsdp", axis=0, tiled=True),
        lax.all_gather(value_weight, "fsdp", axis=0, tiled=True),
        lax.all_gather(output_weight, "fsdp", axis=1, tiled=True),
        lax.all_gather(first_gain, "fsdp", axis=0, tiled=True),
    )
    id_row = lax.dynamic_index_in_dim(block_ids, lax.axis_index("fsdp"), 0, keepdims=False)
    start_own = lax.dynamic_index_in_dim(piece_order, here, 0, keepdims=False) * rows
    offsets = jnp.arange(rows, dtype=jnp.int32)
    cosine, sine = rope_tables((start_own + offsets).astype(jnp.float32))
    own_ids = lax.dynamic_slice_in_dim(id_row, start_own, rows)
    query_ids = jnp.tile(own_ids, group)

    def visible(source):
        key_start = lax.dynamic_index_in_dim(piece_order, source, 0, keepdims=False) * rows
        key_ids = lax.dynamic_slice_in_dim(id_row, key_start, rows)
        return key_ids[None, :] <= query_ids[:, None]

    inputs = tokens[0].astype(jnp.float32)
    scale_one = lax.rsqrt(jnp.mean(inputs * inputs, axis=-1, keepdims=True) + epsilon)
    unit_one = inputs * scale_one
    normed = (unit_one * gain_one.astype(jnp.float32)).astype(jnp.bfloat16)
    query = jnp.dot(normed, whole_query, preferred_element_type=jnp.float32).reshape(rows, H, HD)
    query_rot = rotate(query, cosine, sine).astype(jnp.bfloat16)
    keys = jnp.dot(normed, whole_key, preferred_element_type=jnp.float32).reshape(rows, KVH, HD)
    keys_rot = rotate(keys, cosine, sine).astype(jnp.bfloat16).reshape(rows, key_cols)
    values = jnp.dot(normed, whole_value, preferred_element_type=jnp.float32).astype(jnp.bfloat16)
    key_value = jnp.concatenate([keys_rot, values], axis=-1)
    grouped = (
        query_rot.reshape(rows, KVH, group, HD).transpose(1, 2, 0, 3).reshape(KVH, group * rows, HD)
    )

    def forward_step(state, block, source):
        running, total, weighted = state
        key_part, value_part = split_heads(block)
        allowed = visible(source)
        scores = (
            jnp.einsum("hqd,hkd->hqk", grouped, key_part, preferred_element_type=jnp.float32)
            * scale
        )
        scores = jnp.where(allowed[None], scores, masked_score)
        newest = jnp.maximum(running, jnp.max(scores, axis=-1))
        factor = jnp.exp(running - newest)
        shares = jnp.where(allowed[None], jnp.exp(scores - newest[..., None]), 0.0)
        total = total * factor + jnp.sum(shares, axis=-1)
        weighted = weighted * factor[..., None] + jnp.einsum(
            "hqk,hkd->hqd",
            shares.astype(jnp.bfloat16),
            value_part,
            preferred_element_type=jnp.float32,
        )
        return (newest, total, weighted)

    start_state = (
        jnp.full((KVH, group * rows), masked_score, jnp.float32),
        jnp.zeros((KVH, group * rows), jnp.float32),
        jnp.zeros((KVH, group * rows, HD), jnp.float32),
    )
    state = forward_step(start_state, key_value, here)

    def forward_turn(turn, carry):
        block, inner = carry
        block = passed_along(block, "ctx", 1)
        source = (here - turn) % ctx_count
        return (block, forward_step(inner, block, source))

    passed_block, state = lax.fori_loop(1, ctx_count, forward_turn, (key_value, state))
    running, total, weighted = state
    attended = weighted / total[..., None]
    log_total = running + jnp.log(total)
    attended_low = (
        attended.reshape(KVH, group, rows, HD)
        .transpose(2, 0, 1, 3)
        .reshape(rows, query_cols)
        .astype(jnp.bfloat16)
    )
    middle = inputs + jnp.dot(attended_low, whole_output, preferred_element_type=jnp.float32)
    gain_two, whole_gate, whole_up, whole_down = (
        lax.all_gather(second_gain, "fsdp", axis=0, tiled=True),
        lax.all_gather(gate_weight, "fsdp", axis=0, tiled=True),
        lax.all_gather(up_weight, "fsdp", axis=0, tiled=True),
        lax.all_gather(down_weight, "fsdp", axis=1, tiled=True),
    )
    scale_two = lax.rsqrt(jnp.mean(middle * middle, axis=-1, keepdims=True) + epsilon)
    unit_two = middle * scale_two
    normed_two = (unit_two * gain_two.astype(jnp.float32)).astype(jnp.bfloat16)
    gate = jnp.dot(normed_two, whole_gate, preferred_element_type=jnp.float32)
    up = jnp.dot(normed_two, whole_up, preferred_element_type=jnp.float32)
    sigmoid_gate = jax.nn.sigmoid(gate)
    activated = gate * sigmoid_gate
    hidden = (activated * up).astype(jnp.bfloat16)
    result = middle + jnp.dot(hidden, whole_down, preferred_element_type=jnp.float32)
    output = result.astype(jnp.bfloat16)[None]
    upstream = cotangent[0]
    hidden_grad = jnp.einsum("tm,fm->tf", upstream, whole_down, preferred_element_type=jnp.float32)
    gate_grad = (hidden_grad * up * sigmoid_gate * (1.0 + gate * (1.0 - sigmoid_gate))).astype(
        jnp.bfloat16
    )
    up_grad = (hidden_grad * activated).astype(jnp.bfloat16)
    normed_two_grad = jnp.einsum(
        "tf,mf->tm", gate_grad, whole_gate, preferred_element_type=jnp.float32
    ) + jnp.einsum("tf,mf->tm", up_grad, whole_up, preferred_element_type=jnp.float32)
    gain_two_term = jnp.sum(normed_two_grad * unit_two, axis=0)
    unit_two_grad = normed_two_grad * gain_two.astype(jnp.float32)
    middle_grad = upstream.astype(jnp.float32) + scale_two * (
        unit_two_grad - unit_two * jnp.mean(unit_two_grad * unit_two, axis=-1, keepdims=True)
    )
    branch_grad = middle_grad.astype(jnp.bfloat16)
    attended_grad = jnp.einsum(
        "tm,cm->tc", branch_grad, whole_output, preferred_element_type=jnp.float32
    ).astype(jnp.bfloat16)
    grad_grouped = (
        attended_grad.reshape(rows, KVH, group, HD)
        .transpose(1, 2, 0, 3)
        .reshape(KVH, group * rows, HD)
    )
    delta = jnp.sum(grad_grouped.astype(jnp.float32) * attended, axis=-1)

    def backward_step(query_total, block, source):
        key_part, value_part = split_heads(block)
        allowed = visible(source)
        scores = (
            jnp.einsum("hqd,hkd->hqk", grouped, key_part, preferred_element_type=jnp.float32)
            * scale
        )
        scores = jnp.where(allowed[None], scores, masked_score)
        shares = jnp.where(allowed[None], jnp.exp(scores - log_total[..., None]), 0.0)
        value_grad = jnp.einsum(
            "hqk,hqd->hkd",
            shares.astype(jnp.bfloat16),
            grad_grouped,
            preferred_element_type=jnp.float32,
        )
        share_grad = jnp.einsum(
            "hqd,hkd->hqk", grad_grouped, value_part, preferred_element_type=jnp.float32
        )
        score_grad = (shares * (share_grad - delta[..., None])).astype(jnp.bfloat16)
        query_total = query_total + jnp.einsum(
            "hqk,hkd->hqd", score_grad, key_part, preferred_element_type=jnp.float32
        )
        key_grad = (
            jnp.einsum("hqk,hqd->hkd", score_grad, grouped, preferred_element_type=jnp.float32)
            * scale
        )
        return (
            query_total,
            jnp.concatenate([merge_heads(key_grad), merge_heads(value_grad)], axis=-1),
        )

    query_total, first_grad = backward_step(
        jnp.zeros((KVH, group * rows, HD), jnp.float32), key_value, here
    )
    held = first_grad

    def backward_turn(turn, carry):
        block, kept, total_query = carry
        block = passed_along(block, "ctx", 1)
        source = (here - turn) % ctx_count
        total_query, block_grad = backward_step(total_query, block, source)
        kept = passed_along(kept.astype(jnp.bfloat16), "ctx", 1).astype(kept.dtype) + block_grad
        return (block, kept, total_query)

    passed_again, held, query_total = lax.fori_loop(
        1, ctx_count, backward_turn, (key_value, held, query_total)
    )
    own_grad = passed_along(held.astype(jnp.bfloat16), "ctx", 1).astype(held.dtype)
    query_rot_grad = (
        (query_total * scale)
        .reshape(KVH, group, rows, HD)
        .transpose(2, 0, 1, 3)
        .reshape(rows, H, HD)
    )
    query_grad = (
        rotate_back(query_rot_grad, cosine, sine).reshape(rows, query_cols).astype(jnp.bfloat16)
    )
    key_grad = (
        rotate_back(own_grad[:, :key_cols].reshape(rows, KVH, HD), cosine, sine)
        .reshape(rows, key_cols)
        .astype(jnp.bfloat16)
    )
    value_grad = own_grad[:, key_cols:].astype(jnp.bfloat16)
    normed_grad = jnp.einsum(
        "tc,mc->tm", query_grad, whole_query, preferred_element_type=jnp.float32
    )
    normed_grad = normed_grad + jnp.einsum(
        "tc,mc->tm", key_grad, whole_key, preferred_element_type=jnp.float32
    )
    normed_grad = normed_grad + jnp.einsum(
        "tc,mc->tm", value_grad, whole_value, preferred_element_type=jnp.float32
    )
    gain_one_term = jnp.sum(normed_grad * unit_one, axis=0)
    unit_one_grad = normed_grad * gain_one.astype(jnp.float32)
    tokens_grad = middle_grad + scale_one * (
        unit_one_grad - unit_one * jnp.mean(unit_one_grad * unit_one, axis=-1, keepdims=True)
    )
    projected = jnp.concatenate([query_grad, key_grad, value_grad], axis=-1)
    gate_up = jnp.concatenate([gate_grad, up_grad], axis=-1)
    lefts = jnp.stack([normed, branch_grad, normed_two, upstream])
    rights = (projected, attended_low, gate_up, hidden)
    piece = lax.psum_scatter(
        weight_terms(lefts, rights).astype(jnp.bfloat16), "fsdp", scatter_dimension=0, tiled=True
    )
    shard = lax.psum(piece, "ctx").astype(jnp.float32)
    gain_one_sum, gain_two_sum = lax.psum((gain_one_term, gain_two_term), ("ctx", "fsdp"))
    own_rows = width // fsdp_count
    own_start = lax.axis_index("fsdp") * own_rows
    value_begin = query_cols + key_cols
    output_begin = value_begin + key_cols
    gate_begin = output_begin + query_cols
    up_begin = gate_begin + hidden_cols
    down_begin = up_begin + hidden_cols
    return (
        output,
        tokens_grad[None],
        shard[:, :query_cols],
        shard[:, query_cols:value_begin],
        shard[:, value_begin:output_begin],
        shard[:, output_begin:gate_begin].T,
        lax.dynamic_slice_in_dim(gain_one_sum, own_start, own_rows),
        shard[:, gate_begin:up_begin],
        shard[:, up_begin:down_begin],
        shard[:, down_begin : down_begin + hidden_cols].T,
        lax.dynamic_slice_in_dim(gain_two_sum, own_start, own_rows),
    )


VMEM_BYTES = 58 * 1024 * 1024
BF16 = jnp.bfloat16
F32 = jnp.float32
QUARTERS = 4
MESH = pl.DeviceIdType.MESH
TICKS = (2, 1, 2, 2, 3, 2, 1, 1, 1, 2, 4, 2, 2)
LINES = 2


def matmul(a, b):
    return lax.dot_general(a, b, (((1,), (0,)), ((), ())), preferred_element_type=F32)


def matmul_nt(a, b):
    return lax.dot_general(a, b, (((1,), (1,)), ((), ())), preferred_element_type=F32)


def matmul_tn(a, b):
    return lax.dot_general(a, b, (((0,), (0,)), ((), ())), preferred_element_type=F32)


def cost(flops, arrays, outs, exps=0):
    moved = sum(a.size * a.dtype.itemsize for a in arrays) + sum(
        o.size * o.dtype.itemsize for o in outs
    )
    return pl.CostEstimate(flops=int(flops), bytes_accessed=int(moved), transcendentals=int(exps))


def run_whole(body, me, arrays, outs, scratch=(), flops=0, in_hbm=0, name=None):
    count = len(arrays) - in_hbm
    return pl.pallas_call(
        body,
        out_shape=outs,
        in_specs=[pl.BlockSpec(memory_space=pltpu.SMEM)]
        + [pl.BlockSpec(memory_space=pltpu.VMEM)] * count
        + [pl.BlockSpec(memory_space=pl.ANY)] * in_hbm,
        out_specs=jax.tree.map(lambda _: pl.BlockSpec(memory_space=pltpu.VMEM), outs),
        scratch_shapes=list(scratch),
        cost_estimate=cost(flops, arrays, jax.tree.leaves(outs)),
        compiler_params=pltpu.CompilerParams(vmem_limit_bytes=VMEM_BYTES),
        name=name,
    )(me, *arrays)


def run_grid(body, me, grid, arrays, in_specs, outs, out_specs, scratch=(), flops=0, aliases=None, name=None):
    return pl.pallas_call(
        body,
        out_shape=outs,
        grid_spec=pltpu.PrefetchScalarGridSpec(
            num_scalar_prefetch=1,
            grid=grid,
            in_specs=in_specs,
            out_specs=out_specs,
            scratch_shapes=list(scratch),
        ),
        cost_estimate=cost(flops, arrays, jax.tree.leaves(outs)),
        input_output_aliases=aliases or {},
        compiler_params=pltpu.CompilerParams(vmem_limit_bytes=VMEM_BYTES),
        name=name,
    )(me, *arrays)


def shape(dims, kind=BF16):
    return jax.ShapeDtypeStruct(tuple(dims), kind)


def fixed(block):
    return pl.BlockSpec(block, lambda i, me: (0,) * len(block), pipeline_mode=pl.Buffered(1))


def column(index, wide):
    return pl.ds(pl.multiple_of(index * wide, wide), wide)


def turn(values):
    half = values.shape[-1] // 2
    return jnp.concatenate([-values[:, half:], values[:, :half]], axis=-1)


def turn_back(values):
    half = values.shape[-1] // 2
    return jnp.concatenate([values[:, half:], -values[:, :half]], axis=-1)


def plane_layer(
    tokens,
    query_weight,
    key_weight,
    value_weight,
    output_weight,
    first_gain,
    gate_weight,
    up_weight,
    down_weight,
    second_gain,
    cotangent,
    block_ids,
    piece_order,
):
    ctx_count = lax.axis_size("ctx")
    n = lax.axis_size("fsdp")
    planes = ctx_count // 2
    ctx = lax.axis_index("ctx")
    z, core = ctx // 2, ctx % 2
    f = lax.axis_index("fsdp")
    me = jnp.stack([f, core]).astype(jnp.int32)
    rows, width = tokens.shape[1:]
    pair = 2 * rows
    plane_rows = n * pair
    wide = width // n
    hidden_cols = gate_weight.shape[1]
    part = hidden_cols // (2 * n)
    quarter = part // QUARTERS
    scale = HD ** (-0.5)

    def across(value, d):
        return lax.ppermute(value, "fsdp", [(i, i ^ d) for i in range(n)])

    def sibling(value):
        return lax.ppermute(value, "ctx", [(i, i ^ 1) for i in range(ctx_count)])

    def along(value, step):
        pairs = [(i, i + 2 * step) for i in range(ctx_count)]
        return lax.ppermute(value, "ctx", [(a, b) for a, b in pairs if 0 <= b < ctx_count])

    def between_planes(value, moves):
        return lax.ppermute(
            value, "ctx", [(2 * a + side, 2 * b + side) for a, b in moves for side in range(2)]
        )

    def gathered(value):
        own = [value] + [across(value, d) for d in range(1, n)]
        return own, [sibling(block) for block in own]

    def reduced(own, other):
        near = [sibling(block) for block in other]
        sent = [
            across((own[d].astype(F32) + near[d].astype(F32)).astype(BF16), d) for d in range(1, n)
        ]
        return [own[0], near[0]] + sent

    middle_left, middle_right = planes // 2 - 1, planes // 2
    folds = [
        [(s, s + 1), (planes - 1 - s, planes - 2 - s)] for s in range(middle_left)
    ]

    def summed_over_planes(value):
        for moves in folds:
            value = (
                value.astype(F32) + between_planes(value, moves).astype(F32)
            ).astype(value.dtype)
        crossed = between_planes(value, [(middle_left, middle_right), (middle_right, middle_left)])
        value = (value.astype(F32) + crossed.astype(F32)).astype(value.dtype)
        for s, moves in reversed(list(enumerate(folds))):
            back = between_planes(value, [(b, a) for a, b in moves])
            receives = (z == s) | (z == planes - 1 - s)
            value = jnp.where(receives, back, value)
        return value

    place = jnp.arange(rows, dtype=jnp.int32)
    own_pieces = lax.dynamic_slice_in_dim(piece_order, 2 * z, 2)
    positions = (own_pieces[:, None] * rows + place[None, :]).reshape(pair).astype(F32)
    cosine, sine = rope_tables(positions)
    is_value = core == 1
    kv_cosine = jnp.where(is_value, 1.0, cosine)
    kv_sine = jnp.where(is_value, 0.0, sine)
    chips = f ^ jnp.arange(n, dtype=jnp.int32)
    ring = (z - jnp.arange(planes, dtype=jnp.int32)) % planes
    ring_ctx = (2 * ring[:, None] + jnp.arange(2, dtype=jnp.int32)[None, :]).reshape(-1)
    id_pieces = block_ids.reshape(n, ctx_count, rows)
    ids = id_pieces[chips[:, None], piece_order[ring_ctx][None, :]]
    key_ids = ids.reshape(n, planes, 1, pair)
    query_ids = ids[:, :2].reshape(n, pair, 1)

    def cut_weights(me_ref, *refs):
        keys, values, (one, two), outs = refs[:n], refs[n : 2 * n], refs[2 * n : 2 * n + 2], refs[2 * n + 2 :]
        keys_here = me_ref[1] == 0
        for d in range(n):

            @pl.when(keys_here)
            def _():
                outs[d][:wide, :] = keys[d][...]

            @pl.when(jnp.logical_not(keys_here))
            def _():
                outs[d][:wide, :] = values[d][...]

            pick = lax.broadcasted_iota(jnp.int32, (16, HD), 0) < 8
            for g, gain in enumerate((one, two)):
                halves = [gain[:, h * HD : (h + 1) * HD].astype(F32) for h in range(2)]
                outs[d][wide + 16 * g : wide + 16 * (g + 1), :] = jnp.where(pick, *halves).astype(BF16)

    def chip_of(d):
        return lambda i, me: (0, me[0] ^ d)

    own_tokens = tokens[0]
    near_tokens = [own_tokens] + [across(own_tokens, d) for d in (1, 2)]
    gain_spec = pl.BlockSpec((1, wide), lambda i, me: (0, 0))
    cut = run_grid(
        cut_weights,
        me,
        (1,),
        [key_weight] * n
        + [value_weight] * n
        + [first_gain.reshape(1, wide), second_gain.reshape(1, wide)],
        [pl.BlockSpec((wide, HD), chip_of(d)) for d in range(n)] * 2 + [gain_spec, gain_spec],
        [shape((wide + 32, HD))] * n,
        [pl.BlockSpec((wide + 32, HD), lambda i, me: (0, 0))] * n,
        name="cut_weights",
    )
    weights_in = [cut[0]] + [across(cut[d], d) for d in range(1, n)]
    piece = (wide + quarter, 2 * quarter)
    own_cotangent = cotangent[0]
    block = (rows, width)

    tiles_count = 3 * QUARTERS + 3
    query_at, output_at, kv_at = tiles_count - 3, tiles_count - 2, tiles_count - 1
    units = 2 * tiles_count
    unit = (2, quarter, wide)
    held_sums, held_ends, ahead = 4, 3, 2
    MID, BACK, OUT, ONE = range(4)
    query_slot, attended_slot, query_grad_slot, kv_grad_slot = range(2 * planes, 2 * planes + 4)
    kept_slots = 2 * planes + 2
    columns = (plane_rows, HD)
    lanes = (8, wide)
    dma = pltpu.SemaphoreType.DMA

    in_hbm = dict(
        near_tokens=near_tokens,
        in_weight=weights_in,
        query_weight=query_weight,
        output_weight=output_weight,
        gate_weight=gate_weight,
        up_weight=up_weight,
        down_weight=down_weight,
        cotangent=own_cotangent,
        tokens=own_tokens,
    )
    in_vmem = dict(
        tables=jnp.stack([cosine, sine, kv_cosine, kv_sine]),
        query_ids=query_ids,
        key_ids=key_ids,
    )
    unit_array = shape((units,) + unit)
    out_hbm = dict(
        tiles=unit_array,
        from_end=unit_array,
        from_middle=unit_array,
        finals=unit_array,
        owned=unit_array,
        near=unit_array,
        row_near=shape((4, n) + block),
        row_far=shape((4, n) + block),
        cot_all=shape((2, n) + block),
        query_in=shape((n, wide, HD)),
        kept=shape((kept_slots,) + columns),
        out_weight=shape((2, 2, HD, wide)),
        normed=shape((plane_rows, width)),
        middle=shape(block, F32),
        branch_all=shape((n, 2) + block),
        kv_other=shape((planes,) + columns),
        kv_down=shape((planes,) + columns),
        kv_up=shape((planes,) + columns),
        out_own=shape(block),
        tokens_grad=shape(block, F32),
        output=shape(block),
        gain_out=shape(lanes, F32),
    )
    scratch = dict(
        work=pltpu.VMEM((2 * plane_rows, width), BF16),
        feed=pltpu.VMEM((QUARTERS, n) + piece, BF16),
        heads=pltpu.VMEM((3 * QUARTERS, plane_rows, HD), BF16),
        turned=pltpu.VMEM((3, HD, plane_rows), BF16),
        stage=pltpu.VMEM((2, n, quarter, wide), BF16),
        mine=pltpu.VMEM((2,) + unit, BF16),
        theirs=pltpu.VMEM((2,) + unit, BF16),
        crossed=pltpu.VMEM((2,) + unit, BF16),
        sums=pltpu.VMEM((held_sums,) + unit, BF16),
        ends=pltpu.VMEM((held_ends,) + unit, BF16),
        some_rows=pltpu.VMEM((n,) + block, BF16),
        wide_rows=pltpu.VMEM(block, F32),
        own_rows=pltpu.VMEM(block, BF16),
        kv_some=pltpu.VMEM((2,) + columns, BF16),
        flat=pltpu.VMEM((8, width), F32),
        gain_mine=pltpu.VMEM((n,) + lanes, F32),
        gain_far=pltpu.VMEM((n,) + lanes, F32),
        gain_sum=pltpu.VMEM((4,) + lanes, F32),
        gain_in=pltpu.VMEM((4,) + lanes, F32),
        load_sem=dma((4 * n + n,)),
        gains=pltpu.VMEM((8, width), F32),
        gain_rows=pltpu.VMEM((n, 32, HD), BF16),
        feed_local=dma((3 * QUARTERS,)),
        feed_send=dma((3 * QUARTERS * n,)),
        feed_recv=dma((3 * QUARTERS * n,)),
        stage_sem=dma((2, 2)),
        one_send=dma((units,)),
        one_recv=dma((units,)),
        two_send=dma((units,)),
        two_recv=dma((units,)),
        three_send=dma((units,)),
        three_recv=dma((units,)),
        mine_sem=dma((2,)),
        theirs_sem=dma((2,)),
        crossed_sem=dma((2,)),
        final_sem=dma((held_ends,)),
        deal_local=dma((units,)),
        deal_send=dma((2 * units,)),
        deal_recv=dma((2 * units,)),
        sib_send=dma((units,)),
        sib_recv=dma((units,)),
        row_sem=dma((n,)),
        row_near_send=dma((4 * n,)),
        row_near_recv=dma((4 * n,)),
        row_far_send=dma((4 * n,)),
        row_far_recv=dma((4 * n,)),
        token_send=dma((n,)),
        token_recv=dma((n,)),
        query_send=dma((n,)),
        query_recv=dma((n,)),
        out_send=dma((n,)),
        out_recv=dma((n,)),
        cot_send=dma((n,)),
        cot_recv=dma((n,)),
        cot_near_send=dma((n,)),
        cot_near_recv=dma((n,)),
        two_local=dma((1,)),
        two_far_send=dma((n,)),
        two_far_recv=dma((n,)),
        two_near_send=dma((n,)),
        two_near_recv=dma((n,)),
        two_half_send=dma((n,)),
        two_half_recv=dma((n,)),
        branch_half_send=dma((n,)),
        branch_half_recv=dma((n,)),
        climb_send=dma((n * planes,)),
        climb_recv=dma((n * planes,)),
        fall_send=dma((n * planes,)),
        fall_recv=dma((n * planes,)),
        soft=pltpu.VMEM((2 * n, pair, 1), F32),
        pass_send=dma((n * planes,)),
        pass_recv=dma((n * planes,)),
        cot_half_send=dma((n,)),
        cot_half_recv=dma((n,)),
        share_send=dma((2 * n,)),
        share_recv=dma((2 * n,)),
        token_half_send=dma((n,)),
        token_half_recv=dma((n,)),
        keep_sem=dma((3,)),
        branch_local=dma((1,)),
        branch_send=dma((n,)),
        branch_recv=dma((n,)),
        branch_near_send=dma((n,)),
        branch_near_recv=dma((n,)),
        kv_sem=dma((2,)),
        kv_send=dma((planes,)),
        kv_recv=dma((planes,)),
        down_send=dma((planes,)),
        down_recv=dma((planes,)),
        up_send=dma((planes,)),
        up_recv=dma((planes,)),
        gain_send=dma((n + 4,)),
        gain_recv=dma((n + 4,)),
    )

    def backward(*refs):
        r, first = types.SimpleNamespace(), 0
        for group in (in_hbm, in_vmem, out_hbm):
            leaves, form = jax.tree.flatten(group)
            vars(r).update(jax.tree.unflatten(form, refs[first : first + len(leaves)]))
            first += len(leaves)
        vars(r).update(zip(scratch, refs[first:]))
        here = lax.axis_index("ctx")
        chip = lax.axis_index("fsdp")
        z, side = here // 2, here % 2
        is_middle = (z == 1) | (z == 2)
        is_end = jnp.logical_not(is_middle)
        chips = [chip, chip + 1 - 2 * (chip % 2), (chip + 2) % 4, 3 - chip]
        partner = (2 * (z + 1 - 2 * (z % 2)) + side, chip)
        other_middle = (2 * (3 - z) + side, chip)
        other_core = (here + 1 - 2 * side, chip)
        below, above = (here - 2, chip), (here + 2, chip)
        blocks = [pl.ds(pl.multiple_of(c * wide, wide), wide) for c in chips]
        work, feed, heads, turned, stage = r.work, r.feed, r.heads, r.turned, r.stage

        barrier = pltpu.get_barrier_semaphore()
        for peer in [(here, c) for c in chips[1:]] + [partner, other_core]:
            pl.semaphore_signal(barrier, inc=1, device_id=peer, device_id_type=MESH)

        @pl.when(is_middle)
        def _():
            pl.semaphore_signal(barrier, inc=1, device_id=other_middle, device_id_type=MESH)
            pl.semaphore_wait(barrier, n + 2)

        @pl.when(is_end)
        def _():
            pl.semaphore_wait(barrier, n + 1)

        def remote(source, target, send, recv, peer):
            return pltpu.make_async_remote_copy(
                src_ref=source,
                dst_ref=target,
                send_sem=send,
                recv_sem=recv,
                device_id=peer,
                device_id_type=MESH,
            )

        local = pltpu.make_async_copy

        def span(first, count):
            return pl.ds(pl.multiple_of(first, count), count)

        def head_of(d):
            return span((2 * chips[d] + side) * HD, HD)

        def feed_parts(q, d, first=0, count=wide):
            there = span(((2 * chips[d] + side) * QUARTERS + q) * quarter, quarter)
            rows_in = pl.ds(first, count)
            below = 0 if count == wide else pl.multiple_of(first // 2, quarter // 2)
            some = pl.ds(
                pl.multiple_of(
                    ((2 * chips[d] + side) * QUARTERS + q) * quarter + below, quarter // 2
                ),
                count // 2,
            )
            below = wide if count == wide else pl.multiple_of(wide + below, quarter // 2)
            return (
                (r.gate_weight.at[rows_in, there], feed.at[q, d, rows_in, pl.ds(0, quarter)]),
                (r.up_weight.at[rows_in, there], feed.at[q, d, rows_in, pl.ds(quarter, quarter)]),
                (r.down_weight.at[some], feed.at[q, d, pl.ds(below, count // 2)]),
            )

        def feed_far(q, d, *rows_of):
            copies = []
            for part, (source, target) in enumerate(feed_parts(q, d, *rows_of)):
                at = (q * n + d) * 3 + part
                copies.append(
                    remote(source, target, r.feed_send.at[at], r.feed_recv.at[at], (here, chips[d]))
                )
            return copies

        def feed_own(q):
            return [
                local(source, target, r.feed_local.at[3 * q + part])
                for part, (source, target) in enumerate(feed_parts(q, 0))
            ]

        def every(copies, use):
            for copy in copies:
                use(copy)

        starts, waits = lambda c: c.start(), lambda c: c.wait()
        arrives, leaves = lambda c: c.wait_recv(), lambda c: c.wait_send()

        def hop_one(i):
            return remote(r.tiles.at[i], r.from_end.at[i], r.one_send.at[i], r.one_recv.at[i], partner)

        def hop_two(i):
            return remote(
                r.sums.at[i % held_sums],
                r.from_middle.at[i],
                r.two_send.at[i],
                r.two_recv.at[i],
                other_middle,
            )

        def hop_three(i):
            return remote(
                r.ends.at[i % held_ends], r.finals.at[i], r.three_send.at[i], r.three_recv.at[i], partner
            )

        def load_mine(i):
            return local(r.tiles.at[i], r.mine.at[i % 2], r.mine_sem.at[i % 2])

        def load_theirs(i):
            return local(r.from_end.at[i], r.theirs.at[i % 2], r.theirs_sem.at[i % 2])

        def load_crossed(i):
            return local(r.from_middle.at[i], r.crossed.at[i % 2], r.crossed_sem.at[i % 2])

        def keep_final(i):
            return local(r.ends.at[i % held_ends], r.finals.at[i], r.final_sem.at[i % held_ends])

        def keep_own(i):
            return local(r.finals.at[i, 0], r.owned.at[i, 0], r.deal_local.at[i])

        def deal_to(i, b, d):
            at = 2 * i + b
            return remote(
                r.finals.at[i, b],
                r.owned.at[i, b],
                r.deal_send.at[at],
                r.deal_recv.at[at],
                (here, chips[d]),
            )

        def to_sibling(i):
            return remote(r.owned.at[i], r.near.at[i], r.sib_send.at[i], r.sib_recv.at[i], other_core)

        def add(target, a, b):
            def some(s, _):
                at = (s // 4, span((s % 4) * (quarter // 4), quarter // 4))
                target[at] = a[at] + b[at]
                return 0

            lax.fori_loop(0, 8, some, 0)

        def when_in(i, *conditions):
            return pl.when(functools.reduce(jnp.logical_and, conditions, (i >= 0) & (i < units)))

        def step(i, _=0):
            @when_in(i + ahead, is_end, i >= 0)
            def _():
                hop_one(i + ahead).start()

            @when_in(i - 1, is_middle)
            def _():
                at = i - 1
                load_mine(at).wait()
                load_theirs(at).wait()

                @pl.when(at >= held_sums)
                def _():
                    hop_two(at - held_sums).wait_send()

                add(r.sums.at[at % held_sums], r.mine.at[at % 2], r.theirs.at[at % 2])
                hop_two(at).start()

            @when_in(i - 4, is_middle)
            def _():
                at = i - 4
                load_crossed(at).wait()

                @pl.when(at >= held_ends)
                def _():
                    hop_three(at - held_ends).wait_send()

                add(r.ends.at[at % held_ends], r.sums.at[at % held_sums], r.crossed.at[at % 2])
                hop_three(at).start()
                keep_final(at).start()

            @when_in(i, is_middle)
            def _():
                hop_one(i).wait_recv()
                load_mine(i).start()
                load_theirs(i).start()

            @when_in(i - 3, is_middle)
            def _():
                hop_two(i - 3).wait_recv()
                load_crossed(i - 3).start()

            @when_in(i - 6)
            def _():
                at = i - 6

                @pl.when(is_middle)
                def _():
                    keep_final(at).wait()

                @pl.when(is_end)
                def _():
                    hop_three(at).wait_recv()

                @pl.when(at % 2 == 0)
                def _():
                    keep_own(at).start()
                    deal_to(at, 1, 1).start()

                @pl.when(at % 2 == 1)
                def _():
                    deal_to(at, 0, 2).start()
                    deal_to(at, 1, 3).start()

            @when_in(i - 9)
            def _():
                at = i - 9

                @pl.when(at % 2 == 0)
                def _():
                    keep_own(at).wait()

                @pl.when(at % 2 == 1)
                def _():
                    deal_to(at, 0, 2).wait_recv()

                deal_to(at, 1, 3).wait_recv()
                to_sibling(at).start()

            return 0

        steps_done = [0]

        def advance(count):
            first = steps_done[0]
            steps_done[0] = first + count
            lax.fori_loop(first, first + count, step, 0)

        def finish():
            def one(i, _):
                @pl.when(is_end)
                def _():
                    hop_one(i).wait_send()

                @pl.when(is_middle & (i >= units - held_sums))
                def _():
                    hop_two(i).wait_send()

                @pl.when(is_middle & (i >= units - held_ends))
                def _():
                    hop_three(i).wait_send()

                @pl.when(i % 2 == 1)
                def _():
                    deal_to(i, 0, 2).wait_send()

                deal_to(i, 1, 3).wait_send()
                to_sibling(i).wait()
                return 0

            lax.fori_loop(0, units, one, 0)

        def stage_copy(t, h):
            return local(r.stage.at[t % 2, pl.ds(2 * h, 2)], r.tiles.at[2 * t + h], r.stage_sem.at[t % 2, h])

        def staged(t):
            for h in range(2):
                stage_copy(t, h).wait()

            @pl.when(is_end & (t == 0))
            def _():
                for i in range(ahead):
                    hop_one(i).start()

        def outer(t, left, right_rows):
            for j in range(n):
                stage[t % 2, j] = matmul(left, work[right_rows, blocks[j]]).astype(BF16)
            for h in range(2):
                stage_copy(t, h).start()

        def row_near(s, base, d):
            at = s * n + d
            return remote(
                work.at[pl.ds(base + (2 * d + 1) * rows, rows)],
                r.row_near.at[s, d],
                r.row_near_send.at[at],
                r.row_near_recv.at[at],
                other_core,
            )

        def row_far(s, base, d):
            at = s * n + d
            return remote(
                work.at[pl.ds(base + 2 * d * rows, rows)],
                r.row_far.at[s, d],
                r.row_far_send.at[at],
                r.row_far_recv.at[at],
                (here, chips[d]),
            )

        def near_load(s, d):
            return local(r.row_near.at[s, d], r.some_rows.at[d], r.row_sem.at[d])

        def far_load(s, d):
            return local(r.row_far.at[s, d], r.some_rows.at[d], r.row_sem.at[d])

        few = 16

        def row_send(s, base, d):
            row_near(s, base, d).wait_recv()
            near_load(s, d).start()
            near_load(s, d).wait()

            def some(c, _):
                at = span(c * few, few)
                own = pl.ds(pl.multiple_of(base + 2 * d * rows + c * few, few), few)
                work[own, :] = work[own, :] + r.some_rows[d, at, :]
                return 0

            lax.fori_loop(0, rows // few, some, 0)
            row_far(s, base, d).start()

        far_first = (1, 2, 3, 0)

        def rows_reduced(s, base, compute, send=True, ticks=0):
            def one(i, _):
                d = (i + 1) % n
                compute(d)
                for at in range(n):

                    @pl.when(i == at)
                    def _():
                        row_near(s, base, far_first[at]).start()
                        if send and at > 0:
                            row_send(s, base, far_first[at - 1])

                if ticks:

                    @pl.when(i >= n - ticks)
                    def _():
                        step(first + i - (n - ticks))

                return 0

            first = steps_done[0]
            steps_done[0] = first + ticks
            lax.fori_loop(0, n, one, 0)

        def rows_arrive(s, base):
            row_near(s, base, 0).wait_recv()
            near_load(s, 0).start()
            for d in range(1, n):
                row_far(s, base, d).wait_recv()
                far_load(s, d).start()
            near_load(s, 0).wait()
            for d in range(1, n):
                far_load(s, d).wait()

        def rows_sent(s, base):
            for d in range(n):
                row_near(s, base, d).wait_send()
            for d in range(1, n):
                row_far(s, base, d).wait_send()

        def norm_rows_back(base, value_ref, gain_row, use):
            r.flat[...] = jnp.zeros_like(r.flat)

            def some(c, _):
                at = span(c * few, few)
                grad = work[pl.ds(pl.multiple_of(base + c * few, few), few), :].astype(F32)
                for d in range(n):
                    grad += r.some_rows[d, at, :].astype(F32)
                values = value_ref[at, :].astype(F32)
                inverse = lax.rsqrt(jnp.mean(values * values, axis=-1, keepdims=True) + epsilon)
                unit_rows = values * inverse
                scaled = grad * gain_row
                back = inverse * (
                    scaled - unit_rows * jnp.mean(scaled * unit_rows, axis=-1, keepdims=True)
                )
                use(at, back)
                terms = grad * unit_rows
                r.flat[...] += terms[:8] + terms[8:]
                return 0

            lax.fori_loop(0, rows // few, some, 0)

        def gain_terms(at):
            total = jnp.sum(r.flat[...], axis=0, keepdims=True)
            r.flat[0:1, :] = total
            for j in range(n):
                r.gain_mine[j, at : at + 1, :] = r.flat[0:1, blocks[j]]

        r.gain_mine[...] = jnp.zeros_like(r.gain_mine)
        loads = []

        def load(source, target):
            copy = local(source, target, r.load_sem.at[len(loads)])
            copy.start()
            loads.append(copy)

        def loaded():
            while loads:
                loads.pop().wait()

        def out_far(d):
            return remote(
                r.output_weight.at[head_of(d)],
                r.theirs.at[d // 2, d % 2],
                r.out_send.at[d],
                r.out_recv.at[d],
                (here, chips[d]),
            )

        def cot_far(d):
            return remote(
                r.cotangent, r.cot_all.at[0, d], r.cot_send.at[d], r.cot_recv.at[d], (here, chips[d])
            )

        def cot_near(d):
            source = r.cotangent if d == 0 else r.cot_all.at[0, d]
            return remote(
                source, r.cot_all.at[1, d], r.cot_near_send.at[d], r.cot_near_recv.at[d], other_core
            )

        def query_far(d):
            return remote(
                r.query_weight.at[:, head_of(d)],
                r.query_in.at[d],
                r.query_send.at[d],
                r.query_recv.at[d],
                (here, chips[d]),
            )

        def kv_piece(j):
            return r.kv_some.at[j // 3, pl.ds(j % 3 * wide, wide)]

        def query_piece(j):
            return heads.at[query_grad_slot + j // 3, pl.ds(j % 3 * wide, wide)]

        half_rows = rows // 2

        def cot_half(d):
            some = pl.ds((d - 1) * half_rows, half_rows)
            return remote(
                r.cot_all.at[0, d, some],
                r.cot_all.at[0, 3, some],
                r.cot_half_send.at[d],
                r.cot_half_recv.at[d],
                (here, chips[3 - d]),
            )

        parity = z % 2

        def feed_half(d):
            return feed_far(0, d, pl.multiple_of(parity * (wide // 2), wide // 2), wide // 2)

        def feed_share(d):
            copies = []
            for part, (first, count) in enumerate(((0, wide // 2), (wide, quarter // 2))):
                some = feed.at[0, d, span(first + parity * count, count)]
                at = 2 * d + part
                copies.append(remote(some, some, r.share_send.at[at], r.share_recv.at[at], partner))
            return copies

        def token_near(d):
            source = work.at[pl.ds(plane_rows + 2 * d * rows, rows)] if d == 3 else r.near_tokens[d]
            return remote(
                source,
                work.at[pl.ds(plane_rows + (2 * d + 1) * rows, rows)],
                r.token_send.at[d],
                r.token_recv.at[d],
                other_core,
            )

        def token_half(d):
            return remote(
                r.near_tokens[d].at[pl.ds((d - 1) * half_rows, half_rows)],
                work.at[pl.ds(plane_rows + 6 * rows + (d - 1) * half_rows, half_rows)],
                r.token_half_send.at[d],
                r.token_half_recv.at[d],
                (here, chips[3 - d]),
            )

        for d in (1, 2):
            token_half(d).start()
        for d in range(1, n):
            query_far(d).start()
        for d in range(1, n):
            out_far(d).start()
        cot_near(0).start()
        for d in range(n - 1):
            token_near(d).start()
            load(r.near_tokens[d], work.at[pl.ds(plane_rows + 2 * d * rows, rows)])
        for j in range(n):
            load(r.in_weight[j].at[pl.ds(0, wide)], kv_piece(j))
            load(r.in_weight[j].at[pl.ds(wide, 32)], r.gain_rows.at[j])
        loaded()
        load(r.output_weight.at[head_of(0)], r.theirs.at[0, 0])
        load(r.query_weight.at[:, head_of(0)], query_piece(0))
        for q in range(QUARTERS):
            every(feed_own(q), starts)
        for j in range(n):
            both = r.gain_rows[j].astype(F32)
            for g in range(2):
                for h in range(2):
                    here_half = pl.ds(pl.multiple_of(chips[j] * wide + h * HD, HD), HD)
                    r.gains[g : g + 1, here_half] = both[16 * g + 8 * h : 16 * g + 8 * h + 1]

        def project(d):
            for c in range(2):
                first = (2 * d + (side + c) % 2) * rows

                def some(s, _, c=c, first=first):
                    now = pl.ds(pl.multiple_of(plane_rows + first + s * few, few), few)
                    then = pl.ds(pl.multiple_of((2 * d + c) * rows + s * few, few), few)
                    values = work[now, :].astype(F32)
                    inverse = lax.rsqrt(jnp.mean(values * values, axis=-1, keepdims=True) + epsilon)
                    work[then, :] = (values * inverse * r.gains[0:1, :]).astype(BF16)
                    return 0

                lax.fori_loop(0, rows // few, some, 0)
            now = span(d * pair, pair)
            kv = jnp.zeros((pair, HD), F32)
            for j in range(n):
                kv += matmul(work[now, blocks[j]], kv_piece(j)[...])
            kv = kv * r.tables[2] + turn(kv) * r.tables[3]
            heads[0, now, :] = kv.astype(BF16)

        def block_of(k, d):
            return heads.at[k, span(d * pair, pair)]

        def climb(s, d):
            at = s * n + d
            return remote(
                block_of(s - 1, d), block_of(s, d), r.climb_send.at[at], r.climb_recv.at[at], above
            )

        def fall(s, d):
            at = s * n + d
            return remote(
                block_of((planes - s + 1) % planes, d),
                block_of(planes - s, d),
                r.fall_send.at[at],
                r.fall_recv.at[at],
                below,
            )

        def pass_on(k, d):
            at = k * n + d
            return remote(
                block_of(k, d),
                block_of(planes + k, d),
                r.pass_send.at[at],
                r.pass_recv.at[at],
                other_core,
            )

        def kv_leave(s, d):
            @pl.when((z - s + 1 >= 0) & (z + 1 < planes))
            def _():
                climb(s, d).start()

            @pl.when((z + s - 1 < planes) & (z >= 1))
            def _():
                fall(s, d).start()

        def kv_come(s, d):
            @pl.when(z - s >= 0)
            def _():
                climb(s, d).wait_recv()

            @pl.when(z + s < planes)
            def _():
                fall(s, d).wait_recv()

        def passing(condition, k, d):
            @pl.when(condition)
            def _():
                pass_on(k, d).start()

        def passed(condition, k, d):
            @pl.when(condition)
            def _():
                pass_on(k, d).wait_recv()

        def by_chip(use):
            def one(i, _):
                use((i + 1) % n)
                return 0

            lax.fori_loop(0, n, one, 0)

        def start_kv(d):
            for at in range(n):

                @pl.when(d == at)
                def _():
                    if at == 3:
                        for far in (1, 2):
                            token_half(far).wait_recv()
                        token_near(3).start()
                    token_near(at).wait_recv()

            project(d)
            kv_leave(1, d)
            pass_on(0, d).start()

        by_chip(start_kv)
        token_near(3).wait_send()
        keep_normed = local(work.at[pl.ds(0, plane_rows)], r.normed, r.keep_sem.at[0])
        keep_normed.start()
        for d in range(1, n):
            query_far(d).wait_recv()
            load(r.query_in.at[d], query_piece(d))
        for d in (1, 2):
            cot_far(d).start()
        loaded()

        def project_query(d, _):
            now = span(d * pair, pair)
            query = jnp.zeros((pair, HD), F32)
            for j in range(n):
                query += matmul(work[now, blocks[j]], query_piece(j)[...])
            query = query * r.tables[0] + turn(query) * r.tables[1]
            heads[query_slot, now, :] = query.astype(BF16)
            return 0

        lax.fori_loop(0, n, project_query, 0)
        for d in range(1, n):
            out_far(d).wait_recv()
        keep_out = local(r.theirs, r.out_weight, r.keep_sem.at[1])
        keep_out.start()

        def put_rows(base, d, now_values, block_at):
            first = pl.ds(pl.multiple_of(base + (2 * d + side) * rows, rows), rows)
            second = pl.ds(pl.multiple_of(base + (2 * d + 1 - side) * rows, rows), rows)
            work[first, block_at] = now_values[:rows]
            work[second, block_at] = now_values[rows:]

        def totals(d):
            return [r.wide_rows.at[:, span((2 * d + c) * HD, HD)] for c in range(2)]

        def attend_block(k, d, first, last):
            now = span(d * pair, pair)
            a, b = heads[k, now, :], heads[planes + k, now, :]
            keys, values = jnp.where(side == 0, a, b), jnp.where(side == 0, b, a)
            score = matmul_nt(heads[query_slot, now, :], keys) * scale
            score = jnp.where(r.key_ids[d, k] <= r.query_ids[d], score, masked_score)
            top = jnp.max(score, axis=-1, keepdims=True)
            if not first:
                before = r.soft[d]
                top = jnp.maximum(top, before)
                factor = jnp.exp(before - top)
            raised = jnp.exp(score - top)
            weight = jnp.sum(raised, axis=-1, keepdims=True)
            total = matmul(raised.astype(BF16), values)
            if not first:
                weight += r.soft[n + d] * factor
                total += jnp.concatenate([t[...] for t in totals(d)], axis=0) * factor
            if last:
                return total, weight
            r.soft[d] = top
            r.soft[n + d] = weight
            for c, target in enumerate(totals(d)):
                target[...] = total[c * rows : (c + 1) * rows]
            return None

        def attend_to(k, first=False):
            by_chip(lambda d: attend_block(k, d, first, False) and None)

        def when_middle(there, otherwise):
            return jnp.where(is_middle, there, otherwise)

        by_chip(lambda d: pass_on(0, d).wait_recv())
        attend_to(0, first=True)

        def first_come(d):
            kv_come(1, d)
            kv_leave(2, d)
            passing(z >= 1, 1, d)
            passing(z + 1 < planes, 3, d)

        def first_passed(d):
            passed(z >= 1, 1, d)
            passed(z + 1 < planes, 3, d)

        by_chip(first_come)
        by_chip(first_passed)
        attend_to(jnp.where(z >= 1, 1, 3))
        for d in (1, 2):
            cot_far(d).wait_recv()
            cot_half(d).start()
            cot_near(d).start()
        for d in range(1, n):
            every(feed_half(d), starts)

        def second_come(d):
            kv_come(2, d)
            kv_leave(3, d)
            pass_on(2, d).start()

        by_chip(second_come)
        by_chip(lambda d: pass_on(2, d).wait_recv())
        attend_to(when_middle(3, 2))
        keep_normed.wait()

        def attend(d):
            kv_come(3, d)
            passing(z == 0, 1, d)
            passing(z == planes - 1, 3, d)
            passed(z == 0, 1, d)
            passed(z == planes - 1, 3, d)
            now = span(d * pair, pair)
            last_block = jnp.where(z == 0, 1, when_middle(2, 3))
            total, weight = attend_block(last_block, d, False, True)
            low_total = (total * (1.0 / weight)).astype(BF16)
            heads[attended_slot, now, :] = low_total
            for j in range(n):
                put_rows(
                    plane_rows,
                    d,
                    matmul(low_total, r.theirs[j // 2, j % 2]).astype(BF16),
                    blocks[j],
                )

        rows_reduced(MID, plane_rows, attend)
        keep_heads = local(heads.at[pl.ds(0, kept_slots)], r.kept, r.keep_sem.at[2])
        keep_heads.start()
        load(r.tokens, r.own_rows)
        loaded()
        keep_out.wait()
        for d in (1, 2):
            cot_half(d).wait_recv()
        cot_near(3).start()
        for d in range(1, n):
            every(feed_half(d), arrives)
            every(feed_share(d), starts)

        def kv_left(d):
            for s in range(1, planes):

                @pl.when((z - s + 1 >= 0) & (z + 1 < planes))
                def _():
                    climb(s, d).wait_send()

                @pl.when((z + s - 1 < planes) & (z >= 1))
                def _():
                    fall(s, d).wait_send()

            for k in range(planes):
                pass_on(k, d).wait_send()

        by_chip(kv_left)

        rows_arrive(MID, plane_rows)

        def second_norm(c, _):
            at = span(c * few, few)
            total = r.own_rows[at, :].astype(F32)
            total += work[pl.ds(pl.multiple_of(plane_rows + c * few, few), few), :].astype(F32)
            for d in range(n):
                total += r.some_rows[d, at, :].astype(F32)
            inverse = lax.rsqrt(jnp.mean(total * total, axis=-1, keepdims=True) + epsilon)
            r.wide_rows[at, :] = total
            r.own_rows[at, :] = (total * inverse * r.gains[1:2, :]).astype(BF16)
            return 0

        lax.fori_loop(0, rows // few, second_norm, 0)

        def two_far(d):
            return remote(
                r.own_rows,
                work.at[pl.ds(2 * d * rows, rows)],
                r.two_far_send.at[d],
                r.two_far_recv.at[d],
                (here, chips[d]),
            )

        def two_near(d):
            source = r.own_rows if d == 0 else work.at[pl.ds(2 * d * rows, rows)]
            return remote(
                source,
                work.at[pl.ds((2 * d + 1) * rows, rows)],
                r.two_near_send.at[d],
                r.two_near_recv.at[d],
                other_core,
            )

        def two_half(d):
            return remote(
                work.at[pl.ds(2 * d * rows + (d - 1) * half_rows, half_rows)],
                work.at[pl.ds(2 * 3 * rows + (d - 1) * half_rows, half_rows)],
                r.two_half_send.at[d],
                r.two_half_recv.at[d],
                (here, chips[3 - d]),
            )

        for d in (1, 2):
            two_far(d).start()
        two_near(0).start()
        two_own = local(r.own_rows, work.at[pl.ds(0, rows)], r.two_local.at[0])
        two_own.start()
        load(r.wide_rows, r.middle)
        rows_sent(MID, plane_rows)
        for d in range(n):
            cot_near(d).wait_recv()
            source = r.cotangent if d == 0 else r.cot_all.at[0, d]
            load(source, work.at[pl.ds(plane_rows + 2 * d * rows, rows)])
            load(r.cot_all.at[1, d], work.at[pl.ds(plane_rows + (2 * d + 1) * rows, rows)])
        keep_heads.wait()
        for d in range(1, n):
            every(feed_share(d), arrives)
        loaded()

        def rows_of_chip(t, arrive, half_way, pass_along):
            for at in range(n):

                @pl.when(t == at)
                def _():
                    for d in ((), (1, 2), (), ())[at]:
                        arrive(d).wait_recv()
                        half_way(d).start()
                        pass_along(d).start()
                    if at == 2:
                        half_way(1).wait_recv()
                        half_way(2).wait_recv()
                        pass_along(3).start()
                    pass_along(at).wait_recv()

        two_own.wait()

        def quarter_step(q, _):
            step(3 * q - 3)
            every(feed_own(q), waits)

            @pl.when(q > 0)
            def _():
                for d in range(1, n):
                    every(feed_far(q, d), arrives)

            @pl.when((q > 0) & (q < QUARTERS - 1))
            def _():
                for d in range(1, n):
                    every(feed_far(q + 1, d), starts)

            def forward(t, _):
                @pl.when(q == 0)
                def _():
                    rows_of_chip(t, two_far, two_half, two_near)

                now = span(t * pair, pair)
                cot_now = pl.ds(pl.multiple_of(plane_rows + t * pair, pair), pair)
                both = jnp.zeros((pair, 2 * quarter), F32)
                hidden_grad = jnp.zeros((pair, quarter), F32)
                for j in range(n):
                    both += matmul(work[now, blocks[j]], feed[q, j, :wide, :])
                    hidden_grad += matmul_nt(work[cot_now, blocks[j]], feed[q, j, wide:, :])
                gate, up = both[:, :quarter], both[:, quarter:]
                share = 1.0 / (1.0 + jnp.exp(-gate))
                activated = gate * share
                results = (
                    activated * up,
                    hidden_grad * up * share * (1.0 + gate * (1.0 - share)),
                    hidden_grad * activated,
                )
                for w, result in enumerate(results):
                    heads[q * 3 + w, now, :] = result.astype(BF16)
                    turned[w, :, now] = result.T.astype(BF16)
                return 0

            lax.fori_loop(0, n, forward, 0)

            @pl.when(q == 0)
            def _():
                for d in range(1, n):
                    every(feed_far(1, d), starts)

            step(3 * q - 2)

            def one(w, _):
                t = 3 * q + w

                outer(t, turned[w], span(jnp.where(w == 0, plane_rows, 0), plane_rows))

                @pl.when(w > 0)
                def _():
                    staged(t - 1)

                return 0

            lax.fori_loop(0, 3, one, 0)
            step(3 * q - 1)
            staged(3 * q + 2)
            return 0

        lax.fori_loop(0, QUARTERS, quarter_step, 0)
        steps_done[0] = 3 * QUARTERS - 3
        for d in range(1, n):
            two_near(d).wait_send()
        for d in (1, 2):
            two_half(d).wait_send()

        def back_step(d):
            now = span(d * pair, pair)
            lefts = [
                jnp.concatenate([heads[q * 3 + 1, now, :], heads[q * 3 + 2, now, :]], axis=1)
                for q in range(QUARTERS)
            ]
            for j in range(n):
                total = jnp.zeros((pair, wide), F32)
                for q in range(QUARTERS):
                    total += matmul_nt(lefts[q], feed[q, j, :wide, :])
                work[now, blocks[j]] = total.astype(BF16)

        half = n // 2
        rows_reduced(BACK, 0, back_step, ticks=TICKS[0] + TICKS[1])

        def out_step(d):
            now = span(d * pair, pair)
            then = pl.ds(pl.multiple_of(plane_rows + d * pair, pair), pair)
            for j in range(n):
                total = jnp.zeros((pair, wide), F32)
                for q in range(QUARTERS):
                    total += matmul(heads[q * 3, now, :], feed[q, j, wide:, :])
                work[then, blocks[j]] = total.astype(BF16)

        rows_reduced(OUT, plane_rows, out_step, send=False, ticks=TICKS[2] + TICKS[3])

        for d in range(1, n):
            every(feed_share(d), leaves)
        load(r.kept, heads.at[pl.ds(0, kept_slots)])
        for j in range(n):
            query_source = r.query_weight.at[:, head_of(0)] if j == 0 else r.query_in.at[j]
            load(query_source, feed.at[0, j, pl.ds(0, wide), pl.ds(0, HD)])
            load(r.in_weight[j].at[pl.ds(0, wide)], feed.at[0, j, pl.ds(0, wide), pl.ds(HD, HD)])
            load(r.out_weight.at[j // 2, j % 2], feed.at[0, j, pl.ds(wide, HD)])

        rows_arrive(BACK, 0)
        loaded()
        for d in (1, 2):
            two_far(d).wait_send()
        two_near(0).wait_send()
        load(r.cotangent, r.own_rows)
        loaded()

        def second_use(at, back):
            grad = r.own_rows[at, :].astype(F32) + back
            r.wide_rows[at, :] = grad
            r.own_rows[at, :] = grad.astype(BF16)

        norm_rows_back(0, r.wide_rows, r.gains[1:2, :], second_use)

        def branch_far(d):
            return remote(
                r.own_rows,
                r.branch_all.at[d, side],
                r.branch_send.at[d],
                r.branch_recv.at[d],
                (here, chips[d]),
            )

        def branch_near(d):
            source = r.own_rows if d == 0 else r.branch_all.at[d, side]
            return remote(
                source,
                r.branch_all.at[d, side],
                r.branch_near_send.at[d],
                r.branch_near_recv.at[d],
                other_core,
            )

        def branch_half(d):
            some = pl.ds((d - 1) * half_rows, half_rows)
            return remote(
                r.branch_all.at[d, side, some],
                r.branch_all.at[3, side, some],
                r.branch_half_send.at[d],
                r.branch_half_recv.at[d],
                (here, chips[3 - d]),
            )

        for d in (1, 2):
            branch_far(d).start()
        branch_near(0).start()
        branch_own = local(r.own_rows, r.branch_all.at[0, side], r.branch_local.at[0])
        branch_own.start()
        gain_terms(1)
        advance(TICKS[4])
        rows_sent(BACK, 0)
        branch_own.wait()
        loaded()

        def scored(d, now):
            keys, values, scores = [], [], []
            for k in range(planes):
                a, b = heads[k, now, :], heads[planes + k, now, :]
                keys.append(jnp.where(side == 0, a, b))
                values.append(jnp.where(side == 0, b, a))
                score = matmul_nt(heads[query_slot, now, :], keys[k]) * scale
                scores.append(jnp.where(r.key_ids[d, k] <= r.query_ids[d], score, masked_score))
            top = functools.reduce(jnp.maximum, [jnp.max(s, axis=-1, keepdims=True) for s in scores])
            raised = [jnp.exp(s - top) for s in scores]
            inverse = 1.0 / sum(jnp.sum(e, axis=-1, keepdims=True) for e in raised)
            return keys, values, [e * inverse for e in raised]

        def attend_back(d, _):
            rows_of_chip(d, branch_far, branch_half, branch_near)

            @pl.when(d == half)
            def _():
                for at in (3, 1, 2):
                    row_send(OUT, plane_rows, at)

            now = span(d * pair, pair)
            for c in range(2):
                load(r.branch_all.at[d, c], work.at[pl.ds(pl.multiple_of((2 * d + c) * rows, rows), rows)])
            loaded()
            query = heads[query_slot, now, :]
            attended_grad = jnp.zeros((pair, HD), F32)
            for j in range(n):
                attended_grad += matmul_nt(work[now, blocks[j]], feed[0, j, wide:, :])
            attended_grad = attended_grad.astype(BF16)
            keys, values, probs = scored(d, now)
            low = [p.astype(BF16) for p in probs]
            shares = [matmul_nt(attended_grad, values[k]) for k in range(planes)]
            delta = sum(
                jnp.sum(low[k].astype(F32) * shares[k], axis=-1, keepdims=True) for k in range(planes)
            )
            query_grad = jnp.zeros((pair, HD), F32)
            for k in range(planes):
                score_grad = (probs[k] * (shares[k] - delta)).astype(BF16)
                query_grad += matmul(score_grad, keys[k])
                key_grad = matmul_tn(score_grad, query) * scale
                value_grad = matmul_tn(low[k], attended_grad)
                heads[k, now, :] = jnp.where(side == 0, key_grad, value_grad).astype(BF16)
                heads[planes + k, now, :] = jnp.where(side == 0, value_grad, key_grad).astype(BF16)
            query_grad = query_grad * scale
            query_grad = query_grad * r.tables[0] + turn_back(query_grad * r.tables[1])
            heads[query_grad_slot, now, :] = query_grad.astype(BF16)
            return 0

        lax.fori_loop(0, half, attend_back, 0)
        advance(TICKS[5])
        lax.fori_loop(half, n, attend_back, 0)

        def kv_hand_over(k):
            return remote(
                heads.at[planes + k], r.kv_other.at[k], r.kv_send.at[k], r.kv_recv.at[k], other_core
            )

        def kv_load(source, slot):
            return local(source, r.kv_some.at[slot], r.kv_sem.at[slot])

        def kv_add(k, slot):
            def some(c, _):
                at = span(c * 64, 64)
                heads[k, at, :] = heads[k, at, :] + r.kv_some[slot, at, :]
                return 0

            lax.fori_loop(0, plane_rows // 64, some, 0)

        def kv_down(k):
            return remote(heads.at[k], r.kv_down.at[k], r.down_send.at[k], r.down_recv.at[k], below)

        def kv_up(k):
            return remote(
                heads.at[planes - k], r.kv_up.at[k], r.up_send.at[k], r.up_recv.at[k], above
            )

        order = list(range(planes - 1, -1, -1))
        for k in order:
            kv_hand_over(k).start()
        for at, k in enumerate(order):
            kv_hand_over(k).wait_recv()
            kv_load(r.kv_other.at[k], at % 2).start()
            kv_load(r.kv_other.at[k], at % 2).wait()
            kv_add(k, at % 2)

        def kv_send(k):
            @pl.when(z >= k)
            def _():
                kv_down(k).start()

            @pl.when(z + k < planes)
            def _():
                kv_up(k).start()

        def kv_receive(k, down_to, up_to):
            @pl.when((z + 1 >= k) & (z + 1 < planes))
            def _():
                kv_down(k).wait_recv()
                if down_to is not None:
                    copy = kv_load(r.kv_down.at[k], 0)
                    copy.start()
                    copy.wait()
                    kv_add(down_to, 0)

            @pl.when((z >= 1) & (z - 1 + k < planes))
            def _():
                kv_up(k).wait_recv()
                if up_to is not None:
                    copy = kv_load(r.kv_up.at[k], 1)
                    copy.start()
                    copy.wait()
                    kv_add(up_to, 1)

        kv_send(3)
        rows_sent(OUT, plane_rows)
        load(work.at[pl.ds(plane_rows, rows)], r.out_own)
        loaded()
        load(r.normed, work.at[pl.ds(plane_rows, plane_rows)])
        low_half, high_half = pl.ds(0, plane_rows), pl.ds(plane_rows, plane_rows)
        advance(TICKS[6])
        turned[0] = heads[attended_slot].astype(F32).T.astype(BF16)
        turned[1] = heads[query_grad_slot].astype(F32).T.astype(BF16)
        loaded()
        outer(query_at, turned[1], high_half)
        outer(output_at, turned[0], low_half)
        staged(query_at)
        staged(output_at)
        advance(TICKS[7])
        kv_receive(3, 2, 2)
        kv_send(2)
        advance(TICKS[8])
        kv_receive(2, 1, 3)
        kv_send(1)
        advance(TICKS[9])
        kv_receive(1, 0, 0)

        def kv_back(d, _):
            now = span(d * pair, pair)
            grad = heads[0, now, :].astype(F32)
            grad = grad * r.tables[2] + turn_back(grad * r.tables[3])
            heads[kv_grad_slot, now, :] = grad.astype(BF16)
            turned[2, :, now] = grad.T.astype(BF16)
            return 0

        lax.fori_loop(0, n, kv_back, 0)
        outer(kv_at, turned[2], high_half)

        def project_back(d):
            now = span(d * pair, pair)
            left = jnp.concatenate([heads[query_grad_slot, now, :], heads[kv_grad_slot, now, :]], axis=1)
            for j in range(n):
                put_rows(0, d, matmul_nt(left, feed[0, j, :wide, :]).astype(BF16), blocks[j])

        staged(kv_at)
        rows_reduced(ONE, 0, project_back)
        advance(TICKS[10])

        for d in (1, 2):
            branch_far(d).wait_send()
            branch_half(d).wait_send()
        for d in range(n):
            branch_near(d).wait_send()
        load(r.tokens, r.own_rows)
        rows_arrive(ONE, 0)
        loaded()

        def first_use(at, back):
            r.wide_rows[at, :] = r.wide_rows[at, :] + back

        norm_rows_back(0, r.own_rows, r.gains[0:1, :], first_use)
        load(r.wide_rows, r.tokens_grad)
        gain_terms(0)

        def gain_copy(at, source, target, peer):
            return remote(source, target, r.gain_send.at[at], r.gain_recv.at[at], peer)

        def gain_far(d):
            return gain_copy(d, r.gain_mine.at[d], r.gain_far.at[d], (here, chips[d]))

        def gain_hop(s, peer):
            return gain_copy(n + s, r.gain_sum.at[s], r.gain_in.at[s], peer)

        for d in range(1, n):
            gain_far(d).start()
        advance(TICKS[11])
        for d in range(1, n):
            gain_far(d).wait()
        r.gain_sum[0] = r.gain_mine[0] + r.gain_far[1] + r.gain_far[2] + r.gain_far[3]
        gain_hop(0, other_core).start()
        gain_hop(0, other_core).wait()
        r.gain_sum[1] = r.gain_sum[0] + r.gain_in[0]

        @pl.when(is_end)
        def _():
            gain_hop(1, partner).start()
            gain_hop(1, partner).wait_send()

        advance(TICKS[12])

        @pl.when(is_middle)
        def _():
            gain_hop(1, partner).wait_recv()
            r.gain_sum[2] = r.gain_sum[1] + r.gain_in[1]
            gain_hop(2, other_middle).start()
            gain_hop(2, other_middle).wait()
            r.gain_sum[3] = r.gain_sum[2] + r.gain_in[2]
            gain_hop(3, partner).start()
            gain_hop(3, partner).wait_send()

        @pl.when(is_end)
        def _():
            gain_hop(3, partner).wait_recv()
            r.gain_sum[3] = r.gain_in[3]

        load(r.gain_sum.at[3], r.gain_out)

        loaded()
        load(r.middle, r.wide_rows)
        load(r.out_own, r.own_rows)
        rows_arrive(OUT, plane_rows)
        loaded()

        def last_rows(c, _):
            at = span(c * few, few)
            total = r.wide_rows[at, :] + r.own_rows[at, :].astype(F32)
            for d in range(n):
                total += r.some_rows[d, at, :].astype(F32)
            r.own_rows[at, :] = total.astype(BF16)
            return 0

        lax.fori_loop(0, rows // few, last_rows, 0)
        load(r.own_rows, r.output)
        advance(units + 9 - steps_done[0])

        loaded()
        rows_sent(ONE, 0)
        for q in range(1, QUARTERS):
            for d in range(1, n):
                every(feed_far(q, d), leaves)
        for d in range(1, n):
            every(feed_half(d), leaves)
        for d in (1, 2):
            token_half(d).wait_send()
            cot_far(d).wait_send()
            cot_half(d).wait_send()
        for d in range(1, n):
            query_far(d).wait_send()
            out_far(d).wait_send()
        for d in range(n - 1):
            token_near(d).wait_send()
        for d in range(n):
            cot_near(d).wait_send()
        for k in range(planes):
            kv_hand_over(k).wait_send()
        for k in range(1, planes):

            @pl.when(z >= k)
            def _():
                kv_down(k).wait_send()

            @pl.when(z + k < planes)
            def _():
                kv_up(k).wait_send()

        finish()

    arrays = jax.tree.leaves((in_hbm, in_vmem))
    results = pl.pallas_call(
        backward,
        out_shape=jax.tree.leaves(out_hbm),
        in_specs=[pl.BlockSpec(memory_space=pl.ANY)] * len(jax.tree.leaves(in_hbm))
        + [pl.BlockSpec(memory_space=pltpu.VMEM)] * len(in_vmem),
        out_specs=[pl.BlockSpec(memory_space=pl.ANY)] * len(out_hbm),
        scratch_shapes=list(scratch.values()),
        cost_estimate=cost(30 * plane_rows * width * part, arrays, [unit_array] * 6),
        compiler_params=pltpu.CompilerParams(
            collective_id=0, has_side_effects=True, vmem_limit_bytes=63 * 1024 * 1024
        ),
        name="backward",
    )(*arrays)
    results = types.SimpleNamespace(**jax.tree.unflatten(jax.tree.structure(out_hbm), results))
    owned_tiles, near_tiles = (
        a.reshape(tiles_count, n, quarter, wide) for a in (results.owned, results.near)
    )

    def place(me_ref, own_ref, near_ref, gate, up, down, query, out, key, value):
        for source, e in ((own_ref, 0), (near_ref, 1)):

            @pl.when(pl.program_id(1) == e)
            def _():
                for q in range(QUARTERS):
                    here = slice(q * quarter, (q + 1) * quarter)
                    down[here, :] = source[3 * q, 0].astype(F32)
                    gate[:, here] = source[3 * q + 1, 0].T.astype(F32)
                    up[:, here] = source[3 * q + 2, 0].T.astype(F32)
                query[...] = source[query_at, 0].T.astype(F32)
                out[...] = source[output_at, 0].astype(F32)

                @pl.when(me_ref[1] == e)
                def _():
                    key[...] = source[kv_at, 0].T.astype(F32)

                @pl.when(me_ref[1] != e)
                def _():
                    value[...] = source[kv_at, 0].T.astype(F32)

    def owner(d, e, me):
        return 2 * (me[0] ^ d) + (me[1] ^ e)

    by_chip = pl.BlockSpec((tiles_count, 1, quarter, wide), lambda d, e, me: (0, d, 0, 0))
    placed = run_grid(
        place,
        me,
        (n, 2),
        [owned_tiles, near_tiles],
        [by_chip, by_chip],
        [
            shape(a.shape, F32)
            for a in (
                gate_weight,
                up_weight,
                down_weight,
                query_weight,
                output_weight,
                key_weight,
                value_weight,
            )
        ],
        [pl.BlockSpec((wide, part), lambda d, e, me: (0, owner(d, e, me)))] * 2
        + [
            pl.BlockSpec((part, wide), lambda d, e, me: (owner(d, e, me), 0)),
            pl.BlockSpec((wide, HD), lambda d, e, me: (0, owner(d, e, me))),
            pl.BlockSpec((HD, wide), lambda d, e, me: (owner(d, e, me), 0)),
        ]
        + [pl.BlockSpec((wide, HD), lambda d, e, me: (0, me[0] ^ d))] * 2,
        name="place",
    )
    gate_grad, up_grad, down_grad, query_grad, output_grad, key_grad, value_grad = placed

    return (
        results.output[None],
        results.tokens_grad[None],
        query_grad,
        key_grad,
        value_grad,
        output_grad,
        results.gain_out[0],
        gate_grad,
        up_grad,
        down_grad,
        results.gain_out[1],
    )


def solution(mesh):
    chips, pieces = mesh.shape["fsdp"], mesh.shape["ctx"]
    one_head_each = 2 * chips == H and chips == KVH and pieces == 8
    return jax.shard_map(
        plane_layer if one_head_each else ring_layer,
        mesh=mesh,
        in_specs=(
            P("fsdp", "ctx", None),
            P("fsdp", None),
            P("fsdp", None),
            P("fsdp", None),
            P(None, "fsdp"),
            P("fsdp"),
            P("fsdp", None),
            P("fsdp", None),
            P(None, "fsdp"),
            P("fsdp"),
            P("fsdp", "ctx", None),
            P(),
            P(),
        ),
        out_specs=(
            P("fsdp", "ctx", None),
            P("fsdp", "ctx", None),
            P("fsdp", None),
            P("fsdp", None),
            P("fsdp", None),
            P(None, "fsdp"),
            P("fsdp"),
            P("fsdp", None),
            P("fsdp", None),
            P(None, "fsdp"),
            P("fsdp"),
        ),
        check_vma=False,
    )
```

```python
import functools
import types

import jax
import jax.numpy as jnp
from jax import lax
from jax.experimental import pallas as pl
from jax.experimental.pallas import tpu as pltpu
from jax.sharding import PartitionSpec as P

H = 8
KVH = 4
HD = 256


epsilon = 1e-06
theta = 1000042.0
masked_score = -1e30


def passed_along(value, axis, by):
    devices = lax.axis_size(axis)
    return lax.ppermute(value, axis, [(i, (i + by) % devices) for i in range(devices)])


def rope_tables(positions):
    half = HD // 2
    frequency = theta ** (-(jnp.arange(half, dtype=jnp.float32) * 2.0 / HD))
    angle = positions[:, None] * frequency[None, :]
    angle = jnp.concatenate([angle, angle], axis=-1)
    return (jnp.cos(angle), jnp.sin(angle))


def rotate(values, cosine, sine):
    half = values.shape[-1] // 2
    turned = jnp.concatenate([-values[..., half:], values[..., :half]], axis=-1)
    return values * cosine[:, None, :] + turned * sine[:, None, :]


def rotate_back(grads, cosine, sine):
    half = grads.shape[-1] // 2
    scaled = grads * sine[:, None, :]
    turned = jnp.concatenate([scaled[..., half:], -scaled[..., :half]], axis=-1)
    return grads * cosine[:, None, :] + turned


def split_heads(block):
    count = block.shape[0]
    key_cols = KVH * HD
    key_part = block[:, :key_cols].reshape(count, KVH, HD).transpose(1, 0, 2)
    value_part = block[:, key_cols:].reshape(count, KVH, HD).transpose(1, 0, 2)
    return (key_part, value_part)


def merge_heads(grouped):
    return grouped.transpose(1, 0, 2).reshape(grouped.shape[1], KVH * HD)


def weight_terms(lefts, rights):
    pieces = []
    for index in range(4):
        column = lefts[index]
        pieces.append(
            jnp.einsum("tc,tn->cn", column, rights[index], preferred_element_type=jnp.float32)
        )
    return jnp.concatenate(pieces, axis=1)


def ring_layer(
    tokens,
    query_weight,
    key_weight,
    value_weight,
    output_weight,
    first_gain,
    gate_weight,
    up_weight,
    down_weight,
    second_gain,
    cotangent,
    block_ids,
    piece_order,
):
    ctx_count = lax.axis_size("ctx")
    fsdp_count = lax.axis_size("fsdp")
    here = lax.axis_index("ctx")
    rows = tokens.shape[1]
    width = tokens.shape[2]
    group = H // KVH
    query_cols = H * HD
    key_cols = KVH * HD
    hidden_cols = gate_weight.shape[1]
    scale = HD ** (-0.5)
    whole_query, whole_key, whole_value, whole_output, gain_one = (
        lax.all_gather(query_weight, "fsdp", axis=0, tiled=True),
        lax.all_gather(key_weight, "fsdp", axis=0, tiled=True),
        lax.all_gather(value_weight, "fsdp", axis=0, tiled=True),
        lax.all_gather(output_weight, "fsdp", axis=1, tiled=True),
        lax.all_gather(first_gain, "fsdp", axis=0, tiled=True),
    )
    id_row = lax.dynamic_index_in_dim(block_ids, lax.axis_index("fsdp"), 0, keepdims=False)
    start_own = lax.dynamic_index_in_dim(piece_order, here, 0, keepdims=False) * rows
    offsets = jnp.arange(rows, dtype=jnp.int32)
    cosine, sine = rope_tables((start_own + offsets).astype(jnp.float32))
    own_ids = lax.dynamic_slice_in_dim(id_row, start_own, rows)
    query_ids = jnp.tile(own_ids, group)

    def visible(source):
        key_start = lax.dynamic_index_in_dim(piece_order, source, 0, keepdims=False) * rows
        key_ids = lax.dynamic_slice_in_dim(id_row, key_start, rows)
        return key_ids[None, :] <= query_ids[:, None]

    inputs = tokens[0].astype(jnp.float32)
    scale_one = lax.rsqrt(jnp.mean(inputs * inputs, axis=-1, keepdims=True) + epsilon)
    unit_one = inputs * scale_one
    normed = (unit_one * gain_one.astype(jnp.float32)).astype(jnp.bfloat16)
    query = jnp.dot(normed, whole_query, preferred_element_type=jnp.float32).reshape(rows, H, HD)
    query_rot = rotate(query, cosine, sine).astype(jnp.bfloat16)
    keys = jnp.dot(normed, whole_key, preferred_element_type=jnp.float32).reshape(rows, KVH, HD)
    keys_rot = rotate(keys, cosine, sine).astype(jnp.bfloat16).reshape(rows, key_cols)
    values = jnp.dot(normed, whole_value, preferred_element_type=jnp.float32).astype(jnp.bfloat16)
    key_value = jnp.concatenate([keys_rot, values], axis=-1)
    grouped = (
        query_rot.reshape(rows, KVH, group, HD).transpose(1, 2, 0, 3).reshape(KVH, group * rows, HD)
    )

    def forward_step(state, block, source):
        running, total, weighted = state
        key_part, value_part = split_heads(block)
        allowed = visible(source)
        scores = (
            jnp.einsum("hqd,hkd->hqk", grouped, key_part, preferred_element_type=jnp.float32)
            * scale
        )
        scores = jnp.where(allowed[None], scores, masked_score)
        newest = jnp.maximum(running, jnp.max(scores, axis=-1))
        factor = jnp.exp(running - newest)
        shares = jnp.where(allowed[None], jnp.exp(scores - newest[..., None]), 0.0)
        total = total * factor + jnp.sum(shares, axis=-1)
        weighted = weighted * factor[..., None] + jnp.einsum(
            "hqk,hkd->hqd",
            shares.astype(jnp.bfloat16),
            value_part,
            preferred_element_type=jnp.float32,
        )
        return (newest, total, weighted)

    start_state = (
        jnp.full((KVH, group * rows), masked_score, jnp.float32),
        jnp.zeros((KVH, group * rows), jnp.float32),
        jnp.zeros((KVH, group * rows, HD), jnp.float32),
    )
    state = forward_step(start_state, key_value, here)

    def forward_turn(turn, carry):
        block, inner = carry
        block = passed_along(block, "ctx", 1)
        source = (here - turn) % ctx_count
        return (block, forward_step(inner, block, source))

    passed_block, state = lax.fori_loop(1, ctx_count, forward_turn, (key_value, state))
    running, total, weighted = state
    attended = weighted / total[..., None]
    log_total = running + jnp.log(total)
    attended_low = (
        attended.reshape(KVH, group, rows, HD)
        .transpose(2, 0, 1, 3)
        .reshape(rows, query_cols)
        .astype(jnp.bfloat16)
    )
    middle = inputs + jnp.dot(attended_low, whole_output, preferred_element_type=jnp.float32)
    gain_two, whole_gate, whole_up, whole_down = (
        lax.all_gather(second_gain, "fsdp", axis=0, tiled=True),
        lax.all_gather(gate_weight, "fsdp", axis=0, tiled=True),
        lax.all_gather(up_weight, "fsdp", axis=0, tiled=True),
        lax.all_gather(down_weight, "fsdp", axis=1, tiled=True),
    )
    scale_two = lax.rsqrt(jnp.mean(middle * middle, axis=-1, keepdims=True) + epsilon)
    unit_two = middle * scale_two
    normed_two = (unit_two * gain_two.astype(jnp.float32)).astype(jnp.bfloat16)
    gate = jnp.dot(normed_two, whole_gate, preferred_element_type=jnp.float32)
    up = jnp.dot(normed_two, whole_up, preferred_element_type=jnp.float32)
    sigmoid_gate = jax.nn.sigmoid(gate)
    activated = gate * sigmoid_gate
    hidden = (activated * up).astype(jnp.bfloat16)
    result = middle + jnp.dot(hidden, whole_down, preferred_element_type=jnp.float32)
    output = result.astype(jnp.bfloat16)[None]
    upstream = cotangent[0]
    hidden_grad = jnp.einsum("tm,fm->tf", upstream, whole_down, preferred_element_type=jnp.float32)
    gate_grad = (hidden_grad * up * sigmoid_gate * (1.0 + gate * (1.0 - sigmoid_gate))).astype(
        jnp.bfloat16
    )
    up_grad = (hidden_grad * activated).astype(jnp.bfloat16)
    normed_two_grad = jnp.einsum(
        "tf,mf->tm", gate_grad, whole_gate, preferred_element_type=jnp.float32
    ) + jnp.einsum("tf,mf->tm", up_grad, whole_up, preferred_element_type=jnp.float32)
    gain_two_term = jnp.sum(normed_two_grad * unit_two, axis=0)
    unit_two_grad = normed_two_grad * gain_two.astype(jnp.float32)
    middle_grad = upstream.astype(jnp.float32) + scale_two * (
        unit_two_grad - unit_two * jnp.mean(unit_two_grad * unit_two, axis=-1, keepdims=True)
    )
    branch_grad = middle_grad.astype(jnp.bfloat16)
    attended_grad = jnp.einsum(
        "tm,cm->tc", branch_grad, whole_output, preferred_element_type=jnp.float32
    ).astype(jnp.bfloat16)
    grad_grouped = (
        attended_grad.reshape(rows, KVH, group, HD)
        .transpose(1, 2, 0, 3)
        .reshape(KVH, group * rows, HD)
    )
    delta = jnp.sum(grad_grouped.astype(jnp.float32) * attended, axis=-1)

    def backward_step(query_total, block, source):
        key_part, value_part = split_heads(block)
        allowed = visible(source)
        scores = (
            jnp.einsum("hqd,hkd->hqk", grouped, key_part, preferred_element_type=jnp.float32)
            * scale
        )
        scores = jnp.where(allowed[None], scores, masked_score)
        shares = jnp.where(allowed[None], jnp.exp(scores - log_total[..., None]), 0.0)
        value_grad = jnp.einsum(
            "hqk,hqd->hkd",
            shares.astype(jnp.bfloat16),
            grad_grouped,
            preferred_element_type=jnp.float32,
        )
        share_grad = jnp.einsum(
            "hqd,hkd->hqk", grad_grouped, value_part, preferred_element_type=jnp.float32
        )
        score_grad = (shares * (share_grad - delta[..., None])).astype(jnp.bfloat16)
        query_total = query_total + jnp.einsum(
            "hqk,hkd->hqd", score_grad, key_part, preferred_element_type=jnp.float32
        )
        key_grad = (
            jnp.einsum("hqk,hqd->hkd", score_grad, grouped, preferred_element_type=jnp.float32)
            * scale
        )
        return (
            query_total,
            jnp.concatenate([merge_heads(key_grad), merge_heads(value_grad)], axis=-1),
        )

    query_total, first_grad = backward_step(
        jnp.zeros((KVH, group * rows, HD), jnp.float32), key_value, here
    )
    held = first_grad

    def backward_turn(turn, carry):
        block, kept, total_query = carry
        block = passed_along(block, "ctx", 1)
        source = (here - turn) % ctx_count
        total_query, block_grad = backward_step(total_query, block, source)
        kept = passed_along(kept.astype(jnp.bfloat16), "ctx", 1).astype(kept.dtype) + block_grad
        return (block, kept, total_query)

    passed_again, held, query_total = lax.fori_loop(
        1, ctx_count, backward_turn, (key_value, held, query_total)
    )
    own_grad = passed_along(held.astype(jnp.bfloat16), "ctx", 1).astype(held.dtype)
    query_rot_grad = (
        (query_total * scale)
        .reshape(KVH, group, rows, HD)
        .transpose(2, 0, 1, 3)
        .reshape(rows, H, HD)
    )
    query_grad = (
        rotate_back(query_rot_grad, cosine, sine).reshape(rows, query_cols).astype(jnp.bfloat16)
    )
    key_grad = (
        rotate_back(own_grad[:, :key_cols].reshape(rows, KVH, HD), cosine, sine)
        .reshape(rows, key_cols)
        .astype(jnp.bfloat16)
    )
    value_grad = own_grad[:, key_cols:].astype(jnp.bfloat16)
    normed_grad = jnp.einsum(
        "tc,mc->tm", query_grad, whole_query, preferred_element_type=jnp.float32
    )
    normed_grad = normed_grad + jnp.einsum(
        "tc,mc->tm", key_grad, whole_key, preferred_element_type=jnp.float32
    )
    normed_grad = normed_grad + jnp.einsum(
        "tc,mc->tm", value_grad, whole_value, preferred_element_type=jnp.float32
    )
    gain_one_term = jnp.sum(normed_grad * unit_one, axis=0)
    unit_one_grad = normed_grad * gain_one.astype(jnp.float32)
    tokens_grad = middle_grad + scale_one * (
        unit_one_grad - unit_one * jnp.mean(unit_one_grad * unit_one, axis=-1, keepdims=True)
    )
    projected = jnp.concatenate([query_grad, key_grad, value_grad], axis=-1)
    gate_up = jnp.concatenate([gate_grad, up_grad], axis=-1)
    lefts = jnp.stack([normed, branch_grad, normed_two, upstream])
    rights = (projected, attended_low, gate_up, hidden)
    piece = lax.psum_scatter(
        weight_terms(lefts, rights).astype(jnp.bfloat16), "fsdp", scatter_dimension=0, tiled=True
    )
    shard = lax.psum(piece, "ctx").astype(jnp.float32)
    gain_one_sum, gain_two_sum = lax.psum((gain_one_term, gain_two_term), ("ctx", "fsdp"))
    own_rows = width // fsdp_count
    own_start = lax.axis_index("fsdp") * own_rows
    value_begin = query_cols + key_cols
    output_begin = value_begin + key_cols
    gate_begin = output_begin + query_cols
    up_begin = gate_begin + hidden_cols
    down_begin = up_begin + hidden_cols
    return (
        output,
        tokens_grad[None],
        shard[:, :query_cols],
        shard[:, query_cols:value_begin],
        shard[:, value_begin:output_begin],
        shard[:, output_begin:gate_begin].T,
        lax.dynamic_slice_in_dim(gain_one_sum, own_start, own_rows),
        shard[:, gate_begin:up_begin],
        shard[:, up_begin:down_begin],
        shard[:, down_begin : down_begin + hidden_cols].T,
        lax.dynamic_slice_in_dim(gain_two_sum, own_start, own_rows),
    )


VMEM_BYTES = 58 * 1024 * 1024
BF16 = jnp.bfloat16
F32 = jnp.float32
QUARTERS = 4
MESH = pl.DeviceIdType.MESH
TICKS = (2, 1, 2, 2, 3, 2, 1, 1, 1, 2, 6, 2, 2)
LINES = 2


def matmul(a, b):
    return lax.dot_general(a, b, (((1,), (0,)), ((), ())), preferred_element_type=F32)


def matmul_nt(a, b):
    return lax.dot_general(a, b, (((1,), (1,)), ((), ())), preferred_element_type=F32)


def matmul_tn(a, b):
    return lax.dot_general(a, b, (((0,), (0,)), ((), ())), preferred_element_type=F32)


def cost(flops, arrays, outs, exps=0):
    moved = sum(a.size * a.dtype.itemsize for a in arrays) + sum(
        o.size * o.dtype.itemsize for o in outs
    )
    return pl.CostEstimate(flops=int(flops), bytes_accessed=int(moved), transcendentals=int(exps))


def run_whole(body, me, arrays, outs, scratch=(), flops=0, in_hbm=0, name=None):
    count = len(arrays) - in_hbm
    return pl.pallas_call(
        body,
        out_shape=outs,
        in_specs=[pl.BlockSpec(memory_space=pltpu.SMEM)]
        + [pl.BlockSpec(memory_space=pltpu.VMEM)] * count
        + [pl.BlockSpec(memory_space=pl.ANY)] * in_hbm,
        out_specs=jax.tree.map(lambda _: pl.BlockSpec(memory_space=pltpu.VMEM), outs),
        scratch_shapes=list(scratch),
        cost_estimate=cost(flops, arrays, jax.tree.leaves(outs)),
        compiler_params=pltpu.CompilerParams(vmem_limit_bytes=VMEM_BYTES),
        name=name,
    )(me, *arrays)


def run_grid(body, me, grid, arrays, in_specs, outs, out_specs, scratch=(), flops=0, aliases=None, name=None):
    return pl.pallas_call(
        body,
        out_shape=outs,
        grid_spec=pltpu.PrefetchScalarGridSpec(
            num_scalar_prefetch=1,
            grid=grid,
            in_specs=in_specs,
            out_specs=out_specs,
            scratch_shapes=list(scratch),
        ),
        cost_estimate=cost(flops, arrays, jax.tree.leaves(outs)),
        input_output_aliases=aliases or {},
        compiler_params=pltpu.CompilerParams(vmem_limit_bytes=VMEM_BYTES),
        name=name,
    )(me, *arrays)


def shape(dims, kind=BF16):
    return jax.ShapeDtypeStruct(tuple(dims), kind)


def fixed(block):
    return pl.BlockSpec(block, lambda i, me: (0,) * len(block), pipeline_mode=pl.Buffered(1))


def column(index, wide):
    return pl.ds(pl.multiple_of(index * wide, wide), wide)


def turn(values):
    half = values.shape[-1] // 2
    return jnp.concatenate([-values[:, half:], values[:, :half]], axis=-1)


def turn_back(values):
    half = values.shape[-1] // 2
    return jnp.concatenate([values[:, half:], -values[:, :half]], axis=-1)


def plane_layer(
    tokens,
    query_weight,
    key_weight,
    value_weight,
    output_weight,
    first_gain,
    gate_weight,
    up_weight,
    down_weight,
    second_gain,
    cotangent,
    block_ids,
    piece_order,
):
    ctx_count = lax.axis_size("ctx")
    n = lax.axis_size("fsdp")
    planes = ctx_count // 2
    ctx = lax.axis_index("ctx")
    z, core = ctx // 2, ctx % 2
    f = lax.axis_index("fsdp")
    me = jnp.stack([f, core]).astype(jnp.int32)
    rows, width = tokens.shape[1:]
    pair = 2 * rows
    plane_rows = n * pair
    wide = width // n
    hidden_cols = gate_weight.shape[1]
    part = hidden_cols // (2 * n)
    quarter = part // QUARTERS
    scale = HD ** (-0.5)

    def across(value, d):
        return lax.ppermute(value, "fsdp", [(i, i ^ d) for i in range(n)])

    def sibling(value):
        return lax.ppermute(value, "ctx", [(i, i ^ 1) for i in range(ctx_count)])

    def along(value, step):
        pairs = [(i, i + 2 * step) for i in range(ctx_count)]
        return lax.ppermute(value, "ctx", [(a, b) for a, b in pairs if 0 <= b < ctx_count])

    def between_planes(value, moves):
        return lax.ppermute(
            value, "ctx", [(2 * a + side, 2 * b + side) for a, b in moves for side in range(2)]
        )

    def gathered(value):
        own = [value] + [across(value, d) for d in range(1, n)]
        return own, [sibling(block) for block in own]

    def reduced(own, other):
        near = [sibling(block) for block in other]
        sent = [
            across((own[d].astype(F32) + near[d].astype(F32)).astype(BF16), d) for d in range(1, n)
        ]
        return [own[0], near[0]] + sent

    middle_left, middle_right = planes // 2 - 1, planes // 2
    folds = [
        [(s, s + 1), (planes - 1 - s, planes - 2 - s)] for s in range(middle_left)
    ]

    def summed_over_planes(value):
        for moves in folds:
            value = (
                value.astype(F32) + between_planes(value, moves).astype(F32)
            ).astype(value.dtype)
        crossed = between_planes(value, [(middle_left, middle_right), (middle_right, middle_left)])
        value = (value.astype(F32) + crossed.astype(F32)).astype(value.dtype)
        for s, moves in reversed(list(enumerate(folds))):
            back = between_planes(value, [(b, a) for a, b in moves])
            receives = (z == s) | (z == planes - 1 - s)
            value = jnp.where(receives, back, value)
        return value

    place = jnp.arange(rows, dtype=jnp.int32)
    own_pieces = lax.dynamic_slice_in_dim(piece_order, 2 * z, 2)
    positions = (own_pieces[:, None] * rows + place[None, :]).reshape(pair).astype(F32)
    cosine, sine = rope_tables(positions)
    is_value = core == 1
    kv_cosine = jnp.where(is_value, 1.0, cosine)
    kv_sine = jnp.where(is_value, 0.0, sine)
    chips = f ^ jnp.arange(n, dtype=jnp.int32)
    ring = (z - jnp.arange(planes, dtype=jnp.int32)) % planes
    ring_ctx = (2 * ring[:, None] + jnp.arange(2, dtype=jnp.int32)[None, :]).reshape(-1)
    id_pieces = block_ids.reshape(n, ctx_count, rows)
    ids = id_pieces[chips[:, None], piece_order[ring_ctx][None, :]]
    key_ids = ids.reshape(n, planes, 1, pair)
    query_ids = ids[:, :2].reshape(n, pair, 1)

    def cut_weights(me_ref, *refs):
        keys, values, (one, two), outs = refs[:n], refs[n : 2 * n], refs[2 * n : 2 * n + 2], refs[2 * n + 2 :]
        keys_here = me_ref[1] == 0
        for d in range(n):

            @pl.when(keys_here)
            def _():
                outs[d][:wide, :] = keys[d][...]

            @pl.when(jnp.logical_not(keys_here))
            def _():
                outs[d][:wide, :] = values[d][...]

            pick = lax.broadcasted_iota(jnp.int32, (16, HD), 0) < 8
            for g, gain in enumerate((one, two)):
                halves = [gain[:, h * HD : (h + 1) * HD].astype(F32) for h in range(2)]
                outs[d][wide + 16 * g : wide + 16 * (g + 1), :] = jnp.where(pick, *halves).astype(BF16)

    def chip_of(d):
        return lambda i, me: (0, me[0] ^ d)

    own_tokens = tokens[0]
    near_tokens = [own_tokens] + [across(own_tokens, d) for d in (1, 2)]
    gain_spec = pl.BlockSpec((1, wide), lambda i, me: (0, 0))
    cut = run_grid(
        cut_weights,
        me,
        (1,),
        [key_weight] * n
        + [value_weight] * n
        + [first_gain.reshape(1, wide), second_gain.reshape(1, wide)],
        [pl.BlockSpec((wide, HD), chip_of(d)) for d in range(n)] * 2 + [gain_spec, gain_spec],
        [shape((wide + 32, HD))] * n,
        [pl.BlockSpec((wide + 32, HD), lambda i, me: (0, 0))] * n,
        name="cut_weights",
    )
    weights_in = [cut[0]] + [across(cut[d], d) for d in range(1, n)]
    piece = (wide + quarter, 2 * quarter)
    own_cotangent = cotangent[0]
    block = (rows, width)

    tiles_count = 3 * QUARTERS + 3
    query_at, output_at, kv_at = tiles_count - 3, tiles_count - 2, tiles_count - 1
    units = 2 * tiles_count
    unit = (2, quarter, wide)
    held_sums, held_ends, ahead = 4, 3, 2
    MID, BACK, OUT, ONE = range(4)
    query_slot, attended_slot, query_grad_slot, kv_grad_slot = range(2 * planes, 2 * planes + 4)
    kept_slots = 2 * planes + 2
    columns = (plane_rows, HD)
    lanes = (8, wide)
    dma = pltpu.SemaphoreType.DMA

    in_hbm = dict(
        near_tokens=near_tokens,
        in_weight=weights_in,
        query_weight=query_weight,
        output_weight=output_weight,
        gate_weight=gate_weight,
        up_weight=up_weight,
        down_weight=down_weight,
        cotangent=own_cotangent,
        tokens=own_tokens,
    )
    in_vmem = dict(
        tables=jnp.stack([cosine, sine, kv_cosine, kv_sine]),
        query_ids=query_ids,
        key_ids=key_ids,
    )
    unit_array = shape((units,) + unit)
    out_hbm = dict(
        tiles=unit_array,
        from_end=unit_array,
        from_middle=unit_array,
        finals=unit_array,
        owned=unit_array,
        near=unit_array,
        row_near=shape((4, n) + block),
        row_far=shape((4, n) + block),
        cot_all=shape((2, n) + block),
        query_in=shape((n, wide, HD)),
        kept=shape((kept_slots,) + columns),
        out_weight=shape((2, 2, HD, wide)),
        normed=shape((plane_rows, width)),
        middle=shape(block, F32),
        branch_all=shape((n, 2) + block),
        kv_other=shape((planes,) + columns),
        kv_down=shape((planes,) + columns),
        kv_up=shape((planes,) + columns),
        out_own=shape(block),
        tokens_grad=shape(block, F32),
        output=shape(block),
        gain_out=shape(lanes, F32),
    )
    scratch = dict(
        work=pltpu.VMEM((2 * plane_rows, width), BF16),
        feed=pltpu.VMEM((QUARTERS, n) + piece, BF16),
        heads=pltpu.VMEM((3 * QUARTERS, plane_rows, HD), BF16),
        turned=pltpu.VMEM((3, HD, plane_rows), BF16),
        stage=pltpu.VMEM((2, n, quarter, wide), BF16),
        mine=pltpu.VMEM((2,) + unit, BF16),
        theirs=pltpu.VMEM((2,) + unit, BF16),
        crossed=pltpu.VMEM((2,) + unit, BF16),
        sums=pltpu.VMEM((held_sums,) + unit, BF16),
        ends=pltpu.VMEM((held_ends,) + unit, BF16),
        some_rows=pltpu.VMEM((n,) + block, BF16),
        wide_rows=pltpu.VMEM(block, F32),
        own_rows=pltpu.VMEM(block, BF16),
        kv_some=pltpu.VMEM((2,) + columns, BF16),
        flat=pltpu.VMEM((8, width), F32),
        gain_mine=pltpu.VMEM((n,) + lanes, F32),
        gain_far=pltpu.VMEM((n,) + lanes, F32),
        gain_sum=pltpu.VMEM((4,) + lanes, F32),
        gain_in=pltpu.VMEM((4,) + lanes, F32),
        load_sem=dma((4 * n + n,)),
        gains=pltpu.VMEM((8, width), F32),
        gain_rows=pltpu.VMEM((n, 32, HD), BF16),
        feed_local=dma((3 * QUARTERS,)),
        feed_send=dma((3 * QUARTERS * n,)),
        feed_recv=dma((3 * QUARTERS * n,)),
        stage_sem=dma((2, 2)),
        one_send=dma((units,)),
        one_recv=dma((units,)),
        two_send=dma((units,)),
        two_recv=dma((units,)),
        three_send=dma((units,)),
        three_recv=dma((units,)),
        mine_sem=dma((2,)),
        theirs_sem=dma((2,)),
        crossed_sem=dma((2,)),
        final_sem=dma((held_ends,)),
        deal_local=dma((units,)),
        deal_send=dma((2 * units,)),
        deal_recv=dma((2 * units,)),
        sib_send=dma((units,)),
        sib_recv=dma((units,)),
        row_sem=dma((n,)),
        row_near_send=dma((4 * n,)),
        row_near_recv=dma((4 * n,)),
        row_far_send=dma((4 * n,)),
        row_far_recv=dma((4 * n,)),
        token_send=dma((n,)),
        token_recv=dma((n,)),
        query_send=dma((n,)),
        query_recv=dma((n,)),
        out_send=dma((n,)),
        out_recv=dma((n,)),
        cot_send=dma((n,)),
        cot_recv=dma((n,)),
        cot_near_send=dma((n,)),
        cot_near_recv=dma((n,)),
        two_local=dma((1,)),
        two_far_send=dma((n,)),
        two_far_recv=dma((n,)),
        two_near_send=dma((n,)),
        two_near_recv=dma((n,)),
        two_half_send=dma((n,)),
        two_half_recv=dma((n,)),
        branch_half_send=dma((n,)),
        branch_half_recv=dma((n,)),
        climb_send=dma((n * planes,)),
        climb_recv=dma((n * planes,)),
        fall_send=dma((n * planes,)),
        fall_recv=dma((n * planes,)),
        soft=pltpu.VMEM((2 * n, pair, 1), F32),
        pass_send=dma((n * planes,)),
        pass_recv=dma((n * planes,)),
        cot_half_send=dma((n,)),
        cot_half_recv=dma((n,)),
        share_send=dma((2 * n,)),
        share_recv=dma((2 * n,)),
        token_half_send=dma((n,)),
        token_half_recv=dma((n,)),
        keep_sem=dma((3,)),
        branch_local=dma((1,)),
        branch_send=dma((n,)),
        branch_recv=dma((n,)),
        branch_near_send=dma((n,)),
        branch_near_recv=dma((n,)),
        kv_sem=dma((2,)),
        kv_send=dma((planes,)),
        kv_recv=dma((planes,)),
        down_send=dma((planes,)),
        down_recv=dma((planes,)),
        up_send=dma((planes,)),
        up_recv=dma((planes,)),
        gain_send=dma((n + 4,)),
        gain_recv=dma((n + 4,)),
    )

    def backward(*refs):
        r, first = types.SimpleNamespace(), 0
        for group in (in_hbm, in_vmem, out_hbm):
            leaves, form = jax.tree.flatten(group)
            vars(r).update(jax.tree.unflatten(form, refs[first : first + len(leaves)]))
            first += len(leaves)
        vars(r).update(zip(scratch, refs[first:]))
        here = lax.axis_index("ctx")
        chip = lax.axis_index("fsdp")
        z, side = here // 2, here % 2
        is_middle = (z == 1) | (z == 2)
        is_end = jnp.logical_not(is_middle)
        chips = [chip, chip + 1 - 2 * (chip % 2), (chip + 2) % 4, 3 - chip]
        partner = (2 * (z + 1 - 2 * (z % 2)) + side, chip)
        other_middle = (2 * (3 - z) + side, chip)
        other_core = (here + 1 - 2 * side, chip)
        below, above = (here - 2, chip), (here + 2, chip)
        blocks = [pl.ds(pl.multiple_of(c * wide, wide), wide) for c in chips]
        work, feed, heads, turned, stage = r.work, r.feed, r.heads, r.turned, r.stage

        barrier = pltpu.get_barrier_semaphore()
        for peer in [(here, c) for c in chips[1:]] + [partner, other_core]:
            pl.semaphore_signal(barrier, inc=1, device_id=peer, device_id_type=MESH)

        @pl.when(is_middle)
        def _():
            pl.semaphore_signal(barrier, inc=1, device_id=other_middle, device_id_type=MESH)
            pl.semaphore_wait(barrier, n + 2)

        @pl.when(is_end)
        def _():
            pl.semaphore_wait(barrier, n + 1)

        def remote(source, target, send, recv, peer):
            return pltpu.make_async_remote_copy(
                src_ref=source,
                dst_ref=target,
                send_sem=send,
                recv_sem=recv,
                device_id=peer,
                device_id_type=MESH,
            )

        local = pltpu.make_async_copy

        def span(first, count):
            return pl.ds(pl.multiple_of(first, count), count)

        def head_of(d):
            return span((2 * chips[d] + side) * HD, HD)

        def feed_parts(q, d, first=0, count=wide):
            there = span(((2 * chips[d] + side) * QUARTERS + q) * quarter, quarter)
            rows_in = pl.ds(first, count)
            below = 0 if count == wide else pl.multiple_of(first // 2, quarter // 2)
            some = pl.ds(
                pl.multiple_of(
                    ((2 * chips[d] + side) * QUARTERS + q) * quarter + below, quarter // 2
                ),
                count // 2,
            )
            below = wide if count == wide else pl.multiple_of(wide + below, quarter // 2)
            return (
                (r.gate_weight.at[rows_in, there], feed.at[q, d, rows_in, pl.ds(0, quarter)]),
                (r.up_weight.at[rows_in, there], feed.at[q, d, rows_in, pl.ds(quarter, quarter)]),
                (r.down_weight.at[some], feed.at[q, d, pl.ds(below, count // 2)]),
            )

        def feed_far(q, d, *rows_of):
            copies = []
            for part, (source, target) in enumerate(feed_parts(q, d, *rows_of)):
                at = (q * n + d) * 3 + part
                copies.append(
                    remote(source, target, r.feed_send.at[at], r.feed_recv.at[at], (here, chips[d]))
                )
            return copies

        def feed_own(q):
            return [
                local(source, target, r.feed_local.at[3 * q + part])
                for part, (source, target) in enumerate(feed_parts(q, 0))
            ]

        def every(copies, use):
            for copy in copies:
                use(copy)

        starts, waits = lambda c: c.start(), lambda c: c.wait()
        arrives, leaves = lambda c: c.wait_recv(), lambda c: c.wait_send()

        def hop_one(i):
            return remote(r.tiles.at[i], r.from_end.at[i], r.one_send.at[i], r.one_recv.at[i], partner)

        def hop_two(i):
            return remote(
                r.sums.at[i % held_sums],
                r.from_middle.at[i],
                r.two_send.at[i],
                r.two_recv.at[i],
                other_middle,
            )

        def hop_three(i):
            return remote(
                r.ends.at[i % held_ends], r.finals.at[i], r.three_send.at[i], r.three_recv.at[i], partner
            )

        def load_mine(i):
            return local(r.tiles.at[i], r.mine.at[i % 2], r.mine_sem.at[i % 2])

        def load_theirs(i):
            return local(r.from_end.at[i], r.theirs.at[i % 2], r.theirs_sem.at[i % 2])

        def load_crossed(i):
            return local(r.from_middle.at[i], r.crossed.at[i % 2], r.crossed_sem.at[i % 2])

        def keep_final(i):
            return local(r.ends.at[i % held_ends], r.finals.at[i], r.final_sem.at[i % held_ends])

        def keep_own(i):
            return local(r.finals.at[i, 0], r.owned.at[i, 0], r.deal_local.at[i])

        def deal_to(i, b, d):
            at = 2 * i + b
            return remote(
                r.finals.at[i, b],
                r.owned.at[i, b],
                r.deal_send.at[at],
                r.deal_recv.at[at],
                (here, chips[d]),
            )

        def to_sibling(i):
            return remote(r.owned.at[i], r.near.at[i], r.sib_send.at[i], r.sib_recv.at[i], other_core)

        def add(target, a, b):
            def some(s, _):
                at = (s // 4, span((s % 4) * (quarter // 4), quarter // 4))
                target[at] = a[at] + b[at]
                return 0

            lax.fori_loop(0, 8, some, 0)

        def when_in(i, *conditions):
            return pl.when(functools.reduce(jnp.logical_and, conditions, (i >= 0) & (i < units)))

        def step(i, _=0):
            @when_in(i + ahead, is_end, i >= 0)
            def _():
                hop_one(i + ahead).start()

            @when_in(i - 1, is_middle)
            def _():
                at = i - 1
                load_mine(at).wait()
                load_theirs(at).wait()

                @pl.when(at >= held_sums)
                def _():
                    hop_two(at - held_sums).wait_send()

                add(r.sums.at[at % held_sums], r.mine.at[at % 2], r.theirs.at[at % 2])
                hop_two(at).start()

            @when_in(i - 4, is_middle)
            def _():
                at = i - 4
                load_crossed(at).wait()

                @pl.when(at >= held_ends)
                def _():
                    hop_three(at - held_ends).wait_send()

                add(r.ends.at[at % held_ends], r.sums.at[at % held_sums], r.crossed.at[at % 2])
                hop_three(at).start()
                keep_final(at).start()

            @when_in(i, is_middle)
            def _():
                hop_one(i).wait_recv()
                load_mine(i).start()
                load_theirs(i).start()

            @when_in(i - 3, is_middle)
            def _():
                hop_two(i - 3).wait_recv()
                load_crossed(i - 3).start()

            @when_in(i - 6)
            def _():
                at = i - 6

                @pl.when(is_middle)
                def _():
                    keep_final(at).wait()

                @pl.when(is_end)
                def _():
                    hop_three(at).wait_recv()

                @pl.when(at % 2 == 0)
                def _():
                    keep_own(at).start()
                    deal_to(at, 1, 1).start()

                @pl.when(at % 2 == 1)
                def _():
                    deal_to(at, 0, 2).start()
                    deal_to(at, 1, 3).start()

            @when_in(i - 9)
            def _():
                at = i - 9

                @pl.when(at % 2 == 0)
                def _():
                    keep_own(at).wait()

                @pl.when(at % 2 == 1)
                def _():
                    deal_to(at, 0, 2).wait_recv()

                deal_to(at, 1, 3).wait_recv()
                to_sibling(at).start()

            return 0

        steps_done = [0]

        def advance(count):
            first = steps_done[0]
            steps_done[0] = first + count
            lax.fori_loop(first, first + count, step, 0)

        def finish():
            def one(i, _):
                @pl.when(is_end)
                def _():
                    hop_one(i).wait_send()

                @pl.when(is_middle & (i >= units - held_sums))
                def _():
                    hop_two(i).wait_send()

                @pl.when(is_middle & (i >= units - held_ends))
                def _():
                    hop_three(i).wait_send()

                @pl.when(i % 2 == 1)
                def _():
                    deal_to(i, 0, 2).wait_send()

                deal_to(i, 1, 3).wait_send()
                to_sibling(i).wait()
                return 0

            lax.fori_loop(0, units, one, 0)

        def stage_copy(t, h):
            return local(r.stage.at[t % 2, pl.ds(2 * h, 2)], r.tiles.at[2 * t + h], r.stage_sem.at[t % 2, h])

        def staged(t):
            for h in range(2):
                stage_copy(t, h).wait()

            @pl.when(is_end & (t == 0))
            def _():
                for i in range(ahead):
                    hop_one(i).start()

        def outer(t, left, right_rows):
            for j in range(n):
                stage[t % 2, j] = matmul(left, work[right_rows, blocks[j]]).astype(BF16)
            for h in range(2):
                stage_copy(t, h).start()

        def row_near(s, base, d):
            at = s * n + d
            return remote(
                work.at[pl.ds(base + (2 * d + 1) * rows, rows)],
                r.row_near.at[s, d],
                r.row_near_send.at[at],
                r.row_near_recv.at[at],
                other_core,
            )

        def row_far(s, base, d):
            at = s * n + d
            return remote(
                work.at[pl.ds(base + 2 * d * rows, rows)],
                r.row_far.at[s, d],
                r.row_far_send.at[at],
                r.row_far_recv.at[at],
                (here, chips[d]),
            )

        def near_load(s, d):
            return local(r.row_near.at[s, d], r.some_rows.at[d], r.row_sem.at[d])

        def far_load(s, d):
            return local(r.row_far.at[s, d], r.some_rows.at[d], r.row_sem.at[d])

        few = 16

        def row_send(s, base, d):
            row_near(s, base, d).wait_recv()
            near_load(s, d).start()
            near_load(s, d).wait()

            def some(c, _):
                at = span(c * few, few)
                own = pl.ds(pl.multiple_of(base + 2 * d * rows + c * few, few), few)
                work[own, :] = work[own, :] + r.some_rows[d, at, :]
                return 0

            lax.fori_loop(0, rows // few, some, 0)
            row_far(s, base, d).start()

        far_first = (1, 2, 3, 0)

        def rows_reduced(s, base, compute, send=True, ticks=0):
            def one(i, _):
                d = (i + 1) % n
                compute(d)
                for at in range(n):

                    @pl.when(i == at)
                    def _():
                        row_near(s, base, far_first[at]).start()
                        if send and at > 0:
                            row_send(s, base, far_first[at - 1])

                if ticks:

                    @pl.when(i >= n - ticks)
                    def _():
                        step(first + i - (n - ticks))

                return 0

            first = steps_done[0]
            steps_done[0] = first + ticks
            lax.fori_loop(0, n, one, 0)

        def rows_arrive(s, base):
            row_near(s, base, 0).wait_recv()
            near_load(s, 0).start()
            for d in range(1, n):
                row_far(s, base, d).wait_recv()
                far_load(s, d).start()
            near_load(s, 0).wait()
            for d in range(1, n):
                far_load(s, d).wait()

        def rows_sent(s, base):
            for d in range(n):
                row_near(s, base, d).wait_send()
            for d in range(1, n):
                row_far(s, base, d).wait_send()

        def norm_rows_back(base, value_ref, gain_row, use):
            r.flat[...] = jnp.zeros_like(r.flat)

            def some(c, _):
                at = span(c * few, few)
                grad = work[pl.ds(pl.multiple_of(base + c * few, few), few), :].astype(F32)
                for d in range(n):
                    grad += r.some_rows[d, at, :].astype(F32)
                values = value_ref[at, :].astype(F32)
                inverse = lax.rsqrt(jnp.mean(values * values, axis=-1, keepdims=True) + epsilon)
                unit_rows = values * inverse
                scaled = grad * gain_row
                back = inverse * (
                    scaled - unit_rows * jnp.mean(scaled * unit_rows, axis=-1, keepdims=True)
                )
                use(at, back)
                terms = grad * unit_rows
                r.flat[...] += terms[:8] + terms[8:]
                return 0

            lax.fori_loop(0, rows // few, some, 0)

        def gain_terms(at):
            total = jnp.sum(r.flat[...], axis=0, keepdims=True)
            r.flat[0:1, :] = total
            for j in range(n):
                r.gain_mine[j, at : at + 1, :] = r.flat[0:1, blocks[j]]

        r.gain_mine[...] = jnp.zeros_like(r.gain_mine)
        loads = []

        def load(source, target):
            copy = local(source, target, r.load_sem.at[len(loads)])
            copy.start()
            loads.append(copy)

        def loaded():
            while loads:
                loads.pop().wait()

        def out_far(d):
            return remote(
                r.output_weight.at[head_of(d)],
                r.theirs.at[d // 2, d % 2],
                r.out_send.at[d],
                r.out_recv.at[d],
                (here, chips[d]),
            )

        def cot_far(d):
            return remote(
                r.cotangent, r.cot_all.at[0, d], r.cot_send.at[d], r.cot_recv.at[d], (here, chips[d])
            )

        def cot_near(d):
            source = r.cotangent if d == 0 else r.cot_all.at[0, d]
            return remote(
                source, r.cot_all.at[1, d], r.cot_near_send.at[d], r.cot_near_recv.at[d], other_core
            )

        def query_far(d):
            return remote(
                r.query_weight.at[:, head_of(d)],
                r.query_in.at[d],
                r.query_send.at[d],
                r.query_recv.at[d],
                (here, chips[d]),
            )

        def kv_piece(j):
            return r.kv_some.at[j // 3, pl.ds(j % 3 * wide, wide)]

        def query_piece(j):
            return heads.at[query_grad_slot + j // 3, pl.ds(j % 3 * wide, wide)]

        half_rows = rows // 2

        def cot_half(d):
            some = pl.ds((d - 1) * half_rows, half_rows)
            return remote(
                r.cot_all.at[0, d, some],
                r.cot_all.at[0, 3, some],
                r.cot_half_send.at[d],
                r.cot_half_recv.at[d],
                (here, chips[3 - d]),
            )

        parity = z % 2

        def feed_half(d):
            return feed_far(0, d, pl.multiple_of(parity * (wide // 2), wide // 2), wide // 2)

        def feed_share(d):
            copies = []
            for part, (first, count) in enumerate(((0, wide // 2), (wide, quarter // 2))):
                some = feed.at[0, d, span(first + parity * count, count)]
                at = 2 * d + part
                copies.append(remote(some, some, r.share_send.at[at], r.share_recv.at[at], partner))
            return copies

        def token_near(d):
            source = work.at[pl.ds(plane_rows + 2 * d * rows, rows)] if d == 3 else r.near_tokens[d]
            return remote(
                source,
                work.at[pl.ds(plane_rows + (2 * d + 1) * rows, rows)],
                r.token_send.at[d],
                r.token_recv.at[d],
                other_core,
            )

        def token_half(d):
            return remote(
                r.near_tokens[d].at[pl.ds((d - 1) * half_rows, half_rows)],
                work.at[pl.ds(plane_rows + 6 * rows + (d - 1) * half_rows, half_rows)],
                r.token_half_send.at[d],
                r.token_half_recv.at[d],
                (here, chips[3 - d]),
            )

        for d in (1, 2):
            token_half(d).start()
        for d in range(1, n):
            query_far(d).start()
        for d in range(1, n):
            out_far(d).start()
        cot_near(0).start()
        for d in range(n - 1):
            token_near(d).start()
            load(r.near_tokens[d], work.at[pl.ds(plane_rows + 2 * d * rows, rows)])
        for j in range(n):
            load(r.in_weight[j].at[pl.ds(0, wide)], kv_piece(j))
            load(r.in_weight[j].at[pl.ds(wide, 32)], r.gain_rows.at[j])
        loaded()
        load(r.output_weight.at[head_of(0)], r.theirs.at[0, 0])
        load(r.query_weight.at[:, head_of(0)], query_piece(0))
        for q in range(QUARTERS):
            every(feed_own(q), starts)
        for j in range(n):
            both = r.gain_rows[j].astype(F32)
            for g in range(2):
                for h in range(2):
                    here_half = pl.ds(pl.multiple_of(chips[j] * wide + h * HD, HD), HD)
                    r.gains[g : g + 1, here_half] = both[16 * g + 8 * h : 16 * g + 8 * h + 1]

        def project(d):
            for c in range(2):
                first = (2 * d + (side + c) % 2) * rows

                def some(s, _, c=c, first=first):
                    now = pl.ds(pl.multiple_of(plane_rows + first + s * few, few), few)
                    then = pl.ds(pl.multiple_of((2 * d + c) * rows + s * few, few), few)
                    values = work[now, :].astype(F32)
                    inverse = lax.rsqrt(jnp.mean(values * values, axis=-1, keepdims=True) + epsilon)
                    work[then, :] = (values * inverse * r.gains[0:1, :]).astype(BF16)
                    return 0

                lax.fori_loop(0, rows // few, some, 0)
            now = span(d * pair, pair)
            kv = jnp.zeros((pair, HD), F32)
            for j in range(n):
                kv += matmul(work[now, blocks[j]], kv_piece(j)[...])
            kv = kv * r.tables[2] + turn(kv) * r.tables[3]
            heads[0, now, :] = kv.astype(BF16)

        def block_of(k, d):
            return heads.at[k, span(d * pair, pair)]

        def climb(s, d):
            at = s * n + d
            return remote(
                block_of(s - 1, d), block_of(s, d), r.climb_send.at[at], r.climb_recv.at[at], above
            )

        def fall(s, d):
            at = s * n + d
            return remote(
                block_of((planes - s + 1) % planes, d),
                block_of(planes - s, d),
                r.fall_send.at[at],
                r.fall_recv.at[at],
                below,
            )

        def pass_on(k, d):
            at = k * n + d
            return remote(
                block_of(k, d),
                block_of(planes + k, d),
                r.pass_send.at[at],
                r.pass_recv.at[at],
                other_core,
            )

        def kv_leave(s, d):
            @pl.when((z - s + 1 >= 0) & (z + 1 < planes))
            def _():
                climb(s, d).start()

            @pl.when((z + s - 1 < planes) & (z >= 1))
            def _():
                fall(s, d).start()

        def kv_come(s, d):
            @pl.when(z - s >= 0)
            def _():
                climb(s, d).wait_recv()

            @pl.when(z + s < planes)
            def _():
                fall(s, d).wait_recv()

        def passing(condition, k, d):
            @pl.when(condition)
            def _():
                pass_on(k, d).start()

        def passed(condition, k, d):
            @pl.when(condition)
            def _():
                pass_on(k, d).wait_recv()

        def by_chip(use):
            def one(i, _):
                use((i + 1) % n)
                return 0

            lax.fori_loop(0, n, one, 0)

        def start_kv(d):
            for at in range(n):

                @pl.when(d == at)
                def _():
                    if at == 3:
                        for far in (1, 2):
                            token_half(far).wait_recv()
                        token_near(3).start()
                    token_near(at).wait_recv()

            project(d)
            kv_leave(1, d)
            pass_on(0, d).start()

        by_chip(start_kv)
        token_near(3).wait_send()
        keep_normed = local(work.at[pl.ds(0, plane_rows)], r.normed, r.keep_sem.at[0])
        keep_normed.start()
        for d in range(1, n):
            query_far(d).wait_recv()
            load(r.query_in.at[d], query_piece(d))
        for d in (1, 2):
            cot_far(d).start()
        loaded()

        def project_query(d, _):
            now = span(d * pair, pair)
            query = jnp.zeros((pair, HD), F32)
            for j in range(n):
                query += matmul(work[now, blocks[j]], query_piece(j)[...])
            query = query * r.tables[0] + turn(query) * r.tables[1]
            heads[query_slot, now, :] = query.astype(BF16)
            return 0

        lax.fori_loop(0, n, project_query, 0)
        for d in range(1, n):
            out_far(d).wait_recv()
        keep_out = local(r.theirs, r.out_weight, r.keep_sem.at[1])
        keep_out.start()

        def put_rows(base, d, now_values, block_at):
            first = pl.ds(pl.multiple_of(base + (2 * d + side) * rows, rows), rows)
            second = pl.ds(pl.multiple_of(base + (2 * d + 1 - side) * rows, rows), rows)
            work[first, block_at] = now_values[:rows]
            work[second, block_at] = now_values[rows:]

        def totals(d):
            return [r.wide_rows.at[:, span((2 * d + c) * HD, HD)] for c in range(2)]

        def attend_block(k, d, first, last):
            now = span(d * pair, pair)
            a, b = heads[k, now, :], heads[planes + k, now, :]
            keys, values = jnp.where(side == 0, a, b), jnp.where(side == 0, b, a)
            score = matmul_nt(heads[query_slot, now, :], keys) * scale
            score = jnp.where(r.key_ids[d, k] <= r.query_ids[d], score, masked_score)
            top = jnp.max(score, axis=-1, keepdims=True)
            if not first:
                before = r.soft[d]
                top = jnp.maximum(top, before)
                factor = jnp.exp(before - top)
            raised = jnp.exp(score - top)
            weight = jnp.sum(raised, axis=-1, keepdims=True)
            total = matmul(raised.astype(BF16), values)
            if not first:
                weight += r.soft[n + d] * factor
                total += jnp.concatenate([t[...] for t in totals(d)], axis=0) * factor
            if last:
                return total, weight
            r.soft[d] = top
            r.soft[n + d] = weight
            for c, target in enumerate(totals(d)):
                target[...] = total[c * rows : (c + 1) * rows]
            return None

        def attend_to(k, first=False):
            by_chip(lambda d: attend_block(k, d, first, False) and None)

        def when_middle(there, otherwise):
            return jnp.where(is_middle, there, otherwise)

        by_chip(lambda d: pass_on(0, d).wait_recv())
        attend_to(0, first=True)

        def first_come(d):
            kv_come(1, d)
            kv_leave(2, d)
            passing(z >= 1, 1, d)
            passing(z + 1 < planes, 3, d)

        def first_passed(d):
            passed(z >= 1, 1, d)
            passed(z + 1 < planes, 3, d)

        by_chip(first_come)
        by_chip(first_passed)
        attend_to(jnp.where(z >= 1, 1, 3))
        for d in (1, 2):
            cot_far(d).wait_recv()
            cot_half(d).start()
            cot_near(d).start()
        for d in range(1, n):
            every(feed_half(d), starts)

        def second_come(d):
            kv_come(2, d)
            kv_leave(3, d)
            pass_on(2, d).start()

        by_chip(second_come)
        by_chip(lambda d: pass_on(2, d).wait_recv())
        attend_to(when_middle(3, 2))
        keep_normed.wait()

        def attend(d):
            kv_come(3, d)
            passing(z == 0, 1, d)
            passing(z == planes - 1, 3, d)
            passed(z == 0, 1, d)
            passed(z == planes - 1, 3, d)
            now = span(d * pair, pair)
            last_block = jnp.where(z == 0, 1, when_middle(2, 3))
            total, weight = attend_block(last_block, d, False, True)
            low_total = (total * (1.0 / weight)).astype(BF16)
            heads[attended_slot, now, :] = low_total
            for j in range(n):
                put_rows(
                    plane_rows,
                    d,
                    matmul(low_total, r.theirs[j // 2, j % 2]).astype(BF16),
                    blocks[j],
                )

        rows_reduced(MID, plane_rows, attend)
        keep_heads = local(heads.at[pl.ds(0, kept_slots)], r.kept, r.keep_sem.at[2])
        keep_heads.start()
        load(r.tokens, r.own_rows)
        loaded()
        keep_out.wait()
        for d in (1, 2):
            cot_half(d).wait_recv()
        cot_near(3).start()
        for d in range(1, n):
            every(feed_half(d), arrives)
            every(feed_share(d), starts)

        def kv_left(d):
            for s in range(1, planes):

                @pl.when((z - s + 1 >= 0) & (z + 1 < planes))
                def _():
                    climb(s, d).wait_send()

                @pl.when((z + s - 1 < planes) & (z >= 1))
                def _():
                    fall(s, d).wait_send()

            for k in range(planes):
                pass_on(k, d).wait_send()

        by_chip(kv_left)

        rows_arrive(MID, plane_rows)

        def second_norm(c, _):
            at = span(c * few, few)
            total = r.own_rows[at, :].astype(F32)
            total += work[pl.ds(pl.multiple_of(plane_rows + c * few, few), few), :].astype(F32)
            for d in range(n):
                total += r.some_rows[d, at, :].astype(F32)
            inverse = lax.rsqrt(jnp.mean(total * total, axis=-1, keepdims=True) + epsilon)
            r.wide_rows[at, :] = total
            r.own_rows[at, :] = (total * inverse * r.gains[1:2, :]).astype(BF16)
            return 0

        lax.fori_loop(0, rows // few, second_norm, 0)

        def two_far(d):
            return remote(
                r.own_rows,
                work.at[pl.ds(2 * d * rows, rows)],
                r.two_far_send.at[d],
                r.two_far_recv.at[d],
                (here, chips[d]),
            )

        def two_near(d):
            source = r.own_rows if d == 0 else work.at[pl.ds(2 * d * rows, rows)]
            return remote(
                source,
                work.at[pl.ds((2 * d + 1) * rows, rows)],
                r.two_near_send.at[d],
                r.two_near_recv.at[d],
                other_core,
            )

        def two_half(d):
            return remote(
                work.at[pl.ds(2 * d * rows + (d - 1) * half_rows, half_rows)],
                work.at[pl.ds(2 * 3 * rows + (d - 1) * half_rows, half_rows)],
                r.two_half_send.at[d],
                r.two_half_recv.at[d],
                (here, chips[3 - d]),
            )

        for d in (1, 2):
            two_far(d).start()
        two_near(0).start()
        two_own = local(r.own_rows, work.at[pl.ds(0, rows)], r.two_local.at[0])
        two_own.start()
        load(r.wide_rows, r.middle)
        rows_sent(MID, plane_rows)
        for d in range(n):
            cot_near(d).wait_recv()
            source = r.cotangent if d == 0 else r.cot_all.at[0, d]
            load(source, work.at[pl.ds(plane_rows + 2 * d * rows, rows)])
            load(r.cot_all.at[1, d], work.at[pl.ds(plane_rows + (2 * d + 1) * rows, rows)])
        keep_heads.wait()
        for d in range(1, n):
            every(feed_share(d), arrives)
        loaded()

        def rows_of_chip(t, arrive, half_way, pass_along):
            for at in range(n):

                @pl.when(t == at)
                def _():
                    for d in ((), (1, 2), (), ())[at]:
                        arrive(d).wait_recv()
                        half_way(d).start()
                        pass_along(d).start()
                    if at == 2:
                        half_way(1).wait_recv()
                        half_way(2).wait_recv()
                        pass_along(3).start()
                    pass_along(at).wait_recv()

        two_own.wait()

        def quarter_step(q, _):
            step(3 * q - 3)
            every(feed_own(q), waits)

            @pl.when(q > 0)
            def _():
                for d in range(1, n):
                    every(feed_far(q, d), arrives)

            @pl.when((q > 0) & (q < QUARTERS - 1))
            def _():
                for d in range(1, n):
                    every(feed_far(q + 1, d), starts)

            def forward(t, _):
                @pl.when(q == 0)
                def _():
                    rows_of_chip(t, two_far, two_half, two_near)

                now = span(t * pair, pair)
                cot_now = pl.ds(pl.multiple_of(plane_rows + t * pair, pair), pair)
                both = jnp.zeros((pair, 2 * quarter), F32)
                hidden_grad = jnp.zeros((pair, quarter), F32)
                for j in range(n):
                    both += matmul(work[now, blocks[j]], feed[q, j, :wide, :])
                    hidden_grad += matmul_nt(work[cot_now, blocks[j]], feed[q, j, wide:, :])
                gate, up = both[:, :quarter], both[:, quarter:]
                share = 1.0 / (1.0 + jnp.exp(-gate))
                activated = gate * share
                results = (
                    activated * up,
                    hidden_grad * up * share * (1.0 + gate * (1.0 - share)),
                    hidden_grad * activated,
                )
                for w, result in enumerate(results):
                    heads[q * 3 + w, now, :] = result.astype(BF16)
                    turned[w, :, now] = result.T.astype(BF16)
                return 0

            lax.fori_loop(0, n, forward, 0)

            @pl.when(q == 0)
            def _():
                for d in range(1, n):
                    every(feed_far(1, d), starts)

            step(3 * q - 2)

            def one(w, _):
                t = 3 * q + w

                outer(t, turned[w], span(jnp.where(w == 0, plane_rows, 0), plane_rows))

                @pl.when(w > 0)
                def _():
                    staged(t - 1)

                return 0

            lax.fori_loop(0, 3, one, 0)
            step(3 * q - 1)
            staged(3 * q + 2)
            return 0

        lax.fori_loop(0, QUARTERS, quarter_step, 0)
        steps_done[0] = 3 * QUARTERS - 3
        for d in range(1, n):
            two_near(d).wait_send()
        for d in (1, 2):
            two_half(d).wait_send()

        def back_step(d):
            now = span(d * pair, pair)
            lefts = [
                jnp.concatenate([heads[q * 3 + 1, now, :], heads[q * 3 + 2, now, :]], axis=1)
                for q in range(QUARTERS)
            ]
            for j in range(n):
                total = jnp.zeros((pair, wide), F32)
                for q in range(QUARTERS):
                    total += matmul_nt(lefts[q], feed[q, j, :wide, :])
                work[now, blocks[j]] = total.astype(BF16)

        half = n // 2
        rows_reduced(BACK, 0, back_step, ticks=TICKS[0] + TICKS[1])

        def out_step(d):
            now = span(d * pair, pair)
            then = pl.ds(pl.multiple_of(plane_rows + d * pair, pair), pair)
            for j in range(n):
                total = jnp.zeros((pair, wide), F32)
                for q in range(QUARTERS):
                    total += matmul(heads[q * 3, now, :], feed[q, j, wide:, :])
                work[then, blocks[j]] = total.astype(BF16)

        rows_reduced(OUT, plane_rows, out_step, send=False, ticks=TICKS[2] + TICKS[3])

        for d in range(1, n):
            every(feed_share(d), leaves)
        load(r.kept, heads.at[pl.ds(0, kept_slots)])
        for j in range(n):
            query_source = r.query_weight.at[:, head_of(0)] if j == 0 else r.query_in.at[j]
            load(query_source, feed.at[0, j, pl.ds(0, wide), pl.ds(0, HD)])
            load(r.in_weight[j].at[pl.ds(0, wide)], feed.at[0, j, pl.ds(0, wide), pl.ds(HD, HD)])
            load(r.out_weight.at[j // 2, j % 2], feed.at[0, j, pl.ds(wide, HD)])

        rows_arrive(BACK, 0)
        loaded()
        for d in (1, 2):
            two_far(d).wait_send()
        two_near(0).wait_send()
        load(r.cotangent, r.own_rows)
        loaded()

        def second_use(at, back):
            grad = r.own_rows[at, :].astype(F32) + back
            r.wide_rows[at, :] = grad
            r.own_rows[at, :] = grad.astype(BF16)

        norm_rows_back(0, r.wide_rows, r.gains[1:2, :], second_use)

        def branch_far(d):
            return remote(
                r.own_rows,
                r.branch_all.at[d, side],
                r.branch_send.at[d],
                r.branch_recv.at[d],
                (here, chips[d]),
            )

        def branch_near(d):
            source = r.own_rows if d == 0 else r.branch_all.at[d, side]
            return remote(
                source,
                r.branch_all.at[d, side],
                r.branch_near_send.at[d],
                r.branch_near_recv.at[d],
                other_core,
            )

        def branch_half(d):
            some = pl.ds((d - 1) * half_rows, half_rows)
            return remote(
                r.branch_all.at[d, side, some],
                r.branch_all.at[3, side, some],
                r.branch_half_send.at[d],
                r.branch_half_recv.at[d],
                (here, chips[3 - d]),
            )

        for d in (1, 2):
            branch_far(d).start()
        branch_near(0).start()
        branch_own = local(r.own_rows, r.branch_all.at[0, side], r.branch_local.at[0])
        branch_own.start()
        gain_terms(1)
        advance(TICKS[4])
        rows_sent(BACK, 0)
        branch_own.wait()
        loaded()

        def scored(d, now):
            keys, values, scores = [], [], []
            for k in range(planes):
                a, b = heads[k, now, :], heads[planes + k, now, :]
                keys.append(jnp.where(side == 0, a, b))
                values.append(jnp.where(side == 0, b, a))
                score = matmul_nt(heads[query_slot, now, :], keys[k]) * scale
                scores.append(jnp.where(r.key_ids[d, k] <= r.query_ids[d], score, masked_score))
            top = functools.reduce(jnp.maximum, [jnp.max(s, axis=-1, keepdims=True) for s in scores])
            raised = [jnp.exp(s - top) for s in scores]
            inverse = 1.0 / sum(jnp.sum(e, axis=-1, keepdims=True) for e in raised)
            return keys, values, [e * inverse for e in raised]

        def attend_back(d, _):
            rows_of_chip(d, branch_far, branch_half, branch_near)

            @pl.when(d == half)
            def _():
                for at in (3, 1, 2):
                    row_send(OUT, plane_rows, at)

            now = span(d * pair, pair)
            for c in range(2):
                load(r.branch_all.at[d, c], work.at[pl.ds(pl.multiple_of((2 * d + c) * rows, rows), rows)])
            loaded()
            query = heads[query_slot, now, :]
            attended_grad = jnp.zeros((pair, HD), F32)
            for j in range(n):
                attended_grad += matmul_nt(work[now, blocks[j]], feed[0, j, wide:, :])
            attended_grad = attended_grad.astype(BF16)
            keys, values, probs = scored(d, now)
            low = [p.astype(BF16) for p in probs]
            shares = [matmul_nt(attended_grad, values[k]) for k in range(planes)]
            delta = sum(
                jnp.sum(low[k].astype(F32) * shares[k], axis=-1, keepdims=True) for k in range(planes)
            )
            query_grad = jnp.zeros((pair, HD), F32)
            for k in range(planes):
                score_grad = (probs[k] * (shares[k] - delta)).astype(BF16)
                query_grad += matmul(score_grad, keys[k])
                key_grad = matmul_tn(score_grad, query) * scale
                value_grad = matmul_tn(low[k], attended_grad)
                heads[k, now, :] = jnp.where(side == 0, key_grad, value_grad).astype(BF16)
                heads[planes + k, now, :] = jnp.where(side == 0, value_grad, key_grad).astype(BF16)
            query_grad = query_grad * scale
            query_grad = query_grad * r.tables[0] + turn_back(query_grad * r.tables[1])
            heads[query_grad_slot, now, :] = query_grad.astype(BF16)
            return 0

        lax.fori_loop(0, half, attend_back, 0)
        advance(TICKS[5])
        lax.fori_loop(half, n, attend_back, 0)

        def kv_hand_over(k):
            return remote(
                heads.at[planes + k], r.kv_other.at[k], r.kv_send.at[k], r.kv_recv.at[k], other_core
            )

        def kv_load(source, slot):
            return local(source, r.kv_some.at[slot], r.kv_sem.at[slot])

        def kv_add(k, slot):
            def some(c, _):
                at = span(c * 64, 64)
                heads[k, at, :] = heads[k, at, :] + r.kv_some[slot, at, :]
                return 0

            lax.fori_loop(0, plane_rows // 64, some, 0)

        def kv_down(k):
            return remote(heads.at[k], r.kv_down.at[k], r.down_send.at[k], r.down_recv.at[k], below)

        def kv_up(k):
            return remote(
                heads.at[planes - k], r.kv_up.at[k], r.up_send.at[k], r.up_recv.at[k], above
            )

        order = list(range(planes - 1, -1, -1))
        for k in order:
            kv_hand_over(k).start()
        for at, k in enumerate(order):
            kv_hand_over(k).wait_recv()
            kv_load(r.kv_other.at[k], at % 2).start()
            kv_load(r.kv_other.at[k], at % 2).wait()
            kv_add(k, at % 2)

        def kv_send(k):
            @pl.when(z >= k)
            def _():
                kv_down(k).start()

            @pl.when(z + k < planes)
            def _():
                kv_up(k).start()

        def kv_receive(k, down_to, up_to):
            @pl.when((z + 1 >= k) & (z + 1 < planes))
            def _():
                kv_down(k).wait_recv()
                if down_to is not None:
                    copy = kv_load(r.kv_down.at[k], 0)
                    copy.start()
                    copy.wait()
                    kv_add(down_to, 0)

            @pl.when((z >= 1) & (z - 1 + k < planes))
            def _():
                kv_up(k).wait_recv()
                if up_to is not None:
                    copy = kv_load(r.kv_up.at[k], 1)
                    copy.start()
                    copy.wait()
                    kv_add(up_to, 1)

        kv_send(3)
        rows_sent(OUT, plane_rows)
        load(work.at[pl.ds(plane_rows, rows)], r.out_own)
        loaded()
        load(r.normed, work.at[pl.ds(plane_rows, plane_rows)])
        low_half, high_half = pl.ds(0, plane_rows), pl.ds(plane_rows, plane_rows)
        advance(TICKS[6])
        turned[0] = heads[attended_slot].astype(F32).T.astype(BF16)
        turned[1] = heads[query_grad_slot].astype(F32).T.astype(BF16)
        loaded()
        outer(query_at, turned[1], high_half)
        outer(output_at, turned[0], low_half)
        staged(query_at)
        staged(output_at)
        advance(TICKS[7])
        kv_receive(3, 2, 2)
        kv_send(2)
        advance(TICKS[8])
        kv_receive(2, 1, 3)
        kv_send(1)
        advance(TICKS[9])
        kv_receive(1, 0, 0)

        def kv_back(d, _):
            now = span(d * pair, pair)
            grad = heads[0, now, :].astype(F32)
            grad = grad * r.tables[2] + turn_back(grad * r.tables[3])
            heads[kv_grad_slot, now, :] = grad.astype(BF16)
            turned[2, :, now] = grad.T.astype(BF16)
            return 0

        lax.fori_loop(0, n, kv_back, 0)
        outer(kv_at, turned[2], high_half)

        def project_back(d):
            now = span(d * pair, pair)
            left = jnp.concatenate([heads[query_grad_slot, now, :], heads[kv_grad_slot, now, :]], axis=1)
            for j in range(n):
                put_rows(0, d, matmul_nt(left, feed[0, j, :wide, :]).astype(BF16), blocks[j])

        staged(kv_at)
        rows_reduced(ONE, 0, project_back)
        advance(TICKS[10])

        for d in (1, 2):
            branch_far(d).wait_send()
            branch_half(d).wait_send()
        for d in range(n):
            branch_near(d).wait_send()
        load(r.tokens, r.own_rows)
        rows_arrive(ONE, 0)
        loaded()

        def first_use(at, back):
            r.wide_rows[at, :] = r.wide_rows[at, :] + back

        norm_rows_back(0, r.own_rows, r.gains[0:1, :], first_use)
        load(r.wide_rows, r.tokens_grad)
        gain_terms(0)

        def gain_copy(at, source, target, peer):
            return remote(source, target, r.gain_send.at[at], r.gain_recv.at[at], peer)

        def gain_far(d):
            return gain_copy(d, r.gain_mine.at[d], r.gain_far.at[d], (here, chips[d]))

        def gain_hop(s, peer):
            return gain_copy(n + s, r.gain_sum.at[s], r.gain_in.at[s], peer)

        for d in range(1, n):
            gain_far(d).start()
        advance(TICKS[11])
        for d in range(1, n):
            gain_far(d).wait()
        r.gain_sum[0] = r.gain_mine[0] + r.gain_far[1] + r.gain_far[2] + r.gain_far[3]
        gain_hop(0, other_core).start()
        gain_hop(0, other_core).wait()
        r.gain_sum[1] = r.gain_sum[0] + r.gain_in[0]

        @pl.when(is_end)
        def _():
            gain_hop(1, partner).start()
            gain_hop(1, partner).wait_send()

        advance(TICKS[12])

        @pl.when(is_middle)
        def _():
            gain_hop(1, partner).wait_recv()
            r.gain_sum[2] = r.gain_sum[1] + r.gain_in[1]
            gain_hop(2, other_middle).start()
            gain_hop(2, other_middle).wait()
            r.gain_sum[3] = r.gain_sum[2] + r.gain_in[2]
            gain_hop(3, partner).start()
            gain_hop(3, partner).wait_send()

        @pl.when(is_end)
        def _():
            gain_hop(3, partner).wait_recv()
            r.gain_sum[3] = r.gain_in[3]

        load(r.gain_sum.at[3], r.gain_out)

        loaded()
        load(r.middle, r.wide_rows)
        load(r.out_own, r.own_rows)
        rows_arrive(OUT, plane_rows)
        loaded()

        def last_rows(c, _):
            at = span(c * few, few)
            total = r.wide_rows[at, :] + r.own_rows[at, :].astype(F32)
            for d in range(n):
                total += r.some_rows[d, at, :].astype(F32)
            r.own_rows[at, :] = total.astype(BF16)
            return 0

        lax.fori_loop(0, rows // few, last_rows, 0)
        load(r.own_rows, r.output)
        advance(units + 9 - steps_done[0])

        loaded()
        rows_sent(ONE, 0)
        for q in range(1, QUARTERS):
            for d in range(1, n):
                every(feed_far(q, d), leaves)
        for d in range(1, n):
            every(feed_half(d), leaves)
        for d in (1, 2):
            token_half(d).wait_send()
            cot_far(d).wait_send()
            cot_half(d).wait_send()
        for d in range(1, n):
            query_far(d).wait_send()
            out_far(d).wait_send()
        for d in range(n - 1):
            token_near(d).wait_send()
        for d in range(n):
            cot_near(d).wait_send()
        for k in range(planes):
            kv_hand_over(k).wait_send()
        for k in range(1, planes):

            @pl.when(z >= k)
            def _():
                kv_down(k).wait_send()

            @pl.when(z + k < planes)
            def _():
                kv_up(k).wait_send()

        finish()

    arrays = jax.tree.leaves((in_hbm, in_vmem))
    results = pl.pallas_call(
        backward,
        out_shape=jax.tree.leaves(out_hbm),
        in_specs=[pl.BlockSpec(memory_space=pl.ANY)] * len(jax.tree.leaves(in_hbm))
        + [pl.BlockSpec(memory_space=pltpu.VMEM)] * len(in_vmem),
        out_specs=[pl.BlockSpec(memory_space=pl.ANY)] * len(out_hbm),
        scratch_shapes=list(scratch.values()),
        cost_estimate=cost(30 * plane_rows * width * part, arrays, [unit_array] * 6),
        compiler_params=pltpu.CompilerParams(
            collective_id=0, has_side_effects=True, vmem_limit_bytes=63 * 1024 * 1024
        ),
        name="backward",
    )(*arrays)
    results = types.SimpleNamespace(**jax.tree.unflatten(jax.tree.structure(out_hbm), results))
    owned_tiles, near_tiles = (
        a.reshape(tiles_count, n, quarter, wide) for a in (results.owned, results.near)
    )

    def place(
        me_ref, own_ref, near_ref, gate, up, down, query, out, key, value, taken, turned, straight, in_sem, out_sem
    ):
        chip, side = me_ref[0], me_ref[1]
        steps = 2 * n

        def take(s, t, source):
            return pltpu.make_async_copy(source.at[t, s // 2], taken.at[t], in_sem.at[t])

        def start_taking(s, t):
            for source, e in ((own_ref, 0), (near_ref, 1)):

                @pl.when(s % 2 == e)
                def _():
                    take(s, t, source).start()

        def is_straight(t):
            return t == output_at or (t < query_at and t % 3 == 0)

        def goal(s, t):
            owner = 2 * (chip ^ (s // 2)) + (side ^ (s % 2))
            if t == query_at:
                return query.at[:, column(owner, HD)]
            if t == output_at:
                return out.at[column(owner, HD)]
            here = column(owner * QUARTERS + t // 3, quarter)
            return (down.at[here], gate.at[:, here], up.at[:, here])[t % 3]

        def put(s, t, use):
            source = straight.at[t // 3] if is_straight(t) else turned.at[t]
            if t != kv_at:
                use(pltpu.make_async_copy(source, goal(s, t), out_sem.at[t]))
                return
            for target, e in ((key, 0), (value, 1)):

                @pl.when((side + s) % 2 == e)
                def _():
                    there = target.at[:, column(chip ^ (s // 2), HD)]
                    use(pltpu.make_async_copy(source, there, out_sem.at[t]))

        for t in range(tiles_count):
            start_taking(0, t)

        def one(s, _):
            for t in range(tiles_count):
                take(s, t, own_ref).wait()

                @pl.when(s > 0)
                def _():
                    put(s - 1, t, lambda copy: copy.wait())

                if is_straight(t):
                    straight[t // 3] = taken[t].astype(F32)
                else:
                    turned[t] = taken[t].T.astype(F32)
                put(s, t, lambda copy: copy.start())

                @pl.when(s + 1 < steps)
                def _():
                    start_taking(s + 1, t)

            return 0

        lax.fori_loop(0, steps, one, 0)
        for t in range(tiles_count):
            put(steps - 1, t, lambda copy: copy.wait())

    in_place = pl.BlockSpec(memory_space=pl.ANY)
    placed = pl.pallas_call(
        place,
        out_shape=[
            shape(a.shape, F32)
            for a in (
                gate_weight,
                up_weight,
                down_weight,
                query_weight,
                output_weight,
                key_weight,
                value_weight,
            )
        ],
        in_specs=[pl.BlockSpec(memory_space=pltpu.SMEM), in_place, in_place],
        out_specs=[in_place] * 7,
        scratch_shapes=[
            pltpu.VMEM((tiles_count, quarter, wide), BF16),
            pltpu.VMEM((tiles_count, wide, quarter), F32),
            pltpu.VMEM((QUARTERS + 1, quarter, wide), F32),
            dma((tiles_count,)),
            dma((tiles_count,)),
        ],
        compiler_params=pltpu.CompilerParams(vmem_limit_bytes=VMEM_BYTES),
        name="place",
    )(me, owned_tiles, near_tiles)
    gate_grad, up_grad, down_grad, query_grad, output_grad, key_grad, value_grad = placed

    return (
        results.output[None],
        results.tokens_grad[None],
        query_grad,
        key_grad,
        value_grad,
        output_grad,
        results.gain_out[0],
        gate_grad,
        up_grad,
        down_grad,
        results.gain_out[1],
    )


def solution(mesh):
    chips, pieces = mesh.shape["fsdp"], mesh.shape["ctx"]
    one_head_each = 2 * chips == H and chips == KVH and pieces == 8
    return jax.shard_map(
        plane_layer if one_head_each else ring_layer,
        mesh=mesh,
        in_specs=(
            P("fsdp", "ctx", None),
            P("fsdp", None),
            P("fsdp", None),
            P("fsdp", None),
            P(None, "fsdp"),
            P("fsdp"),
            P("fsdp", None),
            P("fsdp", None),
            P(None, "fsdp"),
            P("fsdp"),
            P("fsdp", "ctx", None),
            P(),
            P(),
        ),
        out_specs=(
            P("fsdp", "ctx", None),
            P("fsdp", "ctx", None),
            P("fsdp", None),
            P("fsdp", None),
            P("fsdp", None),
            P(None, "fsdp"),
            P("fsdp"),
            P("fsdp", None),
            P("fsdp", None),
            P(None, "fsdp"),
            P("fsdp"),
        ),
        check_vma=False,
    )
```

```python
import functools
import types

import jax
import jax.numpy as jnp
from jax import lax
from jax.experimental import pallas as pl
from jax.experimental.pallas import tpu as pltpu
from jax.sharding import PartitionSpec as P

H = 8
KVH = 4
HD = 256


epsilon = 1e-06
theta = 1000042.0
masked_score = -1e30


def passed_along(value, axis, by):
    devices = lax.axis_size(axis)
    return lax.ppermute(value, axis, [(i, (i + by) % devices) for i in range(devices)])


def rope_tables(positions):
    half = HD // 2
    frequency = theta ** (-(jnp.arange(half, dtype=jnp.float32) * 2.0 / HD))
    angle = positions[:, None] * frequency[None, :]
    angle = jnp.concatenate([angle, angle], axis=-1)
    return (jnp.cos(angle), jnp.sin(angle))


def rotate(values, cosine, sine):
    half = values.shape[-1] // 2
    turned = jnp.concatenate([-values[..., half:], values[..., :half]], axis=-1)
    return values * cosine[:, None, :] + turned * sine[:, None, :]


def rotate_back(grads, cosine, sine):
    half = grads.shape[-1] // 2
    scaled = grads * sine[:, None, :]
    turned = jnp.concatenate([scaled[..., half:], -scaled[..., :half]], axis=-1)
    return grads * cosine[:, None, :] + turned


def split_heads(block):
    count = block.shape[0]
    key_cols = KVH * HD
    key_part = block[:, :key_cols].reshape(count, KVH, HD).transpose(1, 0, 2)
    value_part = block[:, key_cols:].reshape(count, KVH, HD).transpose(1, 0, 2)
    return (key_part, value_part)


def merge_heads(grouped):
    return grouped.transpose(1, 0, 2).reshape(grouped.shape[1], KVH * HD)


def weight_terms(lefts, rights):
    pieces = []
    for index in range(4):
        column = lefts[index]
        pieces.append(
            jnp.einsum("tc,tn->cn", column, rights[index], preferred_element_type=jnp.float32)
        )
    return jnp.concatenate(pieces, axis=1)


def ring_layer(
    tokens,
    query_weight,
    key_weight,
    value_weight,
    output_weight,
    first_gain,
    gate_weight,
    up_weight,
    down_weight,
    second_gain,
    cotangent,
    block_ids,
    piece_order,
):
    ctx_count = lax.axis_size("ctx")
    fsdp_count = lax.axis_size("fsdp")
    here = lax.axis_index("ctx")
    rows = tokens.shape[1]
    width = tokens.shape[2]
    group = H // KVH
    query_cols = H * HD
    key_cols = KVH * HD
    hidden_cols = gate_weight.shape[1]
    scale = HD ** (-0.5)
    whole_query, whole_key, whole_value, whole_output, gain_one = (
        lax.all_gather(query_weight, "fsdp", axis=0, tiled=True),
        lax.all_gather(key_weight, "fsdp", axis=0, tiled=True),
        lax.all_gather(value_weight, "fsdp", axis=0, tiled=True),
        lax.all_gather(output_weight, "fsdp", axis=1, tiled=True),
        lax.all_gather(first_gain, "fsdp", axis=0, tiled=True),
    )
    id_row = lax.dynamic_index_in_dim(block_ids, lax.axis_index("fsdp"), 0, keepdims=False)
    start_own = lax.dynamic_index_in_dim(piece_order, here, 0, keepdims=False) * rows
    offsets = jnp.arange(rows, dtype=jnp.int32)
    cosine, sine = rope_tables((start_own + offsets).astype(jnp.float32))
    own_ids = lax.dynamic_slice_in_dim(id_row, start_own, rows)
    query_ids = jnp.tile(own_ids, group)

    def visible(source):
        key_start = lax.dynamic_index_in_dim(piece_order, source, 0, keepdims=False) * rows
        key_ids = lax.dynamic_slice_in_dim(id_row, key_start, rows)
        return key_ids[None, :] <= query_ids[:, None]

    inputs = tokens[0].astype(jnp.float32)
    scale_one = lax.rsqrt(jnp.mean(inputs * inputs, axis=-1, keepdims=True) + epsilon)
    unit_one = inputs * scale_one
    normed = (unit_one * gain_one.astype(jnp.float32)).astype(jnp.bfloat16)
    query = jnp.dot(normed, whole_query, preferred_element_type=jnp.float32).reshape(rows, H, HD)
    query_rot = rotate(query, cosine, sine).astype(jnp.bfloat16)
    keys = jnp.dot(normed, whole_key, preferred_element_type=jnp.float32).reshape(rows, KVH, HD)
    keys_rot = rotate(keys, cosine, sine).astype(jnp.bfloat16).reshape(rows, key_cols)
    values = jnp.dot(normed, whole_value, preferred_element_type=jnp.float32).astype(jnp.bfloat16)
    key_value = jnp.concatenate([keys_rot, values], axis=-1)
    grouped = (
        query_rot.reshape(rows, KVH, group, HD).transpose(1, 2, 0, 3).reshape(KVH, group * rows, HD)
    )

    def forward_step(state, block, source):
        running, total, weighted = state
        key_part, value_part = split_heads(block)
        allowed = visible(source)
        scores = (
            jnp.einsum("hqd,hkd->hqk", grouped, key_part, preferred_element_type=jnp.float32)
            * scale
        )
        scores = jnp.where(allowed[None], scores, masked_score)
        newest = jnp.maximum(running, jnp.max(scores, axis=-1))
        factor = jnp.exp(running - newest)
        shares = jnp.where(allowed[None], jnp.exp(scores - newest[..., None]), 0.0)
        total = total * factor + jnp.sum(shares, axis=-1)
        weighted = weighted * factor[..., None] + jnp.einsum(
            "hqk,hkd->hqd",
            shares.astype(jnp.bfloat16),
            value_part,
            preferred_element_type=jnp.float32,
        )
        return (newest, total, weighted)

    start_state = (
        jnp.full((KVH, group * rows), masked_score, jnp.float32),
        jnp.zeros((KVH, group * rows), jnp.float32),
        jnp.zeros((KVH, group * rows, HD), jnp.float32),
    )
    state = forward_step(start_state, key_value, here)

    def forward_turn(turn, carry):
        block, inner = carry
        block = passed_along(block, "ctx", 1)
        source = (here - turn) % ctx_count
        return (block, forward_step(inner, block, source))

    passed_block, state = lax.fori_loop(1, ctx_count, forward_turn, (key_value, state))
    running, total, weighted = state
    attended = weighted / total[..., None]
    log_total = running + jnp.log(total)
    attended_low = (
        attended.reshape(KVH, group, rows, HD)
        .transpose(2, 0, 1, 3)
        .reshape(rows, query_cols)
        .astype(jnp.bfloat16)
    )
    middle = inputs + jnp.dot(attended_low, whole_output, preferred_element_type=jnp.float32)
    gain_two, whole_gate, whole_up, whole_down = (
        lax.all_gather(second_gain, "fsdp", axis=0, tiled=True),
        lax.all_gather(gate_weight, "fsdp", axis=0, tiled=True),
        lax.all_gather(up_weight, "fsdp", axis=0, tiled=True),
        lax.all_gather(down_weight, "fsdp", axis=1, tiled=True),
    )
    scale_two = lax.rsqrt(jnp.mean(middle * middle, axis=-1, keepdims=True) + epsilon)
    unit_two = middle * scale_two
    normed_two = (unit_two * gain_two.astype(jnp.float32)).astype(jnp.bfloat16)
    gate = jnp.dot(normed_two, whole_gate, preferred_element_type=jnp.float32)
    up = jnp.dot(normed_two, whole_up, preferred_element_type=jnp.float32)
    sigmoid_gate = jax.nn.sigmoid(gate)
    activated = gate * sigmoid_gate
    hidden = (activated * up).astype(jnp.bfloat16)
    result = middle + jnp.dot(hidden, whole_down, preferred_element_type=jnp.float32)
    output = result.astype(jnp.bfloat16)[None]
    upstream = cotangent[0]
    hidden_grad = jnp.einsum("tm,fm->tf", upstream, whole_down, preferred_element_type=jnp.float32)
    gate_grad = (hidden_grad * up * sigmoid_gate * (1.0 + gate * (1.0 - sigmoid_gate))).astype(
        jnp.bfloat16
    )
    up_grad = (hidden_grad * activated).astype(jnp.bfloat16)
    normed_two_grad = jnp.einsum(
        "tf,mf->tm", gate_grad, whole_gate, preferred_element_type=jnp.float32
    ) + jnp.einsum("tf,mf->tm", up_grad, whole_up, preferred_element_type=jnp.float32)
    gain_two_term = jnp.sum(normed_two_grad * unit_two, axis=0)
    unit_two_grad = normed_two_grad * gain_two.astype(jnp.float32)
    middle_grad = upstream.astype(jnp.float32) + scale_two * (
        unit_two_grad - unit_two * jnp.mean(unit_two_grad * unit_two, axis=-1, keepdims=True)
    )
    branch_grad = middle_grad.astype(jnp.bfloat16)
    attended_grad = jnp.einsum(
        "tm,cm->tc", branch_grad, whole_output, preferred_element_type=jnp.float32
    ).astype(jnp.bfloat16)
    grad_grouped = (
        attended_grad.reshape(rows, KVH, group, HD)
        .transpose(1, 2, 0, 3)
        .reshape(KVH, group * rows, HD)
    )
    delta = jnp.sum(grad_grouped.astype(jnp.float32) * attended, axis=-1)

    def backward_step(query_total, block, source):
        key_part, value_part = split_heads(block)
        allowed = visible(source)
        scores = (
            jnp.einsum("hqd,hkd->hqk", grouped, key_part, preferred_element_type=jnp.float32)
            * scale
        )
        scores = jnp.where(allowed[None], scores, masked_score)
        shares = jnp.where(allowed[None], jnp.exp(scores - log_total[..., None]), 0.0)
        value_grad = jnp.einsum(
            "hqk,hqd->hkd",
            shares.astype(jnp.bfloat16),
            grad_grouped,
            preferred_element_type=jnp.float32,
        )
        share_grad = jnp.einsum(
            "hqd,hkd->hqk", grad_grouped, value_part, preferred_element_type=jnp.float32
        )
        score_grad = (shares * (share_grad - delta[..., None])).astype(jnp.bfloat16)
        query_total = query_total + jnp.einsum(
            "hqk,hkd->hqd", score_grad, key_part, preferred_element_type=jnp.float32
        )
        key_grad = (
            jnp.einsum("hqk,hqd->hkd", score_grad, grouped, preferred_element_type=jnp.float32)
            * scale
        )
        return (
            query_total,
            jnp.concatenate([merge_heads(key_grad), merge_heads(value_grad)], axis=-1),
        )

    query_total, first_grad = backward_step(
        jnp.zeros((KVH, group * rows, HD), jnp.float32), key_value, here
    )
    held = first_grad

    def backward_turn(turn, carry):
        block, kept, total_query = carry
        block = passed_along(block, "ctx", 1)
        source = (here - turn) % ctx_count
        total_query, block_grad = backward_step(total_query, block, source)
        kept = passed_along(kept.astype(jnp.bfloat16), "ctx", 1).astype(kept.dtype) + block_grad
        return (block, kept, total_query)

    passed_again, held, query_total = lax.fori_loop(
        1, ctx_count, backward_turn, (key_value, held, query_total)
    )
    own_grad = passed_along(held.astype(jnp.bfloat16), "ctx", 1).astype(held.dtype)
    query_rot_grad = (
        (query_total * scale)
        .reshape(KVH, group, rows, HD)
        .transpose(2, 0, 1, 3)
        .reshape(rows, H, HD)
    )
    query_grad = (
        rotate_back(query_rot_grad, cosine, sine).reshape(rows, query_cols).astype(jnp.bfloat16)
    )
    key_grad = (
        rotate_back(own_grad[:, :key_cols].reshape(rows, KVH, HD), cosine, sine)
        .reshape(rows, key_cols)
        .astype(jnp.bfloat16)
    )
    value_grad = own_grad[:, key_cols:].astype(jnp.bfloat16)
    normed_grad = jnp.einsum(
        "tc,mc->tm", query_grad, whole_query, preferred_element_type=jnp.float32
    )
    normed_grad = normed_grad + jnp.einsum(
        "tc,mc->tm", key_grad, whole_key, preferred_element_type=jnp.float32
    )
    normed_grad = normed_grad + jnp.einsum(
        "tc,mc->tm", value_grad, whole_value, preferred_element_type=jnp.float32
    )
    gain_one_term = jnp.sum(normed_grad * unit_one, axis=0)
    unit_one_grad = normed_grad * gain_one.astype(jnp.float32)
    tokens_grad = middle_grad + scale_one * (
        unit_one_grad - unit_one * jnp.mean(unit_one_grad * unit_one, axis=-1, keepdims=True)
    )
    projected = jnp.concatenate([query_grad, key_grad, value_grad], axis=-1)
    gate_up = jnp.concatenate([gate_grad, up_grad], axis=-1)
    lefts = jnp.stack([normed, branch_grad, normed_two, upstream])
    rights = (projected, attended_low, gate_up, hidden)
    piece = lax.psum_scatter(
        weight_terms(lefts, rights).astype(jnp.bfloat16), "fsdp", scatter_dimension=0, tiled=True
    )
    shard = lax.psum(piece, "ctx").astype(jnp.float32)
    gain_one_sum, gain_two_sum = lax.psum((gain_one_term, gain_two_term), ("ctx", "fsdp"))
    own_rows = width // fsdp_count
    own_start = lax.axis_index("fsdp") * own_rows
    value_begin = query_cols + key_cols
    output_begin = value_begin + key_cols
    gate_begin = output_begin + query_cols
    up_begin = gate_begin + hidden_cols
    down_begin = up_begin + hidden_cols
    return (
        output,
        tokens_grad[None],
        shard[:, :query_cols],
        shard[:, query_cols:value_begin],
        shard[:, value_begin:output_begin],
        shard[:, output_begin:gate_begin].T,
        lax.dynamic_slice_in_dim(gain_one_sum, own_start, own_rows),
        shard[:, gate_begin:up_begin],
        shard[:, up_begin:down_begin],
        shard[:, down_begin : down_begin + hidden_cols].T,
        lax.dynamic_slice_in_dim(gain_two_sum, own_start, own_rows),
    )


VMEM_BYTES = 58 * 1024 * 1024
BF16 = jnp.bfloat16
F32 = jnp.float32
QUARTERS = 4
MESH = pl.DeviceIdType.MESH
TICKS = (2, 1, 2, 2, 3, 2, 1, 1, 1, 2, 6, 2, 2)
LINES = 2


def matmul(a, b):
    return lax.dot_general(a, b, (((1,), (0,)), ((), ())), preferred_element_type=F32)


def matmul_nt(a, b):
    return lax.dot_general(a, b, (((1,), (1,)), ((), ())), preferred_element_type=F32)


def matmul_tn(a, b):
    return lax.dot_general(a, b, (((0,), (0,)), ((), ())), preferred_element_type=F32)


def cost(flops, arrays, outs, exps=0):
    moved = sum(a.size * a.dtype.itemsize for a in arrays) + sum(
        o.size * o.dtype.itemsize for o in outs
    )
    return pl.CostEstimate(flops=int(flops), bytes_accessed=int(moved), transcendentals=int(exps))


def run_whole(body, me, arrays, outs, scratch=(), flops=0, in_hbm=0, name=None):
    count = len(arrays) - in_hbm
    return pl.pallas_call(
        body,
        out_shape=outs,
        in_specs=[pl.BlockSpec(memory_space=pltpu.SMEM)]
        + [pl.BlockSpec(memory_space=pltpu.VMEM)] * count
        + [pl.BlockSpec(memory_space=pl.ANY)] * in_hbm,
        out_specs=jax.tree.map(lambda _: pl.BlockSpec(memory_space=pltpu.VMEM), outs),
        scratch_shapes=list(scratch),
        cost_estimate=cost(flops, arrays, jax.tree.leaves(outs)),
        compiler_params=pltpu.CompilerParams(vmem_limit_bytes=VMEM_BYTES),
        name=name,
    )(me, *arrays)


def run_grid(body, me, grid, arrays, in_specs, outs, out_specs, scratch=(), flops=0, aliases=None, name=None):
    return pl.pallas_call(
        body,
        out_shape=outs,
        grid_spec=pltpu.PrefetchScalarGridSpec(
            num_scalar_prefetch=1,
            grid=grid,
            in_specs=in_specs,
            out_specs=out_specs,
            scratch_shapes=list(scratch),
        ),
        cost_estimate=cost(flops, arrays, jax.tree.leaves(outs)),
        input_output_aliases=aliases or {},
        compiler_params=pltpu.CompilerParams(vmem_limit_bytes=VMEM_BYTES),
        name=name,
    )(me, *arrays)


def shape(dims, kind=BF16):
    return jax.ShapeDtypeStruct(tuple(dims), kind)


def fixed(block):
    return pl.BlockSpec(block, lambda i, me: (0,) * len(block), pipeline_mode=pl.Buffered(1))


def column(index, wide):
    return pl.ds(pl.multiple_of(index * wide, wide), wide)


def turn(values):
    half = values.shape[-1] // 2
    return jnp.concatenate([-values[:, half:], values[:, :half]], axis=-1)


def turn_back(values):
    half = values.shape[-1] // 2
    return jnp.concatenate([values[:, half:], -values[:, :half]], axis=-1)


def plane_layer(
    tokens,
    query_weight,
    key_weight,
    value_weight,
    output_weight,
    first_gain,
    gate_weight,
    up_weight,
    down_weight,
    second_gain,
    cotangent,
    block_ids,
    piece_order,
):
    ctx_count = lax.axis_size("ctx")
    n = lax.axis_size("fsdp")
    planes = ctx_count // 2
    ctx = lax.axis_index("ctx")
    z, core = ctx // 2, ctx % 2
    f = lax.axis_index("fsdp")
    me = jnp.stack([f, core]).astype(jnp.int32)
    rows, width = tokens.shape[1:]
    pair = 2 * rows
    plane_rows = n * pair
    wide = width // n
    hidden_cols = gate_weight.shape[1]
    part = hidden_cols // (2 * n)
    quarter = part // QUARTERS
    scale = HD ** (-0.5)

    def across(value, d):
        return lax.ppermute(value, "fsdp", [(i, i ^ d) for i in range(n)])

    def sibling(value):
        return lax.ppermute(value, "ctx", [(i, i ^ 1) for i in range(ctx_count)])

    def along(value, step):
        pairs = [(i, i + 2 * step) for i in range(ctx_count)]
        return lax.ppermute(value, "ctx", [(a, b) for a, b in pairs if 0 <= b < ctx_count])

    def between_planes(value, moves):
        return lax.ppermute(
            value, "ctx", [(2 * a + side, 2 * b + side) for a, b in moves for side in range(2)]
        )

    def gathered(value):
        own = [value] + [across(value, d) for d in range(1, n)]
        return own, [sibling(block) for block in own]

    def reduced(own, other):
        near = [sibling(block) for block in other]
        sent = [
            across((own[d].astype(F32) + near[d].astype(F32)).astype(BF16), d) for d in range(1, n)
        ]
        return [own[0], near[0]] + sent

    middle_left, middle_right = planes // 2 - 1, planes // 2
    folds = [
        [(s, s + 1), (planes - 1 - s, planes - 2 - s)] for s in range(middle_left)
    ]

    def summed_over_planes(value):
        for moves in folds:
            value = (
                value.astype(F32) + between_planes(value, moves).astype(F32)
            ).astype(value.dtype)
        crossed = between_planes(value, [(middle_left, middle_right), (middle_right, middle_left)])
        value = (value.astype(F32) + crossed.astype(F32)).astype(value.dtype)
        for s, moves in reversed(list(enumerate(folds))):
            back = between_planes(value, [(b, a) for a, b in moves])
            receives = (z == s) | (z == planes - 1 - s)
            value = jnp.where(receives, back, value)
        return value

    place = jnp.arange(rows, dtype=jnp.int32)
    own_pieces = lax.dynamic_slice_in_dim(piece_order, 2 * z, 2)
    positions = (own_pieces[:, None] * rows + place[None, :]).reshape(pair).astype(F32)
    cosine, sine = rope_tables(positions)
    is_value = core == 1
    kv_cosine = jnp.where(is_value, 1.0, cosine)
    kv_sine = jnp.where(is_value, 0.0, sine)
    chips = f ^ jnp.arange(n, dtype=jnp.int32)
    ring = (z - jnp.arange(planes, dtype=jnp.int32)) % planes
    ring_ctx = (2 * ring[:, None] + jnp.arange(2, dtype=jnp.int32)[None, :]).reshape(-1)
    id_pieces = block_ids.reshape(n, ctx_count, rows)
    ids = id_pieces[chips[:, None], piece_order[ring_ctx][None, :]]
    key_ids = ids.reshape(n, planes, 1, pair)
    query_ids = ids[:, :2].reshape(n, pair, 1)

    def cut_weights(me_ref, *refs):
        keys, values, (one, two), outs = refs[:n], refs[n : 2 * n], refs[2 * n : 2 * n + 2], refs[2 * n + 2 :]
        keys_here = me_ref[1] == 0
        for d in range(n):

            @pl.when(keys_here)
            def _():
                outs[d][:wide, :] = keys[d][...]

            @pl.when(jnp.logical_not(keys_here))
            def _():
                outs[d][:wide, :] = values[d][...]

            pick = lax.broadcasted_iota(jnp.int32, (16, HD), 0) < 8
            for g, gain in enumerate((one, two)):
                halves = [gain[:, h * HD : (h + 1) * HD].astype(F32) for h in range(2)]
                outs[d][wide + 16 * g : wide + 16 * (g + 1), :] = jnp.where(pick, *halves).astype(BF16)

    def chip_of(d):
        return lambda i, me: (0, me[0] ^ d)

    own_tokens = tokens[0]
    near_tokens = [own_tokens] + [across(own_tokens, d) for d in (1, 2)]
    gain_spec = pl.BlockSpec((1, wide), lambda i, me: (0, 0))
    cut = run_grid(
        cut_weights,
        me,
        (1,),
        [key_weight] * n
        + [value_weight] * n
        + [first_gain.reshape(1, wide), second_gain.reshape(1, wide)],
        [pl.BlockSpec((wide, HD), chip_of(d)) for d in range(n)] * 2 + [gain_spec, gain_spec],
        [shape((wide + 32, HD))] * n,
        [pl.BlockSpec((wide + 32, HD), lambda i, me: (0, 0))] * n,
        name="cut_weights",
    )
    weights_in = [cut[0]] + [across(cut[d], d) for d in range(1, n)]
    piece = (wide + quarter, 2 * quarter)
    own_cotangent = cotangent[0]
    block = (rows, width)

    tiles_count = 3 * QUARTERS + 3
    query_at, output_at, kv_at = tiles_count - 3, tiles_count - 2, tiles_count - 1
    units = 2 * tiles_count
    unit = (2, quarter, wide)
    held_sums, held_ends, ahead = 4, 3, 2
    MID, BACK, OUT, ONE = range(4)
    query_slot, attended_slot, query_grad_slot, kv_grad_slot = range(2 * planes, 2 * planes + 4)
    kept_slots = 2 * planes + 2
    columns = (plane_rows, HD)
    lanes = (8, wide)
    dma = pltpu.SemaphoreType.DMA

    in_hbm = dict(
        near_tokens=near_tokens,
        in_weight=weights_in,
        query_weight=query_weight,
        output_weight=output_weight,
        gate_weight=gate_weight,
        up_weight=up_weight,
        down_weight=down_weight,
        cotangent=own_cotangent,
        tokens=own_tokens,
    )
    in_vmem = dict(
        tables=jnp.stack([cosine, sine, kv_cosine, kv_sine]),
        query_ids=query_ids,
        key_ids=key_ids,
    )
    unit_array = shape((units,) + unit)
    out_hbm = dict(
        tiles=unit_array,
        from_end=unit_array,
        from_middle=unit_array,
        finals=unit_array,
        owned=unit_array,
        near=unit_array,
        row_near=shape((4, n) + block),
        row_far=shape((4, n) + block),
        cot_all=shape((2, n) + block),
        query_in=shape((n, wide, HD)),
        kept=shape((kept_slots,) + columns),
        out_weight=shape((2, 2, HD, wide)),
        normed=shape((plane_rows, width)),
        middle=shape(block, F32),
        branch_all=shape((n, 2) + block),
        kv_other=shape((planes,) + columns),
        kv_down=shape((planes,) + columns),
        kv_up=shape((planes,) + columns),
        out_own=shape(block),
        tokens_grad=shape(block, F32),
        output=shape(block),
        gain_out=shape(lanes, F32),
    )
    scratch = dict(
        work=pltpu.VMEM((2 * plane_rows, width), BF16),
        feed=pltpu.VMEM((QUARTERS, n) + piece, BF16),
        heads=pltpu.VMEM((3 * QUARTERS, plane_rows, HD), BF16),
        turned=pltpu.VMEM((3, HD, plane_rows), BF16),
        stage=pltpu.VMEM((2, n, quarter, wide), BF16),
        mine=pltpu.VMEM((2,) + unit, BF16),
        theirs=pltpu.VMEM((2,) + unit, BF16),
        crossed=pltpu.VMEM((2,) + unit, BF16),
        sums=pltpu.VMEM((held_sums,) + unit, BF16),
        ends=pltpu.VMEM((held_ends,) + unit, BF16),
        some_rows=pltpu.VMEM((n,) + block, BF16),
        wide_rows=pltpu.VMEM(block, F32),
        own_rows=pltpu.VMEM(block, BF16),
        kv_some=pltpu.VMEM((2,) + columns, BF16),
        flat=pltpu.VMEM((8, width), F32),
        gain_mine=pltpu.VMEM((n,) + lanes, F32),
        gain_far=pltpu.VMEM((n,) + lanes, F32),
        gain_sum=pltpu.VMEM((4,) + lanes, F32),
        gain_in=pltpu.VMEM((4,) + lanes, F32),
        load_sem=dma((4 * n + n,)),
        gains=pltpu.VMEM((8, width), F32),
        gain_rows=pltpu.VMEM((n, 32, HD), BF16),
        feed_local=dma((3 * QUARTERS,)),
        feed_send=dma((3 * QUARTERS * n,)),
        feed_recv=dma((3 * QUARTERS * n,)),
        stage_sem=dma((2, 2)),
        one_send=dma((units,)),
        one_recv=dma((units,)),
        two_send=dma((units,)),
        two_recv=dma((units,)),
        three_send=dma((units,)),
        three_recv=dma((units,)),
        mine_sem=dma((2,)),
        theirs_sem=dma((2,)),
        crossed_sem=dma((2,)),
        final_sem=dma((held_ends,)),
        deal_local=dma((units,)),
        deal_send=dma((2 * units,)),
        deal_recv=dma((2 * units,)),
        sib_send=dma((units,)),
        sib_recv=dma((units,)),
        row_sem=dma((n,)),
        row_near_send=dma((4 * n,)),
        row_near_recv=dma((4 * n,)),
        row_far_send=dma((4 * n,)),
        row_far_recv=dma((4 * n,)),
        token_send=dma((n,)),
        token_recv=dma((n,)),
        query_send=dma((n,)),
        query_recv=dma((n,)),
        out_send=dma((n,)),
        out_recv=dma((n,)),
        cot_send=dma((n,)),
        cot_recv=dma((n,)),
        cot_near_send=dma((n,)),
        cot_near_recv=dma((n,)),
        two_local=dma((1,)),
        two_far_send=dma((n,)),
        two_far_recv=dma((n,)),
        two_near_send=dma((n,)),
        two_near_recv=dma((n,)),
        two_half_send=dma((n,)),
        two_half_recv=dma((n,)),
        branch_half_send=dma((n,)),
        branch_half_recv=dma((n,)),
        climb_send=dma((n * planes,)),
        climb_recv=dma((n * planes,)),
        fall_send=dma((n * planes,)),
        fall_recv=dma((n * planes,)),
        soft=pltpu.VMEM((2 * n, pair, 1), F32),
        pass_send=dma((n * planes,)),
        pass_recv=dma((n * planes,)),
        cot_half_send=dma((n,)),
        cot_half_recv=dma((n,)),
        share_send=dma((2 * n,)),
        share_recv=dma((2 * n,)),
        token_half_send=dma((n,)),
        token_half_recv=dma((n,)),
        keep_sem=dma((3,)),
        branch_local=dma((1,)),
        branch_send=dma((n,)),
        branch_recv=dma((n,)),
        branch_near_send=dma((n,)),
        branch_near_recv=dma((n,)),
        kv_sem=dma((2,)),
        kv_send=dma((planes,)),
        kv_recv=dma((planes,)),
        down_send=dma((planes,)),
        down_recv=dma((planes,)),
        up_send=dma((planes,)),
        up_recv=dma((planes,)),
        gain_send=dma((n + 4,)),
        gain_recv=dma((n + 4,)),
    )

    def backward(*refs):
        r, first = types.SimpleNamespace(), 0
        for group in (in_hbm, in_vmem, out_hbm):
            leaves, form = jax.tree.flatten(group)
            vars(r).update(jax.tree.unflatten(form, refs[first : first + len(leaves)]))
            first += len(leaves)
        vars(r).update(zip(scratch, refs[first:]))
        here = lax.axis_index("ctx")
        chip = lax.axis_index("fsdp")
        z, side = here // 2, here % 2
        is_middle = (z == 1) | (z == 2)
        is_end = jnp.logical_not(is_middle)
        chips = [chip, chip + 1 - 2 * (chip % 2), (chip + 2) % 4, 3 - chip]
        partner = (2 * (z + 1 - 2 * (z % 2)) + side, chip)
        other_middle = (2 * (3 - z) + side, chip)
        other_core = (here + 1 - 2 * side, chip)
        below, above = (here - 2, chip), (here + 2, chip)
        blocks = [pl.ds(pl.multiple_of(c * wide, wide), wide) for c in chips]
        work, feed, heads, turned, stage = r.work, r.feed, r.heads, r.turned, r.stage

        barrier = pltpu.get_barrier_semaphore()
        for peer in [(here, c) for c in chips[1:]] + [partner, other_core]:
            pl.semaphore_signal(barrier, inc=1, device_id=peer, device_id_type=MESH)

        @pl.when(is_middle)
        def _():
            pl.semaphore_signal(barrier, inc=1, device_id=other_middle, device_id_type=MESH)
            pl.semaphore_wait(barrier, n + 2)

        @pl.when(is_end)
        def _():
            pl.semaphore_wait(barrier, n + 1)

        def remote(source, target, send, recv, peer):
            return pltpu.make_async_remote_copy(
                src_ref=source,
                dst_ref=target,
                send_sem=send,
                recv_sem=recv,
                device_id=peer,
                device_id_type=MESH,
            )

        local = pltpu.make_async_copy

        def span(first, count):
            return pl.ds(pl.multiple_of(first, count), count)

        def head_of(d):
            return span((2 * chips[d] + side) * HD, HD)

        def feed_parts(q, d, first=0, count=wide):
            there = span(((2 * chips[d] + side) * QUARTERS + q) * quarter, quarter)
            rows_in = pl.ds(first, count)
            below = 0 if count == wide else pl.multiple_of(first // 2, quarter // 2)
            some = pl.ds(
                pl.multiple_of(
                    ((2 * chips[d] + side) * QUARTERS + q) * quarter + below, quarter // 2
                ),
                count // 2,
            )
            below = wide if count == wide else pl.multiple_of(wide + below, quarter // 2)
            return (
                (r.gate_weight.at[rows_in, there], feed.at[q, d, rows_in, pl.ds(0, quarter)]),
                (r.up_weight.at[rows_in, there], feed.at[q, d, rows_in, pl.ds(quarter, quarter)]),
                (r.down_weight.at[some], feed.at[q, d, pl.ds(below, count // 2)]),
            )

        def feed_far(q, d, *rows_of):
            copies = []
            for part, (source, target) in enumerate(feed_parts(q, d, *rows_of)):
                at = (q * n + d) * 3 + part
                copies.append(
                    remote(source, target, r.feed_send.at[at], r.feed_recv.at[at], (here, chips[d]))
                )
            return copies

        def feed_own(q):
            return [
                local(source, target, r.feed_local.at[3 * q + part])
                for part, (source, target) in enumerate(feed_parts(q, 0))
            ]

        def every(copies, use):
            for copy in copies:
                use(copy)

        starts, waits = lambda c: c.start(), lambda c: c.wait()
        arrives, leaves = lambda c: c.wait_recv(), lambda c: c.wait_send()

        def hop_one(i):
            return remote(r.tiles.at[i], r.from_end.at[i], r.one_send.at[i], r.one_recv.at[i], partner)

        def hop_two(i):
            return remote(
                r.sums.at[i % held_sums],
                r.from_middle.at[i],
                r.two_send.at[i],
                r.two_recv.at[i],
                other_middle,
            )

        def hop_three(i):
            return remote(
                r.ends.at[i % held_ends], r.finals.at[i], r.three_send.at[i], r.three_recv.at[i], partner
            )

        def load_mine(i):
            return local(r.tiles.at[i], r.mine.at[i % 2], r.mine_sem.at[i % 2])

        def load_theirs(i):
            return local(r.from_end.at[i], r.theirs.at[i % 2], r.theirs_sem.at[i % 2])

        def load_crossed(i):
            return local(r.from_middle.at[i], r.crossed.at[i % 2], r.crossed_sem.at[i % 2])

        def keep_final(i):
            return local(r.ends.at[i % held_ends], r.finals.at[i], r.final_sem.at[i % held_ends])

        def keep_own(i):
            return local(r.finals.at[i, 0], r.owned.at[i, 0], r.deal_local.at[i])

        def deal_to(i, b, d):
            at = 2 * i + b
            return remote(
                r.finals.at[i, b],
                r.owned.at[i, b],
                r.deal_send.at[at],
                r.deal_recv.at[at],
                (here, chips[d]),
            )

        def to_sibling(i):
            return remote(r.owned.at[i], r.near.at[i], r.sib_send.at[i], r.sib_recv.at[i], other_core)

        def add(target, a, b):
            def some(s, _):
                at = (s // 4, span((s % 4) * (quarter // 4), quarter // 4))
                target[at] = a[at] + b[at]
                return 0

            lax.fori_loop(0, 8, some, 0)

        def when_in(i, *conditions):
            return pl.when(functools.reduce(jnp.logical_and, conditions, (i >= 0) & (i < units)))

        def step(i, _=0):
            @when_in(i + ahead, is_end, i >= 0)
            def _():
                hop_one(i + ahead).start()

            @when_in(i - 1, is_middle)
            def _():
                at = i - 1
                load_mine(at).wait()
                load_theirs(at).wait()

                @pl.when(at >= held_sums)
                def _():
                    hop_two(at - held_sums).wait_send()

                add(r.sums.at[at % held_sums], r.mine.at[at % 2], r.theirs.at[at % 2])
                hop_two(at).start()

            @when_in(i - 4, is_middle)
            def _():
                at = i - 4
                load_crossed(at).wait()

                @pl.when(at >= held_ends)
                def _():
                    hop_three(at - held_ends).wait_send()

                add(r.ends.at[at % held_ends], r.sums.at[at % held_sums], r.crossed.at[at % 2])
                hop_three(at).start()
                keep_final(at).start()

            @when_in(i, is_middle)
            def _():
                hop_one(i).wait_recv()
                load_mine(i).start()
                load_theirs(i).start()

            @when_in(i - 3, is_middle)
            def _():
                hop_two(i - 3).wait_recv()
                load_crossed(i - 3).start()

            @when_in(i - 6)
            def _():
                at = i - 6

                @pl.when(is_middle)
                def _():
                    keep_final(at).wait()

                @pl.when(is_end)
                def _():
                    hop_three(at).wait_recv()

                @pl.when(at % 2 == 0)
                def _():
                    keep_own(at).start()
                    deal_to(at, 1, 1).start()

                @pl.when(at % 2 == 1)
                def _():
                    deal_to(at, 0, 2).start()
                    deal_to(at, 1, 3).start()

            @when_in(i - 9)
            def _():
                at = i - 9

                @pl.when(at % 2 == 0)
                def _():
                    keep_own(at).wait()

                @pl.when(at % 2 == 1)
                def _():
                    deal_to(at, 0, 2).wait_recv()

                deal_to(at, 1, 3).wait_recv()
                to_sibling(at).start()

            return 0

        steps_done = [0]

        def advance(count):
            first = steps_done[0]
            steps_done[0] = first + count
            lax.fori_loop(first, first + count, step, 0)

        def finish():
            def one(i, _):
                @pl.when(is_end)
                def _():
                    hop_one(i).wait_send()

                @pl.when(is_middle & (i >= units - held_sums))
                def _():
                    hop_two(i).wait_send()

                @pl.when(is_middle & (i >= units - held_ends))
                def _():
                    hop_three(i).wait_send()

                @pl.when(i % 2 == 1)
                def _():
                    deal_to(i, 0, 2).wait_send()

                deal_to(i, 1, 3).wait_send()
                to_sibling(i).wait()
                return 0

            lax.fori_loop(0, units, one, 0)

        def stage_copy(t, h):
            return local(r.stage.at[t % 2, pl.ds(2 * h, 2)], r.tiles.at[2 * t + h], r.stage_sem.at[t % 2, h])

        def staged(t):
            for h in range(2):
                stage_copy(t, h).wait()

            @pl.when(is_end & (t == 0))
            def _():
                for i in range(ahead):
                    hop_one(i).start()

        def outer(t, left, right_rows):
            for j in range(n):
                stage[t % 2, j] = matmul(left, work[right_rows, blocks[j]]).astype(BF16)
            for h in range(2):
                stage_copy(t, h).start()

        def row_near(s, base, d):
            at = s * n + d
            return remote(
                work.at[pl.ds(base + (2 * d + 1) * rows, rows)],
                r.row_near.at[s, d],
                r.row_near_send.at[at],
                r.row_near_recv.at[at],
                other_core,
            )

        def row_far(s, base, d):
            at = s * n + d
            return remote(
                work.at[pl.ds(base + 2 * d * rows, rows)],
                r.row_far.at[s, d],
                r.row_far_send.at[at],
                r.row_far_recv.at[at],
                (here, chips[d]),
            )

        def near_load(s, d):
            return local(r.row_near.at[s, d], r.some_rows.at[d], r.row_sem.at[d])

        def far_load(s, d):
            return local(r.row_far.at[s, d], r.some_rows.at[d], r.row_sem.at[d])

        few = 16

        def row_send(s, base, d):
            row_near(s, base, d).wait_recv()
            near_load(s, d).start()
            near_load(s, d).wait()

            def some(c, _):
                at = span(c * few, few)
                own = pl.ds(pl.multiple_of(base + 2 * d * rows + c * few, few), few)
                work[own, :] = work[own, :] + r.some_rows[d, at, :]
                return 0

            lax.fori_loop(0, rows // few, some, 0)
            row_far(s, base, d).start()

        far_first = (1, 2, 3, 0)

        def rows_reduced(s, base, compute, send=True, ticks=0):
            def one(i, _):
                d = (i + 1) % n
                compute(d)
                for at in range(n):

                    @pl.when(i == at)
                    def _():
                        row_near(s, base, far_first[at]).start()
                        if send and at > 0:
                            row_send(s, base, far_first[at - 1])

                if ticks:

                    @pl.when(i >= n - ticks)
                    def _():
                        step(first + i - (n - ticks))

                return 0

            first = steps_done[0]
            steps_done[0] = first + ticks
            lax.fori_loop(0, n, one, 0)

        def rows_arrive(s, base):
            row_near(s, base, 0).wait_recv()
            near_load(s, 0).start()
            for d in range(1, n):
                row_far(s, base, d).wait_recv()
                far_load(s, d).start()
            near_load(s, 0).wait()
            for d in range(1, n):
                far_load(s, d).wait()

        def rows_sent(s, base):
            for d in range(n):
                row_near(s, base, d).wait_send()
            for d in range(1, n):
                row_far(s, base, d).wait_send()

        def norm_rows_back(base, value_ref, gain_row, use):
            r.flat[...] = jnp.zeros_like(r.flat)

            def some(c, _):
                at = span(c * few, few)
                grad = work[pl.ds(pl.multiple_of(base + c * few, few), few), :].astype(F32)
                for d in range(n):
                    grad += r.some_rows[d, at, :].astype(F32)
                values = value_ref[at, :].astype(F32)
                inverse = lax.rsqrt(jnp.mean(values * values, axis=-1, keepdims=True) + epsilon)
                unit_rows = values * inverse
                scaled = grad * gain_row
                back = inverse * (
                    scaled - unit_rows * jnp.mean(scaled * unit_rows, axis=-1, keepdims=True)
                )
                use(at, back)
                terms = grad * unit_rows
                r.flat[...] += terms[:8] + terms[8:]
                return 0

            lax.fori_loop(0, rows // few, some, 0)

        def gain_terms(at):
            total = jnp.sum(r.flat[...], axis=0, keepdims=True)
            r.flat[0:1, :] = total
            for j in range(n):
                r.gain_mine[j, at : at + 1, :] = r.flat[0:1, blocks[j]]

        r.gain_mine[...] = jnp.zeros_like(r.gain_mine)
        loads = []

        def load(source, target):
            copy = local(source, target, r.load_sem.at[len(loads)])
            copy.start()
            loads.append(copy)

        def loaded():
            while loads:
                loads.pop().wait()

        def out_far(d):
            return remote(
                r.output_weight.at[head_of(d)],
                r.theirs.at[d // 2, d % 2],
                r.out_send.at[d],
                r.out_recv.at[d],
                (here, chips[d]),
            )

        def cot_far(d):
            return remote(
                r.cotangent, r.cot_all.at[0, d], r.cot_send.at[d], r.cot_recv.at[d], (here, chips[d])
            )

        def cot_near(d):
            source = r.cotangent if d == 0 else r.cot_all.at[0, d]
            return remote(
                source, r.cot_all.at[1, d], r.cot_near_send.at[d], r.cot_near_recv.at[d], other_core
            )

        def query_far(d):
            return remote(
                r.query_weight.at[:, head_of(d)],
                r.query_in.at[d],
                r.query_send.at[d],
                r.query_recv.at[d],
                (here, chips[d]),
            )

        def kv_piece(j):
            return r.kv_some.at[j // 3, pl.ds(j % 3 * wide, wide)]

        def query_piece(j):
            return heads.at[query_grad_slot + j // 3, pl.ds(j % 3 * wide, wide)]

        half_rows = rows // 2

        def cot_half(d):
            some = pl.ds((d - 1) * half_rows, half_rows)
            return remote(
                r.cot_all.at[0, d, some],
                r.cot_all.at[0, 3, some],
                r.cot_half_send.at[d],
                r.cot_half_recv.at[d],
                (here, chips[3 - d]),
            )

        parity = z % 2

        def feed_half(d):
            return feed_far(0, d, pl.multiple_of(parity * (wide // 2), wide // 2), wide // 2)

        def feed_share(d):
            copies = []
            for part, (first, count) in enumerate(((0, wide // 2), (wide, quarter // 2))):
                some = feed.at[0, d, span(first + parity * count, count)]
                at = 2 * d + part
                copies.append(remote(some, some, r.share_send.at[at], r.share_recv.at[at], partner))
            return copies

        def token_near(d):
            source = work.at[pl.ds(plane_rows + 2 * d * rows, rows)] if d == 3 else r.near_tokens[d]
            return remote(
                source,
                work.at[pl.ds(plane_rows + (2 * d + 1) * rows, rows)],
                r.token_send.at[d],
                r.token_recv.at[d],
                other_core,
            )

        def token_half(d):
            return remote(
                r.near_tokens[d].at[pl.ds((d - 1) * half_rows, half_rows)],
                work.at[pl.ds(plane_rows + 6 * rows + (d - 1) * half_rows, half_rows)],
                r.token_half_send.at[d],
                r.token_half_recv.at[d],
                (here, chips[3 - d]),
            )

        for d in (1, 2):
            token_half(d).start()
        for d in range(1, n):
            query_far(d).start()
        for d in range(1, n):
            out_far(d).start()
        cot_near(0).start()
        for d in range(n - 1):
            token_near(d).start()
            load(r.near_tokens[d], work.at[pl.ds(plane_rows + 2 * d * rows, rows)])
        for j in range(n):
            load(r.in_weight[j].at[pl.ds(0, wide)], kv_piece(j))
            load(r.in_weight[j].at[pl.ds(wide, 32)], r.gain_rows.at[j])
        loaded()
        load(r.output_weight.at[head_of(0)], r.theirs.at[0, 0])
        load(r.query_weight.at[:, head_of(0)], query_piece(0))
        for q in range(QUARTERS):
            every(feed_own(q), starts)
        for j in range(n):
            both = r.gain_rows[j].astype(F32)
            for g in range(2):
                for h in range(2):
                    here_half = pl.ds(pl.multiple_of(chips[j] * wide + h * HD, HD), HD)
                    r.gains[g : g + 1, here_half] = both[16 * g + 8 * h : 16 * g + 8 * h + 1]

        def project(d):
            for c in range(2):
                first = (2 * d + (side + c) % 2) * rows

                def some(s, _, c=c, first=first):
                    now = pl.ds(pl.multiple_of(plane_rows + first + s * few, few), few)
                    then = pl.ds(pl.multiple_of((2 * d + c) * rows + s * few, few), few)
                    values = work[now, :].astype(F32)
                    inverse = lax.rsqrt(jnp.mean(values * values, axis=-1, keepdims=True) + epsilon)
                    work[then, :] = (values * inverse * r.gains[0:1, :]).astype(BF16)
                    return 0

                lax.fori_loop(0, rows // few, some, 0)
            now = span(d * pair, pair)
            kv = jnp.zeros((pair, HD), F32)
            for j in range(n):
                kv += matmul(work[now, blocks[j]], kv_piece(j)[...])
            kv = kv * r.tables[2] + turn(kv) * r.tables[3]
            heads[0, now, :] = kv.astype(BF16)

        def block_of(k, d):
            return heads.at[k, span(d * pair, pair)]

        def climb(s, d):
            at = s * n + d
            return remote(
                block_of(s - 1, d), block_of(s, d), r.climb_send.at[at], r.climb_recv.at[at], above
            )

        def fall(s, d):
            at = s * n + d
            return remote(
                block_of((planes - s + 1) % planes, d),
                block_of(planes - s, d),
                r.fall_send.at[at],
                r.fall_recv.at[at],
                below,
            )

        def pass_on(k, d):
            at = k * n + d
            return remote(
                block_of(k, d),
                block_of(planes + k, d),
                r.pass_send.at[at],
                r.pass_recv.at[at],
                other_core,
            )

        def kv_leave(s, d):
            @pl.when((z - s + 1 >= 0) & (z + 1 < planes))
            def _():
                climb(s, d).start()

            @pl.when((z + s - 1 < planes) & (z >= 1))
            def _():
                fall(s, d).start()

        def kv_come(s, d):
            @pl.when(z - s >= 0)
            def _():
                climb(s, d).wait_recv()

            @pl.when(z + s < planes)
            def _():
                fall(s, d).wait_recv()

        def passing(condition, k, d):
            @pl.when(condition)
            def _():
                pass_on(k, d).start()

        def passed(condition, k, d):
            @pl.when(condition)
            def _():
                pass_on(k, d).wait_recv()

        def by_chip(use):
            def one(i, _):
                use((i + 1) % n)
                return 0

            lax.fori_loop(0, n, one, 0)

        def start_kv(d):
            for at in range(n):

                @pl.when(d == at)
                def _():
                    if at == 3:
                        for far in (1, 2):
                            token_half(far).wait_recv()
                        token_near(3).start()
                    token_near(at).wait_recv()

            project(d)
            kv_leave(1, d)
            pass_on(0, d).start()

        by_chip(start_kv)
        token_near(3).wait_send()
        keep_normed = local(work.at[pl.ds(0, plane_rows)], r.normed, r.keep_sem.at[0])
        keep_normed.start()
        for d in range(1, n):
            query_far(d).wait_recv()
            load(r.query_in.at[d], query_piece(d))
        for d in (1, 2):
            cot_far(d).start()
        loaded()

        def project_query(d, _):
            now = span(d * pair, pair)
            query = jnp.zeros((pair, HD), F32)
            for j in range(n):
                query += matmul(work[now, blocks[j]], query_piece(j)[...])
            query = query * r.tables[0] + turn(query) * r.tables[1]
            heads[query_slot, now, :] = query.astype(BF16)
            return 0

        lax.fori_loop(0, n, project_query, 0)
        for d in range(1, n):
            out_far(d).wait_recv()
        keep_out = local(r.theirs, r.out_weight, r.keep_sem.at[1])
        keep_out.start()

        def put_rows(base, d, now_values, block_at):
            first = pl.ds(pl.multiple_of(base + (2 * d + side) * rows, rows), rows)
            second = pl.ds(pl.multiple_of(base + (2 * d + 1 - side) * rows, rows), rows)
            work[first, block_at] = now_values[:rows]
            work[second, block_at] = now_values[rows:]

        def totals(d):
            return [r.wide_rows.at[:, span((2 * d + c) * HD, HD)] for c in range(2)]

        def attend_block(k, d, first, last):
            now = span(d * pair, pair)
            a, b = heads[k, now, :], heads[planes + k, now, :]
            keys, values = jnp.where(side == 0, a, b), jnp.where(side == 0, b, a)
            score = matmul_nt(heads[query_slot, now, :], keys) * scale
            score = jnp.where(r.key_ids[d, k] <= r.query_ids[d], score, masked_score)
            top = jnp.max(score, axis=-1, keepdims=True)
            if not first:
                before = r.soft[d]
                top = jnp.maximum(top, before)
                factor = jnp.exp(before - top)
            raised = jnp.exp(score - top)
            weight = jnp.sum(raised, axis=-1, keepdims=True)
            total = matmul(raised.astype(BF16), values)
            if not first:
                weight += r.soft[n + d] * factor
                total += jnp.concatenate([t[...] for t in totals(d)], axis=0) * factor
            if last:
                return total, weight
            r.soft[d] = top
            r.soft[n + d] = weight
            for c, target in enumerate(totals(d)):
                target[...] = total[c * rows : (c + 1) * rows]
            return None

        def attend_to(k, first=False):
            by_chip(lambda d: attend_block(k, d, first, False) and None)

        def when_middle(there, otherwise):
            return jnp.where(is_middle, there, otherwise)

        by_chip(lambda d: pass_on(0, d).wait_recv())
        attend_to(0, first=True)

        def first_come(d):
            kv_come(1, d)
            kv_leave(2, d)
            passing(z >= 1, 1, d)
            passing(z + 1 < planes, 3, d)

        def first_passed(d):
            passed(z >= 1, 1, d)
            passed(z + 1 < planes, 3, d)

        by_chip(first_come)
        by_chip(first_passed)
        attend_to(jnp.where(z >= 1, 1, 3))
        for d in (1, 2):
            cot_far(d).wait_recv()
            cot_half(d).start()
            cot_near(d).start()
        for d in range(1, n):
            every(feed_half(d), starts)

        def second_come(d):
            kv_come(2, d)
            kv_leave(3, d)
            pass_on(2, d).start()

        by_chip(second_come)
        by_chip(lambda d: pass_on(2, d).wait_recv())
        attend_to(when_middle(3, 2))
        keep_normed.wait()

        def attend(d):
            kv_come(3, d)
            passing(z == 0, 1, d)
            passing(z == planes - 1, 3, d)
            passed(z == 0, 1, d)
            passed(z == planes - 1, 3, d)
            now = span(d * pair, pair)
            last_block = jnp.where(z == 0, 1, when_middle(2, 3))
            total, weight = attend_block(last_block, d, False, True)
            low_total = (total * (1.0 / weight)).astype(BF16)
            heads[attended_slot, now, :] = low_total
            for j in range(n):
                put_rows(
                    plane_rows,
                    d,
                    matmul(low_total, r.theirs[j // 2, j % 2]).astype(BF16),
                    blocks[j],
                )

        rows_reduced(MID, plane_rows, attend)
        keep_heads = local(heads.at[pl.ds(0, kept_slots)], r.kept, r.keep_sem.at[2])
        keep_heads.start()
        load(r.tokens, r.own_rows)
        loaded()
        keep_out.wait()
        for d in (1, 2):
            cot_half(d).wait_recv()
        cot_near(3).start()
        for d in range(1, n):
            every(feed_half(d), arrives)
            every(feed_share(d), starts)

        def kv_left(d):
            for s in range(1, planes):

                @pl.when((z - s + 1 >= 0) & (z + 1 < planes))
                def _():
                    climb(s, d).wait_send()

                @pl.when((z + s - 1 < planes) & (z >= 1))
                def _():
                    fall(s, d).wait_send()

            for k in range(planes):
                pass_on(k, d).wait_send()

        by_chip(kv_left)

        rows_arrive(MID, plane_rows)

        def second_norm(c, _):
            at = span(c * few, few)
            total = r.own_rows[at, :].astype(F32)
            total += work[pl.ds(pl.multiple_of(plane_rows + c * few, few), few), :].astype(F32)
            for d in range(n):
                total += r.some_rows[d, at, :].astype(F32)
            inverse = lax.rsqrt(jnp.mean(total * total, axis=-1, keepdims=True) + epsilon)
            r.wide_rows[at, :] = total
            r.own_rows[at, :] = (total * inverse * r.gains[1:2, :]).astype(BF16)
            return 0

        lax.fori_loop(0, rows // few, second_norm, 0)

        def two_far(d):
            return remote(
                r.own_rows,
                work.at[pl.ds(2 * d * rows, rows)],
                r.two_far_send.at[d],
                r.two_far_recv.at[d],
                (here, chips[d]),
            )

        def two_near(d):
            source = r.own_rows if d == 0 else work.at[pl.ds(2 * d * rows, rows)]
            return remote(
                source,
                work.at[pl.ds((2 * d + 1) * rows, rows)],
                r.two_near_send.at[d],
                r.two_near_recv.at[d],
                other_core,
            )

        def two_half(d):
            return remote(
                work.at[pl.ds(2 * d * rows + (d - 1) * half_rows, half_rows)],
                work.at[pl.ds(2 * 3 * rows + (d - 1) * half_rows, half_rows)],
                r.two_half_send.at[d],
                r.two_half_recv.at[d],
                (here, chips[3 - d]),
            )

        for d in (1, 2):
            two_far(d).start()
        two_near(0).start()
        two_own = local(r.own_rows, work.at[pl.ds(0, rows)], r.two_local.at[0])
        two_own.start()
        load(r.wide_rows, r.middle)
        rows_sent(MID, plane_rows)
        for d in range(n):
            cot_near(d).wait_recv()
            source = r.cotangent if d == 0 else r.cot_all.at[0, d]
            load(source, work.at[pl.ds(plane_rows + 2 * d * rows, rows)])
            load(r.cot_all.at[1, d], work.at[pl.ds(plane_rows + (2 * d + 1) * rows, rows)])
        keep_heads.wait()
        for d in range(1, n):
            every(feed_share(d), arrives)
        loaded()

        def rows_of_chip(t, arrive, half_way, pass_along):
            for at in range(n):

                @pl.when(t == at)
                def _():
                    for d in ((), (1, 2), (), ())[at]:
                        arrive(d).wait_recv()
                        half_way(d).start()
                        pass_along(d).start()
                    if at == 2:
                        half_way(1).wait_recv()
                        half_way(2).wait_recv()
                        pass_along(3).start()
                    pass_along(at).wait_recv()

        two_own.wait()

        def quarter_step(q, _):
            step(3 * q - 3)
            every(feed_own(q), waits)

            @pl.when(q > 0)
            def _():
                for d in range(1, n):
                    every(feed_far(q, d), arrives)

            @pl.when((q > 0) & (q < QUARTERS - 1))
            def _():
                for d in range(1, n):
                    every(feed_far(q + 1, d), starts)

            def forward(t, _):
                @pl.when(q == 0)
                def _():
                    rows_of_chip(t, two_far, two_half, two_near)

                    @pl.when(t == 2)
                    def _():
                        for d in range(1, n):
                            every(feed_far(1, d), starts)


                now = span(t * pair, pair)
                cot_now = pl.ds(pl.multiple_of(plane_rows + t * pair, pair), pair)
                both = jnp.zeros((pair, 2 * quarter), F32)
                hidden_grad = jnp.zeros((pair, quarter), F32)
                for j in range(n):
                    both += matmul(work[now, blocks[j]], feed[q, j, :wide, :])
                    hidden_grad += matmul_nt(work[cot_now, blocks[j]], feed[q, j, wide:, :])
                gate, up = both[:, :quarter], both[:, quarter:]
                share = 1.0 / (1.0 + jnp.exp(-gate))
                activated = gate * share
                results = (
                    activated * up,
                    hidden_grad * up * share * (1.0 + gate * (1.0 - share)),
                    hidden_grad * activated,
                )
                for w, result in enumerate(results):
                    heads[q * 3 + w, now, :] = result.astype(BF16)
                    turned[w, :, now] = result.T.astype(BF16)
                return 0

            lax.fori_loop(0, n, forward, 0)

            step(3 * q - 2)

            def one(w, _):
                t = 3 * q + w

                outer(t, turned[w], span(jnp.where(w == 0, plane_rows, 0), plane_rows))

                @pl.when(w > 0)
                def _():
                    staged(t - 1)

                return 0

            lax.fori_loop(0, 3, one, 0)
            step(3 * q - 1)
            staged(3 * q + 2)
            return 0

        lax.fori_loop(0, QUARTERS, quarter_step, 0)
        steps_done[0] = 3 * QUARTERS - 3
        for d in range(1, n):
            two_near(d).wait_send()
        for d in (1, 2):
            two_half(d).wait_send()

        def back_step(d):
            now = span(d * pair, pair)
            lefts = [
                jnp.concatenate([heads[q * 3 + 1, now, :], heads[q * 3 + 2, now, :]], axis=1)
                for q in range(QUARTERS)
            ]
            for j in range(n):
                total = jnp.zeros((pair, wide), F32)
                for q in range(QUARTERS):
                    total += matmul_nt(lefts[q], feed[q, j, :wide, :])
                work[now, blocks[j]] = total.astype(BF16)

        half = n // 2
        rows_reduced(BACK, 0, back_step, ticks=TICKS[0] + TICKS[1])

        def out_step(d):
            now = span(d * pair, pair)
            then = pl.ds(pl.multiple_of(plane_rows + d * pair, pair), pair)
            for j in range(n):
                total = jnp.zeros((pair, wide), F32)
                for q in range(QUARTERS):
                    total += matmul(heads[q * 3, now, :], feed[q, j, wide:, :])
                work[then, blocks[j]] = total.astype(BF16)

        rows_reduced(OUT, plane_rows, out_step, send=False, ticks=TICKS[2] + TICKS[3])

        for d in range(1, n):
            every(feed_share(d), leaves)
        load(r.kept, heads.at[pl.ds(0, kept_slots)])
        for j in range(n):
            query_source = r.query_weight.at[:, head_of(0)] if j == 0 else r.query_in.at[j]
            load(query_source, feed.at[0, j, pl.ds(0, wide), pl.ds(0, HD)])
            load(r.in_weight[j].at[pl.ds(0, wide)], feed.at[0, j, pl.ds(0, wide), pl.ds(HD, HD)])
            load(r.out_weight.at[j // 2, j % 2], feed.at[0, j, pl.ds(wide, HD)])

        rows_arrive(BACK, 0)
        loaded()
        for d in (1, 2):
            two_far(d).wait_send()
        two_near(0).wait_send()
        load(r.cotangent, r.own_rows)
        loaded()

        def second_use(at, back):
            grad = r.own_rows[at, :].astype(F32) + back
            r.wide_rows[at, :] = grad
            r.own_rows[at, :] = grad.astype(BF16)

        norm_rows_back(0, r.wide_rows, r.gains[1:2, :], second_use)

        def branch_far(d):
            return remote(
                r.own_rows,
                r.branch_all.at[d, side],
                r.branch_send.at[d],
                r.branch_recv.at[d],
                (here, chips[d]),
            )

        def branch_near(d):
            source = r.own_rows if d == 0 else r.branch_all.at[d, side]
            return remote(
                source,
                r.branch_all.at[d, side],
                r.branch_near_send.at[d],
                r.branch_near_recv.at[d],
                other_core,
            )

        def branch_half(d):
            some = pl.ds((d - 1) * half_rows, half_rows)
            return remote(
                r.branch_all.at[d, side, some],
                r.branch_all.at[3, side, some],
                r.branch_half_send.at[d],
                r.branch_half_recv.at[d],
                (here, chips[3 - d]),
            )

        for d in (1, 2):
            branch_far(d).start()
        branch_near(0).start()
        branch_own = local(r.own_rows, r.branch_all.at[0, side], r.branch_local.at[0])
        branch_own.start()
        gain_terms(1)
        advance(TICKS[4])
        rows_sent(BACK, 0)
        branch_own.wait()
        loaded()

        def scored(d, now):
            keys, values, scores = [], [], []
            for k in range(planes):
                a, b = heads[k, now, :], heads[planes + k, now, :]
                keys.append(jnp.where(side == 0, a, b))
                values.append(jnp.where(side == 0, b, a))
                score = matmul_nt(heads[query_slot, now, :], keys[k]) * scale
                scores.append(jnp.where(r.key_ids[d, k] <= r.query_ids[d], score, masked_score))
            top = functools.reduce(jnp.maximum, [jnp.max(s, axis=-1, keepdims=True) for s in scores])
            raised = [jnp.exp(s - top) for s in scores]
            inverse = 1.0 / sum(jnp.sum(e, axis=-1, keepdims=True) for e in raised)
            return keys, values, [e * inverse for e in raised]

        def attend_back(d, _):
            rows_of_chip(d, branch_far, branch_half, branch_near)

            @pl.when(d == half)
            def _():
                for at in (3, 1, 2):
                    row_send(OUT, plane_rows, at)

            now = span(d * pair, pair)
            for c in range(2):
                load(r.branch_all.at[d, c], work.at[pl.ds(pl.multiple_of((2 * d + c) * rows, rows), rows)])
            loaded()
            query = heads[query_slot, now, :]
            attended_grad = jnp.zeros((pair, HD), F32)
            for j in range(n):
                attended_grad += matmul_nt(work[now, blocks[j]], feed[0, j, wide:, :])
            attended_grad = attended_grad.astype(BF16)
            keys, values, probs = scored(d, now)
            low = [p.astype(BF16) for p in probs]
            shares = [matmul_nt(attended_grad, values[k]) for k in range(planes)]
            delta = sum(
                jnp.sum(low[k].astype(F32) * shares[k], axis=-1, keepdims=True) for k in range(planes)
            )
            query_grad = jnp.zeros((pair, HD), F32)
            for k in range(planes):
                score_grad = (probs[k] * (shares[k] - delta)).astype(BF16)
                query_grad += matmul(score_grad, keys[k])
                key_grad = matmul_tn(score_grad, query) * scale
                value_grad = matmul_tn(low[k], attended_grad)
                heads[k, now, :] = jnp.where(side == 0, key_grad, value_grad).astype(BF16)
                heads[planes + k, now, :] = jnp.where(side == 0, value_grad, key_grad).astype(BF16)
            query_grad = query_grad * scale
            query_grad = query_grad * r.tables[0] + turn_back(query_grad * r.tables[1])
            heads[query_grad_slot, now, :] = query_grad.astype(BF16)
            return 0

        lax.fori_loop(0, half, attend_back, 0)
        advance(TICKS[5])
        lax.fori_loop(half, n, attend_back, 0)

        def kv_hand_over(k):
            return remote(
                heads.at[planes + k], r.kv_other.at[k], r.kv_send.at[k], r.kv_recv.at[k], other_core
            )

        def kv_load(source, slot):
            return local(source, r.kv_some.at[slot], r.kv_sem.at[slot])

        def kv_add(k, slot):
            def some(c, _):
                at = span(c * 64, 64)
                heads[k, at, :] = heads[k, at, :] + r.kv_some[slot, at, :]
                return 0

            lax.fori_loop(0, plane_rows // 64, some, 0)

        def kv_down(k):
            return remote(heads.at[k], r.kv_down.at[k], r.down_send.at[k], r.down_recv.at[k], below)

        def kv_up(k):
            return remote(
                heads.at[planes - k], r.kv_up.at[k], r.up_send.at[k], r.up_recv.at[k], above
            )

        order = list(range(planes - 1, -1, -1))
        for k in order:
            kv_hand_over(k).start()
        for at, k in enumerate(order):
            kv_hand_over(k).wait_recv()
            kv_load(r.kv_other.at[k], at % 2).start()
            kv_load(r.kv_other.at[k], at % 2).wait()
            kv_add(k, at % 2)

        def kv_send(k):
            @pl.when(z >= k)
            def _():
                kv_down(k).start()

            @pl.when(z + k < planes)
            def _():
                kv_up(k).start()

        def kv_receive(k, down_to, up_to):
            @pl.when((z + 1 >= k) & (z + 1 < planes))
            def _():
                kv_down(k).wait_recv()
                if down_to is not None:
                    copy = kv_load(r.kv_down.at[k], 0)
                    copy.start()
                    copy.wait()
                    kv_add(down_to, 0)

            @pl.when((z >= 1) & (z - 1 + k < planes))
            def _():
                kv_up(k).wait_recv()
                if up_to is not None:
                    copy = kv_load(r.kv_up.at[k], 1)
                    copy.start()
                    copy.wait()
                    kv_add(up_to, 1)

        kv_send(3)
        rows_sent(OUT, plane_rows)
        load(work.at[pl.ds(plane_rows, rows)], r.out_own)
        loaded()
        load(r.normed, work.at[pl.ds(plane_rows, plane_rows)])
        low_half, high_half = pl.ds(0, plane_rows), pl.ds(plane_rows, plane_rows)
        advance(TICKS[6])
        turned[0] = heads[attended_slot].astype(F32).T.astype(BF16)
        turned[1] = heads[query_grad_slot].astype(F32).T.astype(BF16)
        loaded()
        outer(query_at, turned[1], high_half)
        outer(output_at, turned[0], low_half)
        staged(query_at)
        staged(output_at)
        advance(TICKS[7])
        kv_receive(3, 2, 2)
        kv_send(2)
        advance(TICKS[8])
        kv_receive(2, 1, 3)
        kv_send(1)
        advance(TICKS[9])
        kv_receive(1, 0, 0)

        def kv_back(d, _):
            now = span(d * pair, pair)
            grad = heads[0, now, :].astype(F32)
            grad = grad * r.tables[2] + turn_back(grad * r.tables[3])
            heads[kv_grad_slot, now, :] = grad.astype(BF16)
            turned[2, :, now] = grad.T.astype(BF16)
            return 0

        lax.fori_loop(0, n, kv_back, 0)
        outer(kv_at, turned[2], high_half)

        def project_back(d):
            now = span(d * pair, pair)
            left = jnp.concatenate([heads[query_grad_slot, now, :], heads[kv_grad_slot, now, :]], axis=1)
            for j in range(n):
                put_rows(0, d, matmul_nt(left, feed[0, j, :wide, :]).astype(BF16), blocks[j])

        staged(kv_at)
        rows_reduced(ONE, 0, project_back)
        advance(TICKS[10])

        for d in (1, 2):
            branch_far(d).wait_send()
            branch_half(d).wait_send()
        for d in range(n):
            branch_near(d).wait_send()
        load(r.tokens, r.own_rows)
        rows_arrive(ONE, 0)
        loaded()

        def first_use(at, back):
            r.wide_rows[at, :] = r.wide_rows[at, :] + back

        norm_rows_back(0, r.own_rows, r.gains[0:1, :], first_use)
        load(r.wide_rows, r.tokens_grad)
        gain_terms(0)

        def gain_copy(at, source, target, peer):
            return remote(source, target, r.gain_send.at[at], r.gain_recv.at[at], peer)

        def gain_far(d):
            return gain_copy(d, r.gain_mine.at[d], r.gain_far.at[d], (here, chips[d]))

        def gain_hop(s, peer):
            return gain_copy(n + s, r.gain_sum.at[s], r.gain_in.at[s], peer)

        for d in range(1, n):
            gain_far(d).start()
        advance(TICKS[11])
        for d in range(1, n):
            gain_far(d).wait()
        r.gain_sum[0] = r.gain_mine[0] + r.gain_far[1] + r.gain_far[2] + r.gain_far[3]
        gain_hop(0, other_core).start()
        gain_hop(0, other_core).wait()
        r.gain_sum[1] = r.gain_sum[0] + r.gain_in[0]

        @pl.when(is_end)
        def _():
            gain_hop(1, partner).start()
            gain_hop(1, partner).wait_send()

        advance(TICKS[12])

        @pl.when(is_middle)
        def _():
            gain_hop(1, partner).wait_recv()
            r.gain_sum[2] = r.gain_sum[1] + r.gain_in[1]
            gain_hop(2, other_middle).start()
            gain_hop(2, other_middle).wait()
            r.gain_sum[3] = r.gain_sum[2] + r.gain_in[2]
            gain_hop(3, partner).start()
            gain_hop(3, partner).wait_send()

        @pl.when(is_end)
        def _():
            gain_hop(3, partner).wait_recv()
            r.gain_sum[3] = r.gain_in[3]

        load(r.gain_sum.at[3], r.gain_out)

        loaded()
        load(r.middle, r.wide_rows)
        load(r.out_own, r.own_rows)
        rows_arrive(OUT, plane_rows)
        loaded()

        def last_rows(c, _):
            at = span(c * few, few)
            total = r.wide_rows[at, :] + r.own_rows[at, :].astype(F32)
            for d in range(n):
                total += r.some_rows[d, at, :].astype(F32)
            r.own_rows[at, :] = total.astype(BF16)
            return 0

        lax.fori_loop(0, rows // few, last_rows, 0)
        load(r.own_rows, r.output)
        advance(units + 9 - steps_done[0])

        loaded()
        rows_sent(ONE, 0)
        for q in range(1, QUARTERS):
            for d in range(1, n):
                every(feed_far(q, d), leaves)
        for d in range(1, n):
            every(feed_half(d), leaves)
        for d in (1, 2):
            token_half(d).wait_send()
            cot_far(d).wait_send()
            cot_half(d).wait_send()
        for d in range(1, n):
            query_far(d).wait_send()
            out_far(d).wait_send()
        for d in range(n - 1):
            token_near(d).wait_send()
        for d in range(n):
            cot_near(d).wait_send()
        for k in range(planes):
            kv_hand_over(k).wait_send()
        for k in range(1, planes):

            @pl.when(z >= k)
            def _():
                kv_down(k).wait_send()

            @pl.when(z + k < planes)
            def _():
                kv_up(k).wait_send()

        finish()

    arrays = jax.tree.leaves((in_hbm, in_vmem))
    results = pl.pallas_call(
        backward,
        out_shape=jax.tree.leaves(out_hbm),
        in_specs=[pl.BlockSpec(memory_space=pl.ANY)] * len(jax.tree.leaves(in_hbm))
        + [pl.BlockSpec(memory_space=pltpu.VMEM)] * len(in_vmem),
        out_specs=[pl.BlockSpec(memory_space=pl.ANY)] * len(out_hbm),
        scratch_shapes=list(scratch.values()),
        cost_estimate=cost(30 * plane_rows * width * part, arrays, [unit_array] * 6),
        compiler_params=pltpu.CompilerParams(
            collective_id=0, has_side_effects=True, vmem_limit_bytes=63 * 1024 * 1024
        ),
        name="backward",
    )(*arrays)
    results = types.SimpleNamespace(**jax.tree.unflatten(jax.tree.structure(out_hbm), results))
    owned_tiles, near_tiles = (
        a.reshape(tiles_count, n, quarter, wide) for a in (results.owned, results.near)
    )

    def place(
        me_ref, own_ref, near_ref, gate, up, down, query, out, key, value, taken, turned, straight, in_sem, out_sem
    ):
        chip, side = me_ref[0], me_ref[1]
        steps = 2 * n

        def take(s, t, source):
            return pltpu.make_async_copy(source.at[t, s // 2], taken.at[t], in_sem.at[t])

        def start_taking(s, t):
            for source, e in ((own_ref, 0), (near_ref, 1)):

                @pl.when(s % 2 == e)
                def _():
                    take(s, t, source).start()

        def is_straight(t):
            return t == output_at or (t < query_at and t % 3 == 0)

        def goal(s, t):
            owner = 2 * (chip ^ (s // 2)) + (side ^ (s % 2))
            if t == query_at:
                return query.at[:, column(owner, HD)]
            if t == output_at:
                return out.at[column(owner, HD)]
            here = column(owner * QUARTERS + t // 3, quarter)
            return (down.at[here], gate.at[:, here], up.at[:, here])[t % 3]

        def put(s, t, use):
            source = straight.at[t // 3] if is_straight(t) else turned.at[t]
            if t != kv_at:
                use(pltpu.make_async_copy(source, goal(s, t), out_sem.at[t]))
                return
            for target, e in ((key, 0), (value, 1)):

                @pl.when((side + s) % 2 == e)
                def _():
                    there = target.at[:, column(chip ^ (s // 2), HD)]
                    use(pltpu.make_async_copy(source, there, out_sem.at[t]))

        for t in range(tiles_count):
            start_taking(0, t)

        def one(s, _):
            for t in range(tiles_count):
                take(s, t, own_ref).wait()

                @pl.when(s > 0)
                def _():
                    put(s - 1, t, lambda copy: copy.wait())

                if is_straight(t):
                    straight[t // 3] = taken[t].astype(F32)
                else:
                    turned[t] = taken[t].T.astype(F32)
                put(s, t, lambda copy: copy.start())

                @pl.when(s + 1 < steps)
                def _():
                    start_taking(s + 1, t)

            return 0

        lax.fori_loop(0, steps, one, 0)
        for t in range(tiles_count):
            put(steps - 1, t, lambda copy: copy.wait())

    in_place = pl.BlockSpec(memory_space=pl.ANY)
    placed = pl.pallas_call(
        place,
        out_shape=[
            shape(a.shape, F32)
            for a in (
                gate_weight,
                up_weight,
                down_weight,
                query_weight,
                output_weight,
                key_weight,
                value_weight,
            )
        ],
        in_specs=[pl.BlockSpec(memory_space=pltpu.SMEM), in_place, in_place],
        out_specs=[in_place] * 7,
        scratch_shapes=[
            pltpu.VMEM((tiles_count, quarter, wide), BF16),
            pltpu.VMEM((tiles_count, wide, quarter), F32),
            pltpu.VMEM((QUARTERS + 1, quarter, wide), F32),
            dma((tiles_count,)),
            dma((tiles_count,)),
        ],
        compiler_params=pltpu.CompilerParams(vmem_limit_bytes=VMEM_BYTES),
        name="place",
    )(me, owned_tiles, near_tiles)
    gate_grad, up_grad, down_grad, query_grad, output_grad, key_grad, value_grad = placed

    return (
        results.output[None],
        results.tokens_grad[None],
        query_grad,
        key_grad,
        value_grad,
        output_grad,
        results.gain_out[0],
        gate_grad,
        up_grad,
        down_grad,
        results.gain_out[1],
    )


def solution(mesh):
    chips, pieces = mesh.shape["fsdp"], mesh.shape["ctx"]
    one_head_each = 2 * chips == H and chips == KVH and pieces == 8
    return jax.shard_map(
        plane_layer if one_head_each else ring_layer,
        mesh=mesh,
        in_specs=(
            P("fsdp", "ctx", None),
            P("fsdp", None),
            P("fsdp", None),
            P("fsdp", None),
            P(None, "fsdp"),
            P("fsdp"),
            P("fsdp", None),
            P("fsdp", None),
            P(None, "fsdp"),
            P("fsdp"),
            P("fsdp", "ctx", None),
            P(),
            P(),
        ),
        out_specs=(
            P("fsdp", "ctx", None),
            P("fsdp", "ctx", None),
            P("fsdp", None),
            P("fsdp", None),
            P("fsdp", None),
            P(None, "fsdp"),
            P("fsdp"),
            P("fsdp", None),
            P("fsdp", None),
            P(None, "fsdp"),
            P("fsdp"),
        ),
        check_vma=False,
    )
```

```python
import functools
import types

import jax
import jax.numpy as jnp
from jax import lax
from jax.experimental import pallas as pl
from jax.experimental.pallas import tpu as pltpu
from jax.sharding import PartitionSpec as P

H = 8
KVH = 4
HD = 256


epsilon = 1e-06
theta = 1000042.0
masked_score = -1e30


def passed_along(value, axis, by):
    devices = lax.axis_size(axis)
    return lax.ppermute(value, axis, [(i, (i + by) % devices) for i in range(devices)])


def rope_tables(positions):
    half = HD // 2
    frequency = theta ** (-(jnp.arange(half, dtype=jnp.float32) * 2.0 / HD))
    angle = positions[:, None] * frequency[None, :]
    angle = jnp.concatenate([angle, angle], axis=-1)
    return (jnp.cos(angle), jnp.sin(angle))


def rotate(values, cosine, sine):
    half = values.shape[-1] // 2
    turned = jnp.concatenate([-values[..., half:], values[..., :half]], axis=-1)
    return values * cosine[:, None, :] + turned * sine[:, None, :]


def rotate_back(grads, cosine, sine):
    half = grads.shape[-1] // 2
    scaled = grads * sine[:, None, :]
    turned = jnp.concatenate([scaled[..., half:], -scaled[..., :half]], axis=-1)
    return grads * cosine[:, None, :] + turned


def split_heads(block):
    count = block.shape[0]
    key_cols = KVH * HD
    key_part = block[:, :key_cols].reshape(count, KVH, HD).transpose(1, 0, 2)
    value_part = block[:, key_cols:].reshape(count, KVH, HD).transpose(1, 0, 2)
    return (key_part, value_part)


def merge_heads(grouped):
    return grouped.transpose(1, 0, 2).reshape(grouped.shape[1], KVH * HD)


def weight_terms(lefts, rights):
    pieces = []
    for index in range(4):
        column = lefts[index]
        pieces.append(
            jnp.einsum("tc,tn->cn", column, rights[index], preferred_element_type=jnp.float32)
        )
    return jnp.concatenate(pieces, axis=1)


def ring_layer(
    tokens,
    query_weight,
    key_weight,
    value_weight,
    output_weight,
    first_gain,
    gate_weight,
    up_weight,
    down_weight,
    second_gain,
    cotangent,
    block_ids,
    piece_order,
):
    ctx_count = lax.axis_size("ctx")
    fsdp_count = lax.axis_size("fsdp")
    here = lax.axis_index("ctx")
    rows = tokens.shape[1]
    width = tokens.shape[2]
    group = H // KVH
    query_cols = H * HD
    key_cols = KVH * HD
    hidden_cols = gate_weight.shape[1]
    scale = HD ** (-0.5)
    whole_query, whole_key, whole_value, whole_output, gain_one = (
        lax.all_gather(query_weight, "fsdp", axis=0, tiled=True),
        lax.all_gather(key_weight, "fsdp", axis=0, tiled=True),
        lax.all_gather(value_weight, "fsdp", axis=0, tiled=True),
        lax.all_gather(output_weight, "fsdp", axis=1, tiled=True),
        lax.all_gather(first_gain, "fsdp", axis=0, tiled=True),
    )
    id_row = lax.dynamic_index_in_dim(block_ids, lax.axis_index("fsdp"), 0, keepdims=False)
    start_own = lax.dynamic_index_in_dim(piece_order, here, 0, keepdims=False) * rows
    offsets = jnp.arange(rows, dtype=jnp.int32)
    cosine, sine = rope_tables((start_own + offsets).astype(jnp.float32))
    own_ids = lax.dynamic_slice_in_dim(id_row, start_own, rows)
    query_ids = jnp.tile(own_ids, group)

    def visible(source):
        key_start = lax.dynamic_index_in_dim(piece_order, source, 0, keepdims=False) * rows
        key_ids = lax.dynamic_slice_in_dim(id_row, key_start, rows)
        return key_ids[None, :] <= query_ids[:, None]

    inputs = tokens[0].astype(jnp.float32)
    scale_one = lax.rsqrt(jnp.mean(inputs * inputs, axis=-1, keepdims=True) + epsilon)
    unit_one = inputs * scale_one
    normed = (unit_one * gain_one.astype(jnp.float32)).astype(jnp.bfloat16)
    query = jnp.dot(normed, whole_query, preferred_element_type=jnp.float32).reshape(rows, H, HD)
    query_rot = rotate(query, cosine, sine).astype(jnp.bfloat16)
    keys = jnp.dot(normed, whole_key, preferred_element_type=jnp.float32).reshape(rows, KVH, HD)
    keys_rot = rotate(keys, cosine, sine).astype(jnp.bfloat16).reshape(rows, key_cols)
    values = jnp.dot(normed, whole_value, preferred_element_type=jnp.float32).astype(jnp.bfloat16)
    key_value = jnp.concatenate([keys_rot, values], axis=-1)
    grouped = (
        query_rot.reshape(rows, KVH, group, HD).transpose(1, 2, 0, 3).reshape(KVH, group * rows, HD)
    )

    def forward_step(state, block, source):
        running, total, weighted = state
        key_part, value_part = split_heads(block)
        allowed = visible(source)
        scores = (
            jnp.einsum("hqd,hkd->hqk", grouped, key_part, preferred_element_type=jnp.float32)
            * scale
        )
        scores = jnp.where(allowed[None], scores, masked_score)
        newest = jnp.maximum(running, jnp.max(scores, axis=-1))
        factor = jnp.exp(running - newest)
        shares = jnp.where(allowed[None], jnp.exp(scores - newest[..., None]), 0.0)
        total = total * factor + jnp.sum(shares, axis=-1)
        weighted = weighted * factor[..., None] + jnp.einsum(
            "hqk,hkd->hqd",
            shares.astype(jnp.bfloat16),
            value_part,
            preferred_element_type=jnp.float32,
        )
        return (newest, total, weighted)

    start_state = (
        jnp.full((KVH, group * rows), masked_score, jnp.float32),
        jnp.zeros((KVH, group * rows), jnp.float32),
        jnp.zeros((KVH, group * rows, HD), jnp.float32),
    )
    state = forward_step(start_state, key_value, here)

    def forward_turn(turn, carry):
        block, inner = carry
        block = passed_along(block, "ctx", 1)
        source = (here - turn) % ctx_count
        return (block, forward_step(inner, block, source))

    passed_block, state = lax.fori_loop(1, ctx_count, forward_turn, (key_value, state))
    running, total, weighted = state
    attended = weighted / total[..., None]
    log_total = running + jnp.log(total)
    attended_low = (
        attended.reshape(KVH, group, rows, HD)
        .transpose(2, 0, 1, 3)
        .reshape(rows, query_cols)
        .astype(jnp.bfloat16)
    )
    middle = inputs + jnp.dot(attended_low, whole_output, preferred_element_type=jnp.float32)
    gain_two, whole_gate, whole_up, whole_down = (
        lax.all_gather(second_gain, "fsdp", axis=0, tiled=True),
        lax.all_gather(gate_weight, "fsdp", axis=0, tiled=True),
        lax.all_gather(up_weight, "fsdp", axis=0, tiled=True),
        lax.all_gather(down_weight, "fsdp", axis=1, tiled=True),
    )
    scale_two = lax.rsqrt(jnp.mean(middle * middle, axis=-1, keepdims=True) + epsilon)
    unit_two = middle * scale_two
    normed_two = (unit_two * gain_two.astype(jnp.float32)).astype(jnp.bfloat16)
    gate = jnp.dot(normed_two, whole_gate, preferred_element_type=jnp.float32)
    up = jnp.dot(normed_two, whole_up, preferred_element_type=jnp.float32)
    sigmoid_gate = jax.nn.sigmoid(gate)
    activated = gate * sigmoid_gate
    hidden = (activated * up).astype(jnp.bfloat16)
    result = middle + jnp.dot(hidden, whole_down, preferred_element_type=jnp.float32)
    output = result.astype(jnp.bfloat16)[None]
    upstream = cotangent[0]
    hidden_grad = jnp.einsum("tm,fm->tf", upstream, whole_down, preferred_element_type=jnp.float32)
    gate_grad = (hidden_grad * up * sigmoid_gate * (1.0 + gate * (1.0 - sigmoid_gate))).astype(
        jnp.bfloat16
    )
    up_grad = (hidden_grad * activated).astype(jnp.bfloat16)
    normed_two_grad = jnp.einsum(
        "tf,mf->tm", gate_grad, whole_gate, preferred_element_type=jnp.float32
    ) + jnp.einsum("tf,mf->tm", up_grad, whole_up, preferred_element_type=jnp.float32)
    gain_two_term = jnp.sum(normed_two_grad * unit_two, axis=0)
    unit_two_grad = normed_two_grad * gain_two.astype(jnp.float32)
    middle_grad = upstream.astype(jnp.float32) + scale_two * (
        unit_two_grad - unit_two * jnp.mean(unit_two_grad * unit_two, axis=-1, keepdims=True)
    )
    branch_grad = middle_grad.astype(jnp.bfloat16)
    attended_grad = jnp.einsum(
        "tm,cm->tc", branch_grad, whole_output, preferred_element_type=jnp.float32
    ).astype(jnp.bfloat16)
    grad_grouped = (
        attended_grad.reshape(rows, KVH, group, HD)
        .transpose(1, 2, 0, 3)
        .reshape(KVH, group * rows, HD)
    )
    delta = jnp.sum(grad_grouped.astype(jnp.float32) * attended, axis=-1)

    def backward_step(query_total, block, source):
        key_part, value_part = split_heads(block)
        allowed = visible(source)
        scores = (
            jnp.einsum("hqd,hkd->hqk", grouped, key_part, preferred_element_type=jnp.float32)
            * scale
        )
        scores = jnp.where(allowed[None], scores, masked_score)
        shares = jnp.where(allowed[None], jnp.exp(scores - log_total[..., None]), 0.0)
        value_grad = jnp.einsum(
            "hqk,hqd->hkd",
            shares.astype(jnp.bfloat16),
            grad_grouped,
            preferred_element_type=jnp.float32,
        )
        share_grad = jnp.einsum(
            "hqd,hkd->hqk", grad_grouped, value_part, preferred_element_type=jnp.float32
        )
        score_grad = (shares * (share_grad - delta[..., None])).astype(jnp.bfloat16)
        query_total = query_total + jnp.einsum(
            "hqk,hkd->hqd", score_grad, key_part, preferred_element_type=jnp.float32
        )
        key_grad = (
            jnp.einsum("hqk,hqd->hkd", score_grad, grouped, preferred_element_type=jnp.float32)
            * scale
        )
        return (
            query_total,
            jnp.concatenate([merge_heads(key_grad), merge_heads(value_grad)], axis=-1),
        )

    query_total, first_grad = backward_step(
        jnp.zeros((KVH, group * rows, HD), jnp.float32), key_value, here
    )
    held = first_grad

    def backward_turn(turn, carry):
        block, kept, total_query = carry
        block = passed_along(block, "ctx", 1)
        source = (here - turn) % ctx_count
        total_query, block_grad = backward_step(total_query, block, source)
        kept = passed_along(kept.astype(jnp.bfloat16), "ctx", 1).astype(kept.dtype) + block_grad
        return (block, kept, total_query)

    passed_again, held, query_total = lax.fori_loop(
        1, ctx_count, backward_turn, (key_value, held, query_total)
    )
    own_grad = passed_along(held.astype(jnp.bfloat16), "ctx", 1).astype(held.dtype)
    query_rot_grad = (
        (query_total * scale)
        .reshape(KVH, group, rows, HD)
        .transpose(2, 0, 1, 3)
        .reshape(rows, H, HD)
    )
    query_grad = (
        rotate_back(query_rot_grad, cosine, sine).reshape(rows, query_cols).astype(jnp.bfloat16)
    )
    key_grad = (
        rotate_back(own_grad[:, :key_cols].reshape(rows, KVH, HD), cosine, sine)
        .reshape(rows, key_cols)
        .astype(jnp.bfloat16)
    )
    value_grad = own_grad[:, key_cols:].astype(jnp.bfloat16)
    normed_grad = jnp.einsum(
        "tc,mc->tm", query_grad, whole_query, preferred_element_type=jnp.float32
    )
    normed_grad = normed_grad + jnp.einsum(
        "tc,mc->tm", key_grad, whole_key, preferred_element_type=jnp.float32
    )
    normed_grad = normed_grad + jnp.einsum(
        "tc,mc->tm", value_grad, whole_value, preferred_element_type=jnp.float32
    )
    gain_one_term = jnp.sum(normed_grad * unit_one, axis=0)
    unit_one_grad = normed_grad * gain_one.astype(jnp.float32)
    tokens_grad = middle_grad + scale_one * (
        unit_one_grad - unit_one * jnp.mean(unit_one_grad * unit_one, axis=-1, keepdims=True)
    )
    projected = jnp.concatenate([query_grad, key_grad, value_grad], axis=-1)
    gate_up = jnp.concatenate([gate_grad, up_grad], axis=-1)
    lefts = jnp.stack([normed, branch_grad, normed_two, upstream])
    rights = (projected, attended_low, gate_up, hidden)
    piece = lax.psum_scatter(
        weight_terms(lefts, rights).astype(jnp.bfloat16), "fsdp", scatter_dimension=0, tiled=True
    )
    shard = lax.psum(piece, "ctx").astype(jnp.float32)
    gain_one_sum, gain_two_sum = lax.psum((gain_one_term, gain_two_term), ("ctx", "fsdp"))
    own_rows = width // fsdp_count
    own_start = lax.axis_index("fsdp") * own_rows
    value_begin = query_cols + key_cols
    output_begin = value_begin + key_cols
    gate_begin = output_begin + query_cols
    up_begin = gate_begin + hidden_cols
    down_begin = up_begin + hidden_cols
    return (
        output,
        tokens_grad[None],
        shard[:, :query_cols],
        shard[:, query_cols:value_begin],
        shard[:, value_begin:output_begin],
        shard[:, output_begin:gate_begin].T,
        lax.dynamic_slice_in_dim(gain_one_sum, own_start, own_rows),
        shard[:, gate_begin:up_begin],
        shard[:, up_begin:down_begin],
        shard[:, down_begin : down_begin + hidden_cols].T,
        lax.dynamic_slice_in_dim(gain_two_sum, own_start, own_rows),
    )


VMEM_BYTES = 58 * 1024 * 1024
BF16 = jnp.bfloat16
F32 = jnp.float32
QUARTERS = 4
MESH = pl.DeviceIdType.MESH
TICKS = (2, 1, 2, 2, 3, 2, 1, 1, 1, 2, 6, 2, 2)
LINES = 2


def matmul(a, b):
    return lax.dot_general(a, b, (((1,), (0,)), ((), ())), preferred_element_type=F32)


def matmul_nt(a, b):
    return lax.dot_general(a, b, (((1,), (1,)), ((), ())), preferred_element_type=F32)


def matmul_tn(a, b):
    return lax.dot_general(a, b, (((0,), (0,)), ((), ())), preferred_element_type=F32)


def cost(flops, arrays, outs, exps=0):
    moved = sum(a.size * a.dtype.itemsize for a in arrays) + sum(
        o.size * o.dtype.itemsize for o in outs
    )
    return pl.CostEstimate(flops=int(flops), bytes_accessed=int(moved), transcendentals=int(exps))


def run_whole(body, me, arrays, outs, scratch=(), flops=0, in_hbm=0, name=None):
    count = len(arrays) - in_hbm
    return pl.pallas_call(
        body,
        out_shape=outs,
        in_specs=[pl.BlockSpec(memory_space=pltpu.SMEM)]
        + [pl.BlockSpec(memory_space=pltpu.VMEM)] * count
        + [pl.BlockSpec(memory_space=pl.ANY)] * in_hbm,
        out_specs=jax.tree.map(lambda _: pl.BlockSpec(memory_space=pltpu.VMEM), outs),
        scratch_shapes=list(scratch),
        cost_estimate=cost(flops, arrays, jax.tree.leaves(outs)),
        compiler_params=pltpu.CompilerParams(vmem_limit_bytes=VMEM_BYTES),
        name=name,
    )(me, *arrays)


def run_grid(body, me, grid, arrays, in_specs, outs, out_specs, scratch=(), flops=0, aliases=None, name=None):
    return pl.pallas_call(
        body,
        out_shape=outs,
        grid_spec=pltpu.PrefetchScalarGridSpec(
            num_scalar_prefetch=1,
            grid=grid,
            in_specs=in_specs,
            out_specs=out_specs,
            scratch_shapes=list(scratch),
        ),
        cost_estimate=cost(flops, arrays, jax.tree.leaves(outs)),
        input_output_aliases=aliases or {},
        compiler_params=pltpu.CompilerParams(vmem_limit_bytes=VMEM_BYTES),
        name=name,
    )(me, *arrays)


def shape(dims, kind=BF16):
    return jax.ShapeDtypeStruct(tuple(dims), kind)


def fixed(block):
    return pl.BlockSpec(block, lambda i, me: (0,) * len(block), pipeline_mode=pl.Buffered(1))


def column(index, wide):
    return pl.ds(pl.multiple_of(index * wide, wide), wide)


def turn(values):
    half = values.shape[-1] // 2
    return jnp.concatenate([-values[:, half:], values[:, :half]], axis=-1)


def turn_back(values):
    half = values.shape[-1] // 2
    return jnp.concatenate([values[:, half:], -values[:, :half]], axis=-1)


def plane_layer(
    tokens,
    query_weight,
    key_weight,
    value_weight,
    output_weight,
    first_gain,
    gate_weight,
    up_weight,
    down_weight,
    second_gain,
    cotangent,
    block_ids,
    piece_order,
):
    ctx_count = lax.axis_size("ctx")
    n = lax.axis_size("fsdp")
    planes = ctx_count // 2
    ctx = lax.axis_index("ctx")
    z, core = ctx // 2, ctx % 2
    f = lax.axis_index("fsdp")
    me = jnp.stack([f, core]).astype(jnp.int32)
    rows, width = tokens.shape[1:]
    pair = 2 * rows
    plane_rows = n * pair
    wide = width // n
    hidden_cols = gate_weight.shape[1]
    part = hidden_cols // (2 * n)
    quarter = part // QUARTERS
    scale = HD ** (-0.5)

    def across(value, d):
        return lax.ppermute(value, "fsdp", [(i, i ^ d) for i in range(n)])

    def sibling(value):
        return lax.ppermute(value, "ctx", [(i, i ^ 1) for i in range(ctx_count)])

    def along(value, step):
        pairs = [(i, i + 2 * step) for i in range(ctx_count)]
        return lax.ppermute(value, "ctx", [(a, b) for a, b in pairs if 0 <= b < ctx_count])

    def between_planes(value, moves):
        return lax.ppermute(
            value, "ctx", [(2 * a + side, 2 * b + side) for a, b in moves for side in range(2)]
        )

    def gathered(value):
        own = [value] + [across(value, d) for d in range(1, n)]
        return own, [sibling(block) for block in own]

    def reduced(own, other):
        near = [sibling(block) for block in other]
        sent = [
            across((own[d].astype(F32) + near[d].astype(F32)).astype(BF16), d) for d in range(1, n)
        ]
        return [own[0], near[0]] + sent

    middle_left, middle_right = planes // 2 - 1, planes // 2
    folds = [
        [(s, s + 1), (planes - 1 - s, planes - 2 - s)] for s in range(middle_left)
    ]

    def summed_over_planes(value):
        for moves in folds:
            value = (
                value.astype(F32) + between_planes(value, moves).astype(F32)
            ).astype(value.dtype)
        crossed = between_planes(value, [(middle_left, middle_right), (middle_right, middle_left)])
        value = (value.astype(F32) + crossed.astype(F32)).astype(value.dtype)
        for s, moves in reversed(list(enumerate(folds))):
            back = between_planes(value, [(b, a) for a, b in moves])
            receives = (z == s) | (z == planes - 1 - s)
            value = jnp.where(receives, back, value)
        return value

    place = jnp.arange(rows, dtype=jnp.int32)
    own_pieces = lax.dynamic_slice_in_dim(piece_order, 2 * z, 2)
    positions = (own_pieces[:, None] * rows + place[None, :]).reshape(pair).astype(F32)
    cosine, sine = rope_tables(positions)
    is_value = core == 1
    kv_cosine = jnp.where(is_value, 1.0, cosine)
    kv_sine = jnp.where(is_value, 0.0, sine)
    chips = f ^ jnp.arange(n, dtype=jnp.int32)
    ring = (z - jnp.arange(planes, dtype=jnp.int32)) % planes
    ring_ctx = (2 * ring[:, None] + jnp.arange(2, dtype=jnp.int32)[None, :]).reshape(-1)
    id_pieces = block_ids.reshape(n, ctx_count, rows)
    ids = id_pieces[chips[:, None], piece_order[ring_ctx][None, :]]
    key_ids = ids.reshape(n, planes, 1, pair)
    query_ids = ids[:, :2].reshape(n, pair, 1)

    def cut_weights(me_ref, *refs):
        keys, values, (one, two), outs = refs[:n], refs[n : 2 * n], refs[2 * n : 2 * n + 2], refs[2 * n + 2 :]
        keys_here = me_ref[1] == 0
        for d in range(n):

            @pl.when(keys_here)
            def _():
                outs[d][:wide, :] = keys[d][...]

            @pl.when(jnp.logical_not(keys_here))
            def _():
                outs[d][:wide, :] = values[d][...]

            pick = lax.broadcasted_iota(jnp.int32, (16, HD), 0) < 8
            for g, gain in enumerate((one, two)):
                halves = [gain[:, h * HD : (h + 1) * HD].astype(F32) for h in range(2)]
                outs[d][wide + 16 * g : wide + 16 * (g + 1), :] = jnp.where(pick, *halves).astype(BF16)

    def chip_of(d):
        return lambda i, me: (0, me[0] ^ d)

    own_tokens = tokens[0]
    near_tokens = [own_tokens] + [across(own_tokens, d) for d in (1, 2)]
    gain_spec = pl.BlockSpec((1, wide), lambda i, me: (0, 0))
    cut = run_grid(
        cut_weights,
        me,
        (1,),
        [key_weight] * n
        + [value_weight] * n
        + [first_gain.reshape(1, wide), second_gain.reshape(1, wide)],
        [pl.BlockSpec((wide, HD), chip_of(d)) for d in range(n)] * 2 + [gain_spec, gain_spec],
        [shape((wide + 32, HD))] * n,
        [pl.BlockSpec((wide + 32, HD), lambda i, me: (0, 0))] * n,
        name="cut_weights",
    )
    weights_in = [cut[0]] + [across(cut[d], d) for d in range(1, n)]
    piece = (wide + quarter, 2 * quarter)
    own_cotangent = cotangent[0]
    block = (rows, width)

    tiles_count = 3 * QUARTERS + 3
    query_at, output_at, kv_at = tiles_count - 3, tiles_count - 2, tiles_count - 1
    units = 2 * tiles_count
    unit = (2, quarter, wide)
    held_sums, held_ends, ahead = 4, 3, 2
    MID, BACK, OUT, ONE = range(4)
    query_slot, attended_slot, query_grad_slot, kv_grad_slot = range(2 * planes, 2 * planes + 4)
    kept_slots = 2 * planes + 2
    columns = (plane_rows, HD)
    lanes = (8, wide)
    dma = pltpu.SemaphoreType.DMA

    in_hbm = dict(
        near_tokens=near_tokens,
        in_weight=weights_in,
        query_weight=query_weight,
        output_weight=output_weight,
        gate_weight=gate_weight,
        up_weight=up_weight,
        down_weight=down_weight,
        cotangent=own_cotangent,
        tokens=own_tokens,
    )
    in_vmem = dict(
        tables=jnp.stack([cosine, sine, kv_cosine, kv_sine]),
        query_ids=query_ids,
        key_ids=key_ids,
    )
    unit_array = shape((units,) + unit)
    out_hbm = dict(
        tiles=unit_array,
        from_end=unit_array,
        from_middle=unit_array,
        finals=unit_array,
        owned=unit_array,
        near=unit_array,
        row_near=shape((4, n) + block),
        row_far=shape((4, n) + block),
        cot_all=shape((2, n) + block),
        query_in=shape((n, wide, HD)),
        kept=shape((kept_slots,) + columns),
        out_weight=shape((2, 2, HD, wide)),
        normed=shape((plane_rows, width)),
        middle=shape(block, F32),
        branch_all=shape((n, 2) + block),
        kv_other=shape((planes,) + columns),
        kv_down=shape((planes,) + columns),
        kv_up=shape((planes,) + columns),
        out_own=shape(block),
        tokens_grad=shape(block, F32),
        output=shape(block),
        gain_out=shape(lanes, F32),
    )
    scratch = dict(
        work=pltpu.VMEM((2 * plane_rows, width), BF16),
        feed=pltpu.VMEM((QUARTERS, n) + piece, BF16),
        heads=pltpu.VMEM((3 * QUARTERS, plane_rows, HD), BF16),
        turned=pltpu.VMEM((3, HD, plane_rows), BF16),
        stage=pltpu.VMEM((2, n, quarter, wide), BF16),
        mine=pltpu.VMEM((2,) + unit, BF16),
        theirs=pltpu.VMEM((2,) + unit, BF16),
        crossed=pltpu.VMEM((2,) + unit, BF16),
        sums=pltpu.VMEM((held_sums,) + unit, BF16),
        ends=pltpu.VMEM((held_ends,) + unit, BF16),
        some_rows=pltpu.VMEM((n,) + block, BF16),
        wide_rows=pltpu.VMEM(block, F32),
        own_rows=pltpu.VMEM(block, BF16),
        kv_some=pltpu.VMEM((2,) + columns, BF16),
        flat=pltpu.VMEM((8, width), F32),
        gain_mine=pltpu.VMEM((n,) + lanes, F32),
        gain_far=pltpu.VMEM((n,) + lanes, F32),
        gain_sum=pltpu.VMEM((4,) + lanes, F32),
        gain_in=pltpu.VMEM((4,) + lanes, F32),
        load_sem=dma((4 * n + n,)),
        gains=pltpu.VMEM((8, width), F32),
        gain_rows=pltpu.VMEM((n, 32, HD), BF16),
        feed_local=dma((3 * QUARTERS,)),
        feed_send=dma((3 * QUARTERS * n,)),
        feed_recv=dma((3 * QUARTERS * n,)),
        stage_sem=dma((2, 2)),
        one_send=dma((units,)),
        one_recv=dma((units,)),
        two_send=dma((units,)),
        two_recv=dma((units,)),
        three_send=dma((units,)),
        three_recv=dma((units,)),
        mine_sem=dma((2,)),
        theirs_sem=dma((2,)),
        crossed_sem=dma((2,)),
        final_sem=dma((held_ends,)),
        deal_local=dma((units,)),
        deal_send=dma((2 * units,)),
        deal_recv=dma((2 * units,)),
        sib_send=dma((units,)),
        sib_recv=dma((units,)),
        row_sem=dma((n,)),
        row_near_send=dma((4 * n,)),
        row_near_recv=dma((4 * n,)),
        row_far_send=dma((4 * n,)),
        row_far_recv=dma((4 * n,)),
        token_send=dma((n,)),
        token_recv=dma((n,)),
        query_send=dma((n,)),
        query_recv=dma((n,)),
        out_send=dma((n,)),
        out_recv=dma((n,)),
        cot_send=dma((n,)),
        cot_recv=dma((n,)),
        cot_near_send=dma((n,)),
        cot_near_recv=dma((n,)),
        two_local=dma((1,)),
        two_far_send=dma((n,)),
        two_far_recv=dma((n,)),
        two_near_send=dma((n,)),
        two_near_recv=dma((n,)),
        two_half_send=dma((n,)),
        two_half_recv=dma((n,)),
        branch_half_send=dma((n,)),
        branch_half_recv=dma((n,)),
        climb_send=dma((n * planes,)),
        climb_recv=dma((n * planes,)),
        fall_send=dma((n * planes,)),
        fall_recv=dma((n * planes,)),
        soft=pltpu.VMEM((2 * n, pair, 1), F32),
        pass_send=dma((n * planes,)),
        pass_recv=dma((n * planes,)),
        cot_half_send=dma((n,)),
        cot_half_recv=dma((n,)),
        share_send=dma((2 * n,)),
        share_recv=dma((2 * n,)),
        token_half_send=dma((n,)),
        token_half_recv=dma((n,)),
        keep_sem=dma((3,)),
        branch_local=dma((1,)),
        branch_send=dma((n,)),
        branch_recv=dma((n,)),
        branch_near_send=dma((n,)),
        branch_near_recv=dma((n,)),
        kv_sem=dma((2,)),
        kv_send=dma((planes,)),
        kv_recv=dma((planes,)),
        down_send=dma((planes,)),
        down_recv=dma((planes,)),
        up_send=dma((planes,)),
        up_recv=dma((planes,)),
        gain_send=dma((n + 4,)),
        gain_recv=dma((n + 4,)),
    )

    def backward(*refs):
        r, first = types.SimpleNamespace(), 0
        for group in (in_hbm, in_vmem, out_hbm):
            leaves, form = jax.tree.flatten(group)
            vars(r).update(jax.tree.unflatten(form, refs[first : first + len(leaves)]))
            first += len(leaves)
        vars(r).update(zip(scratch, refs[first:]))
        here = lax.axis_index("ctx")
        chip = lax.axis_index("fsdp")
        z, side = here // 2, here % 2
        is_middle = (z == 1) | (z == 2)
        is_end = jnp.logical_not(is_middle)
        chips = [chip, chip + 1 - 2 * (chip % 2), (chip + 2) % 4, 3 - chip]
        partner = (2 * (z + 1 - 2 * (z % 2)) + side, chip)
        other_middle = (2 * (3 - z) + side, chip)
        other_core = (here + 1 - 2 * side, chip)
        below = ((here + ctx_count - 2) % ctx_count, chip)
        above = ((here + 2) % ctx_count, chip)
        blocks = [pl.ds(pl.multiple_of(c * wide, wide), wide) for c in chips]
        work, feed, heads, turned, stage = r.work, r.feed, r.heads, r.turned, r.stage

        barrier = pltpu.get_barrier_semaphore()
        for peer in [(here, c) for c in chips[1:]] + [partner, other_core]:
            pl.semaphore_signal(barrier, inc=1, device_id=peer, device_id_type=MESH)

        @pl.when(is_middle)
        def _():
            pl.semaphore_signal(barrier, inc=1, device_id=other_middle, device_id_type=MESH)
            pl.semaphore_wait(barrier, n + 2)

        @pl.when(is_end)
        def _():
            pl.semaphore_wait(barrier, n + 1)

        def remote(source, target, send, recv, peer):
            return pltpu.make_async_remote_copy(
                src_ref=source,
                dst_ref=target,
                send_sem=send,
                recv_sem=recv,
                device_id=peer,
                device_id_type=MESH,
            )

        local = pltpu.make_async_copy

        def span(first, count):
            return pl.ds(pl.multiple_of(first, count), count)

        def head_of(d):
            return span((2 * chips[d] + side) * HD, HD)

        def feed_parts(q, d, first=0, count=wide):
            there = span(((2 * chips[d] + side) * QUARTERS + q) * quarter, quarter)
            rows_in = pl.ds(first, count)
            below = 0 if count == wide else pl.multiple_of(first // 2, quarter // 2)
            some = pl.ds(
                pl.multiple_of(
                    ((2 * chips[d] + side) * QUARTERS + q) * quarter + below, quarter // 2
                ),
                count // 2,
            )
            below = wide if count == wide else pl.multiple_of(wide + below, quarter // 2)
            return (
                (r.gate_weight.at[rows_in, there], feed.at[q, d, rows_in, pl.ds(0, quarter)]),
                (r.up_weight.at[rows_in, there], feed.at[q, d, rows_in, pl.ds(quarter, quarter)]),
                (r.down_weight.at[some], feed.at[q, d, pl.ds(below, count // 2)]),
            )

        def feed_far(q, d, *rows_of):
            copies = []
            for part, (source, target) in enumerate(feed_parts(q, d, *rows_of)):
                at = (q * n + d) * 3 + part
                copies.append(
                    remote(source, target, r.feed_send.at[at], r.feed_recv.at[at], (here, chips[d]))
                )
            return copies

        def feed_own(q):
            return [
                local(source, target, r.feed_local.at[3 * q + part])
                for part, (source, target) in enumerate(feed_parts(q, 0))
            ]

        def every(copies, use):
            for copy in copies:
                use(copy)

        starts, waits = lambda c: c.start(), lambda c: c.wait()
        arrives, leaves = lambda c: c.wait_recv(), lambda c: c.wait_send()

        def hop_one(i):
            return remote(r.tiles.at[i], r.from_end.at[i], r.one_send.at[i], r.one_recv.at[i], partner)

        def hop_two(i):
            return remote(
                r.sums.at[i % held_sums],
                r.from_middle.at[i],
                r.two_send.at[i],
                r.two_recv.at[i],
                other_middle,
            )

        def hop_three(i):
            return remote(
                r.ends.at[i % held_ends], r.finals.at[i], r.three_send.at[i], r.three_recv.at[i], partner
            )

        def load_mine(i):
            return local(r.tiles.at[i], r.mine.at[i % 2], r.mine_sem.at[i % 2])

        def load_theirs(i):
            return local(r.from_end.at[i], r.theirs.at[i % 2], r.theirs_sem.at[i % 2])

        def load_crossed(i):
            return local(r.from_middle.at[i], r.crossed.at[i % 2], r.crossed_sem.at[i % 2])

        def keep_final(i):
            return local(r.ends.at[i % held_ends], r.finals.at[i], r.final_sem.at[i % held_ends])

        def keep_own(i):
            return local(r.finals.at[i, 0], r.owned.at[i, 0], r.deal_local.at[i])

        def deal_to(i, b, d):
            at = 2 * i + b
            return remote(
                r.finals.at[i, b],
                r.owned.at[i, b],
                r.deal_send.at[at],
                r.deal_recv.at[at],
                (here, chips[d]),
            )

        def to_sibling(i):
            return remote(r.owned.at[i], r.near.at[i], r.sib_send.at[i], r.sib_recv.at[i], other_core)

        def add(target, a, b):
            def some(s, _):
                at = (s // 4, span((s % 4) * (quarter // 4), quarter // 4))
                target[at] = a[at] + b[at]
                return 0

            lax.fori_loop(0, 8, some, 0)

        def when_in(i, *conditions):
            return pl.when(functools.reduce(jnp.logical_and, conditions, (i >= 0) & (i < units)))

        def step(i, _=0):
            @when_in(i + ahead, is_end, i >= 0)
            def _():
                hop_one(i + ahead).start()

            @when_in(i - 1, is_middle)
            def _():
                at = i - 1
                load_mine(at).wait()
                load_theirs(at).wait()

                @pl.when(at >= held_sums)
                def _():
                    hop_two(at - held_sums).wait_send()

                add(r.sums.at[at % held_sums], r.mine.at[at % 2], r.theirs.at[at % 2])
                hop_two(at).start()

            @when_in(i - 4, is_middle)
            def _():
                at = i - 4
                load_crossed(at).wait()

                @pl.when(at >= held_ends)
                def _():
                    hop_three(at - held_ends).wait_send()

                add(r.ends.at[at % held_ends], r.sums.at[at % held_sums], r.crossed.at[at % 2])
                hop_three(at).start()
                keep_final(at).start()

            @when_in(i, is_middle)
            def _():
                hop_one(i).wait_recv()
                load_mine(i).start()
                load_theirs(i).start()

            @when_in(i - 3, is_middle)
            def _():
                hop_two(i - 3).wait_recv()
                load_crossed(i - 3).start()

            @when_in(i - 6)
            def _():
                at = i - 6

                @pl.when(is_middle)
                def _():
                    keep_final(at).wait()

                @pl.when(is_end)
                def _():
                    hop_three(at).wait_recv()

                @pl.when(at % 2 == 0)
                def _():
                    keep_own(at).start()
                    deal_to(at, 1, 1).start()

                @pl.when(at % 2 == 1)
                def _():
                    deal_to(at, 0, 2).start()
                    deal_to(at, 1, 3).start()

            @when_in(i - 9)
            def _():
                at = i - 9

                @pl.when(at % 2 == 0)
                def _():
                    keep_own(at).wait()

                @pl.when(at % 2 == 1)
                def _():
                    deal_to(at, 0, 2).wait_recv()

                deal_to(at, 1, 3).wait_recv()
                to_sibling(at).start()

            return 0

        steps_done = [0]

        def advance(count):
            first = steps_done[0]
            steps_done[0] = first + count
            lax.fori_loop(first, first + count, step, 0)

        def finish():
            def one(i, _):
                @pl.when(is_end)
                def _():
                    hop_one(i).wait_send()

                @pl.when(is_middle & (i >= units - held_sums))
                def _():
                    hop_two(i).wait_send()

                @pl.when(is_middle & (i >= units - held_ends))
                def _():
                    hop_three(i).wait_send()

                @pl.when(i % 2 == 1)
                def _():
                    deal_to(i, 0, 2).wait_send()

                deal_to(i, 1, 3).wait_send()
                to_sibling(i).wait()
                return 0

            lax.fori_loop(0, units, one, 0)

        def stage_copy(t, h):
            return local(r.stage.at[t % 2, pl.ds(2 * h, 2)], r.tiles.at[2 * t + h], r.stage_sem.at[t % 2, h])

        def staged(t):
            for h in range(2):
                stage_copy(t, h).wait()

            @pl.when(is_end & (t == 0))
            def _():
                for i in range(ahead):
                    hop_one(i).start()

        def outer(t, left, right_rows):
            for j in range(n):
                stage[t % 2, j] = matmul(left, work[right_rows, blocks[j]]).astype(BF16)
            for h in range(2):
                stage_copy(t, h).start()

        def row_near(s, base, d):
            at = s * n + d
            return remote(
                work.at[pl.ds(base + (2 * d + 1) * rows, rows)],
                r.row_near.at[s, d],
                r.row_near_send.at[at],
                r.row_near_recv.at[at],
                other_core,
            )

        def row_far(s, base, d):
            at = s * n + d
            return remote(
                work.at[pl.ds(base + 2 * d * rows, rows)],
                r.row_far.at[s, d],
                r.row_far_send.at[at],
                r.row_far_recv.at[at],
                (here, chips[d]),
            )

        def near_load(s, d):
            return local(r.row_near.at[s, d], r.some_rows.at[d], r.row_sem.at[d])

        def far_load(s, d):
            return local(r.row_far.at[s, d], r.some_rows.at[d], r.row_sem.at[d])

        few = 16

        def row_send(s, base, d):
            row_near(s, base, d).wait_recv()
            near_load(s, d).start()
            near_load(s, d).wait()

            def some(c, _):
                at = span(c * few, few)
                own = pl.ds(pl.multiple_of(base + 2 * d * rows + c * few, few), few)
                work[own, :] = work[own, :] + r.some_rows[d, at, :]
                return 0

            lax.fori_loop(0, rows // few, some, 0)
            row_far(s, base, d).start()

        far_first = (1, 2, 3, 0)

        def rows_reduced(s, base, compute, send=True, ticks=0):
            def one(i, _):
                d = (i + 1) % n
                compute(d)
                for at in range(n):

                    @pl.when(i == at)
                    def _():
                        row_near(s, base, far_first[at]).start()
                        if send and at > 0:
                            row_send(s, base, far_first[at - 1])

                if ticks:

                    @pl.when(i >= n - ticks)
                    def _():
                        step(first + i - (n - ticks))

                return 0

            first = steps_done[0]
            steps_done[0] = first + ticks
            lax.fori_loop(0, n, one, 0)

        def rows_arrive(s, base):
            row_near(s, base, 0).wait_recv()
            near_load(s, 0).start()
            for d in range(1, n):
                row_far(s, base, d).wait_recv()
                far_load(s, d).start()
            near_load(s, 0).wait()
            for d in range(1, n):
                far_load(s, d).wait()

        def rows_sent(s, base):
            for d in range(n):
                row_near(s, base, d).wait_send()
            for d in range(1, n):
                row_far(s, base, d).wait_send()

        def norm_rows_back(base, value_ref, gain_row, use):
            r.flat[...] = jnp.zeros_like(r.flat)

            def some(c, _):
                at = span(c * few, few)
                grad = work[pl.ds(pl.multiple_of(base + c * few, few), few), :].astype(F32)
                for d in range(n):
                    grad += r.some_rows[d, at, :].astype(F32)
                values = value_ref[at, :].astype(F32)
                inverse = lax.rsqrt(jnp.mean(values * values, axis=-1, keepdims=True) + epsilon)
                unit_rows = values * inverse
                scaled = grad * gain_row
                back = inverse * (
                    scaled - unit_rows * jnp.mean(scaled * unit_rows, axis=-1, keepdims=True)
                )
                use(at, back)
                terms = grad * unit_rows
                r.flat[...] += terms[:8] + terms[8:]
                return 0

            lax.fori_loop(0, rows // few, some, 0)

        def gain_terms(at):
            total = jnp.sum(r.flat[...], axis=0, keepdims=True)
            r.flat[0:1, :] = total
            for j in range(n):
                r.gain_mine[j, at : at + 1, :] = r.flat[0:1, blocks[j]]

        r.gain_mine[...] = jnp.zeros_like(r.gain_mine)
        loads = []

        def load(source, target):
            copy = local(source, target, r.load_sem.at[len(loads)])
            copy.start()
            loads.append(copy)

        def loaded():
            while loads:
                loads.pop().wait()

        def out_far(d):
            return remote(
                r.output_weight.at[head_of(d)],
                r.theirs.at[d // 2, d % 2],
                r.out_send.at[d],
                r.out_recv.at[d],
                (here, chips[d]),
            )

        def cot_far(d):
            return remote(
                r.cotangent, r.cot_all.at[0, d], r.cot_send.at[d], r.cot_recv.at[d], (here, chips[d])
            )

        def cot_near(d):
            source = r.cotangent if d == 0 else r.cot_all.at[0, d]
            return remote(
                source, r.cot_all.at[1, d], r.cot_near_send.at[d], r.cot_near_recv.at[d], other_core
            )

        def query_far(d):
            return remote(
                r.query_weight.at[:, head_of(d)],
                r.query_in.at[d],
                r.query_send.at[d],
                r.query_recv.at[d],
                (here, chips[d]),
            )

        def kv_piece(j):
            return r.kv_some.at[j // 3, pl.ds(j % 3 * wide, wide)]

        def query_piece(j):
            return heads.at[query_grad_slot + j // 3, pl.ds(j % 3 * wide, wide)]

        half_rows = rows // 2

        def cot_half(d):
            some = pl.ds((d - 1) * half_rows, half_rows)
            return remote(
                r.cot_all.at[0, d, some],
                r.cot_all.at[0, 3, some],
                r.cot_half_send.at[d],
                r.cot_half_recv.at[d],
                (here, chips[3 - d]),
            )

        parity = z % 2

        def feed_half(d):
            return feed_far(0, d, pl.multiple_of(parity * (wide // 2), wide // 2), wide // 2)

        def feed_share(d):
            copies = []
            for part, (first, count) in enumerate(((0, wide // 2), (wide, quarter // 2))):
                some = feed.at[0, d, span(first + parity * count, count)]
                at = 2 * d + part
                copies.append(remote(some, some, r.share_send.at[at], r.share_recv.at[at], partner))
            return copies

        def token_near(d):
            source = work.at[pl.ds(plane_rows + 2 * d * rows, rows)] if d == 3 else r.near_tokens[d]
            return remote(
                source,
                work.at[pl.ds(plane_rows + (2 * d + 1) * rows, rows)],
                r.token_send.at[d],
                r.token_recv.at[d],
                other_core,
            )

        def token_half(d):
            return remote(
                r.near_tokens[d].at[pl.ds((d - 1) * half_rows, half_rows)],
                work.at[pl.ds(plane_rows + 6 * rows + (d - 1) * half_rows, half_rows)],
                r.token_half_send.at[d],
                r.token_half_recv.at[d],
                (here, chips[3 - d]),
            )

        for d in (1, 2):
            token_half(d).start()
        for d in range(1, n):
            query_far(d).start()
        for d in range(1, n):
            out_far(d).start()
        cot_near(0).start()
        for d in range(n - 1):
            token_near(d).start()
            load(r.near_tokens[d], work.at[pl.ds(plane_rows + 2 * d * rows, rows)])
        for j in range(n):
            load(r.in_weight[j].at[pl.ds(0, wide)], kv_piece(j))
            load(r.in_weight[j].at[pl.ds(wide, 32)], r.gain_rows.at[j])
        loaded()
        load(r.output_weight.at[head_of(0)], r.theirs.at[0, 0])
        load(r.query_weight.at[:, head_of(0)], query_piece(0))
        for q in range(QUARTERS):
            every(feed_own(q), starts)
        for j in range(n):
            both = r.gain_rows[j].astype(F32)
            for g in range(2):
                for h in range(2):
                    here_half = pl.ds(pl.multiple_of(chips[j] * wide + h * HD, HD), HD)
                    r.gains[g : g + 1, here_half] = both[16 * g + 8 * h : 16 * g + 8 * h + 1]

        def project(d):
            for c in range(2):
                first = (2 * d + (side + c) % 2) * rows

                def some(s, _, c=c, first=first):
                    now = pl.ds(pl.multiple_of(plane_rows + first + s * few, few), few)
                    then = pl.ds(pl.multiple_of((2 * d + c) * rows + s * few, few), few)
                    values = work[now, :].astype(F32)
                    inverse = lax.rsqrt(jnp.mean(values * values, axis=-1, keepdims=True) + epsilon)
                    work[then, :] = (values * inverse * r.gains[0:1, :]).astype(BF16)
                    return 0

                lax.fori_loop(0, rows // few, some, 0)
            now = span(d * pair, pair)
            kv = jnp.zeros((pair, HD), F32)
            for j in range(n):
                kv += matmul(work[now, blocks[j]], kv_piece(j)[...])
            kv = kv * r.tables[2] + turn(kv) * r.tables[3]
            heads[0, now, :] = kv.astype(BF16)

        def block_of(k, d):
            return heads.at[k, span(d * pair, pair)]

        def climb(s, d):
            at = s * n + d
            return remote(
                block_of(s - 1, d), block_of(s, d), r.climb_send.at[at], r.climb_recv.at[at], above
            )

        def fall(s, d):
            at = s * n + d
            return remote(
                block_of((planes - s + 1) % planes, d),
                block_of(planes - s, d),
                r.fall_send.at[at],
                r.fall_recv.at[at],
                below,
            )

        def pass_on(k, d):
            at = k * n + d
            return remote(
                block_of(k, d),
                block_of(planes + k, d),
                r.pass_send.at[at],
                r.pass_recv.at[at],
                other_core,
            )

        def kv_leave(s, d):
            @pl.when((z - s + 1 >= 0) & (z + 1 < planes))
            def _():
                climb(s, d).start()

            @pl.when((z + s - 1 < planes) & (z >= 1))
            def _():
                fall(s, d).start()

        def kv_come(s, d):
            @pl.when(z - s >= 0)
            def _():
                climb(s, d).wait_recv()

            @pl.when(z + s < planes)
            def _():
                fall(s, d).wait_recv()

        def passing(condition, k, d):
            @pl.when(condition)
            def _():
                pass_on(k, d).start()

        def passed(condition, k, d):
            @pl.when(condition)
            def _():
                pass_on(k, d).wait_recv()

        def by_chip(use):
            def one(i, _):
                use((i + 1) % n)
                return 0

            lax.fori_loop(0, n, one, 0)

        def start_kv(d):
            for at in range(n):

                @pl.when(d == at)
                def _():
                    if at == 3:
                        for far in (1, 2):
                            token_half(far).wait_recv()
                        token_near(3).start()
                    token_near(at).wait_recv()

            project(d)
            kv_leave(1, d)
            pass_on(0, d).start()

        by_chip(start_kv)
        token_near(3).wait_send()
        keep_normed = local(work.at[pl.ds(0, plane_rows)], r.normed, r.keep_sem.at[0])
        keep_normed.start()
        for d in range(1, n):
            query_far(d).wait_recv()
            load(r.query_in.at[d], query_piece(d))
        for d in (1, 2):
            cot_far(d).start()
        loaded()

        def project_query(d, _):
            now = span(d * pair, pair)
            query = jnp.zeros((pair, HD), F32)
            for j in range(n):
                query += matmul(work[now, blocks[j]], query_piece(j)[...])
            query = query * r.tables[0] + turn(query) * r.tables[1]
            heads[query_slot, now, :] = query.astype(BF16)
            return 0

        lax.fori_loop(0, n, project_query, 0)
        for d in range(1, n):
            out_far(d).wait_recv()
        keep_out = local(r.theirs, r.out_weight, r.keep_sem.at[1])
        keep_out.start()

        def put_rows(base, d, now_values, block_at):
            first = pl.ds(pl.multiple_of(base + (2 * d + side) * rows, rows), rows)
            second = pl.ds(pl.multiple_of(base + (2 * d + 1 - side) * rows, rows), rows)
            work[first, block_at] = now_values[:rows]
            work[second, block_at] = now_values[rows:]

        def totals(d):
            return [r.wide_rows.at[:, span((2 * d + c) * HD, HD)] for c in range(2)]

        def attend_block(k, d, first, last):
            now = span(d * pair, pair)
            a, b = heads[k, now, :], heads[planes + k, now, :]
            keys, values = jnp.where(side == 0, a, b), jnp.where(side == 0, b, a)
            score = matmul_nt(heads[query_slot, now, :], keys) * scale
            score = jnp.where(r.key_ids[d, k] <= r.query_ids[d], score, masked_score)
            top = jnp.max(score, axis=-1, keepdims=True)
            if not first:
                before = r.soft[d]
                top = jnp.maximum(top, before)
                factor = jnp.exp(before - top)
            raised = jnp.exp(score - top)
            weight = jnp.sum(raised, axis=-1, keepdims=True)
            total = matmul(raised.astype(BF16), values)
            if not first:
                weight += r.soft[n + d] * factor
                total += jnp.concatenate([t[...] for t in totals(d)], axis=0) * factor
            if last:
                return total, weight
            r.soft[d] = top
            r.soft[n + d] = weight
            for c, target in enumerate(totals(d)):
                target[...] = total[c * rows : (c + 1) * rows]
            return None

        def attend_to(k, first=False):
            by_chip(lambda d: attend_block(k, d, first, False) and None)

        def when_middle(there, otherwise):
            return jnp.where(is_middle, there, otherwise)

        by_chip(lambda d: pass_on(0, d).wait_recv())
        attend_to(0, first=True)

        def first_come(d):
            kv_come(1, d)
            kv_leave(2, d)
            passing(z >= 1, 1, d)
            passing(z + 1 < planes, 3, d)

        def first_passed(d):
            passed(z >= 1, 1, d)
            passed(z + 1 < planes, 3, d)

        by_chip(first_come)
        by_chip(first_passed)
        attend_to(jnp.where(z >= 1, 1, 3))
        for d in (1, 2):
            cot_far(d).wait_recv()
            cot_half(d).start()
            cot_near(d).start()
        for d in range(1, n):
            every(feed_half(d), starts)

        def second_come(d):
            kv_come(2, d)
            kv_leave(3, d)
            pass_on(2, d).start()

        by_chip(second_come)
        by_chip(lambda d: pass_on(2, d).wait_recv())
        attend_to(when_middle(3, 2))
        keep_normed.wait()

        def attend(d):
            kv_come(3, d)
            passing(z == 0, 1, d)
            passing(z == planes - 1, 3, d)
            passed(z == 0, 1, d)
            passed(z == planes - 1, 3, d)
            now = span(d * pair, pair)
            last_block = jnp.where(z == 0, 1, when_middle(2, 3))
            total, weight = attend_block(last_block, d, False, True)
            low_total = (total * (1.0 / weight)).astype(BF16)
            heads[attended_slot, now, :] = low_total
            for j in range(n):
                put_rows(
                    plane_rows,
                    d,
                    matmul(low_total, r.theirs[j // 2, j % 2]).astype(BF16),
                    blocks[j],
                )

        rows_reduced(MID, plane_rows, attend)
        keep_heads = local(heads.at[pl.ds(0, kept_slots)], r.kept, r.keep_sem.at[2])
        keep_heads.start()
        load(r.tokens, r.own_rows)
        loaded()
        keep_out.wait()
        for d in (1, 2):
            cot_half(d).wait_recv()
        cot_near(3).start()
        for d in range(1, n):
            every(feed_half(d), arrives)
            every(feed_share(d), starts)

        def kv_left(d):
            for s in range(1, planes):

                @pl.when((z - s + 1 >= 0) & (z + 1 < planes))
                def _():
                    climb(s, d).wait_send()

                @pl.when((z + s - 1 < planes) & (z >= 1))
                def _():
                    fall(s, d).wait_send()

            for k in range(planes):
                pass_on(k, d).wait_send()

        by_chip(kv_left)

        rows_arrive(MID, plane_rows)

        def second_norm(c, _):
            at = span(c * few, few)
            total = r.own_rows[at, :].astype(F32)
            total += work[pl.ds(pl.multiple_of(plane_rows + c * few, few), few), :].astype(F32)
            for d in range(n):
                total += r.some_rows[d, at, :].astype(F32)
            inverse = lax.rsqrt(jnp.mean(total * total, axis=-1, keepdims=True) + epsilon)
            r.wide_rows[at, :] = total
            r.own_rows[at, :] = (total * inverse * r.gains[1:2, :]).astype(BF16)
            return 0

        lax.fori_loop(0, rows // few, second_norm, 0)

        def two_far(d):
            return remote(
                r.own_rows,
                work.at[pl.ds(2 * d * rows, rows)],
                r.two_far_send.at[d],
                r.two_far_recv.at[d],
                (here, chips[d]),
            )

        def two_near(d):
            source = r.own_rows if d == 0 else work.at[pl.ds(2 * d * rows, rows)]
            return remote(
                source,
                work.at[pl.ds((2 * d + 1) * rows, rows)],
                r.two_near_send.at[d],
                r.two_near_recv.at[d],
                other_core,
            )

        def two_half(d):
            return remote(
                work.at[pl.ds(2 * d * rows + (d - 1) * half_rows, half_rows)],
                work.at[pl.ds(2 * 3 * rows + (d - 1) * half_rows, half_rows)],
                r.two_half_send.at[d],
                r.two_half_recv.at[d],
                (here, chips[3 - d]),
            )

        for d in (1, 2):
            two_far(d).start()
        two_near(0).start()
        two_own = local(r.own_rows, work.at[pl.ds(0, rows)], r.two_local.at[0])
        two_own.start()
        load(r.wide_rows, r.middle)
        rows_sent(MID, plane_rows)
        for d in range(n):
            cot_near(d).wait_recv()
            source = r.cotangent if d == 0 else r.cot_all.at[0, d]
            load(source, work.at[pl.ds(plane_rows + 2 * d * rows, rows)])
            load(r.cot_all.at[1, d], work.at[pl.ds(plane_rows + (2 * d + 1) * rows, rows)])
        keep_heads.wait()
        for d in range(1, n):
            every(feed_share(d), arrives)
        loaded()

        def rows_of_chip(t, arrive, half_way, pass_along):
            for at in range(n):

                @pl.when(t == at)
                def _():
                    for d in ((), (1, 2), (), ())[at]:
                        arrive(d).wait_recv()
                        half_way(d).start()
                        pass_along(d).start()
                    if at == 2:
                        half_way(1).wait_recv()
                        half_way(2).wait_recv()
                        pass_along(3).start()
                    pass_along(at).wait_recv()

        two_own.wait()

        def quarter_step(q, _):
            step(3 * q - 3)
            every(feed_own(q), waits)

            @pl.when(q > 0)
            def _():
                for d in range(1, n):
                    every(feed_far(q, d), arrives)

            @pl.when((q > 0) & (q < QUARTERS - 1))
            def _():
                for d in range(1, n):
                    every(feed_far(q + 1, d), starts)

            def forward(t, _):
                @pl.when(q == 0)
                def _():
                    rows_of_chip(t, two_far, two_half, two_near)

                    @pl.when(t == 2)
                    def _():
                        for d in range(1, n):
                            every(feed_far(1, d), starts)


                now = span(t * pair, pair)
                cot_now = pl.ds(pl.multiple_of(plane_rows + t * pair, pair), pair)
                both = jnp.zeros((pair, 2 * quarter), F32)
                hidden_grad = jnp.zeros((pair, quarter), F32)
                for j in range(n):
                    both += matmul(work[now, blocks[j]], feed[q, j, :wide, :])
                    hidden_grad += matmul_nt(work[cot_now, blocks[j]], feed[q, j, wide:, :])
                gate, up = both[:, :quarter], both[:, quarter:]
                share = 1.0 / (1.0 + jnp.exp(-gate))
                activated = gate * share
                results = (
                    activated * up,
                    hidden_grad * up * share * (1.0 + gate * (1.0 - share)),
                    hidden_grad * activated,
                )
                for w, result in enumerate(results):
                    heads[q * 3 + w, now, :] = result.astype(BF16)
                    turned[w, :, now] = result.T.astype(BF16)
                return 0

            lax.fori_loop(0, n, forward, 0)

            step(3 * q - 2)

            def one(w, _):
                t = 3 * q + w

                outer(t, turned[w], span(jnp.where(w == 0, plane_rows, 0), plane_rows))

                @pl.when(w > 0)
                def _():
                    staged(t - 1)

                return 0

            lax.fori_loop(0, 3, one, 0)
            step(3 * q - 1)
            staged(3 * q + 2)
            return 0

        lax.fori_loop(0, QUARTERS, quarter_step, 0)
        steps_done[0] = 3 * QUARTERS - 3
        for d in range(1, n):
            two_near(d).wait_send()
        for d in (1, 2):
            two_half(d).wait_send()

        def back_step(d):
            now = span(d * pair, pair)
            lefts = [
                jnp.concatenate([heads[q * 3 + 1, now, :], heads[q * 3 + 2, now, :]], axis=1)
                for q in range(QUARTERS)
            ]
            for j in range(n):
                total = jnp.zeros((pair, wide), F32)
                for q in range(QUARTERS):
                    total += matmul_nt(lefts[q], feed[q, j, :wide, :])
                work[now, blocks[j]] = total.astype(BF16)

        half = n // 2
        rows_reduced(BACK, 0, back_step, ticks=TICKS[0] + TICKS[1])

        def out_step(d):
            now = span(d * pair, pair)
            then = pl.ds(pl.multiple_of(plane_rows + d * pair, pair), pair)
            for j in range(n):
                total = jnp.zeros((pair, wide), F32)
                for q in range(QUARTERS):
                    total += matmul(heads[q * 3, now, :], feed[q, j, wide:, :])
                work[then, blocks[j]] = total.astype(BF16)

        rows_reduced(OUT, plane_rows, out_step, send=False, ticks=TICKS[2] + TICKS[3])

        for d in range(1, n):
            every(feed_share(d), leaves)
        load(r.kept, heads.at[pl.ds(0, kept_slots)])
        for j in range(n):
            query_source = r.query_weight.at[:, head_of(0)] if j == 0 else r.query_in.at[j]
            load(query_source, feed.at[0, j, pl.ds(0, wide), pl.ds(0, HD)])
            load(r.in_weight[j].at[pl.ds(0, wide)], feed.at[0, j, pl.ds(0, wide), pl.ds(HD, HD)])
            load(r.out_weight.at[j // 2, j % 2], feed.at[0, j, pl.ds(wide, HD)])

        rows_arrive(BACK, 0)
        loaded()
        for d in (1, 2):
            two_far(d).wait_send()
        two_near(0).wait_send()
        load(r.cotangent, r.own_rows)
        loaded()

        def second_use(at, back):
            grad = r.own_rows[at, :].astype(F32) + back
            r.wide_rows[at, :] = grad
            r.own_rows[at, :] = grad.astype(BF16)

        norm_rows_back(0, r.wide_rows, r.gains[1:2, :], second_use)

        def branch_far(d):
            return remote(
                r.own_rows,
                r.branch_all.at[d, side],
                r.branch_send.at[d],
                r.branch_recv.at[d],
                (here, chips[d]),
            )

        def branch_near(d):
            source = r.own_rows if d == 0 else r.branch_all.at[d, side]
            return remote(
                source,
                r.branch_all.at[d, side],
                r.branch_near_send.at[d],
                r.branch_near_recv.at[d],
                other_core,
            )

        def branch_half(d):
            some = pl.ds((d - 1) * half_rows, half_rows)
            return remote(
                r.branch_all.at[d, side, some],
                r.branch_all.at[3, side, some],
                r.branch_half_send.at[d],
                r.branch_half_recv.at[d],
                (here, chips[3 - d]),
            )

        for d in (1, 2):
            branch_far(d).start()
        branch_near(0).start()
        branch_own = local(r.own_rows, r.branch_all.at[0, side], r.branch_local.at[0])
        branch_own.start()
        gain_terms(1)
        advance(TICKS[4])
        rows_sent(BACK, 0)
        branch_own.wait()
        loaded()

        def scored(d, now):
            keys, values, scores = [], [], []
            for k in range(planes):
                a, b = heads[k, now, :], heads[planes + k, now, :]
                keys.append(jnp.where(side == 0, a, b))
                values.append(jnp.where(side == 0, b, a))
                score = matmul_nt(heads[query_slot, now, :], keys[k]) * scale
                scores.append(jnp.where(r.key_ids[d, k] <= r.query_ids[d], score, masked_score))
            top = functools.reduce(jnp.maximum, [jnp.max(s, axis=-1, keepdims=True) for s in scores])
            raised = [jnp.exp(s - top) for s in scores]
            inverse = 1.0 / sum(jnp.sum(e, axis=-1, keepdims=True) for e in raised)
            return keys, values, [e * inverse for e in raised]

        def attend_back(d, _):
            rows_of_chip(d, branch_far, branch_half, branch_near)

            @pl.when(d == half)
            def _():
                for at in (3, 1, 2):
                    row_send(OUT, plane_rows, at)

            now = span(d * pair, pair)
            for c in range(2):
                load(r.branch_all.at[d, c], work.at[pl.ds(pl.multiple_of((2 * d + c) * rows, rows), rows)])
            loaded()
            query = heads[query_slot, now, :]
            attended_grad = jnp.zeros((pair, HD), F32)
            for j in range(n):
                attended_grad += matmul_nt(work[now, blocks[j]], feed[0, j, wide:, :])
            attended_grad = attended_grad.astype(BF16)
            keys, values, probs = scored(d, now)
            low = [p.astype(BF16) for p in probs]
            shares = [matmul_nt(attended_grad, values[k]) for k in range(planes)]
            delta = sum(
                jnp.sum(low[k].astype(F32) * shares[k], axis=-1, keepdims=True) for k in range(planes)
            )
            query_grad = jnp.zeros((pair, HD), F32)
            for k in range(planes):
                score_grad = (probs[k] * (shares[k] - delta)).astype(BF16)
                query_grad += matmul(score_grad, keys[k])
                key_grad = matmul_tn(score_grad, query) * scale
                value_grad = matmul_tn(low[k], attended_grad)
                heads[k, now, :] = jnp.where(side == 0, key_grad, value_grad).astype(BF16)
                heads[planes + k, now, :] = jnp.where(side == 0, value_grad, key_grad).astype(BF16)
            query_grad = query_grad * scale
            query_grad = query_grad * r.tables[0] + turn_back(query_grad * r.tables[1])
            heads[query_grad_slot, now, :] = query_grad.astype(BF16)
            return 0

        lax.fori_loop(0, half, attend_back, 0)
        advance(TICKS[5])
        lax.fori_loop(half, n, attend_back, 0)

        def kv_hand_over(k):
            return remote(
                heads.at[planes + k], r.kv_other.at[k], r.kv_send.at[k], r.kv_recv.at[k], other_core
            )

        def kv_load(source, slot):
            return local(source, r.kv_some.at[slot], r.kv_sem.at[slot])

        def kv_add(k, slot):
            def some(c, _):
                at = span(c * 64, 64)
                heads[k, at, :] = heads[k, at, :] + r.kv_some[slot, at, :]
                return 0

            lax.fori_loop(0, plane_rows // 64, some, 0)

        def kv_down(k):
            return remote(heads.at[k], r.kv_down.at[k], r.down_send.at[k], r.down_recv.at[k], below)

        def kv_up(k):
            return remote(
                heads.at[planes - k], r.kv_up.at[k], r.up_send.at[k], r.up_recv.at[k], above
            )

        order = list(range(planes - 1, -1, -1))
        for k in order:
            kv_hand_over(k).start()
        for at, k in enumerate(order):
            kv_hand_over(k).wait_recv()
            kv_load(r.kv_other.at[k], at % 2).start()
            kv_load(r.kv_other.at[k], at % 2).wait()
            kv_add(k, at % 2)

        def kv_send(k):
            @pl.when(z >= k)
            def _():
                kv_down(k).start()

            @pl.when(z + k < planes)
            def _():
                kv_up(k).start()

        def kv_receive(k, down_to, up_to):
            @pl.when((z + 1 >= k) & (z + 1 < planes))
            def _():
                kv_down(k).wait_recv()
                if down_to is not None:
                    copy = kv_load(r.kv_down.at[k], 0)
                    copy.start()
                    copy.wait()
                    kv_add(down_to, 0)

            @pl.when((z >= 1) & (z - 1 + k < planes))
            def _():
                kv_up(k).wait_recv()
                if up_to is not None:
                    copy = kv_load(r.kv_up.at[k], 1)
                    copy.start()
                    copy.wait()
                    kv_add(up_to, 1)

        kv_send(3)
        rows_sent(OUT, plane_rows)
        load(work.at[pl.ds(plane_rows, rows)], r.out_own)
        loaded()
        load(r.normed, work.at[pl.ds(plane_rows, plane_rows)])
        low_half, high_half = pl.ds(0, plane_rows), pl.ds(plane_rows, plane_rows)
        advance(TICKS[6])
        turned[0] = heads[attended_slot].astype(F32).T.astype(BF16)
        turned[1] = heads[query_grad_slot].astype(F32).T.astype(BF16)
        loaded()
        outer(query_at, turned[1], high_half)
        outer(output_at, turned[0], low_half)
        staged(query_at)
        staged(output_at)
        advance(TICKS[7])
        kv_receive(3, 2, 2)
        kv_send(2)
        advance(TICKS[8])
        kv_receive(2, 1, 3)
        kv_send(1)
        advance(TICKS[9])
        kv_receive(1, 0, 0)

        def kv_back(d, _):
            now = span(d * pair, pair)
            grad = heads[0, now, :].astype(F32)
            grad = grad * r.tables[2] + turn_back(grad * r.tables[3])
            heads[kv_grad_slot, now, :] = grad.astype(BF16)
            turned[2, :, now] = grad.T.astype(BF16)
            return 0

        lax.fori_loop(0, n, kv_back, 0)
        outer(kv_at, turned[2], high_half)

        def project_back(d):
            now = span(d * pair, pair)
            left = jnp.concatenate([heads[query_grad_slot, now, :], heads[kv_grad_slot, now, :]], axis=1)
            for j in range(n):
                put_rows(0, d, matmul_nt(left, feed[0, j, :wide, :]).astype(BF16), blocks[j])

        staged(kv_at)
        rows_reduced(ONE, 0, project_back)
        advance(TICKS[10])

        for d in (1, 2):
            branch_far(d).wait_send()
            branch_half(d).wait_send()
        for d in range(n):
            branch_near(d).wait_send()
        load(r.tokens, r.own_rows)
        rows_arrive(ONE, 0)
        loaded()

        def first_use(at, back):
            r.wide_rows[at, :] = r.wide_rows[at, :] + back

        norm_rows_back(0, r.own_rows, r.gains[0:1, :], first_use)
        load(r.wide_rows, r.tokens_grad)
        gain_terms(0)

        def gain_copy(at, source, target, peer):
            return remote(source, target, r.gain_send.at[at], r.gain_recv.at[at], peer)

        def gain_far(d):
            return gain_copy(d, r.gain_mine.at[d], r.gain_far.at[d], (here, chips[d]))

        def gain_hop(s, peer):
            return gain_copy(n + s, r.gain_sum.at[s], r.gain_in.at[s], peer)

        for d in range(1, n):
            gain_far(d).start()
        advance(TICKS[11])
        for d in range(1, n):
            gain_far(d).wait()
        r.gain_sum[0] = r.gain_mine[0] + r.gain_far[1] + r.gain_far[2] + r.gain_far[3]
        gain_hop(0, other_core).start()
        gain_hop(0, other_core).wait()
        r.gain_sum[1] = r.gain_sum[0] + r.gain_in[0]

        @pl.when(is_end)
        def _():
            gain_hop(1, partner).start()
            gain_hop(1, partner).wait_send()

        advance(TICKS[12])

        @pl.when(is_middle)
        def _():
            gain_hop(1, partner).wait_recv()
            r.gain_sum[2] = r.gain_sum[1] + r.gain_in[1]
            gain_hop(2, other_middle).start()
            gain_hop(2, other_middle).wait()
            r.gain_sum[3] = r.gain_sum[2] + r.gain_in[2]
            gain_hop(3, partner).start()
            gain_hop(3, partner).wait_send()

        @pl.when(is_end)
        def _():
            gain_hop(3, partner).wait_recv()
            r.gain_sum[3] = r.gain_in[3]

        load(r.gain_sum.at[3], r.gain_out)

        loaded()
        load(r.middle, r.wide_rows)
        load(r.out_own, r.own_rows)
        rows_arrive(OUT, plane_rows)
        loaded()

        def last_rows(c, _):
            at = span(c * few, few)
            total = r.wide_rows[at, :] + r.own_rows[at, :].astype(F32)
            for d in range(n):
                total += r.some_rows[d, at, :].astype(F32)
            r.own_rows[at, :] = total.astype(BF16)
            return 0

        lax.fori_loop(0, rows // few, last_rows, 0)
        load(r.own_rows, r.output)
        advance(units + 9 - steps_done[0])

        loaded()
        rows_sent(ONE, 0)
        for q in range(1, QUARTERS):
            for d in range(1, n):
                every(feed_far(q, d), leaves)
        for d in range(1, n):
            every(feed_half(d), leaves)
        for d in (1, 2):
            token_half(d).wait_send()
            cot_far(d).wait_send()
            cot_half(d).wait_send()
        for d in range(1, n):
            query_far(d).wait_send()
            out_far(d).wait_send()
        for d in range(n - 1):
            token_near(d).wait_send()
        for d in range(n):
            cot_near(d).wait_send()
        for k in range(planes):
            kv_hand_over(k).wait_send()
        for k in range(1, planes):

            @pl.when(z >= k)
            def _():
                kv_down(k).wait_send()

            @pl.when(z + k < planes)
            def _():
                kv_up(k).wait_send()

        finish()

    arrays = jax.tree.leaves((in_hbm, in_vmem))
    results = pl.pallas_call(
        backward,
        out_shape=jax.tree.leaves(out_hbm),
        in_specs=[pl.BlockSpec(memory_space=pl.ANY)] * len(jax.tree.leaves(in_hbm))
        + [pl.BlockSpec(memory_space=pltpu.VMEM)] * len(in_vmem),
        out_specs=[pl.BlockSpec(memory_space=pl.ANY)] * len(out_hbm),
        scratch_shapes=list(scratch.values()),
        cost_estimate=cost(30 * plane_rows * width * part, arrays, [unit_array] * 6),
        compiler_params=pltpu.CompilerParams(
            collective_id=0, has_side_effects=True, vmem_limit_bytes=63 * 1024 * 1024
        ),
        name="backward",
    )(*arrays)
    results = types.SimpleNamespace(**jax.tree.unflatten(jax.tree.structure(out_hbm), results))
    owned_tiles, near_tiles = (
        a.reshape(tiles_count, n, quarter, wide) for a in (results.owned, results.near)
    )

    def place(
        me_ref, own_ref, near_ref, gate, up, down, query, out, key, value, taken, turned, straight, in_sem, out_sem
    ):
        chip, side = me_ref[0], me_ref[1]
        steps = 2 * n

        def take(s, t, source):
            return pltpu.make_async_copy(source.at[t, s // 2], taken.at[t], in_sem.at[t])

        def start_taking(s, t):
            for source, e in ((own_ref, 0), (near_ref, 1)):

                @pl.when(s % 2 == e)
                def _():
                    take(s, t, source).start()

        def is_straight(t):
            return t == output_at or (t < query_at and t % 3 == 0)

        def goal(s, t):
            owner = 2 * (chip ^ (s // 2)) + (side ^ (s % 2))
            if t == query_at:
                return query.at[:, column(owner, HD)]
            if t == output_at:
                return out.at[column(owner, HD)]
            here = column(owner * QUARTERS + t // 3, quarter)
            return (down.at[here], gate.at[:, here], up.at[:, here])[t % 3]

        def put(s, t, use):
            source = straight.at[t // 3] if is_straight(t) else turned.at[t]
            if t != kv_at:
                use(pltpu.make_async_copy(source, goal(s, t), out_sem.at[t]))
                return
            for target, e in ((key, 0), (value, 1)):

                @pl.when((side + s) % 2 == e)
                def _():
                    there = target.at[:, column(chip ^ (s // 2), HD)]
                    use(pltpu.make_async_copy(source, there, out_sem.at[t]))

        for t in range(tiles_count):
            start_taking(0, t)

        def one(s, _):
            for t in range(tiles_count):
                take(s, t, own_ref).wait()

                @pl.when(s > 0)
                def _():
                    put(s - 1, t, lambda copy: copy.wait())

                if is_straight(t):
                    straight[t // 3] = taken[t].astype(F32)
                else:
                    turned[t] = taken[t].T.astype(F32)
                put(s, t, lambda copy: copy.start())

                @pl.when(s + 1 < steps)
                def _():
                    start_taking(s + 1, t)

            return 0

        lax.fori_loop(0, steps, one, 0)
        for t in range(tiles_count):
            put(steps - 1, t, lambda copy: copy.wait())

    in_place = pl.BlockSpec(memory_space=pl.ANY)
    placed = pl.pallas_call(
        place,
        out_shape=[
            shape(a.shape, F32)
            for a in (
                gate_weight,
                up_weight,
                down_weight,
                query_weight,
                output_weight,
                key_weight,
                value_weight,
            )
        ],
        in_specs=[pl.BlockSpec(memory_space=pltpu.SMEM), in_place, in_place],
        out_specs=[in_place] * 7,
        scratch_shapes=[
            pltpu.VMEM((tiles_count, quarter, wide), BF16),
            pltpu.VMEM((tiles_count, wide, quarter), F32),
            pltpu.VMEM((QUARTERS + 1, quarter, wide), F32),
            dma((tiles_count,)),
            dma((tiles_count,)),
        ],
        compiler_params=pltpu.CompilerParams(vmem_limit_bytes=VMEM_BYTES),
        name="place",
    )(me, owned_tiles, near_tiles)
    gate_grad, up_grad, down_grad, query_grad, output_grad, key_grad, value_grad = placed

    return (
        results.output[None],
        results.tokens_grad[None],
        query_grad,
        key_grad,
        value_grad,
        output_grad,
        results.gain_out[0],
        gate_grad,
        up_grad,
        down_grad,
        results.gain_out[1],
    )


def solution(mesh):
    chips, pieces = mesh.shape["fsdp"], mesh.shape["ctx"]
    one_head_each = 2 * chips == H and chips == KVH and pieces == 8
    return jax.shard_map(
        plane_layer if one_head_each else ring_layer,
        mesh=mesh,
        in_specs=(
            P("fsdp", "ctx", None),
            P("fsdp", None),
            P("fsdp", None),
            P("fsdp", None),
            P(None, "fsdp"),
            P("fsdp"),
            P("fsdp", None),
            P("fsdp", None),
            P(None, "fsdp"),
            P("fsdp"),
            P("fsdp", "ctx", None),
            P(),
            P(),
        ),
        out_specs=(
            P("fsdp", "ctx", None),
            P("fsdp", "ctx", None),
            P("fsdp", None),
            P("fsdp", None),
            P("fsdp", None),
            P(None, "fsdp"),
            P("fsdp"),
            P("fsdp", None),
            P("fsdp", None),
            P(None, "fsdp"),
            P("fsdp"),
        ),
        check_vma=False,
    )
```
